32 devices in a mesh: dp: 8 (over y, x, core), mp: 4 (over z).
Axes of the slice: x: 2, y: 2, z: 4, core: 2. Of those that a mesh axis runs over, the one named last changes fastest.
Arguments:
- patches: bfloat16 [256, 256, 1152], P('dp', 'mp'), may hold values from -6 to 6
- cotangent: bfloat16 [128, 256, 1152], P('dp', 'mp'), may hold values from -6 to 6
- time_bins: int32 [256], P('dp'), may hold values from 0 to 15
- labels: int32 [256], P('dp'), may hold values from 0 to 999
- image_counts: int32 [8], replicated, may hold values from 1 to 32, 128 in all
- dest_perm: int32 [8], replicated, may hold values from 0 to 7, each once
- time_table: bfloat16 [16, 1152], replicated, may hold values from -4 to 4
- class_table: bfloat16 [1000, 1152], replicated, may hold values from -4 to 4
- ada_weight: bfloat16 [1152, 6, 1152], replicated, may hold values from -0.09375 to 0.09375
- qkv_weight: bfloat16 [1152, 3, 1152], P(None, None, 'mp'), may hold values from -0.1875 to 0.1875
- norm_gains: bfloat16 [2, 72], replicated, may hold values from 0.59765625 to 1.59375
- out_weight: bfloat16 [1152, 1152], P('mp'), may hold values from -0.75 to 0.75
- expand_weight: bfloat16 [1152, 2, 3072], P(None, None, 'mp'), may hold values from -0.1875 to 0.1875
- down_weight: bfloat16 [3072, 1152], P('mp'), may hold values from -0.109375 to 0.109375
Outputs:
- result: bfloat16 [128, 256, 1152], P('dp', 'mp')
- patch_grad: bfloat16 [256, 256, 1152], P('dp', 'mp')
- time_grad: float32 [16, 1152], P(None, 'dp')
- class_grad: float32 [1000, 1152], P(None, 'dp')
- ada_grad: float32 [1152, 6, 1152], P('dp', None, 'mp')
- qkv_grad: float32 [1152, 3, 1152], P('dp', None, 'mp')
- gains_grad: float32 [2, 72], replicated
- out_grad: float32 [1152, 1152], P('mp', 'dp')
- expand_grad: float32 [1152, 2, 3072], P('dp', None, 'mp')
- down_grad: float32 [3072, 1152], P('mp', 'dp')
The draws below stay inside these ranges and needn't reach their ends.
Inputs may be any that keep to these rules, and one draw needn't show every extreme that they name: `image_counts`: entry s counts the live slots of dp index s, which are its first ones; the entries sum to 128, and one index has all 32 slots live. `dest_perm`: each dp index appears once.
All inputs are finite; a program needn't handle non-finite values.
Results may differ from the reference program's by a relative error of at most 0.02.
Values may be sent and summed in bfloat16 or wider, within the bound.
No kernel may reach another device: no remote copies, remote signals or barrier semaphores. Data moves between devices by JAX's collectives and lax.ppermute only.
A program may use at most 320 MiB of HBM per device.

```python
import math
import jax
import jax.numpy as jnp
import numpy as np
from jax import lax

D = 1152
H = 16
HD = 72
FF = 3072
GRID = 16
NCLS = 1000
NBINS = 16
IMG_DEV = 16
S = 256
CAP = 32
IMAGES = 128
N_DP = 8


def draw_time_bins(key, part):
    key = jax.random.fold_in(key, 11)
    owners = jnp.arange(N_DP * CAP) // CAP
    lowest = owners * NBINS // N_DP
    jitter = jax.random.randint(key, (N_DP * CAP,), 0, NBINS // 4)
    return jnp.minimum(lowest + jitter, NBINS - 1).astype(jnp.int32)


def touch_ends(drawn, key, least, high):
    longest = drawn.shape.index(max(drawn.shape))
    spots = []
    for shift in (0, 1):
        where = [jax.random.randint(jax.random.fold_in(key, axis), (), 0, length) for axis, length in enumerate(drawn.shape)]
        where[longest] = (where[longest] + shift) % drawn.shape[longest]
        spots.append(tuple(where))
    return drawn.at[spots[0]].set(least).at[spots[1]].set(high)


def steps_of(stream_key, shape, split, low, top_value):
    factor_of = 1.0
    for axis_at, shards_of in split:
        steps = jax.random.uniform(jax.random.fold_in(jax.random.fold_in(stream_key, 6), axis_at), (shards_of,), jnp.float32, low / len(split), top_value / len(split))
        factor_of = factor_of * jnp.repeat(jnp.exp(steps), shape[axis_at] // shards_of).reshape((-1,) + (1,) * (len(shape) - 1 - axis_at))
    return factor_of


def split_up(number_of, total, reach, skew):
    weights = [(1 << 20) // math.isqrt(standing ** skew) + 1 for standing in range(2, number_of + 1)]
    rest, holding = total - reach - (number_of - 1), [1] * (number_of - 1)
    while rest > 0:
        free = [i for i in range(number_of - 1) if holding[i] < reach]
        whole, left = sum([weights[i] for i in free]), rest
        for i in free:
            addition = min(reach - holding[i], max(1, left * weights[i] // whole), rest)
            holding[i] = holding[i] + addition
            rest = rest - addition
    return np.array([reach] + holding)


def uneven(key, number_of, total, bound, skew):
    if number_of == 2:
        one = jax.random.randint(key, (), max(1, total - bound), min(bound, total - 1) + 1)
        return jnp.stack([one, total - one])
    lengths = jnp.asarray(split_up(number_of, total, bound, skew), jnp.int32)
    twos = (number_of - 1) // 2
    source_of, taker = lengths[1:1 + 2 * twos:2], lengths[2:2 + 2 * twos:2]
    room = jnp.minimum(source_of - 1, bound - taker)
    passed = jax.random.randint(jax.random.fold_in(key, 1), (twos,), 0, 1 << 20) % (room + 1)
    lengths = lengths.at[1:1 + 2 * twos:2].set(source_of - passed).at[2:2 + 2 * twos:2].set(taker + passed)
    return lengths[jax.random.permutation(jax.random.fold_in(key, 2), number_of)]


def bell_draw(rng, extent, scale, most, shards=(), held_as=jnp.bfloat16):
    level = steps_of(rng, extent, shards, -0.22, 0.18) if shards else 1.0
    array = jax.random.normal(rng, extent, jnp.float32) * scale * level
    return jnp.minimum(jnp.maximum(array, -most), most).astype(held_as)


def setup_inputs(seed: int = 0) -> dict:
    key_list = jax.random.split(jax.random.key(seed), 15)
    patches = bell_draw(key_list[0], (N_DP * CAP, S, D), 1.0, 6.0, ((0, 8), (1, 4)))
    cotangent = bell_draw(key_list[1], (IMAGES, S, D), 1.0, 6.0, ((0, 8), (1, 4)))
    time_bins = draw_time_bins(jax.random.fold_in(key_list[14], 71), 0)
    labels = touch_ends(jax.random.randint(key_list[3], (N_DP * CAP,), 0, NCLS), jax.random.fold_in(key_list[3], 1), 0, NCLS - 1).astype(jnp.int32)
    image_counts = uneven(key_list[4], N_DP, IMAGES, CAP, 1).astype(jnp.int32)
    dest_perm = jax.random.permutation(key_list[5], N_DP).astype(jnp.int32)
    time_table = bell_draw(key_list[6], (NBINS, D), 1.0, 4.0)
    class_table = bell_draw(key_list[7], (NCLS, D), 1.0, 4.0)
    ada_weight = bell_draw(key_list[8], (D, 6, D), (4 * D) ** -0.5, 0.09375)
    qkv_weight = bell_draw(key_list[9], (D, 3, D), D ** -0.5, 0.1875, ((2, 4),))
    norm_gains = jnp.clip(jax.random.uniform(key_list[10], (2, HD), jnp.float32, 0.59765625, 1.59375), 0.59765625, 1.59375).astype(jnp.bfloat16)
    out_weight = bell_draw(key_list[11], (D, D), (D // 16) ** -0.5, 0.75, ((0, 4),))
    expand_weight = bell_draw(key_list[12], (D, 2, FF), D ** -0.5, 0.1875, ((2, 4),))
    down_weight = bell_draw(key_list[13], (FF, D), FF ** -0.5, 0.109375, ((0, 4),))
    return dict(patches=patches, cotangent=cotangent, time_bins=time_bins, labels=labels, image_counts=image_counts, dest_perm=dest_perm, time_table=time_table, class_table=class_table, ada_weight=ada_weight, qkv_weight=qkv_weight, norm_gains=norm_gains, out_weight=out_weight, expand_weight=expand_weight, down_weight=down_weight)


@jax.custom_vjp
def low(v):
    return lax.optimization_barrier(v.astype(jnp.bfloat16)).astype(jnp.float32)

@jax.custom_vjp
def low_back(v):
    return v

def low_keep(v):
    return (low(v), None)

def low_pass(kept, grad):
    return (grad,)

def back_keep(v):
    return (v, None)

def back_low(kept, grad):
    return (low(grad),)
low.defvjp(low_keep, low_pass)
low_back.defvjp(back_keep, back_low)
highest = lax.Precision.HIGHEST
epsilon = 1e-06
rope_base = 10000.0

def rms_scale(values, scaling, shifting):
    return values * lax.rsqrt(lax.optimization_barrier(jnp.mean(values * values, -1, keepdims=True)) + epsilon) * (1.0 + scaling) + shifting

def head_norm(values):
    return values * lax.rsqrt(lax.optimization_barrier(jnp.mean(values * values, -1, keepdims=True)) + epsilon)

def rope_tables(length):
    quarter = HD // 4
    position = jnp.arange(length)
    row_pos = (position // GRID).astype(jnp.float32)
    col_pos = (position % GRID).astype(jnp.float32)
    frequency = rope_base ** (-jnp.arange(quarter).astype(jnp.float32) / quarter)
    row_angle = row_pos[:, None] * frequency[None, :]
    col_angle = col_pos[:, None] * frequency[None, :]
    return (jnp.cos(row_angle), jnp.sin(row_angle), jnp.cos(col_angle), jnp.sin(col_angle))

def rotate(half_vec, cosine_tab, sine_tab):
    quarter = cosine_tab.shape[1]
    front_part = half_vec[..., :quarter]
    back_part = half_vec[..., quarter:]
    cosine_tab = cosine_tab[None, :, None, :]
    sine_tab = sine_tab[None, :, None, :]
    return jnp.concatenate([front_part * cosine_tab - back_part * sine_tab, front_part * sine_tab + back_part * cosine_tab], -1)

def apply_rope(values, tables):
    halfway = values.shape[-1] // 2
    return jnp.concatenate([rotate(values[..., :halfway], tables[0], tables[1]), rotate(values[..., halfway:], tables[2], tables[3])], -1)

def prepare(queries, key_vecs, gains, tables):
    query_pre = apply_rope(head_norm(queries) * gains[0], tables) * HD ** (-0.5)
    key_pre = apply_rope(head_norm(key_vecs) * gains[1], tables)
    return (query_pre, key_pre)

def swish_mul(gate_part, up_part):
    return jax.nn.silu(gate_part) * up_part

def layer_forward(latent, bin_ids, label_ids, time_table, class_table, ada_weight, qkv_weight, norm_gains, out_weight, expand_weight, down_weight):
    groups = latent.shape[0]
    length = latent.shape[1]
    tables = rope_tables(length)
    condition = low_back(low(time_table[bin_ids] + class_table[label_ids]))
    silu_cond = low(jax.nn.silu(condition))
    modulation = low_back(jnp.einsum('gd,dke->gke', silu_cond, ada_weight, precision=highest))
    shift_one = modulation[:, 0][:, None, :]
    scale_one = modulation[:, 1][:, None, :]
    gate_one = modulation[:, 2][:, None, :]
    shift_two = modulation[:, 3][:, None, :]
    scale_two = modulation[:, 4][:, None, :]
    gate_two = modulation[:, 5][:, None, :]
    normed = low(rms_scale(latent, scale_one, shift_one))
    projected = low_back(jnp.einsum('gsd,dke->gske', normed, qkv_weight, precision=highest))
    heads_shape = (groups, length, H, HD)
    queries = projected[:, :, 0].reshape(heads_shape)
    key_vecs = projected[:, :, 1].reshape(heads_shape)
    values_raw = projected[:, :, 2].reshape(heads_shape)
    query_pre, key_pre = prepare(queries, key_vecs, norm_gains, tables)
    query_low = low(query_pre)
    key_low = low(key_pre)
    value_low = low(values_raw)
    scores = low_back(jnp.einsum('gqhe,gkhe->ghqk', query_low, key_low, precision=highest))
    probs_low = low(jax.nn.softmax(scores, axis=-1))
    attended = low_back(low(jnp.einsum('ghqk,gkhe->gqhe', probs_low, value_low, precision=highest))).reshape(groups, length, D)
    branch_one = low_back(jnp.einsum('gsd,de->gse', attended, out_weight, precision=highest))
    middle = latent + gate_one * branch_one
    normed_two = low(rms_scale(middle, scale_two, shift_two))
    expanded = low_back(jnp.einsum('gsd,dkf->gskf', normed_two, expand_weight, precision=highest))
    hidden = low(swish_mul(expanded[:, :, 0], expanded[:, :, 1]))
    branch_two = low_back(jnp.einsum('gsf,fd->gsd', hidden, down_weight, precision=highest))
    return middle + gate_two * branch_two

def reference(patches, cotangent, time_bins, labels, image_counts, dest_perm, time_table, class_table, ada_weight, qkv_weight, norm_gains, out_weight, expand_weight, down_weight):
    slot_total = N_DP * CAP
    slot_ids = jnp.arange(slot_total)
    owners = slot_ids // CAP
    slot_live = slot_ids % CAP < image_counts[owners]
    bin_hot = (time_bins[:, None] == jnp.arange(NBINS)[None, :]) & slot_live[:, None]
    bin_totals = lax.optimization_barrier(jnp.sum(bin_hot.astype(jnp.float32), axis=0))
    starts = jnp.cumsum(image_counts) - image_counts
    finish = starts + image_counts
    matches = (dest_perm[:, None] == jnp.arange(N_DP)[None, :]).astype(jnp.int32)
    inverse = lax.optimization_barrier(jnp.sum(jnp.arange(N_DP)[:, None] * matches, axis=0))
    balanced = jnp.arange(IMAGES)
    rank_ids = balanced % IMG_DEV * N_DP + inverse[balanced // IMG_DEV]
    source = lax.optimization_barrier(jnp.sum((finish[None, :] <= rank_ids[:, None]).astype(jnp.int32), axis=1))
    sources = (source * CAP + rank_ids - starts[source]).astype(jnp.int32)
    bal_bins = time_bins[sources]
    bal_labels = labels[sources]
    weights = IMAGES / (NBINS * bin_totals[bal_bins])
    latent = patches[sources].astype(jnp.float32)
    out_cot = cotangent.astype(jnp.float32) * weights[:, None, None]
    params = (time_table.astype(jnp.float32), class_table.astype(jnp.float32), ada_weight.astype(jnp.float32), qkv_weight.astype(jnp.float32), norm_gains.astype(jnp.float32), out_weight.astype(jnp.float32), expand_weight.astype(jnp.float32), down_weight.astype(jnp.float32))

    def group_step(totals, group_items):
        latent_g, bins_g, labels_g, cot_g = group_items

        def forward(latent_in, time_in, class_in, ada_in, qkv_in, gains_in, out_in, expand_in, down_in):
            return layer_forward(latent_in, bins_g, labels_g, time_in, class_in, ada_in, qkv_in, gains_in, out_in, expand_in, down_in)
        output, pullback = jax.vjp(forward, latent_g, *params)
        gradients = pullback(cot_g)
        totals = jax.tree.map(lambda running, addend: running + addend, totals, tuple(gradients[1:]))
        return (totals, (output.astype(jnp.bfloat16), gradients[0]))
    zero_grads = tuple((jnp.zeros_like(param_arr) for param_arr in params))
    group_items = (latent.reshape(N_DP, IMG_DEV, S, D), bal_bins.reshape(N_DP, IMG_DEV), bal_labels.reshape(N_DP, IMG_DEV), out_cot.reshape(N_DP, IMG_DEV, S, D))
    totals, (outputs, latent_grads) = lax.scan(group_step, zero_grads, group_items)
    result = outputs.reshape(IMAGES, S, D)
    patch_grad = jnp.zeros((slot_total, S, D), jnp.float32).at[sources].set(latent_grads.reshape(IMAGES, S, D)).astype(jnp.bfloat16)
    return (result, patch_grad, totals[0], totals[1], totals[2], totals[3], totals[4], totals[5], totals[6], totals[7])
```

```python
import jax
import jax.numpy as jnp
from jax import lax
from jax.experimental import pallas as pl
from jax.experimental.pallas import tpu as pltpu
from jax.sharding import PartitionSpec as P

GRID = 16
NCLS = 1000
NBINS = 16

epsilon = 1e-06
rope_base = 10000.0
f32 = jnp.float32
bf16 = jnp.bfloat16


def rms_scale(values, scaling, shifting):
    return (
        values * lax.rsqrt(jnp.mean(values * values, -1, keepdims=True) + epsilon) * (1.0 + scaling)
        + shifting
    )


def feature_order(head_dim):
    quarter = head_dim // 4
    firsts = list(range(quarter)) + list(range(2 * quarter, 3 * quarter))
    cut = len(firsts) // 8 * 8
    seconds = [i + quarter for i in firsts]
    return firsts[:cut] + seconds[:cut] + firsts[cut:] + seconds[cut:], cut


def rope_tables(length, head_dim):
    quarter = head_dim // 4
    order, cut = feature_order(head_dim)
    position = jnp.arange(length)
    places = jnp.stack([position // GRID, position % GRID]).astype(f32)
    frequency = rope_base ** (-jnp.arange(quarter).astype(f32) / quarter)
    angle = (frequency[None, :, None] * places[:, None, :]).reshape(2 * quarter, length)
    cosine, sine = jnp.cos(angle), jnp.sin(angle)
    cos_tab = jnp.concatenate([cosine[:cut], cosine[:cut], cosine[cut:], cosine[cut:]])
    sin_tab = jnp.concatenate([-sine[:cut], sine[:cut], -sine[cut:], sine[cut:]])
    return cos_tab, sin_tab


def partner(values, cut):
    rest = values[2 * cut :]
    half = rest.shape[0] // 2
    return jnp.concatenate(
        [values[cut : 2 * cut], values[:cut], pltpu.roll(rest, half, 0)], axis=0
    )


def head_scale(values):
    return lax.rsqrt(jnp.mean(values * values, axis=0, keepdims=True) + epsilon)


def dot_00(a, b):
    return lax.dot_general(a, b, (((0,), (0,)), ((), ())), preferred_element_type=f32)


def dot_11(a, b):
    return lax.dot_general(a, b, (((1,), (1,)), ((), ())), preferred_element_type=f32)


def dot_10(a, b):
    return lax.dot_general(a, b, (((1,), (0,)), ((), ())), preferred_element_type=f32)


def softmax_first(scores):
    shifted = jnp.exp(scores - jnp.max(scores, axis=0, keepdims=True))
    return shifted * (1.0 / jnp.sum(shifted, axis=0, keepdims=True))


def attend_kernel(proj_ref, gains_ref, cos_ref, sin_ref, out_ref):
    head_dim = gains_ref.shape[1]
    cut = feature_order(head_dim)[1]
    cos_tab, sin_tab = cos_ref[...], sin_ref[...]
    outs = []
    for head in range(proj_ref.shape[2] // head_dim):
        rows = slice(head * head_dim, (head + 1) * head_dim)
        lows = []
        for kind in range(2):
            raw = proj_ref[0, kind, rows, :]
            scaled = raw * head_scale(raw) * gains_ref[kind]
            turned = scaled * cos_tab + partner(scaled, cut) * sin_tab
            lows.append(turned.astype(bf16))
        value_low = proj_ref[0, 2, rows, :].astype(bf16)
        probs = softmax_first(dot_00(lows[1], lows[0]))
        outs.append(dot_10(value_low, probs.astype(bf16)))
    out_ref[0] = jnp.concatenate(outs, axis=0).astype(bf16)


def attend_back_kernel(
    proj_ref, cot_ref, gains_ref, cos_ref, sin_ref, out_ref, gain_grad_ref
):
    head_dim = gains_ref.shape[1]
    cut = feature_order(head_dim)[1]
    cos_tab, sin_tab = cos_ref[...], sin_ref[...]

    @pl.when((pl.program_id(0) == 0) & (pl.program_id(1) == 0))
    def _():
        gain_grad_ref[...] = jnp.zeros_like(gain_grad_ref)

    outs = [[], [], []]
    cot_all = cot_ref[0].astype(f32)
    for head in range(proj_ref.shape[2] // head_dim):
        rows = slice(head * head_dim, (head + 1) * head_dim)
        lows, units, scales = [], [], []
        for kind in range(2):
            raw = proj_ref[0, kind, rows, :]
            scale = head_scale(raw)
            unit = raw * scale
            scaled = unit * gains_ref[kind]
            turned = scaled * cos_tab + partner(scaled, cut) * sin_tab
            lows.append(turned.astype(bf16))
            units.append(unit)
            scales.append(scale)
        value_low = proj_ref[0, 2, rows, :].astype(bf16)
        cot_low = cot_all[rows].astype(bf16)
        probs = softmax_first(dot_00(lows[1], lows[0]))
        prob_grad = dot_00(value_low, cot_low)
        outs[2].append(dot_11(cot_low, probs.astype(bf16)))
        mean = jnp.sum(probs * prob_grad, axis=0, keepdims=True)
        score_low = (probs * (prob_grad - mean)).astype(bf16)
        turned_grads = (dot_10(lows[1], score_low), dot_11(lows[0], score_low))
        for kind in range(2):
            grad = turned_grads[kind]
            grad = grad * cos_tab + partner(grad * sin_tab, cut)
            gain_grad_ref[kind] += grad * units[kind]
            grad = grad * gains_ref[kind]
            along = jnp.mean(grad * units[kind], axis=0, keepdims=True)
            outs[kind].append(scales[kind] * (grad - units[kind] * along))
    for kind in range(3):
        out_ref[0, kind] = jnp.concatenate(outs[kind], axis=0).astype(bf16)


def attend_specs(groups, rows, own, length, head_dim):
    proj = pl.BlockSpec((1, 3, rows, length), lambda g, i: (g, 0, 0, i))
    att = pl.BlockSpec((1, rows, length), lambda g, i: (g, 0, i))
    gains = pl.BlockSpec((2, head_dim, 1), lambda g, i: (0, 0, 0))
    table = pl.BlockSpec((head_dim, length), lambda g, i: (0, 0))
    grads = pl.BlockSpec((2, head_dim, length), lambda g, i: (0, 0, 0))
    return proj, att, gains, table, grads


def attend(proj, gains, tables, own):
    groups, _, rows, tokens = proj.shape
    length, head_dim = tokens // own, gains.shape[1]
    proj_s, att_s, gains_s, table_s, _ = attend_specs(groups, rows, own, length, head_dim)
    return pl.pallas_call(
        attend_kernel,
        grid=(groups, own),
        in_specs=[proj_s, gains_s, table_s, table_s],
        out_specs=att_s,
        out_shape=jax.ShapeDtypeStruct((groups, rows, tokens), bf16),
        compiler_params=pltpu.CompilerParams(vmem_limit_bytes=48 << 20),
        cost_estimate=pl.CostEstimate(
            flops=4 * groups * rows * tokens * length,
            bytes_accessed=proj.size * 4 + groups * rows * tokens * 2,
            transcendentals=groups * rows // head_dim * tokens * length,
        ),
        name="attend",
    )(proj, gains, *tables)


def attend_back(proj, cot, gains, tables, own):
    groups, _, rows, tokens = proj.shape
    length, head_dim = tokens // own, gains.shape[1]
    proj_s, att_s, gains_s, table_s, grads_s = attend_specs(groups, rows, own, length, head_dim)
    return pl.pallas_call(
        attend_back_kernel,
        grid=(groups, own),
        in_specs=[proj_s, att_s, gains_s, table_s, table_s],
        out_specs=[proj_s, grads_s],
        out_shape=[
            jax.ShapeDtypeStruct(proj.shape, bf16),
            jax.ShapeDtypeStruct((2, head_dim, length), f32),
        ],
        compiler_params=pltpu.CompilerParams(vmem_limit_bytes=48 << 20),
        cost_estimate=pl.CostEstimate(
            flops=10 * groups * rows * tokens * length,
            bytes_accessed=proj.size * 6 + groups * rows * tokens * 2,
            transcendentals=groups * rows // head_dim * tokens * length,
        ),
        name="attend_back",
    )(proj, cot, gains, *tables)


def swish_mul(gate_part, up_part):
    return jax.nn.silu(gate_part) * up_part


def dot(a, b):
    return jnp.dot(a, b, preferred_element_type=f32)


def ein(spec, a, b):
    return jnp.einsum(spec, a, b, preferred_element_type=f32)


def gather_rows(block, dp_size):
    rows, width = block.shape
    share = -(-rows // dp_size)
    if rows % dp_size:
        block = jnp.pad(block, ((0, share * dp_size - rows), (0, 0)))
    piece = lax.dynamic_slice_in_dim(block, lax.axis_index("dp") * share, share, 0)
    whole = lax.all_gather(piece, ("mp", "dp"), axis=0, tiled=True)
    if rows % dp_size:
        whole = whole.reshape(-1, share * dp_size, width)[:, :rows].reshape(-1, width)
    return whole


def reduce_grad(grad, mp_size):
    rows = lax.psum_scatter(grad, "dp", scatter_dimension=0, tiled=True)
    rows = rows.reshape(rows.shape[0], mp_size, -1).swapaxes(0, 1)
    return lax.psum_scatter(rows, "mp", scatter_dimension=0, tiled=False).astype(f32)


def shards(
    patches,
    cotangent,
    time_bins,
    labels,
    image_counts,
    dest_perm,
    time_table,
    class_table,
    ada_weight,
    qkv_weight,
    norm_gains,
    out_weight,
    expand_weight,
    down_weight,
):
    dp_size = lax.axis_size("dp")
    mp_size = lax.axis_size("mp")
    capacity = patches.shape[0]
    slot_count = capacity // dp_size
    images = cotangent.shape[0]
    local_len = patches.shape[1]
    model_width = patches.shape[2]
    length = local_len * mp_size
    head_dim = norm_gains.shape[1]
    local_dim = out_weight.shape[0]
    unit_count = down_weight.shape[0]
    units = unit_count * mp_size
    own = images // mp_size
    total_images = images * dp_size
    order = jnp.array(feature_order(head_dim)[0])
    tables = rope_tables(length, head_dim)
    gains_f = norm_gains.astype(f32)[:, order]
    gains_f = (gains_f * jnp.array([[head_dim ** (-0.5)], [1.0]], f32))[:, :, None]
    dp_index = lax.axis_index("dp")
    mp_index = lax.axis_index("mp")

    columns = jnp.arange(3 * local_dim)
    places = columns // head_dim * head_dim + order[columns % head_dim]
    places = jnp.where(columns < 2 * local_dim, places, columns)
    turn = (places[:, None] == columns[None, :]).astype(bf16)
    qkv_block = ein("rc,dc->rd", turn, qkv_weight.reshape(model_width, -1)).astype(bf16)
    qkv_full = gather_rows(qkv_block, dp_size)
    out_full = gather_rows(out_weight, dp_size)
    expand_full = gather_rows(expand_weight.reshape(model_width, -1).T, dp_size)
    down_full = gather_rows(down_weight, dp_size)

    starts = jnp.cumsum(image_counts) - image_counts
    finish = starts + image_counts
    my_start = starts[dp_index]
    my_count = image_counts[dp_index]
    device_ids = jnp.arange(dp_size)
    matches = (dest_perm[:, None] == device_ids[None, :]).astype(jnp.int32)
    inverse = jnp.sum(device_ids[:, None] * matches, axis=0)
    my_place = inverse[dp_index]
    pair_ids = jnp.arange(dp_size * slot_count)
    pair_peer = pair_ids // slot_count
    pair_slot = pair_ids % slot_count
    send_index = pair_slot * dp_size + jnp.mod(inverse[pair_peer] - my_start, dp_size)
    send_index = jnp.minimum(send_index, capacity - 1)
    send_patches = jnp.take(patches, send_index, axis=0)
    recv_patches = lax.all_to_all(send_patches, "dp", split_axis=0, concat_axis=0, tiled=True)
    rank_ids = jnp.arange(images) * dp_size + my_place
    source = jnp.sum((finish[None, :] <= rank_ids[:, None]).astype(jnp.int32), axis=1)
    within = rank_ids - starts[source]
    recv_index = source * slot_count + within // dp_size
    latent = jnp.take(recv_patches, recv_index, axis=0)
    latent = lax.all_to_all(latent, "mp", split_axis=0, concat_axis=1, tiled=True)
    cot = lax.all_to_all(cotangent, "mp", split_axis=0, concat_axis=1, tiled=True)

    info = lax.all_gather(jnp.stack([time_bins, labels]), "dp", axis=1, tiled=True)
    slot_all = jnp.arange(dp_size * capacity)
    live_all = (slot_all % capacity) < jnp.repeat(image_counts, capacity)
    bin_totals = jnp.sum(
        ((info[0][:, None] == jnp.arange(NBINS)[None, :]) & live_all[:, None]).astype(f32), axis=0
    )
    row_all = jnp.arange(total_images)
    rank_all = (row_all % images) * dp_size + jnp.repeat(inverse, images)
    source_all = jnp.sum((finish[None, :] <= rank_all[:, None]).astype(jnp.int32), axis=1)
    start_all = jnp.sum(
        jnp.where(source_all[:, None] == device_ids[None, :], starts[None, :], 0), axis=1
    )
    slots_all = source_all * capacity + rank_all - start_all
    slot_hit = slots_all[:, None] == slot_all[None, :]
    bins_all = jnp.sum(jnp.where(slot_hit, info[0][None, :], 0), axis=1)
    labels_all = jnp.sum(jnp.where(slot_hit, info[1][None, :], 0), axis=1)
    bin_hot = (bins_all[:, None] == jnp.arange(NBINS)[None, :])
    label_hot = (labels_all[:, None] == jnp.arange(NCLS)[None, :])
    weights_all = total_images / (NBINS * jnp.sum(bin_hot.astype(f32) * bin_totals[None, :], axis=1))
    bin_hot = bin_hot.astype(bf16)
    label_hot = label_hot.astype(bf16)
    cond_all = (dot(bin_hot, time_table) + dot(label_hot, class_table)).astype(bf16).astype(f32)
    silu_all = jax.nn.silu(cond_all).astype(bf16)
    first = dp_index * images + mp_index * own
    silu_cond = lax.dynamic_slice_in_dim(silu_all, first, own, 0)
    weights = lax.dynamic_slice_in_dim(weights_all, first, own, 0)

    modulation = dot(silu_cond, ada_weight.reshape(model_width, 6 * model_width))
    modulation = modulation.reshape(own, 6, 1, model_width)
    shift_one = modulation[:, 0]
    scale_one = modulation[:, 1]
    gate_one = modulation[:, 2]
    shift_two = modulation[:, 3]
    scale_two = modulation[:, 4]
    gate_two = modulation[:, 5]

    latent_f = latent.astype(f32)
    out_cot = cot.astype(f32) * weights[:, None, None]
    normed = rms_scale(latent_f, scale_one, shift_one).astype(bf16)
    normed_flat = normed.reshape(-1, model_width)
    proj = ein("cd,nd->cn", qkv_full, normed_flat)
    proj = proj.reshape(mp_size, 3, local_dim, own * length)
    attended = attend(proj, gains_f, tables, own)
    branch_one = ein("mcn,mcd->nd", attended, out_full.reshape(mp_size, local_dim, -1))
    branch_one = branch_one.reshape(own, length, model_width)
    middle = latent_f + gate_one * branch_one
    normed_two = rms_scale(middle, scale_two, shift_two).astype(bf16)
    two_flat = normed_two.reshape(-1, model_width)
    expanded = ein("nd,fd->nf", two_flat, expand_full).reshape(-1, mp_size, 2, unit_count)
    swish_val, swish_pull = jax.vjp(swish_mul, expanded[:, :, 0], expanded[:, :, 1])
    hidden = swish_val.astype(bf16).reshape(-1, units)
    branch_two = dot(hidden, down_full).reshape(own, length, model_width)
    result = (middle + gate_two * branch_two).astype(bf16)
    result = lax.all_to_all(result, "mp", split_axis=1, concat_axis=0, tiled=True)

    down_low = (gate_two * out_cot).astype(bf16)
    gate_two_grad = jnp.sum(out_cot * branch_two, axis=1)
    down_low = down_low.reshape(-1, model_width)
    down_term = ein("nd,nf->df", down_low, hidden).astype(bf16)
    hidden_grad = ein("nd,fd->nf", down_low, down_full).reshape(-1, mp_size, unit_count)
    gate_grad, up_grad = swish_pull(hidden_grad)
    expand_low = jnp.stack([gate_grad, up_grad], 2).astype(bf16).reshape(-1, 2 * units)
    expand_term = ein("nd,nf->df", two_flat, expand_low).astype(bf16)
    two_grad = ein("nf,fd->nd", expand_low, expand_full).reshape(own, length, model_width)
    norm_val, norm_pull = jax.vjp(rms_scale, middle, scale_two, shift_two)
    middle_grad, scale_two_grad, shift_two_grad = norm_pull(two_grad)
    middle_grad = middle_grad + out_cot
    gate_one_grad = jnp.sum(middle_grad * branch_one, axis=1)
    branch_low = (gate_one * middle_grad).astype(bf16).reshape(-1, model_width)
    out_term = ein("nd,mcn->dmc", branch_low, attended).astype(bf16)
    attended_low = ein("cd,nd->cn", out_full, branch_low).astype(bf16)
    attended_low = attended_low.reshape(mp_size, local_dim, own * length)
    projected_low, gains_grad = attend_back(proj, attended_low, gains_f, tables, own)
    gains_grad = jnp.sum(gains_grad, axis=2) * jnp.array([[head_dim ** (-0.5)], [1.0]], f32)
    qkv_term = ein("nd,mkcn->dmkc", normed_flat, projected_low).astype(bf16)
    normed_grad = ein("cn,cd->nd", projected_low.reshape(-1, own * length), qkv_full)
    normed_grad = normed_grad.reshape(own, length, model_width)
    norm_val, norm_pull = jax.vjp(rms_scale, latent_f, scale_one, shift_one)
    latent_grad, scale_one_grad, shift_one_grad = norm_pull(normed_grad)
    latent_grad = (latent_grad + middle_grad).astype(bf16)

    latent_back = lax.all_to_all(latent_grad, "mp", split_axis=1, concat_axis=0, tiled=True)
    back_within = pair_slot * dp_size + jnp.mod(my_place - starts[pair_peer], dp_size)
    back_slot = jnp.clip((starts[pair_peer] + back_within - my_place) // dp_size, 0, images - 1)
    back_patches = jnp.take(latent_back, back_slot, axis=0)
    got_patches = lax.all_to_all(back_patches, "dp", split_axis=0, concat_axis=0, tiled=True)
    slot_ids = jnp.arange(capacity)
    slot_live = slot_ids < my_count
    home_peer = dest_perm[jnp.mod(my_start + slot_ids, dp_size)]
    home_index = home_peer * slot_count + jnp.minimum(slot_ids // dp_size, slot_count - 1)
    patch_grad = jnp.where(slot_live[:, None, None], jnp.take(got_patches, home_index, axis=0), 0)

    modulation_grad = jnp.stack(
        [
            shift_one_grad[:, 0],
            scale_one_grad[:, 0],
            gate_one_grad,
            shift_two_grad[:, 0],
            scale_two_grad[:, 0],
            gate_two_grad,
        ],
        1,
    ).astype(bf16)
    mod_all = lax.all_gather(modulation_grad, ("dp", "mp"), axis=0, tiled=True)
    gains_total = lax.all_gather(gains_grad.astype(bf16), ("dp", "mp"), axis=0)
    gains_total = jnp.sum(gains_total.astype(f32), axis=0)
    gains_total = jnp.sum(
        jnp.where(order[:, None] == jnp.arange(head_dim)[None, :], gains_total[:, :, None], 0.0), axis=1
    )
    width_dp = model_width // dp_size
    width_mp = model_width // mp_size
    row0 = dp_index * width_dp
    silu_rows = lax.dynamic_slice_in_dim(silu_all, row0, width_dp, 1)
    mod_cols = lax.dynamic_slice_in_dim(mod_all, mp_index * width_mp, width_mp, 2)
    ada_grad = ein("id,ikc->dkc", silu_rows, mod_cols)
    ada_rows = lax.dynamic_slice_in_dim(ada_weight, row0, width_dp, 0)
    silu_grad = ein("ikc,dkc->id", mod_all, ada_rows)
    cond_rows = lax.dynamic_slice_in_dim(cond_all, row0, width_dp, 1)
    silu_val, silu_pull = jax.vjp(jax.nn.silu, cond_rows)
    condition_low = silu_pull(silu_grad)[0].astype(bf16)
    time_grad = ein("in,id->nd", bin_hot, condition_low)
    class_grad = ein("in,id->nd", label_hot, condition_low)

    down_grad = reduce_grad(down_term, mp_size).T
    expand_grad = reduce_grad(expand_term.reshape(model_width, -1), mp_size)
    expand_grad = expand_grad.reshape(-1, 2, unit_count)
    out_grad = reduce_grad(out_term, mp_size).T
    qkv_grad = reduce_grad(qkv_term.reshape(model_width, -1), mp_size)
    qkv_grad = lax.dot_general(
        qkv_grad,
        turn.astype(f32),
        (((1,), (0,)), ((), ())),
        precision=lax.Precision.HIGHEST,
        preferred_element_type=f32,
    )
    qkv_grad = qkv_grad.reshape(-1, 3, local_dim)
    return (
        result,
        patch_grad,
        time_grad,
        class_grad,
        ada_grad,
        qkv_grad,
        gains_total,
        out_grad,
        expand_grad,
        down_grad,
    )


def solution(mesh):
    in_specs = (
        P("dp", "mp", None),
        P("dp", "mp", None),
        P("dp"),
        P("dp"),
        P(),
        P(),
        P(),
        P(),
        P(),
        P(None, None, "mp"),
        P(),
        P("mp", None),
        P(None, None, "mp"),
        P("mp", None),
    )
    out_specs = (
        P("dp", "mp", None),
        P("dp", "mp", None),
        P(None, "dp"),
        P(None, "dp"),
        P("dp", None, "mp"),
        P("dp", None, "mp"),
        P(),
        P("mp", "dp"),
        P("dp", None, "mp"),
        P("mp", "dp"),
    )
    return jax.shard_map(shards, mesh=mesh, in_specs=in_specs, out_specs=out_specs, check_vma=False)
```

```python
import math

import jax
import jax.numpy as jnp
from jax import lax
from jax.experimental import pallas as pl
from jax.experimental.pallas import tpu as pltpu
from jax.sharding import PartitionSpec as P

GRID = 16
NCLS = 1000
NBINS = 16

epsilon = 1e-06
rope_base = 10000.0
f32 = jnp.float32
bf16 = jnp.bfloat16


def rms_scale(values, scaling, shifting):
    return (
        values * lax.rsqrt(jnp.mean(values * values, -1, keepdims=True) + epsilon) * (1.0 + scaling)
        + shifting
    )


def feature_order(head_dim):
    quarter = head_dim // 4
    firsts = list(range(quarter)) + list(range(2 * quarter, 3 * quarter))
    cut = len(firsts) // 8 * 8
    seconds = [i + quarter for i in firsts]
    return firsts[:cut] + seconds[:cut] + firsts[cut:] + seconds[cut:], cut


def rope_tables(length, head_dim):
    quarter = head_dim // 4
    order, cut = feature_order(head_dim)
    position = jnp.arange(length)
    places = jnp.stack([position // GRID, position % GRID]).astype(f32)
    frequency = rope_base ** (-jnp.arange(quarter).astype(f32) / quarter)
    angle = (frequency[None, :, None] * places[:, None, :]).reshape(2 * quarter, length)
    cosine, sine = jnp.cos(angle), jnp.sin(angle)
    cos_tab = jnp.concatenate([cosine[:cut], cosine[:cut], cosine[cut:], cosine[cut:]])
    sin_tab = jnp.concatenate([-sine[:cut], sine[:cut], -sine[cut:], sine[cut:]])
    return cos_tab, sin_tab


def partner(values, cut):
    rest = values[2 * cut :]
    half = rest.shape[0] // 2
    return jnp.concatenate(
        [values[cut : 2 * cut], values[:cut], pltpu.roll(rest, half, 0)], axis=0
    )


def head_scale(values):
    return lax.rsqrt(jnp.mean(values * values, axis=0, keepdims=True) + epsilon)


def dot_00(a, b):
    return lax.dot_general(a, b, (((0,), (0,)), ((), ())), preferred_element_type=f32)


def dot_11(a, b):
    return lax.dot_general(a, b, (((1,), (1,)), ((), ())), preferred_element_type=f32)


def dot_10(a, b):
    return lax.dot_general(a, b, (((1,), (0,)), ((), ())), preferred_element_type=f32)


def softmax_first(scores):
    shifted = jnp.exp(scores - jnp.max(scores, axis=0, keepdims=True))
    return shifted * (1.0 / jnp.sum(shifted, axis=0, keepdims=True))


def attend_kernel(proj_ref, gains_ref, cos_ref, sin_ref, out_ref):
    head_dim = gains_ref.shape[1]
    cut = feature_order(head_dim)[1]
    cos_tab, sin_tab = cos_ref[...], sin_ref[...]
    outs = []
    for head in range(proj_ref.shape[2] // head_dim):
        rows = slice(head * head_dim, (head + 1) * head_dim)
        lows = []
        for kind in range(2):
            raw = proj_ref[0, kind, rows, :]
            scaled = raw * head_scale(raw) * gains_ref[kind]
            turned = scaled * cos_tab + partner(scaled, cut) * sin_tab
            lows.append(turned.astype(bf16))
        value_low = proj_ref[0, 2, rows, :].astype(bf16)
        probs = softmax_first(dot_00(lows[1], lows[0]))
        outs.append(dot_10(value_low, probs.astype(bf16)))
    out_ref[0] = jnp.concatenate(outs, axis=0).astype(bf16)


def attend_back_kernel(
    proj_ref, cot_ref, gains_ref, cos_ref, sin_ref, out_ref, gain_grad_ref
):
    head_dim = gains_ref.shape[1]
    cut = feature_order(head_dim)[1]
    cos_tab, sin_tab = cos_ref[...], sin_ref[...]

    @pl.when((pl.program_id(0) == 0) & (pl.program_id(1) == 0))
    def _():
        gain_grad_ref[...] = jnp.zeros_like(gain_grad_ref)

    outs = [[], [], []]
    cot_all = cot_ref[0].astype(f32)
    for head in range(proj_ref.shape[2] // head_dim):
        rows = slice(head * head_dim, (head + 1) * head_dim)
        lows, units, scales = [], [], []
        for kind in range(2):
            raw = proj_ref[0, kind, rows, :]
            scale = head_scale(raw)
            unit = raw * scale
            scaled = unit * gains_ref[kind]
            turned = scaled * cos_tab + partner(scaled, cut) * sin_tab
            lows.append(turned.astype(bf16))
            units.append(unit)
            scales.append(scale)
        value_low = proj_ref[0, 2, rows, :].astype(bf16)
        cot_low = cot_all[rows].astype(bf16)
        probs = softmax_first(dot_00(lows[1], lows[0]))
        prob_grad = dot_00(value_low, cot_low)
        outs[2].append(dot_11(cot_low, probs.astype(bf16)))
        mean = jnp.sum(probs * prob_grad, axis=0, keepdims=True)
        score_low = (probs * (prob_grad - mean)).astype(bf16)
        turned_grads = (dot_10(lows[1], score_low), dot_11(lows[0], score_low))
        for kind in range(2):
            grad = turned_grads[kind]
            grad = grad * cos_tab + partner(grad * sin_tab, cut)
            gain_grad_ref[kind] += grad * units[kind]
            grad = grad * gains_ref[kind]
            along = jnp.mean(grad * units[kind], axis=0, keepdims=True)
            outs[kind].append(scales[kind] * (grad - units[kind] * along))
    for kind in range(3):
        out_ref[0, kind] = jnp.concatenate(outs[kind], axis=0).astype(bf16)


def attend_specs(groups, rows, own, length, head_dim):
    proj = pl.BlockSpec((1, 3, rows, length), lambda g, i: (g, 0, 0, i))
    att = pl.BlockSpec((1, rows, length), lambda g, i: (g, 0, i))
    gains = pl.BlockSpec((2, head_dim, 1), lambda g, i: (0, 0, 0))
    table = pl.BlockSpec((head_dim, length), lambda g, i: (0, 0))
    grads = pl.BlockSpec((2, head_dim, length), lambda g, i: (0, 0, 0))
    return proj, att, gains, table, grads


def attend(proj, gains, tables, own):
    groups, _, rows, tokens = proj.shape
    length, head_dim = tokens // own, gains.shape[1]
    proj_s, att_s, gains_s, table_s, _ = attend_specs(groups, rows, own, length, head_dim)
    return pl.pallas_call(
        attend_kernel,
        grid=(groups, own),
        in_specs=[proj_s, gains_s, table_s, table_s],
        out_specs=att_s,
        out_shape=jax.ShapeDtypeStruct((groups, rows, tokens), bf16),
        compiler_params=pltpu.CompilerParams(vmem_limit_bytes=48 << 20),
        cost_estimate=pl.CostEstimate(
            flops=4 * groups * rows * tokens * length,
            bytes_accessed=proj.size * 4 + groups * rows * tokens * 2,
            transcendentals=groups * rows // head_dim * tokens * length,
        ),
        name="attend",
    )(proj, gains, *tables)


def attend_back(proj, cot, gains, tables, own):
    groups, _, rows, tokens = proj.shape
    length, head_dim = tokens // own, gains.shape[1]
    proj_s, att_s, gains_s, table_s, grads_s = attend_specs(groups, rows, own, length, head_dim)
    return pl.pallas_call(
        attend_back_kernel,
        grid=(groups, own),
        in_specs=[proj_s, att_s, gains_s, table_s, table_s],
        out_specs=[proj_s, grads_s],
        out_shape=[
            jax.ShapeDtypeStruct(proj.shape, bf16),
            jax.ShapeDtypeStruct((2, head_dim, length), f32),
        ],
        compiler_params=pltpu.CompilerParams(vmem_limit_bytes=48 << 20),
        cost_estimate=pl.CostEstimate(
            flops=10 * groups * rows * tokens * length,
            bytes_accessed=proj.size * 6 + groups * rows * tokens * 2,
            transcendentals=groups * rows // head_dim * tokens * length,
        ),
        name="attend_back",
    )(proj, cot, gains, *tables)


def sigmoid(values):
    return 1.0 / (1.0 + jnp.exp(-values))


def mlp_kernel(x_ref, w_ref, d_ref, save_ref, out_ref):
    first = (pl.program_id(0) == 0) & (pl.program_id(1) == 0)
    step = math.gcd(x_ref.shape[0], 256)

    def body(index, carry):
        rows = pl.ds(pl.multiple_of(index * step, step), step)
        x_rows = x_ref[rows, :]
        gate = dot_11(x_rows, w_ref[0, 0])
        up = dot_11(x_rows, w_ref[0, 1])
        save_ref[0, 0, rows, :] = gate
        save_ref[0, 1, rows, :] = up
        hidden = (gate * sigmoid(gate) * up).astype(bf16)
        part = dot_10(hidden, d_ref[0])

        @pl.when(first)
        def _():
            out_ref[rows, :] = part

        @pl.when(jnp.logical_not(first))
        def _():
            out_ref[rows, :] += part

        return carry

    lax.fori_loop(0, x_ref.shape[0] // step, body, 0)


def mlp(x, expand, down):
    groups, _, units, width = expand.shape
    tokens = x.shape[0]
    block = math.gcd(units, 384)
    return pl.pallas_call(
        mlp_kernel,
        grid=(groups, units // block),
        in_specs=[
            pl.BlockSpec((tokens, width), lambda g, h: (0, 0)),
            pl.BlockSpec((1, 2, block, width), lambda g, h: (g, 0, h, 0)),
            pl.BlockSpec((1, block, width), lambda g, h: (g, h, 0)),
        ],
        out_specs=[
            pl.BlockSpec((1, 2, tokens, block), lambda g, h: (g, 0, 0, h)),
            pl.BlockSpec((tokens, width), lambda g, h: (0, 0)),
        ],
        out_shape=[
            jax.ShapeDtypeStruct((groups, 2, tokens, units), f32),
            jax.ShapeDtypeStruct((tokens, width), f32),
        ],
        compiler_params=pltpu.CompilerParams(vmem_limit_bytes=56 << 20),
        cost_estimate=pl.CostEstimate(
            flops=6 * groups * units * tokens * width,
            bytes_accessed=8 * groups * units * tokens + 6 * groups * units * width,
            transcendentals=groups * units * tokens,
        ),
        name="mlp",
    )(x, expand, down)


def fill_rows(order_ref, source_ref, target_ref):
    blocks, rows = source_ref.shape[0], source_ref.shape[1]
    for place in range(blocks):
        target_ref[place * rows : (place + 1) * rows, :] = source_ref[order_ref[place]]


def mlp_back_kernel(
    m_ref, e_ref, xt_ref, lowt_ref, low_ref, save_ref, w_ref, d_ref,
    keep_ref, send_ref, two_ref, xs, lows, parts,
):
    first = (pl.program_id(0) == 0) & (pl.program_id(1) == 0)
    tokens, width = low_ref.shape
    step = math.gcd(tokens, 256)

    @pl.when(first)
    def _():
        fill_rows(e_ref, xt_ref, xs)
        fill_rows(e_ref, lowt_ref, lows)

    def body(index, carry):
        rows = pl.ds(pl.multiple_of(index * step, step), step)
        hidden_grad = dot_11(low_ref[rows, :], d_ref[0])
        gate = save_ref[0, 0, rows, :]
        up = save_ref[0, 1, rows, :]
        sig = sigmoid(gate)
        swish = gate * sig
        gate_low = (hidden_grad * up * (sig + swish * (1.0 - sig))).astype(bf16)
        up_low = (hidden_grad * swish).astype(bf16)
        parts[0, rows, :] = gate_low
        parts[1, rows, :] = up_low
        parts[2, rows, :] = (swish * up).astype(bf16)
        part = dot_10(gate_low, w_ref[0, 0]) + dot_10(up_low, w_ref[0, 1])

        @pl.when(first)
        def _():
            two_ref[rows, :] = part

        @pl.when(jnp.logical_not(first))
        def _():
            two_ref[rows, :] += part

        return carry

    lax.fori_loop(0, tokens // step, body, 0)
    half = width // 2
    tile = math.gcd(half, 288)

    for out_ref, base in ((keep_ref, 0), (send_ref, half)):

        def grads(index, carry):
            place = pl.multiple_of(index * tile, tile)
            rows = pl.ds(pl.multiple_of(base + place, tile), tile)
            x_rows = xs[rows, :]
            for kind in range(2):
                out_ref[0, kind, pl.ds(place, tile), :] = dot_10(x_rows, parts[kind]).astype(bf16)
            out_ref[0, 2, pl.ds(place, tile), :] = dot_10(lows[rows, :], parts[2]).astype(bf16)
            return carry

        lax.fori_loop(0, half // tile, grads, 0)


def mlp_back(m_order, e_order, xt, lowt, low, save, expand, down):
    units, width = down.shape[1:]
    tokens = low.shape[0]
    blocks = m_order.shape[0]
    block = math.gcd(units, 384)
    whole = lambda p, h, m, e: (0, 0)
    whole3 = lambda p, h, m, e: (0, 0, 0)
    half = jax.ShapeDtypeStruct((blocks, 3, width // 2, units), bf16)
    half_spec = pl.BlockSpec((1, 3, width // 2, block), lambda p, h, m, e: (p, 0, 0, h))
    return pl.pallas_call(
        mlp_back_kernel,
        grid_spec=pltpu.PrefetchScalarGridSpec(
            num_scalar_prefetch=2,
            grid=(blocks, units // block),
            in_specs=[
                pl.BlockSpec(xt.shape, whole3),
                pl.BlockSpec(lowt.shape, whole3),
                pl.BlockSpec((tokens, width), whole),
                pl.BlockSpec((1, 2, tokens, block), lambda p, h, m, e: (m[p], 0, 0, h)),
                pl.BlockSpec((1, 2, block, width), lambda p, h, m, e: (m[p], 0, h, 0)),
                pl.BlockSpec((1, block, width), lambda p, h, m, e: (m[p], h, 0)),
            ],
            out_specs=[half_spec, half_spec, pl.BlockSpec((tokens, width), whole)],
            scratch_shapes=[
                pltpu.VMEM((width, tokens), bf16),
                pltpu.VMEM((width, tokens), bf16),
                pltpu.VMEM((3, tokens, block), bf16),
            ],
        ),
        out_shape=[half, half, jax.ShapeDtypeStruct((tokens, width), f32)],
        compiler_params=pltpu.CompilerParams(vmem_limit_bytes=60 << 20),
        cost_estimate=pl.CostEstimate(
            flops=12 * blocks * units * tokens * width,
            bytes_accessed=8 * blocks * units * tokens + 12 * blocks * units * width,
            transcendentals=blocks * units * tokens,
        ),
        name="mlp_back",
    )(m_order, e_order, xt, lowt, low, save, expand, down)


def attend_grads_kernel(
    m_ref, e_ref, xt_ref, lowt_ref, proj_ref, att_ref, keep_ref, send_ref, xs, lows
):
    @pl.when(pl.program_id(0) == 0)
    def _():
        fill_rows(e_ref, xt_ref, xs)
        fill_rows(e_ref, lowt_ref, lows)

    width = xs.shape[0]
    half = width // 2
    tile = math.gcd(half, 288)
    columns = proj_ref.shape[1]

    for out_ref, base in ((keep_ref, 0), (send_ref, half)):

        def grads(index, carry):
            place = pl.multiple_of(index * tile, tile)
            rows = pl.ds(pl.multiple_of(base + place, tile), tile)
            part = dot_11(xs[rows, :], proj_ref[0]).astype(bf16)
            out_ref[0, pl.ds(place, tile), :columns] = part
            part = dot_11(lows[rows, :], att_ref[0]).astype(bf16)
            out_ref[0, pl.ds(place, tile), columns:] = part
            return carry

        lax.fori_loop(0, half // tile, grads, 0)


def attend_grads(m_order, e_order, xt, lowt, proj, att):
    rows, tokens = att.shape[1:]
    width = xt.shape[0] * xt.shape[1]
    blocks = m_order.shape[0]
    whole3 = lambda p, m, e: (0, 0, 0)
    half = jax.ShapeDtypeStruct((blocks, width // 2, 4 * rows), bf16)
    half_spec = pl.BlockSpec((1, width // 2, 4 * rows), lambda p, m, e: (p, 0, 0))
    return pl.pallas_call(
        attend_grads_kernel,
        grid_spec=pltpu.PrefetchScalarGridSpec(
            num_scalar_prefetch=2,
            grid=(blocks,),
            in_specs=[
                pl.BlockSpec(xt.shape, whole3),
                pl.BlockSpec(lowt.shape, whole3),
                pl.BlockSpec((1, 3 * rows, tokens), lambda p, m, e: (m[p], 0, 0)),
                pl.BlockSpec((1, rows, tokens), lambda p, m, e: (m[p], 0, 0)),
            ],
            out_specs=[half_spec, half_spec],
            scratch_shapes=[
                pltpu.VMEM((width, tokens), bf16),
                pltpu.VMEM((width, tokens), bf16),
            ],
        ),
        out_shape=[half, half],
        compiler_params=pltpu.CompilerParams(vmem_limit_bytes=56 << 20),
        cost_estimate=pl.CostEstimate(
            flops=8 * blocks * rows * tokens * width,
            bytes_accessed=8 * blocks * rows * (tokens + width),
            transcendentals=0,
        ),
        name="attend_grads",
    )(m_order, e_order, xt, lowt, proj, att)


def dot(a, b):
    return jnp.dot(a, b, preferred_element_type=f32)


def ein(spec, a, b):
    return jnp.einsum(spec, a, b, preferred_element_type=f32)


def gather_rows(block, dp_size):
    rows, width = block.shape
    share = -(-rows // dp_size)
    if rows % dp_size:
        block = jnp.pad(block, ((0, share * dp_size - rows), (0, 0)))
    piece = lax.dynamic_slice_in_dim(block, lax.axis_index("dp") * share, share, 0)
    whole = lax.all_gather(piece, ("mp", "dp"), axis=0, tiled=True)
    if rows % dp_size:
        whole = whole.reshape(-1, share * dp_size, width)[:, :rows].reshape(-1, width)
    return whole


def bits_of(size):
    return [1 << i for i in range(size.bit_length() - 1)]


def swap(values, axis, bit):
    size = lax.axis_size(axis)
    return lax.ppermute(values, axis, [(i, i ^ bit) for i in range(size)])


def xor_gather(values, axes_bits):
    names = sorted({axis for axis, _ in axes_bits})
    places = [{name: 0 for name in names}]
    values = values[None]
    for axis, bit in axes_bits:
        values = jnp.concatenate([values, swap(values, axis, bit)], axis=0)
        places = places + [dict(place, **{axis: place[axis] ^ bit}) for place in places]
    return values, {name: [place[name] for place in places] for name in names}


def halving_order(bits):
    order = [0]
    for bit in reversed(bits):
        order = order + [place ^ bit for place in order]
    return order


def add_low(kept, received):
    return (kept.astype(f32) + received.astype(f32)).astype(bf16)


def halve(values, axis, bits, dim):
    for bit in bits:
        size = values.shape[dim] // 2
        received = swap(lax.slice_in_dim(values, size, 2 * size, axis=dim), axis, bit)
        values = add_low(lax.slice_in_dim(values, 0, size, axis=dim), received)
    return values


def shards(
    patches,
    cotangent,
    time_bins,
    labels,
    image_counts,
    dest_perm,
    time_table,
    class_table,
    ada_weight,
    qkv_weight,
    norm_gains,
    out_weight,
    expand_weight,
    down_weight,
):
    dp_size = lax.axis_size("dp")
    mp_size = lax.axis_size("mp")
    capacity = patches.shape[0]
    slot_count = capacity // dp_size
    images = cotangent.shape[0]
    local_len = patches.shape[1]
    model_width = patches.shape[2]
    length = local_len * mp_size
    head_dim = norm_gains.shape[1]
    local_dim = out_weight.shape[0]
    unit_count = down_weight.shape[0]
    own = images // mp_size
    total_images = images * dp_size
    order = jnp.array(feature_order(head_dim)[0])
    tables = rope_tables(length, head_dim)
    gains_f = norm_gains.astype(f32)[:, order]
    gains_f = (gains_f * jnp.array([[head_dim ** (-0.5)], [1.0]], f32))[:, :, None]
    dp_index = lax.axis_index("dp")
    mp_index = lax.axis_index("mp")

    columns = jnp.arange(3 * local_dim)
    places = columns // head_dim * head_dim + order[columns % head_dim]
    places = jnp.where(columns < 2 * local_dim, places, columns)
    turn = (places[:, None] == columns[None, :]).astype(bf16)
    qkv_block = ein("rc,dc->rd", turn, qkv_weight.reshape(model_width, -1)).astype(bf16)
    qkv_full = gather_rows(qkv_block, dp_size)
    out_full = gather_rows(out_weight, dp_size)
    expand_full = gather_rows(expand_weight.reshape(model_width, -1).T, dp_size)
    down_full = gather_rows(down_weight, dp_size)

    starts = jnp.cumsum(image_counts) - image_counts
    finish = starts + image_counts
    my_start = starts[dp_index]
    my_count = image_counts[dp_index]
    device_ids = jnp.arange(dp_size)
    matches = (dest_perm[:, None] == device_ids[None, :]).astype(jnp.int32)
    inverse = jnp.sum(device_ids[:, None] * matches, axis=0)
    my_place = inverse[dp_index]
    pair_ids = jnp.arange(dp_size * slot_count)
    pair_peer = pair_ids // slot_count
    pair_slot = pair_ids % slot_count
    send_index = pair_slot * dp_size + jnp.mod(inverse[pair_peer] - my_start, dp_size)
    send_index = jnp.minimum(send_index, capacity - 1)
    send_patches = jnp.take(patches, send_index, axis=0)
    recv_patches = lax.all_to_all(send_patches, "dp", split_axis=0, concat_axis=0, tiled=True)
    rank_ids = jnp.arange(images) * dp_size + my_place
    source = jnp.sum((finish[None, :] <= rank_ids[:, None]).astype(jnp.int32), axis=1)
    within = rank_ids - starts[source]
    recv_index = source * slot_count + within // dp_size
    latent = jnp.take(recv_patches, recv_index, axis=0)
    latent = lax.all_to_all(latent, "mp", split_axis=0, concat_axis=1, tiled=True)
    cot = lax.all_to_all(cotangent, "mp", split_axis=0, concat_axis=1, tiled=True)

    info, info_places = xor_gather(
        jnp.stack([time_bins, labels]), [("dp", bit) for bit in bits_of(dp_size)]
    )
    info = info.swapaxes(0, 1).reshape(2, -1)
    info_owner = jnp.repeat(dp_index ^ jnp.array(info_places["dp"]), capacity)
    info_slot = jnp.tile(jnp.arange(capacity), dp_size)
    info_count = jnp.sum(
        jnp.where(info_owner[:, None] == device_ids[None, :], image_counts[None, :], 0), axis=1
    )
    live_all = info_slot < info_count
    bin_totals = jnp.sum(
        ((info[0][:, None] == jnp.arange(NBINS)[None, :]) & live_all[:, None]).astype(f32), axis=0
    )
    gather_bits = [("mp", bit) for bit in bits_of(mp_size)[::-1]]
    gather_bits = gather_bits + [("dp", bit) for bit in bits_of(dp_size)[::-1]]
    places = {"dp": [0], "mp": [0]}
    for axis, bit in gather_bits:
        places = {
            name: places[name] + [place ^ (bit if name == axis else 0) for place in places[name]]
            for name in places
        }
    owner_all = jnp.repeat(dp_index ^ jnp.array(places["dp"]), own)
    group_all = jnp.repeat(mp_index ^ jnp.array(places["mp"]), own)
    row_all = group_all * own + jnp.tile(jnp.arange(own), dp_size * mp_size)
    place_all = jnp.sum(
        jnp.where(owner_all[:, None] == device_ids[None, :], inverse[None, :], 0), axis=1
    )
    rank_all = row_all * dp_size + place_all
    source_all = jnp.sum((finish[None, :] <= rank_all[:, None]).astype(jnp.int32), axis=1)
    start_all = jnp.sum(
        jnp.where(source_all[:, None] == device_ids[None, :], starts[None, :], 0), axis=1
    )
    slots_all = source_all * capacity + rank_all - start_all
    slot_hit = slots_all[:, None] == (info_owner * capacity + info_slot)[None, :]
    bins_all = jnp.sum(jnp.where(slot_hit, info[0][None, :], 0), axis=1)
    labels_all = jnp.sum(jnp.where(slot_hit, info[1][None, :], 0), axis=1)
    bin_hot = (bins_all[:, None] == jnp.arange(NBINS)[None, :])
    label_hot = (labels_all[:, None] == jnp.arange(NCLS)[None, :])
    weights_all = total_images / (NBINS * jnp.sum(bin_hot.astype(f32) * bin_totals[None, :], axis=1))
    bin_hot = bin_hot.astype(bf16)
    label_hot = label_hot.astype(bf16)
    cond_all = (dot(bin_hot, time_table) + dot(label_hot, class_table)).astype(bf16).astype(f32)
    silu_all = jax.nn.silu(cond_all).astype(bf16)
    silu_cond = silu_all[:own]
    weights = weights_all[:own]

    modulation = dot(silu_cond, ada_weight.reshape(model_width, 6 * model_width))
    modulation = modulation.reshape(own, 6, 1, model_width)
    shift_one = modulation[:, 0]
    scale_one = modulation[:, 1]
    gate_one = modulation[:, 2]
    shift_two = modulation[:, 3]
    scale_two = modulation[:, 4]
    gate_two = modulation[:, 5]

    latent_f = latent.astype(f32)
    out_cot = cot.astype(f32) * weights[:, None, None]
    normed = rms_scale(latent_f, scale_one, shift_one).astype(bf16)
    normed_flat = normed.reshape(-1, model_width)
    proj = ein("cd,nd->cn", qkv_full, normed_flat)
    proj = proj.reshape(mp_size, 3, local_dim, own * length)
    attended = attend(proj, gains_f, tables, own)
    branch_one = ein("mcn,mcd->nd", attended, out_full.reshape(mp_size, local_dim, -1))
    branch_one = branch_one.reshape(own, length, model_width)
    middle = latent_f + gate_one * branch_one
    normed_two = rms_scale(middle, scale_two, shift_two).astype(bf16)
    two_flat = normed_two.reshape(-1, model_width)
    expand_blocks = expand_full.reshape(mp_size, 2, unit_count, model_width)
    down_blocks = down_full.reshape(mp_size, unit_count, model_width)
    save, branch_two = mlp(two_flat, expand_blocks, down_blocks)
    branch_two = branch_two.reshape(own, length, model_width)
    result = (middle + gate_two * branch_two).astype(bf16)
    result = lax.all_to_all(result, "mp", split_axis=1, concat_axis=0, tiled=True)

    down_low = (gate_two * out_cot).astype(bf16)
    gate_two_grad = jnp.sum(out_cot * branch_two, axis=1)
    down_low = down_low.reshape(-1, model_width)
    dp_bits = bits_of(dp_size)
    dp_bits = (dp_bits, dp_bits[:1] + dp_bits[1:][::-1])
    mp_bits = bits_of(mp_size)
    e_orders = [(dp_index ^ jnp.array(halving_order(bits))).astype(jnp.int32) for bits in dp_bits]
    m_order = (mp_index ^ jnp.array(halving_order(mp_bits))).astype(jnp.int32)
    m_orders = (m_order[: mp_size // 2], m_order[mp_size // 2 :])

    def by_owner(values):
        return values.T.reshape(dp_size, model_width // dp_size, -1)

    def reduce(kept, sent, which, dim):
        kept = add_low(kept, swap(sent, "dp", dp_bits[which][0]))
        return halve(kept, "dp", dp_bits[which][1:], dim)

    def reduce_mp(kept, sent):
        kept = add_low(kept, swap(sent, "mp", mp_bits[0]))
        return halve(kept, "mp", mp_bits[1:], 0)[0].astype(f32)

    two_t, down_t = by_owner(two_flat), by_owner(down_low)
    mlp_parts, two_parts = [None, None], [None, None]
    for which in (1, 0):
        kept, sent, two_parts[which] = mlp_back(
            m_orders[which], e_orders[which], two_t, down_t, down_low, save, expand_blocks, down_blocks
        )
        mlp_parts[which] = reduce(kept, sent, which, 2)
    mlp_grad = reduce_mp(*mlp_parts)
    two_grad = (two_parts[0] + two_parts[1]).reshape(own, length, model_width)
    norm_val, norm_pull = jax.vjp(rms_scale, middle, scale_two, shift_two)
    middle_grad, scale_two_grad, shift_two_grad = norm_pull(two_grad)
    middle_grad = middle_grad + out_cot
    gate_one_grad = jnp.sum(middle_grad * branch_one, axis=1)
    branch_low = (gate_one * middle_grad).astype(bf16).reshape(-1, model_width)
    attended_low = ein("cd,nd->cn", out_full, branch_low).astype(bf16)
    attended_low = attended_low.reshape(mp_size, local_dim, own * length)
    projected_low, gains_grad = attend_back(proj, attended_low, gains_f, tables, own)
    gains_grad = jnp.sum(gains_grad, axis=2) * jnp.array([[head_dim ** (-0.5)], [1.0]], f32)
    grad_parts = [None, None]
    normed_t, branch_t = by_owner(normed_flat), by_owner(branch_low)
    for which in (1, 0):
        kept, sent = attend_grads(
            m_orders[which],
            e_orders[which],
            normed_t,
            branch_t,
            projected_low.reshape(mp_size, 3 * local_dim, -1),
            attended,
        )
        grad_parts[which] = reduce(kept, sent, which, 1)
    attend_grad = reduce_mp(*grad_parts)
    normed_grad = ein("cn,cd->nd", projected_low.reshape(-1, own * length), qkv_full)
    normed_grad = normed_grad.reshape(own, length, model_width)
    norm_val, norm_pull = jax.vjp(rms_scale, latent_f, scale_one, shift_one)
    latent_grad, scale_one_grad, shift_one_grad = norm_pull(normed_grad)
    latent_grad = (latent_grad + middle_grad).astype(bf16)

    latent_back = lax.all_to_all(latent_grad, "mp", split_axis=1, concat_axis=0, tiled=True)
    back_within = pair_slot * dp_size + jnp.mod(my_place - starts[pair_peer], dp_size)
    back_slot = jnp.clip((starts[pair_peer] + back_within - my_place) // dp_size, 0, images - 1)
    back_patches = jnp.take(latent_back, back_slot, axis=0)
    got_patches = lax.all_to_all(back_patches, "dp", split_axis=0, concat_axis=0, tiled=True)
    slot_ids = jnp.arange(capacity)
    slot_live = slot_ids < my_count
    home_peer = dest_perm[jnp.mod(my_start + slot_ids, dp_size)]
    home_index = home_peer * slot_count + jnp.minimum(slot_ids // dp_size, slot_count - 1)
    patch_grad = jnp.where(slot_live[:, None, None], jnp.take(got_patches, home_index, axis=0), 0)

    modulation_grad = jnp.stack(
        [
            shift_one_grad[:, 0],
            scale_one_grad[:, 0],
            gate_one_grad,
            shift_two_grad[:, 0],
            scale_two_grad[:, 0],
            gate_two_grad,
        ],
        1,
    ).astype(bf16)
    packed = jnp.concatenate([modulation_grad.reshape(-1), gains_grad.astype(bf16).reshape(-1)])
    packed = xor_gather(packed, gather_bits)[0]
    mod_all = packed[:, : own * 6 * model_width].reshape(total_images, 6, model_width)
    gains_total = packed[:, own * 6 * model_width :].reshape(-1, 2, head_dim)
    gains_total = jnp.sum(gains_total.astype(f32), axis=0)
    gains_total = jnp.sum(
        jnp.where(order[:, None] == jnp.arange(head_dim)[None, :], gains_total[:, :, None], 0.0), axis=1
    )
    width_dp = model_width // dp_size
    width_mp = model_width // mp_size
    row0 = dp_index * width_dp
    silu_rows = lax.dynamic_slice_in_dim(silu_all, row0, width_dp, 1)
    mod_cols = lax.dynamic_slice_in_dim(mod_all, mp_index * width_mp, width_mp, 2)
    ada_grad = ein("id,ikc->dkc", silu_rows, mod_cols)
    ada_rows = lax.dynamic_slice_in_dim(ada_weight, row0, width_dp, 0)
    silu_grad = ein("ikc,dkc->id", mod_all, ada_rows)
    cond_rows = lax.dynamic_slice_in_dim(cond_all, row0, width_dp, 1)
    silu_val, silu_pull = jax.vjp(jax.nn.silu, cond_rows)
    condition_low = silu_pull(silu_grad)[0].astype(bf16)
    time_grad = ein("in,id->nd", bin_hot, condition_low)
    class_grad = ein("in,id->nd", label_hot, condition_low)

    expand_grad = mlp_grad[:2].swapaxes(0, 1)
    down_grad = mlp_grad[2].T
    out_grad = attend_grad[:, 3 * local_dim :].T
    qkv_grad = lax.dot_general(
        attend_grad[:, : 3 * local_dim],
        turn.astype(f32),
        (((1,), (0,)), ((), ())),
        precision=lax.Precision.HIGHEST,
        preferred_element_type=f32,
    )
    qkv_grad = qkv_grad.reshape(-1, 3, local_dim)
    return (
        result,
        patch_grad,
        time_grad,
        class_grad,
        ada_grad,
        qkv_grad,
        gains_total,
        out_grad,
        expand_grad,
        down_grad,
    )


def solution(mesh):
    in_specs = (
        P("dp", "mp", None),
        P("dp", "mp", None),
        P("dp"),
        P("dp"),
        P(),
        P(),
        P(),
        P(),
        P(),
        P(None, None, "mp"),
        P(),
        P("mp", None),
        P(None, None, "mp"),
        P("mp", None),
    )
    out_specs = (
        P("dp", "mp", None),
        P("dp", "mp", None),
        P(None, "dp"),
        P(None, "dp"),
        P("dp", None, "mp"),
        P("dp", None, "mp"),
        P(),
        P("mp", "dp"),
        P("dp", None, "mp"),
        P("mp", "dp"),
    )
    return jax.shard_map(shards, mesh=mesh, in_specs=in_specs, out_specs=out_specs, check_vma=False)
```

```python
import math

import jax
import jax.numpy as jnp
from jax import lax
from jax.experimental import pallas as pl
from jax.experimental.pallas import tpu as pltpu
from jax.sharding import PartitionSpec as P

GRID = 16
NCLS = 1000
NBINS = 16

epsilon = 1e-06
rope_base = 10000.0
f32 = jnp.float32
bf16 = jnp.bfloat16


def rms_scale(values, scaling, shifting):
    return (
        values * lax.rsqrt(jnp.mean(values * values, -1, keepdims=True) + epsilon) * (1.0 + scaling)
        + shifting
    )


def feature_order(head_dim):
    quarter = head_dim // 4
    firsts = list(range(quarter)) + list(range(2 * quarter, 3 * quarter))
    cut = len(firsts) // 8 * 8
    seconds = [i + quarter for i in firsts]
    return firsts[:cut] + seconds[:cut] + firsts[cut:] + seconds[cut:], cut


def rope_tables(length, head_dim):
    quarter = head_dim // 4
    order, cut = feature_order(head_dim)
    position = jnp.arange(length)
    places = jnp.stack([position // GRID, position % GRID]).astype(f32)
    frequency = rope_base ** (-jnp.arange(quarter).astype(f32) / quarter)
    angle = (frequency[None, :, None] * places[:, None, :]).reshape(2 * quarter, length)
    cosine, sine = jnp.cos(angle), jnp.sin(angle)
    cos_tab = jnp.concatenate([cosine[:cut], cosine[:cut], cosine[cut:], cosine[cut:]])
    sin_tab = jnp.concatenate([-sine[:cut], sine[:cut], -sine[cut:], sine[cut:]])
    return cos_tab, sin_tab


def partner(values, cut):
    rest = values[2 * cut :]
    half = rest.shape[0] // 2
    return jnp.concatenate(
        [values[cut : 2 * cut], values[:cut], pltpu.roll(rest, half, 0)], axis=0
    )


def head_scale(values):
    return lax.rsqrt(jnp.mean(values * values, axis=0, keepdims=True) + epsilon)


def dot_00(a, b):
    return lax.dot_general(a, b, (((0,), (0,)), ((), ())), preferred_element_type=f32)


def dot_11(a, b):
    return lax.dot_general(a, b, (((1,), (1,)), ((), ())), preferred_element_type=f32)


def dot_10(a, b):
    return lax.dot_general(a, b, (((1,), (0,)), ((), ())), preferred_element_type=f32)


def softmax_first(scores):
    shifted = jnp.exp(scores - jnp.max(scores, axis=0, keepdims=True))
    return shifted * (1.0 / jnp.sum(shifted, axis=0, keepdims=True))


def attend_kernel(proj_ref, gains_ref, cos_ref, sin_ref, out_ref):
    head_dim = gains_ref.shape[1]
    cut = feature_order(head_dim)[1]
    cos_tab, sin_tab = cos_ref[...], sin_ref[...]
    outs = []
    for head in range(proj_ref.shape[2] // head_dim):
        rows = slice(head * head_dim, (head + 1) * head_dim)
        lows = []
        for kind in range(2):
            raw = proj_ref[0, kind, rows, :]
            scaled = raw * head_scale(raw) * gains_ref[kind]
            turned = scaled * cos_tab + partner(scaled, cut) * sin_tab
            lows.append(turned.astype(bf16))
        value_low = proj_ref[0, 2, rows, :].astype(bf16)
        probs = softmax_first(dot_00(lows[1], lows[0]))
        outs.append(dot_10(value_low, probs.astype(bf16)))
    out_ref[0] = jnp.concatenate(outs, axis=0).astype(bf16)


def attend_back_kernel(
    proj_ref, cot_ref, gains_ref, cos_ref, sin_ref, out_ref, gain_grad_ref
):
    head_dim = gains_ref.shape[1]
    cut = feature_order(head_dim)[1]
    cos_tab, sin_tab = cos_ref[...], sin_ref[...]

    @pl.when((pl.program_id(0) == 0) & (pl.program_id(1) == 0))
    def _():
        gain_grad_ref[...] = jnp.zeros_like(gain_grad_ref)

    outs = [[], [], []]
    cot_all = cot_ref[0].astype(f32)
    for head in range(proj_ref.shape[2] // head_dim):
        rows = slice(head * head_dim, (head + 1) * head_dim)
        lows, units, scales = [], [], []
        for kind in range(2):
            raw = proj_ref[0, kind, rows, :]
            scale = head_scale(raw)
            unit = raw * scale
            scaled = unit * gains_ref[kind]
            turned = scaled * cos_tab + partner(scaled, cut) * sin_tab
            lows.append(turned.astype(bf16))
            units.append(unit)
            scales.append(scale)
        value_low = proj_ref[0, 2, rows, :].astype(bf16)
        cot_low = cot_all[rows].astype(bf16)
        probs = softmax_first(dot_00(lows[1], lows[0]))
        prob_grad = dot_00(value_low, cot_low)
        outs[2].append(dot_11(cot_low, probs.astype(bf16)))
        mean = jnp.sum(probs * prob_grad, axis=0, keepdims=True)
        score_low = (probs * (prob_grad - mean)).astype(bf16)
        turned_grads = (dot_10(lows[1], score_low), dot_11(lows[0], score_low))
        for kind in range(2):
            grad = turned_grads[kind]
            grad = grad * cos_tab + partner(grad * sin_tab, cut)
            gain_grad_ref[kind] += grad * units[kind]
            grad = grad * gains_ref[kind]
            along = jnp.mean(grad * units[kind], axis=0, keepdims=True)
            outs[kind].append(scales[kind] * (grad - units[kind] * along))
    for kind in range(3):
        out_ref[0, kind] = jnp.concatenate(outs[kind], axis=0).astype(bf16)


def attend_specs(groups, rows, own, length, head_dim):
    proj = pl.BlockSpec((1, 3, rows, length), lambda g, i: (g, 0, 0, i))
    att = pl.BlockSpec((1, rows, length), lambda g, i: (g, 0, i))
    gains = pl.BlockSpec((2, head_dim, 1), lambda g, i: (0, 0, 0))
    table = pl.BlockSpec((head_dim, length), lambda g, i: (0, 0))
    grads = pl.BlockSpec((2, head_dim, length), lambda g, i: (0, 0, 0))
    return proj, att, gains, table, grads


def attend(proj, gains, tables, own):
    groups, _, rows, tokens = proj.shape
    length, head_dim = tokens // own, gains.shape[1]
    proj_s, att_s, gains_s, table_s, _ = attend_specs(groups, rows, own, length, head_dim)
    return pl.pallas_call(
        attend_kernel,
        grid=(groups, own),
        in_specs=[proj_s, gains_s, table_s, table_s],
        out_specs=att_s,
        out_shape=jax.ShapeDtypeStruct((groups, rows, tokens), bf16),
        compiler_params=pltpu.CompilerParams(vmem_limit_bytes=48 << 20),
        cost_estimate=pl.CostEstimate(
            flops=4 * groups * rows * tokens * length,
            bytes_accessed=proj.size * 4 + groups * rows * tokens * 2,
            transcendentals=groups * rows // head_dim * tokens * length,
        ),
        name="attend",
    )(proj, gains, *tables)


def attend_back(proj, cot, gains, tables, own):
    groups, _, rows, tokens = proj.shape
    length, head_dim = tokens // own, gains.shape[1]
    proj_s, att_s, gains_s, table_s, grads_s = attend_specs(groups, rows, own, length, head_dim)
    return pl.pallas_call(
        attend_back_kernel,
        grid=(groups, own),
        in_specs=[proj_s, att_s, gains_s, table_s, table_s],
        out_specs=[proj_s, grads_s],
        out_shape=[
            jax.ShapeDtypeStruct(proj.shape, bf16),
            jax.ShapeDtypeStruct((2, head_dim, length), f32),
        ],
        compiler_params=pltpu.CompilerParams(vmem_limit_bytes=48 << 20),
        cost_estimate=pl.CostEstimate(
            flops=10 * groups * rows * tokens * length,
            bytes_accessed=proj.size * 6 + groups * rows * tokens * 2,
            transcendentals=groups * rows // head_dim * tokens * length,
        ),
        name="attend_back",
    )(proj, cot, gains, *tables)


def sigmoid(values):
    return 1.0 / (1.0 + jnp.exp(-values))


def mlp_kernel(x_ref, w_ref, d_ref, save_ref, out_ref):
    first = (pl.program_id(0) == 0) & (pl.program_id(1) == 0)
    step = math.gcd(x_ref.shape[0], 256)

    def body(index, carry):
        rows = pl.ds(pl.multiple_of(index * step, step), step)
        x_rows = x_ref[rows, :]
        gate = dot_11(x_rows, w_ref[0, 0])
        up = dot_11(x_rows, w_ref[0, 1])
        save_ref[0, 0, rows, :] = gate
        save_ref[0, 1, rows, :] = up
        hidden = (gate * sigmoid(gate) * up).astype(bf16)
        part = dot_10(hidden, d_ref[0])

        @pl.when(first)
        def _():
            out_ref[rows, :] = part

        @pl.when(jnp.logical_not(first))
        def _():
            out_ref[rows, :] += part

        return carry

    lax.fori_loop(0, x_ref.shape[0] // step, body, 0)


def mlp(x, expand, down):
    groups, _, units, width = expand.shape
    tokens = x.shape[0]
    block = math.gcd(units, 384)
    return pl.pallas_call(
        mlp_kernel,
        grid=(groups, units // block),
        in_specs=[
            pl.BlockSpec((tokens, width), lambda g, h: (0, 0)),
            pl.BlockSpec((1, 2, block, width), lambda g, h: (g, 0, h, 0)),
            pl.BlockSpec((1, block, width), lambda g, h: (g, h, 0)),
        ],
        out_specs=[
            pl.BlockSpec((1, 2, tokens, block), lambda g, h: (g, 0, 0, h)),
            pl.BlockSpec((tokens, width), lambda g, h: (0, 0)),
        ],
        out_shape=[
            jax.ShapeDtypeStruct((groups, 2, tokens, units), f32),
            jax.ShapeDtypeStruct((tokens, width), f32),
        ],
        compiler_params=pltpu.CompilerParams(vmem_limit_bytes=56 << 20),
        cost_estimate=pl.CostEstimate(
            flops=6 * groups * units * tokens * width,
            bytes_accessed=8 * groups * units * tokens + 6 * groups * units * width,
            transcendentals=groups * units * tokens,
        ),
        name="mlp",
    )(x, expand, down)


def fill_rows(order_ref, source_ref, target_ref):
    blocks, rows = source_ref.shape[0], source_ref.shape[1]
    for place in range(blocks):
        target_ref[place * rows : (place + 1) * rows, :] = source_ref[order_ref[place]]


def mlp_back_kernel(
    m_ref, e_ref, xt_ref, lowt_ref, low_ref, save_ref, w_ref, d_ref,
    keep_ref, send_ref, two_ref, xs, lows, parts,
):
    first = (pl.program_id(0) == 0) & (pl.program_id(1) == 0)
    tokens, width = low_ref.shape
    step = math.gcd(tokens, 256)

    @pl.when(first)
    def _():
        fill_rows(e_ref, xt_ref, xs)
        fill_rows(e_ref, lowt_ref, lows)

    def body(index, carry):
        rows = pl.ds(pl.multiple_of(index * step, step), step)
        hidden_grad = dot_11(low_ref[rows, :], d_ref[0])
        gate = save_ref[0, 0, rows, :]
        up = save_ref[0, 1, rows, :]
        sig = sigmoid(gate)
        swish = gate * sig
        gate_low = (hidden_grad * up * (sig + swish * (1.0 - sig))).astype(bf16)
        up_low = (hidden_grad * swish).astype(bf16)
        parts[0, rows, :] = gate_low
        parts[1, rows, :] = up_low
        parts[2, rows, :] = (swish * up).astype(bf16)
        part = dot_10(gate_low, w_ref[0, 0]) + dot_10(up_low, w_ref[0, 1])

        @pl.when(first)
        def _():
            two_ref[rows, :] = part

        @pl.when(jnp.logical_not(first))
        def _():
            two_ref[rows, :] += part

        return carry

    lax.fori_loop(0, tokens // step, body, 0)
    half = width // 2
    tile = math.gcd(half, 288)

    for out_ref, base in ((keep_ref, 0), (send_ref, half)):

        def grads(index, carry):
            place = pl.multiple_of(index * tile, tile)
            rows = pl.ds(pl.multiple_of(base + place, tile), tile)
            x_rows = xs[rows, :]
            for kind in range(2):
                out_ref[0, kind, pl.ds(place, tile), :] = dot_10(x_rows, parts[kind]).astype(bf16)
            out_ref[0, 2, pl.ds(place, tile), :] = dot_10(lows[rows, :], parts[2]).astype(bf16)
            return carry

        lax.fori_loop(0, half // tile, grads, 0)


def mlp_back(m_order, e_order, xt, lowt, low, save, expand, down):
    units, width = down.shape[1:]
    tokens = low.shape[0]
    blocks = m_order.shape[0]
    block = math.gcd(units, 384)
    whole = lambda p, h, m, e: (0, 0)
    whole3 = lambda p, h, m, e: (0, 0, 0)
    half = jax.ShapeDtypeStruct((blocks, 3, width // 2, units), bf16)
    half_spec = pl.BlockSpec((1, 3, width // 2, block), lambda p, h, m, e: (p, 0, 0, h))
    return pl.pallas_call(
        mlp_back_kernel,
        grid_spec=pltpu.PrefetchScalarGridSpec(
            num_scalar_prefetch=2,
            grid=(blocks, units // block),
            in_specs=[
                pl.BlockSpec(xt.shape, whole3),
                pl.BlockSpec(lowt.shape, whole3),
                pl.BlockSpec((tokens, width), whole),
                pl.BlockSpec((1, 2, tokens, block), lambda p, h, m, e: (m[p], 0, 0, h)),
                pl.BlockSpec((1, 2, block, width), lambda p, h, m, e: (m[p], 0, h, 0)),
                pl.BlockSpec((1, block, width), lambda p, h, m, e: (m[p], h, 0)),
            ],
            out_specs=[half_spec, half_spec, pl.BlockSpec((tokens, width), whole)],
            scratch_shapes=[
                pltpu.VMEM((width, tokens), bf16),
                pltpu.VMEM((width, tokens), bf16),
                pltpu.VMEM((3, tokens, block), bf16),
            ],
        ),
        out_shape=[half, half, jax.ShapeDtypeStruct((tokens, width), f32)],
        compiler_params=pltpu.CompilerParams(vmem_limit_bytes=60 << 20),
        cost_estimate=pl.CostEstimate(
            flops=12 * blocks * units * tokens * width,
            bytes_accessed=8 * blocks * units * tokens + 12 * blocks * units * width,
            transcendentals=blocks * units * tokens,
        ),
        name="mlp_back",
    )(m_order, e_order, xt, lowt, low, save, expand, down)


def attend_grads_kernel(
    m_ref, e_ref, xt_ref, lowt_ref, proj_ref, att_ref, keep_ref, send_ref, xs, lows
):
    @pl.when(pl.program_id(0) == 0)
    def _():
        fill_rows(e_ref, xt_ref, xs)
        fill_rows(e_ref, lowt_ref, lows)

    width = xs.shape[0]
    half = width // 2
    tile = math.gcd(half, 288)
    columns = proj_ref.shape[1]

    for out_ref, base in ((keep_ref, 0), (send_ref, half)):

        def grads(index, carry):
            place = pl.multiple_of(index * tile, tile)
            rows = pl.ds(pl.multiple_of(base + place, tile), tile)
            part = dot_11(xs[rows, :], proj_ref[0]).astype(bf16)
            out_ref[0, pl.ds(place, tile), :columns] = part
            part = dot_11(lows[rows, :], att_ref[0]).astype(bf16)
            out_ref[0, pl.ds(place, tile), columns:] = part
            return carry

        lax.fori_loop(0, half // tile, grads, 0)


def attend_grads(m_order, e_order, xt, lowt, proj, att):
    rows, tokens = att.shape[1:]
    width = xt.shape[0] * xt.shape[1]
    blocks = m_order.shape[0]
    whole3 = lambda p, m, e: (0, 0, 0)
    half = jax.ShapeDtypeStruct((blocks, width // 2, 4 * rows), bf16)
    half_spec = pl.BlockSpec((1, width // 2, 4 * rows), lambda p, m, e: (p, 0, 0))
    return pl.pallas_call(
        attend_grads_kernel,
        grid_spec=pltpu.PrefetchScalarGridSpec(
            num_scalar_prefetch=2,
            grid=(blocks,),
            in_specs=[
                pl.BlockSpec(xt.shape, whole3),
                pl.BlockSpec(lowt.shape, whole3),
                pl.BlockSpec((1, 3 * rows, tokens), lambda p, m, e: (m[p], 0, 0)),
                pl.BlockSpec((1, rows, tokens), lambda p, m, e: (m[p], 0, 0)),
            ],
            out_specs=[half_spec, half_spec],
            scratch_shapes=[
                pltpu.VMEM((width, tokens), bf16),
                pltpu.VMEM((width, tokens), bf16),
            ],
        ),
        out_shape=[half, half],
        compiler_params=pltpu.CompilerParams(vmem_limit_bytes=56 << 20),
        cost_estimate=pl.CostEstimate(
            flops=8 * blocks * rows * tokens * width,
            bytes_accessed=8 * blocks * rows * (tokens + width),
            transcendentals=0,
        ),
        name="attend_grads",
    )(m_order, e_order, xt, lowt, proj, att)


def dot(a, b):
    return jnp.dot(a, b, preferred_element_type=f32)


def ein(spec, a, b):
    return jnp.einsum(spec, a, b, preferred_element_type=f32)


def gather_rows(block, dp_size):
    rows, width = block.shape
    share = -(-rows // dp_size)
    if rows % dp_size:
        block = jnp.pad(block, ((0, share * dp_size - rows), (0, 0)))
    piece = lax.dynamic_slice_in_dim(block, lax.axis_index("dp") * share, share, 0)
    whole = lax.all_gather(piece, ("mp", "dp"), axis=0, tiled=True)
    if rows % dp_size:
        whole = whole.reshape(-1, share * dp_size, width)[:, :rows].reshape(-1, width)
    return whole


def bits_of(size):
    return [1 << i for i in range(size.bit_length() - 1)]


def swap(values, axis, bit):
    size = lax.axis_size(axis)
    return lax.ppermute(values, axis, [(i, i ^ bit) for i in range(size)])


def xor_gather(values, axes_bits):
    names = sorted({axis for axis, _ in axes_bits})
    places = [{name: 0 for name in names}]
    values = values[None]
    for axis, bit in axes_bits:
        values = jnp.concatenate([values, swap(values, axis, bit)], axis=0)
        places = places + [dict(place, **{axis: place[axis] ^ bit}) for place in places]
    return values, {name: [place[name] for place in places] for name in names}


def halving_order(bits):
    order = [0]
    for bit in reversed(bits):
        order = order + [place ^ bit for place in order]
    return order


def add_low(kept, received):
    return (kept.astype(f32) + received.astype(f32)).astype(bf16)


def tie(*values):
    return lax.optimization_barrier(values)


def split(values, dim):
    size = values.shape[dim] // 2
    return (
        lax.slice_in_dim(values, 0, size, axis=dim),
        lax.slice_in_dim(values, size, 2 * size, axis=dim),
    )


def halve(values, axis, bits, dim):
    for bit in bits:
        kept, sent = split(values, dim)
        values = add_low(kept, swap(sent, axis, bit))
    return values


def shards(
    patches,
    cotangent,
    time_bins,
    labels,
    image_counts,
    dest_perm,
    time_table,
    class_table,
    ada_weight,
    qkv_weight,
    norm_gains,
    out_weight,
    expand_weight,
    down_weight,
):
    dp_size = lax.axis_size("dp")
    mp_size = lax.axis_size("mp")
    capacity = patches.shape[0]
    slot_count = capacity // dp_size
    images = cotangent.shape[0]
    local_len = patches.shape[1]
    model_width = patches.shape[2]
    length = local_len * mp_size
    head_dim = norm_gains.shape[1]
    local_dim = out_weight.shape[0]
    unit_count = down_weight.shape[0]
    own = images // mp_size
    total_images = images * dp_size
    order = jnp.array(feature_order(head_dim)[0])
    tables = rope_tables(length, head_dim)
    gains_f = norm_gains.astype(f32)[:, order]
    gains_f = (gains_f * jnp.array([[head_dim ** (-0.5)], [1.0]], f32))[:, :, None]
    dp_index = lax.axis_index("dp")
    mp_index = lax.axis_index("mp")

    columns = jnp.arange(3 * local_dim)
    places = columns // head_dim * head_dim + order[columns % head_dim]
    places = jnp.where(columns < 2 * local_dim, places, columns)
    turn = (places[:, None] == columns[None, :]).astype(bf16)
    qkv_block = ein("rc,dc->rd", turn, qkv_weight.reshape(model_width, -1)).astype(bf16)
    qkv_full = gather_rows(qkv_block, dp_size)
    out_full = gather_rows(out_weight, dp_size)
    expand_full = gather_rows(expand_weight.reshape(model_width, -1).T, dp_size)
    down_full = gather_rows(down_weight, dp_size)

    starts = jnp.cumsum(image_counts) - image_counts
    finish = starts + image_counts
    my_start = starts[dp_index]
    my_count = image_counts[dp_index]
    device_ids = jnp.arange(dp_size)
    matches = (dest_perm[:, None] == device_ids[None, :]).astype(jnp.int32)
    inverse = jnp.sum(device_ids[:, None] * matches, axis=0)
    my_place = inverse[dp_index]
    pair_ids = jnp.arange(dp_size * slot_count)
    pair_peer = pair_ids // slot_count
    pair_slot = pair_ids % slot_count
    send_index = pair_slot * dp_size + jnp.mod(inverse[pair_peer] - my_start, dp_size)
    send_index = jnp.minimum(send_index, capacity - 1)
    send_patches = jnp.take(patches, send_index, axis=0)
    recv_patches = lax.all_to_all(send_patches, "dp", split_axis=0, concat_axis=0, tiled=True)
    rank_ids = jnp.arange(images) * dp_size + my_place
    source = jnp.sum((finish[None, :] <= rank_ids[:, None]).astype(jnp.int32), axis=1)
    within = rank_ids - starts[source]
    recv_index = source * slot_count + within // dp_size
    latent = jnp.take(recv_patches, recv_index, axis=0)
    latent = lax.all_to_all(latent, "mp", split_axis=0, concat_axis=1, tiled=True)
    cotangent, latent = tie(cotangent, latent)
    cot = lax.all_to_all(cotangent, "mp", split_axis=0, concat_axis=1, tiled=True)

    info, info_places = xor_gather(
        jnp.stack([time_bins, labels]), [("dp", bit) for bit in bits_of(dp_size)]
    )
    info = info.swapaxes(0, 1).reshape(2, -1)
    info_owner = jnp.repeat(dp_index ^ jnp.array(info_places["dp"]), capacity)
    info_slot = jnp.tile(jnp.arange(capacity), dp_size)
    info_count = jnp.sum(
        jnp.where(info_owner[:, None] == device_ids[None, :], image_counts[None, :], 0), axis=1
    )
    live_all = info_slot < info_count
    bin_totals = jnp.sum(
        ((info[0][:, None] == jnp.arange(NBINS)[None, :]) & live_all[:, None]).astype(f32), axis=0
    )
    gather_bits = [("mp", bit) for bit in bits_of(mp_size)[::-1]]
    gather_bits = gather_bits + [("dp", bit) for bit in bits_of(dp_size)[::-1]]
    places = {"dp": [0], "mp": [0]}
    for axis, bit in gather_bits:
        places = {
            name: places[name] + [place ^ (bit if name == axis else 0) for place in places[name]]
            for name in places
        }
    owner_all = jnp.repeat(dp_index ^ jnp.array(places["dp"]), own)
    group_all = jnp.repeat(mp_index ^ jnp.array(places["mp"]), own)
    row_all = group_all * own + jnp.tile(jnp.arange(own), dp_size * mp_size)
    place_all = jnp.sum(
        jnp.where(owner_all[:, None] == device_ids[None, :], inverse[None, :], 0), axis=1
    )
    rank_all = row_all * dp_size + place_all
    source_all = jnp.sum((finish[None, :] <= rank_all[:, None]).astype(jnp.int32), axis=1)
    start_all = jnp.sum(
        jnp.where(source_all[:, None] == device_ids[None, :], starts[None, :], 0), axis=1
    )
    slots_all = source_all * capacity + rank_all - start_all
    slot_hit = slots_all[:, None] == (info_owner * capacity + info_slot)[None, :]
    bins_all = jnp.sum(jnp.where(slot_hit, info[0][None, :], 0), axis=1)
    labels_all = jnp.sum(jnp.where(slot_hit, info[1][None, :], 0), axis=1)
    bin_hot = (bins_all[:, None] == jnp.arange(NBINS)[None, :])
    label_hot = (labels_all[:, None] == jnp.arange(NCLS)[None, :])
    weights_all = total_images / (NBINS * jnp.sum(bin_hot.astype(f32) * bin_totals[None, :], axis=1))
    bin_hot = bin_hot.astype(bf16)
    label_hot = label_hot.astype(bf16)
    cond_all = (dot(bin_hot, time_table) + dot(label_hot, class_table)).astype(bf16).astype(f32)
    silu_all = jax.nn.silu(cond_all).astype(bf16)
    silu_cond = silu_all[:own]
    weights = weights_all[:own]

    modulation = dot(silu_cond, ada_weight.reshape(model_width, 6 * model_width))
    modulation = modulation.reshape(own, 6, 1, model_width)
    shift_one = modulation[:, 0]
    scale_one = modulation[:, 1]
    gate_one = modulation[:, 2]
    shift_two = modulation[:, 3]
    scale_two = modulation[:, 4]
    gate_two = modulation[:, 5]

    latent_f = latent.astype(f32)
    out_cot = cot.astype(f32) * weights[:, None, None]
    normed = rms_scale(latent_f, scale_one, shift_one).astype(bf16)
    normed_flat = normed.reshape(-1, model_width)
    proj = ein("cd,nd->cn", qkv_full, normed_flat)
    proj = proj.reshape(mp_size, 3, local_dim, own * length)
    attended = attend(proj, gains_f, tables, own)
    branch_one = ein("mcn,mcd->nd", attended, out_full.reshape(mp_size, local_dim, -1))
    branch_one = branch_one.reshape(own, length, model_width)
    middle = latent_f + gate_one * branch_one
    normed_two = rms_scale(middle, scale_two, shift_two).astype(bf16)
    two_flat = normed_two.reshape(-1, model_width)
    expand_blocks = expand_full.reshape(mp_size, 2, unit_count, model_width)
    down_blocks = down_full.reshape(mp_size, unit_count, model_width)
    save, branch_two = mlp(two_flat, expand_blocks, down_blocks)
    branch_two = branch_two.reshape(own, length, model_width)
    result = (middle + gate_two * branch_two).astype(bf16)
    result = lax.all_to_all(result, "mp", split_axis=1, concat_axis=0, tiled=True)

    down_low = (gate_two * out_cot).astype(bf16)
    gate_two_grad = jnp.sum(out_cot * branch_two, axis=1)
    down_low = down_low.reshape(-1, model_width)
    dp_bits = bits_of(dp_size)
    dp_bits = (dp_bits, dp_bits[:1] + dp_bits[1:][::-1])
    mp_bits = bits_of(mp_size)
    e_orders = [(dp_index ^ jnp.array(halving_order(bits))).astype(jnp.int32) for bits in dp_bits]
    m_order = (mp_index ^ jnp.array(halving_order(mp_bits))).astype(jnp.int32)
    m_orders = (m_order[: mp_size // 2], m_order[mp_size // 2 :])

    def by_owner(values):
        return values.T.reshape(dp_size, model_width // dp_size, -1)

    def reduce_mp(kept, sent):
        kept = add_low(kept, swap(sent, "mp", mp_bits[0]))
        return halve(kept, "mp", mp_bits[1:], 0)[0].astype(f32)

    two_t, down_t = by_owner(two_flat), by_owner(down_low)
    kept_one, sent_one, two_one = mlp_back(
        m_orders[1], e_orders[1], two_t, down_t, down_low, save, expand_blocks, down_blocks
    )
    got_one = swap(sent_one, "dp", dp_bits[1][0])
    kept_zero, sent_zero, two_zero = mlp_back(
        m_orders[0], e_orders[0], two_t, down_t, down_low, save, expand_blocks, down_blocks
    )
    got_zero = swap(sent_zero, "dp", dp_bits[0][0])
    two_zero, got_one = tie(two_zero, got_one)
    kept_one, sent_one = split(add_low(kept_one, got_one), 2)
    got_one = swap(sent_one, "dp", dp_bits[1][1])
    two_parts = (two_zero, two_one)
    two_grad = (two_parts[0] + two_parts[1]).reshape(own, length, model_width)
    norm_val, norm_pull = jax.vjp(rms_scale, middle, scale_two, shift_two)
    middle_grad, scale_two_grad, shift_two_grad = norm_pull(two_grad)
    middle_grad = middle_grad + out_cot
    gate_one_grad = jnp.sum(middle_grad * branch_one, axis=1)
    branch_low = (gate_one * middle_grad).astype(bf16).reshape(-1, model_width)
    attended_low = ein("cd,nd->cn", out_full, branch_low).astype(bf16)
    attended_low = attended_low.reshape(mp_size, local_dim, own * length)
    attended_low, got_zero = tie(attended_low, got_zero)
    kept_zero, sent_zero = split(add_low(kept_zero, got_zero), 2)
    got_zero = swap(sent_zero, "dp", dp_bits[0][1])
    projected_low, gains_grad = attend_back(proj, attended_low, gains_f, tables, own)
    gains_grad = jnp.sum(gains_grad, axis=2) * jnp.array([[head_dim ** (-0.5)], [1.0]], f32)
    projected_low, got_one = tie(projected_low, got_one)
    mlp_one = halve(add_low(kept_one, got_one), "dp", dp_bits[1][2:], 2)
    normed_grad = ein("cn,cd->nd", projected_low.reshape(-1, own * length), qkv_full)
    normed_grad = normed_grad.reshape(own, length, model_width)
    norm_val, norm_pull = jax.vjp(rms_scale, latent_f, scale_one, shift_one)
    latent_grad, scale_one_grad, shift_one_grad = norm_pull(normed_grad)
    latent_grad = (latent_grad + middle_grad).astype(bf16)

    normed_t, branch_t, latent_grad = tie(by_owner(normed_flat), by_owner(branch_low), latent_grad)

    def grads_of(which):
        kept, sent = attend_grads(
            m_orders[which],
            e_orders[which],
            normed_t,
            branch_t,
            projected_low.reshape(mp_size, 3 * local_dim, -1),
            attended,
        )
        return kept, swap(sent, "dp", dp_bits[which][0])

    attend_one = halve(add_low(*grads_of(1)), "dp", dp_bits[1][1:], 1)
    normed_t, got_zero = tie(normed_t, got_zero)
    mlp_zero = halve(add_low(kept_zero, got_zero), "dp", dp_bits[0][2:], 2)
    attend_zero = halve(add_low(*grads_of(0)), "dp", dp_bits[0][1:], 1)
    mlp_grad = reduce_mp(mlp_zero, mlp_one)
    attend_grad = reduce_mp(attend_zero, attend_one)

    latent_back = lax.all_to_all(latent_grad, "mp", split_axis=1, concat_axis=0, tiled=True)
    back_within = pair_slot * dp_size + jnp.mod(my_place - starts[pair_peer], dp_size)
    back_slot = jnp.clip((starts[pair_peer] + back_within - my_place) // dp_size, 0, images - 1)
    back_patches = jnp.take(latent_back, back_slot, axis=0)
    got_patches = lax.all_to_all(back_patches, "dp", split_axis=0, concat_axis=0, tiled=True)
    slot_ids = jnp.arange(capacity)
    slot_live = slot_ids < my_count
    home_peer = dest_perm[jnp.mod(my_start + slot_ids, dp_size)]
    home_index = home_peer * slot_count + jnp.minimum(slot_ids // dp_size, slot_count - 1)
    patch_grad = jnp.where(slot_live[:, None, None], jnp.take(got_patches, home_index, axis=0), 0)

    modulation_grad = jnp.stack(
        [
            shift_one_grad[:, 0],
            scale_one_grad[:, 0],
            gate_one_grad,
            shift_two_grad[:, 0],
            scale_two_grad[:, 0],
            gate_two_grad,
        ],
        1,
    ).astype(bf16)
    packed = jnp.concatenate([modulation_grad.reshape(-1), gains_grad.astype(bf16).reshape(-1)])
    packed = xor_gather(packed, gather_bits)[0]
    mod_all = packed[:, : own * 6 * model_width].reshape(total_images, 6, model_width)
    gains_total = packed[:, own * 6 * model_width :].reshape(-1, 2, head_dim)
    gains_total = jnp.sum(gains_total.astype(f32), axis=0)
    gains_total = jnp.sum(
        jnp.where(order[:, None] == jnp.arange(head_dim)[None, :], gains_total[:, :, None], 0.0), axis=1
    )
    width_dp = model_width // dp_size
    width_mp = model_width // mp_size
    row0 = dp_index * width_dp
    silu_rows = lax.dynamic_slice_in_dim(silu_all, row0, width_dp, 1)
    mod_cols = lax.dynamic_slice_in_dim(mod_all, mp_index * width_mp, width_mp, 2)
    ada_grad = ein("id,ikc->dkc", silu_rows, mod_cols)
    ada_rows = lax.dynamic_slice_in_dim(ada_weight, row0, width_dp, 0)
    silu_grad = ein("ikc,dkc->id", mod_all, ada_rows)
    cond_rows = lax.dynamic_slice_in_dim(cond_all, row0, width_dp, 1)
    silu_val, silu_pull = jax.vjp(jax.nn.silu, cond_rows)
    condition_low = silu_pull(silu_grad)[0].astype(bf16)
    time_grad = ein("in,id->nd", bin_hot, condition_low)
    class_grad = ein("in,id->nd", label_hot, condition_low)

    expand_grad = mlp_grad[:2].swapaxes(0, 1)
    down_grad = mlp_grad[2].T
    out_grad = attend_grad[:, 3 * local_dim :].T
    qkv_grad = lax.dot_general(
        attend_grad[:, : 3 * local_dim],
        turn.astype(f32),
        (((1,), (0,)), ((), ())),
        precision=lax.Precision.HIGHEST,
        preferred_element_type=f32,
    )
    qkv_grad = qkv_grad.reshape(-1, 3, local_dim)
    return (
        result,
        patch_grad,
        time_grad,
        class_grad,
        ada_grad,
        qkv_grad,
        gains_total,
        out_grad,
        expand_grad,
        down_grad,
    )


def solution(mesh):
    in_specs = (
        P("dp", "mp", None),
        P("dp", "mp", None),
        P("dp"),
        P("dp"),
        P(),
        P(),
        P(),
        P(),
        P(),
        P(None, None, "mp"),
        P(),
        P("mp", None),
        P(None, None, "mp"),
        P("mp", None),
    )
    out_specs = (
        P("dp", "mp", None),
        P("dp", "mp", None),
        P(None, "dp"),
        P(None, "dp"),
        P("dp", None, "mp"),
        P("dp", None, "mp"),
        P(),
        P("mp", "dp"),
        P("dp", None, "mp"),
        P("mp", "dp"),
    )
    return jax.shard_map(shards, mesh=mesh, in_specs=in_specs, out_specs=out_specs, check_vma=False)
```

```python
import math

import jax
import jax.numpy as jnp
from jax import lax
from jax.experimental import pallas as pl
from jax.experimental.pallas import tpu as pltpu
from jax.sharding import PartitionSpec as P

GRID = 16
NCLS = 1000
NBINS = 16

epsilon = 1e-06
rope_base = 10000.0
f32 = jnp.float32
bf16 = jnp.bfloat16


def rms_scale(values, scaling, shifting):
    return (
        values * lax.rsqrt(jnp.mean(values * values, -1, keepdims=True) + epsilon) * (1.0 + scaling)
        + shifting
    )


def feature_order(head_dim):
    quarter = head_dim // 4
    firsts = list(range(quarter)) + list(range(2 * quarter, 3 * quarter))
    cut = len(firsts) // 8 * 8
    seconds = [i + quarter for i in firsts]
    return firsts[:cut] + seconds[:cut] + firsts[cut:] + seconds[cut:], cut


def rope_tables(length, head_dim):
    quarter = head_dim // 4
    order, cut = feature_order(head_dim)
    position = jnp.arange(length)
    places = jnp.stack([position // GRID, position % GRID]).astype(f32)
    frequency = rope_base ** (-jnp.arange(quarter).astype(f32) / quarter)
    angle = (frequency[None, :, None] * places[:, None, :]).reshape(2 * quarter, length)
    cosine, sine = jnp.cos(angle), jnp.sin(angle)
    cos_tab = jnp.concatenate([cosine[:cut], cosine[:cut], cosine[cut:], cosine[cut:]])
    sin_tab = jnp.concatenate([-sine[:cut], sine[:cut], -sine[cut:], sine[cut:]])
    return cos_tab, sin_tab


def partner(values, cut):
    rest = values[2 * cut :]
    half = rest.shape[0] // 2
    return jnp.concatenate(
        [values[cut : 2 * cut], values[:cut], pltpu.roll(rest, half, 0)], axis=0
    )


def head_scale(values):
    return lax.rsqrt(jnp.mean(values * values, axis=0, keepdims=True) + epsilon)


def dot_00(a, b):
    return lax.dot_general(a, b, (((0,), (0,)), ((), ())), preferred_element_type=f32)


def dot_11(a, b):
    return lax.dot_general(a, b, (((1,), (1,)), ((), ())), preferred_element_type=f32)


def dot_10(a, b):
    return lax.dot_general(a, b, (((1,), (0,)), ((), ())), preferred_element_type=f32)


def softmax_first(scores):
    shifted = jnp.exp(scores - jnp.max(scores, axis=0, keepdims=True))
    return shifted * (1.0 / jnp.sum(shifted, axis=0, keepdims=True))


def attend_kernel(
    x_ref, w_ref, gains_ref, cos_ref, sin_ref, proj_ref, att_ref, out_ref
):
    head_dim = gains_ref.shape[1]
    rows_all, length = att_ref.shape[1:]
    cut = feature_order(head_dim)[1]
    cos_tab, sin_tab = cos_ref[...], sin_ref[...]
    proj = dot_11(w_ref[0, : 3 * rows_all], x_ref[...])
    proj_ref[0] = proj
    outs = []
    for head in range(rows_all // head_dim):
        lows = []
        for kind in range(2):
            start = kind * rows_all + head * head_dim
            raw = proj[start : start + head_dim]
            scaled = raw * head_scale(raw) * gains_ref[kind]
            turned = scaled * cos_tab + partner(scaled, cut) * sin_tab
            lows.append(turned.astype(bf16))
        start = 2 * rows_all + head * head_dim
        value_low = proj[start : start + head_dim].astype(bf16)
        probs = softmax_first(dot_00(lows[1], lows[0]))
        outs.append(dot_10(value_low, probs.astype(bf16)))
    att = jnp.concatenate(outs, axis=0).astype(bf16)
    att_ref[0] = att
    part = dot_00(att, w_ref[0, 3 * rows_all :])
    add_rows(out_ref, part, pl.program_id(0) == 0, pl.program_id(1), length)


def add_rows(out_ref, part, first, index, length):
    rows = pl.ds(pl.multiple_of(index * length, length), length)

    @pl.when(first)
    def _():
        out_ref[rows, :] = part

    @pl.when(jnp.logical_not(first))
    def _():
        out_ref[rows, :] += part


def attend_back_kernel(
    proj_ref, low_ref, w_ref, gains_ref, cos_ref, sin_ref, out_ref, gain_grad_ref, x_grad_ref
):
    head_dim = gains_ref.shape[1]
    rows_all, length = proj_ref.shape[1] // 3, proj_ref.shape[2]
    cut = feature_order(head_dim)[1]
    cos_tab, sin_tab = cos_ref[...], sin_ref[...]

    @pl.when((pl.program_id(0) == 0) & (pl.program_id(1) == 0))
    def _():
        gain_grad_ref[...] = jnp.zeros_like(gain_grad_ref)

    outs = [[], [], []]
    cot_all = dot_11(w_ref[0, 3 * rows_all :], low_ref[...])
    for head in range(rows_all // head_dim):
        lows, units, scales = [], [], []
        for kind in range(2):
            start = kind * rows_all + head * head_dim
            raw = proj_ref[0, start : start + head_dim, :]
            scale = head_scale(raw)
            unit = raw * scale
            scaled = unit * gains_ref[kind]
            turned = scaled * cos_tab + partner(scaled, cut) * sin_tab
            lows.append(turned.astype(bf16))
            units.append(unit)
            scales.append(scale)
        start = 2 * rows_all + head * head_dim
        value_low = proj_ref[0, start : start + head_dim, :].astype(bf16)
        cot_low = cot_all[head * head_dim : (head + 1) * head_dim].astype(bf16)
        probs = softmax_first(dot_00(lows[1], lows[0]))
        prob_grad = dot_00(value_low, cot_low)
        outs[2].append(dot_11(cot_low, probs.astype(bf16)))
        mean = jnp.sum(probs * prob_grad, axis=0, keepdims=True)
        score_low = (probs * (prob_grad - mean)).astype(bf16)
        turned_grads = (dot_10(lows[1], score_low), dot_11(lows[0], score_low))
        for kind in range(2):
            grad = turned_grads[kind]
            grad = grad * cos_tab + partner(grad * sin_tab, cut)
            gain_grad_ref[kind] += grad * units[kind]
            grad = grad * gains_ref[kind]
            along = jnp.mean(grad * units[kind], axis=0, keepdims=True)
            outs[kind].append(scales[kind] * (grad - units[kind] * along))
    grads = jnp.concatenate(outs[0] + outs[1] + outs[2], axis=0).astype(bf16)
    out_ref[0] = grads
    part = dot_00(grads, w_ref[0, : 3 * rows_all])
    add_rows(x_grad_ref, part, pl.program_id(0) == 0, pl.program_id(1), length)


def attend_specs(groups, rows, own, length, width, head_dim):
    proj = pl.BlockSpec((1, 3 * rows, length), lambda g, i: (g, 0, i))
    att = pl.BlockSpec((1, rows, length), lambda g, i: (g, 0, i))
    x = pl.BlockSpec((length, width), lambda g, i: (i, 0))
    w = pl.BlockSpec((1, 4 * rows, width), lambda g, i: (g, 0, 0))
    gains = pl.BlockSpec((2, head_dim, 1), lambda g, i: (0, 0, 0))
    table = pl.BlockSpec((head_dim, length), lambda g, i: (0, 0))
    grads = pl.BlockSpec((2, head_dim, length), lambda g, i: (0, 0, 0))
    total = pl.BlockSpec((own * length, width), lambda g, i: (0, 0))
    return proj, att, x, w, gains, table, grads, total


def attend(x, weights, gains, tables, own):
    groups, rows, width = weights.shape[0], weights.shape[1] // 4, weights.shape[2]
    tokens = x.shape[0]
    length, head_dim = tokens // own, gains.shape[1]
    proj_s, att_s, x_s, w_s, gains_s, table_s, _, total_s = attend_specs(
        groups, rows, own, length, width, head_dim
    )
    return pl.pallas_call(
        attend_kernel,
        grid=(groups, own),
        in_specs=[x_s, w_s, gains_s, table_s, table_s],
        out_specs=[proj_s, att_s, total_s],
        out_shape=[
            jax.ShapeDtypeStruct((groups, 3 * rows, tokens), f32),
            jax.ShapeDtypeStruct((groups, rows, tokens), bf16),
            jax.ShapeDtypeStruct((tokens, width), f32),
        ],
        compiler_params=pltpu.CompilerParams(vmem_limit_bytes=56 << 20),
        cost_estimate=pl.CostEstimate(
            flops=groups * rows * tokens * (4 * length + 8 * width),
            bytes_accessed=14 * groups * rows * tokens,
            transcendentals=groups * rows // head_dim * tokens * length,
        ),
        name="attend",
    )(x, weights, gains, *tables)


def attend_back(proj, low, weights, gains, tables, own):
    groups, rows, width = weights.shape[0], weights.shape[1] // 4, weights.shape[2]
    tokens = low.shape[0]
    length, head_dim = tokens // own, gains.shape[1]
    proj_s, _, x_s, w_s, gains_s, table_s, grads_s, total_s = attend_specs(
        groups, rows, own, length, width, head_dim
    )
    return pl.pallas_call(
        attend_back_kernel,
        grid=(groups, own),
        in_specs=[proj_s, x_s, w_s, gains_s, table_s, table_s],
        out_specs=[proj_s, grads_s, total_s],
        out_shape=[
            jax.ShapeDtypeStruct(proj.shape, bf16),
            jax.ShapeDtypeStruct((2, head_dim, length), f32),
            jax.ShapeDtypeStruct((tokens, width), f32),
        ],
        compiler_params=pltpu.CompilerParams(vmem_limit_bytes=56 << 20),
        cost_estimate=pl.CostEstimate(
            flops=groups * rows * tokens * (10 * length + 8 * width),
            bytes_accessed=18 * groups * rows * tokens,
            transcendentals=groups * rows // head_dim * tokens * length,
        ),
        name="attend_back",
    )(proj, low, weights, gains, *tables)


def sigmoid(values):
    return 1.0 / (1.0 + jnp.exp(-values))


def kind_of(w_ref, kind):
    pieces, _, rows, width = w_ref.shape[1:]
    return w_ref[0, :, kind].reshape(pieces * rows, width)


def mlp_kernel(x_ref, w_ref, save_ref, out_ref):
    first = pl.program_id(0) == 0
    x = x_ref[...]
    gate = dot_11(x, kind_of(w_ref, 0))
    up = dot_11(x, kind_of(w_ref, 1))
    save_ref[0, 0] = gate.astype(bf16)
    save_ref[0, 1] = up.astype(bf16)
    hidden = (gate * sigmoid(gate) * up).astype(bf16)
    part = dot_10(hidden, kind_of(w_ref, 2))
    add_rows(out_ref, part, first, 0, x.shape[0])


def mlp(x, weights):
    groups, pieces, _, rows, width = weights.shape
    units, tokens = pieces * rows, x.shape[0]
    return pl.pallas_call(
        mlp_kernel,
        grid=(groups,),
        in_specs=[
            pl.BlockSpec((tokens, width), lambda g: (0, 0)),
            pl.BlockSpec((1, pieces, 3, rows, width), lambda g: (g, 0, 0, 0, 0)),
        ],
        out_specs=[
            pl.BlockSpec((1, 2, tokens, units), lambda g: (g, 0, 0, 0)),
            pl.BlockSpec((tokens, width), lambda g: (0, 0)),
        ],
        out_shape=[
            jax.ShapeDtypeStruct((groups, 2, tokens, units), bf16),
            jax.ShapeDtypeStruct((tokens, width), f32),
        ],
        compiler_params=pltpu.CompilerParams(vmem_limit_bytes=60 << 20),
        cost_estimate=pl.CostEstimate(
            flops=6 * groups * units * tokens * width,
            bytes_accessed=4 * groups * units * tokens + 6 * groups * units * width,
            transcendentals=groups * units * tokens,
        ),
        name="mlp",
    )(x, weights)


def fill_rows(order_ref, source_ref, target_ref):
    blocks, rows = source_ref.shape[0], source_ref.shape[1]
    for place in range(blocks):
        target_ref[place * rows : (place + 1) * rows, :] = source_ref[order_ref[place]]


def mlp_back_kernel(
    m_ref, e_ref, xt_ref, lowt_ref, low_ref, save_ref, w_ref,
    keep_ref, send_ref, two_ref, xs, lows, parts,
):
    first = pl.program_id(0) == 0
    tokens, width = low_ref.shape
    step = math.gcd(tokens, 512)

    @pl.when(first)
    def _():
        fill_rows(e_ref, xt_ref, xs)
        fill_rows(e_ref, lowt_ref, lows)

    for index in range(tokens // step):
        rows = pl.ds(index * step, step)
        hidden_grad = dot_11(low_ref[rows, :], kind_of(w_ref, 2))
        gate = save_ref[0, 0, rows, :].astype(f32)
        up = save_ref[0, 1, rows, :].astype(f32)
        sig = sigmoid(gate)
        swish = gate * sig
        gate_low = (hidden_grad * up * (sig + swish * (1.0 - sig))).astype(bf16)
        up_low = (hidden_grad * swish).astype(bf16)
        parts[0, rows, :] = gate_low
        parts[1, rows, :] = up_low
        parts[2, rows, :] = (swish * up).astype(bf16)
        part = dot_10(gate_low, kind_of(w_ref, 0)) + dot_10(up_low, kind_of(w_ref, 1))
        add_rows(two_ref, part, first, index, step)

    half = width // 2
    for out_ref, rows in ((keep_ref, slice(0, half)), (send_ref, slice(half, width))):
        x_rows = xs[rows, :]
        for kind in range(2):
            out_ref[0, kind] = dot_10(x_rows, parts[kind]).astype(bf16)
        out_ref[0, 2] = dot_10(lows[rows, :], parts[2]).astype(bf16)


def mlp_back(m_order, e_order, xt, lowt, low, save, weights):
    _, pieces, _, rows, width = weights.shape
    units, tokens = pieces * rows, low.shape[0]
    blocks = m_order.shape[0]
    once = pl.Buffered(1)
    whole = lambda p, m, e: (0, 0)
    whole3 = lambda p, m, e: (0, 0, 0)
    half = jax.ShapeDtypeStruct((blocks, 3, width // 2, units), bf16)
    half_spec = pl.BlockSpec((1, 3, width // 2, units), lambda p, m, e: (p, 0, 0, 0))
    return pl.pallas_call(
        mlp_back_kernel,
        grid_spec=pltpu.PrefetchScalarGridSpec(
            num_scalar_prefetch=2,
            grid=(blocks,),
            in_specs=[
                pl.BlockSpec(xt.shape, whole3, pipeline_mode=once),
                pl.BlockSpec(lowt.shape, whole3, pipeline_mode=once),
                pl.BlockSpec((tokens, width), whole, pipeline_mode=once),
                pl.BlockSpec((1, 2, tokens, units), lambda p, m, e: (m[p], 0, 0, 0)),
                pl.BlockSpec((1, pieces, 3, rows, width), lambda p, m, e: (m[p], 0, 0, 0, 0)),
            ],
            out_specs=[half_spec, half_spec, pl.BlockSpec((tokens, width), whole)],
            scratch_shapes=[
                pltpu.VMEM((width, tokens), bf16),
                pltpu.VMEM((width, tokens), bf16),
                pltpu.VMEM((3, tokens, units), bf16),
            ],
        ),
        out_shape=[half, half, jax.ShapeDtypeStruct((tokens, width), f32)],
        compiler_params=pltpu.CompilerParams(vmem_limit_bytes=62 << 20),
        cost_estimate=pl.CostEstimate(
            flops=12 * blocks * units * tokens * width,
            bytes_accessed=4 * blocks * units * tokens + 12 * blocks * units * width,
            transcendentals=blocks * units * tokens,
        ),
        name="mlp_back",
    )(m_order, e_order, xt, lowt, low, save, weights)


def attend_grads_kernel(
    m_ref, e_ref, xt_ref, lowt_ref, proj_ref, att_ref, keep_ref, send_ref, xs, lows
):
    @pl.when(pl.program_id(0) == 0)
    def _():
        fill_rows(e_ref, xt_ref, xs)
        fill_rows(e_ref, lowt_ref, lows)

    width = xs.shape[0]
    half = width // 2
    columns = proj_ref.shape[1]

    for out_ref, rows in ((keep_ref, slice(0, half)), (send_ref, slice(half, width))):
        out_ref[0, :, :columns] = dot_11(xs[rows, :], proj_ref[0]).astype(bf16)
        out_ref[0, :, columns:] = dot_11(lows[rows, :], att_ref[0]).astype(bf16)


def attend_grads(m_order, e_order, xt, lowt, proj, att):
    rows, tokens = att.shape[1:]
    width = xt.shape[0] * xt.shape[1]
    blocks = m_order.shape[0]
    whole3 = lambda p, m, e: (0, 0, 0)
    half = jax.ShapeDtypeStruct((blocks, width // 2, 4 * rows), bf16)
    half_spec = pl.BlockSpec((1, width // 2, 4 * rows), lambda p, m, e: (p, 0, 0))
    return pl.pallas_call(
        attend_grads_kernel,
        grid_spec=pltpu.PrefetchScalarGridSpec(
            num_scalar_prefetch=2,
            grid=(blocks,),
            in_specs=[
                pl.BlockSpec(xt.shape, whole3, pipeline_mode=pl.Buffered(1)),
                pl.BlockSpec(lowt.shape, whole3, pipeline_mode=pl.Buffered(1)),
                pl.BlockSpec((1, 3 * rows, tokens), lambda p, m, e: (m[p], 0, 0)),
                pl.BlockSpec((1, rows, tokens), lambda p, m, e: (m[p], 0, 0)),
            ],
            out_specs=[half_spec, half_spec],
            scratch_shapes=[
                pltpu.VMEM((width, tokens), bf16),
                pltpu.VMEM((width, tokens), bf16),
            ],
        ),
        out_shape=[half, half],
        compiler_params=pltpu.CompilerParams(vmem_limit_bytes=56 << 20),
        cost_estimate=pl.CostEstimate(
            flops=8 * blocks * rows * tokens * width,
            bytes_accessed=8 * blocks * rows * (tokens + width),
            transcendentals=0,
        ),
        name="attend_grads",
    )(m_order, e_order, xt, lowt, proj, att)


def dot(a, b):
    return jnp.dot(a, b, preferred_element_type=f32)


def ein(spec, a, b):
    return jnp.einsum(spec, a, b, preferred_element_type=f32)


def gather_pieces(piece, mp_size):
    whole = lax.all_gather(piece, ("mp", "dp"), axis=0, tiled=False)
    return whole.reshape((mp_size, -1) + piece.shape)


def take_rows(values, index):
    return jnp.take(values, index, axis=0, mode="clip")


def bits_of(size):
    return [1 << i for i in range(size.bit_length() - 1)]


def swap(values, axis, bit):
    size = lax.axis_size(axis)
    return lax.ppermute(values, axis, [(i, i ^ bit) for i in range(size)])


def xor_gather(values, axes_bits):
    names = sorted({axis for axis, _ in axes_bits})
    places = [{name: 0 for name in names}]
    values = values[None]
    for axis, bit in axes_bits:
        values = jnp.concatenate([values, swap(values, axis, bit)], axis=0)
        places = places + [dict(place, **{axis: place[axis] ^ bit}) for place in places]
    return values, {name: [place[name] for place in places] for name in names}


def halving_order(bits):
    order = [0]
    for bit in reversed(bits):
        order = order + [place ^ bit for place in order]
    return order


def add_low(kept, received):
    return (kept.astype(f32) + received.astype(f32)).astype(bf16)


def tie(*values):
    return lax.optimization_barrier(values)


def split(values, dim):
    size = values.shape[dim] // 2
    return (
        lax.slice_in_dim(values, 0, size, axis=dim),
        lax.slice_in_dim(values, size, 2 * size, axis=dim),
    )


def halve(values, axis, bits, dim):
    for bit in bits:
        kept, sent = split(values, dim)
        values = add_low(kept, swap(sent, axis, bit))
    return values


def shards(
    patches,
    cotangent,
    time_bins,
    labels,
    image_counts,
    dest_perm,
    time_table,
    class_table,
    ada_weight,
    qkv_weight,
    norm_gains,
    out_weight,
    expand_weight,
    down_weight,
):
    dp_size = lax.axis_size("dp")
    mp_size = lax.axis_size("mp")
    capacity = patches.shape[0]
    slot_count = capacity // dp_size
    images = cotangent.shape[0]
    local_len = patches.shape[1]
    model_width = patches.shape[2]
    length = local_len * mp_size
    head_dim = norm_gains.shape[1]
    local_dim = out_weight.shape[0]
    unit_count = down_weight.shape[0]
    own = images // mp_size
    total_images = images * dp_size
    order = jnp.array(feature_order(head_dim)[0])
    tables = rope_tables(length, head_dim)
    gains_f = norm_gains.astype(f32)[:, order]
    gains_f = (gains_f * jnp.array([[head_dim ** (-0.5)], [1.0]], f32))[:, :, None]
    dp_index = lax.axis_index("dp")
    mp_index = lax.axis_index("mp")

    columns = jnp.arange(3 * local_dim)
    places = columns // head_dim * head_dim + order[columns % head_dim]
    places = jnp.where(columns < 2 * local_dim, places, columns)
    turn = (places[:, None] == columns[None, :]).astype(bf16)
    starts = jnp.cumsum(image_counts) - image_counts
    finish = starts + image_counts
    my_start = starts[dp_index]
    my_count = image_counts[dp_index]
    device_ids = jnp.arange(dp_size)
    matches = (dest_perm[:, None] == device_ids[None, :]).astype(jnp.int32)
    inverse = jnp.sum(device_ids[:, None] * matches, axis=0)
    my_place = inverse[dp_index]
    pair_ids = jnp.arange(dp_size * slot_count)
    pair_peer = pair_ids // slot_count
    pair_slot = pair_ids % slot_count
    send_index = pair_slot * dp_size + jnp.mod(inverse[pair_peer] - my_start, dp_size)
    send_index = jnp.minimum(send_index, capacity - 1)
    send_patches = take_rows(patches, send_index)
    qkv_weight, out_weight, expand_weight, down_weight, send_patches = tie(
        qkv_weight, out_weight, expand_weight, down_weight, send_patches
    )
    share = 4 * local_dim // dp_size
    spots = dp_index * share + jnp.arange(share)
    take_qkv = jnp.where(spots < 3 * local_dim, places[jnp.minimum(spots, 3 * local_dim - 1)], -1)
    take_qkv = (take_qkv[:, None] == columns[None, :]).astype(bf16)
    take_out = (spots[:, None] - 3 * local_dim == jnp.arange(local_dim)[None, :]).astype(bf16)
    attend_piece = ein("rc,dc->rd", take_qkv, qkv_weight.reshape(model_width, -1))
    attend_piece = (attend_piece + dot(take_out, out_weight)).astype(bf16)
    share = unit_count // dp_size
    spots = dp_index * share + jnp.arange(share)
    take_units = (spots[:, None] == jnp.arange(unit_count)[None, :]).astype(bf16)
    mlp_piece = jnp.stack(
        [
            ein("rf,df->rd", take_units, expand_weight[:, 0]).astype(bf16),
            ein("rf,df->rd", take_units, expand_weight[:, 1]).astype(bf16),
            lax.dynamic_slice_in_dim(down_weight, dp_index * share, share, 0),
        ]
    )
    attend_full = gather_pieces(attend_piece, mp_size).reshape(mp_size, 4 * local_dim, -1)
    mlp_full = gather_pieces(mlp_piece, mp_size)
    if share % 16:
        mlp_full = mlp_full.swapaxes(1, 2).reshape(mp_size, 1, 3, unit_count, model_width)

    recv_patches = lax.all_to_all(send_patches, "dp", split_axis=0, concat_axis=0, tiled=True)
    rank_ids = jnp.arange(images) * dp_size + my_place
    source = jnp.sum((finish[None, :] <= rank_ids[:, None]).astype(jnp.int32), axis=1)
    within = rank_ids - starts[source]
    recv_index = source * slot_count + within // dp_size
    latent = take_rows(recv_patches, recv_index)
    latent = lax.all_to_all(latent, "mp", split_axis=0, concat_axis=1, tiled=True)
    cotangent, latent = tie(cotangent, latent)
    cot = lax.all_to_all(cotangent, "mp", split_axis=0, concat_axis=1, tiled=True)

    info, info_places = xor_gather(
        jnp.stack([time_bins, labels]), [("dp", bit) for bit in bits_of(dp_size)]
    )
    info = info.swapaxes(0, 1).reshape(2, -1)
    info_owner = jnp.repeat(dp_index ^ jnp.array(info_places["dp"]), capacity)
    info_slot = jnp.tile(jnp.arange(capacity), dp_size)
    info_count = jnp.sum(
        jnp.where(info_owner[:, None] == device_ids[None, :], image_counts[None, :], 0), axis=1
    )
    live_all = info_slot < info_count
    bin_totals = jnp.sum(
        ((info[0][:, None] == jnp.arange(NBINS)[None, :]) & live_all[:, None]).astype(f32), axis=0
    )
    gather_bits = [("mp", bit) for bit in bits_of(mp_size)[::-1]]
    gather_bits = gather_bits + [("dp", bit) for bit in bits_of(dp_size)[::-1]]
    places = {"dp": [0], "mp": [0]}
    for axis, bit in gather_bits:
        places = {
            name: places[name] + [place ^ (bit if name == axis else 0) for place in places[name]]
            for name in places
        }
    owner_all = jnp.repeat(dp_index ^ jnp.array(places["dp"]), own)
    group_all = jnp.repeat(mp_index ^ jnp.array(places["mp"]), own)
    row_all = group_all * own + jnp.tile(jnp.arange(own), dp_size * mp_size)
    place_all = jnp.sum(
        jnp.where(owner_all[:, None] == device_ids[None, :], inverse[None, :], 0), axis=1
    )
    rank_all = row_all * dp_size + place_all
    source_all = jnp.sum((finish[None, :] <= rank_all[:, None]).astype(jnp.int32), axis=1)
    start_all = jnp.sum(
        jnp.where(source_all[:, None] == device_ids[None, :], starts[None, :], 0), axis=1
    )
    slots_all = source_all * capacity + rank_all - start_all
    slot_hit = slots_all[:, None] == (info_owner * capacity + info_slot)[None, :]
    bins_all = jnp.sum(jnp.where(slot_hit, info[0][None, :], 0), axis=1)
    labels_all = jnp.sum(jnp.where(slot_hit, info[1][None, :], 0), axis=1)
    bin_hot = (bins_all[:, None] == jnp.arange(NBINS)[None, :])
    label_hot = (labels_all[:, None] == jnp.arange(NCLS)[None, :])
    weights_all = total_images / (NBINS * jnp.sum(bin_hot.astype(f32) * bin_totals[None, :], axis=1))
    bin_hot = bin_hot.astype(bf16)
    label_hot = label_hot.astype(bf16)
    cond_all = (dot(bin_hot, time_table) + dot(label_hot, class_table)).astype(bf16).astype(f32)
    silu_all = jax.nn.silu(cond_all).astype(bf16)
    silu_cond = silu_all[:own]
    weights = weights_all[:own]

    modulation = dot(silu_cond, ada_weight.reshape(model_width, 6 * model_width))
    modulation = modulation.reshape(own, 6, 1, model_width)
    shift_one = modulation[:, 0]
    scale_one = modulation[:, 1]
    gate_one = modulation[:, 2]
    shift_two = modulation[:, 3]
    scale_two = modulation[:, 4]
    gate_two = modulation[:, 5]

    latent_f = latent.astype(f32)
    normed = rms_scale(latent_f, scale_one, shift_one).astype(bf16)
    normed_flat = normed.reshape(-1, model_width)
    proj, attended, branch_one = attend(normed_flat, attend_full, gains_f, tables, own)
    branch_one = branch_one.reshape(own, length, model_width)
    middle = latent_f + gate_one * branch_one
    normed_two = rms_scale(middle, scale_two, shift_two).astype(bf16)
    two_flat = normed_two.reshape(-1, model_width)
    save, branch_two = mlp(two_flat, mlp_full)
    branch_two, cot = tie(branch_two, cot)
    out_cot = cot.astype(f32) * weights[:, None, None]
    branch_two = branch_two.reshape(own, length, model_width)
    result = (middle + gate_two * branch_two).astype(bf16)
    result = lax.all_to_all(result, "mp", split_axis=1, concat_axis=0, tiled=True)

    down_low = (gate_two * out_cot).astype(bf16)
    gate_two_grad = jnp.sum(out_cot * branch_two, axis=1)
    down_low = down_low.reshape(-1, model_width)
    dp_bits = bits_of(dp_size)
    dp_bits = (dp_bits, dp_bits[:1] + dp_bits[1:][::-1])
    mp_bits = bits_of(mp_size)
    e_orders = [(dp_index ^ jnp.array(halving_order(bits))).astype(jnp.int32) for bits in dp_bits]
    m_order = (mp_index ^ jnp.array(halving_order(mp_bits))).astype(jnp.int32)
    m_orders = (m_order[: mp_size // 2], m_order[mp_size // 2 :])

    def by_owner(values):
        return values.T.reshape(dp_size, model_width // dp_size, -1)

    def reduce_mp(kept, sent):
        kept = add_low(kept, swap(sent, "mp", mp_bits[0]))
        return halve(kept, "mp", mp_bits[1:], 0)[0].astype(f32)

    two_t, down_t = by_owner(two_flat), by_owner(down_low)
    kept_one, sent_one, two_one = mlp_back(
        m_orders[1], e_orders[1], two_t, down_t, down_low, save, mlp_full
    )
    got_one = swap(sent_one, "dp", dp_bits[1][0])
    kept_zero, sent_zero, two_zero = mlp_back(
        m_orders[0], e_orders[0], two_t, down_t, down_low, save, mlp_full
    )
    got_zero = swap(sent_zero, "dp", dp_bits[0][0])
    two_zero, got_one, result = tie(two_zero, got_one, result)
    kept_one, sent_one = split(add_low(kept_one, got_one), 2)
    got_one = swap(sent_one, "dp", dp_bits[1][1])
    two_parts = (two_zero, two_one)
    two_grad = (two_parts[0] + two_parts[1]).reshape(own, length, model_width)
    norm_val, norm_pull = jax.vjp(rms_scale, middle, scale_two, shift_two)
    middle_grad, scale_two_grad, shift_two_grad = norm_pull(two_grad)
    middle_grad = middle_grad + out_cot
    gate_one_grad = jnp.sum(middle_grad * branch_one, axis=1)
    branch_low = (gate_one * middle_grad).astype(bf16).reshape(-1, model_width)
    branch_low, got_zero = tie(branch_low, got_zero)
    kept_zero, sent_zero = split(add_low(kept_zero, got_zero), 2)
    got_zero = swap(sent_zero, "dp", dp_bits[0][1])
    projected_low, gains_grad, normed_grad = attend_back(
        proj, branch_low, attend_full, gains_f, tables, own
    )
    gains_grad = jnp.sum(gains_grad, axis=2) * jnp.array([[head_dim ** (-0.5)], [1.0]], f32)
    projected_low, normed_grad, got_one = tie(projected_low, normed_grad, got_one)
    mlp_one = halve(add_low(kept_one, got_one), "dp", dp_bits[1][2:], 2)
    normed_grad = normed_grad.reshape(own, length, model_width)
    norm_val, norm_pull = jax.vjp(rms_scale, latent_f, scale_one, shift_one)
    latent_grad, scale_one_grad, shift_one_grad = norm_pull(normed_grad)
    latent_grad = (latent_grad + middle_grad).astype(bf16)

    normed_t, branch_t, latent_grad = tie(by_owner(normed_flat), by_owner(branch_low), latent_grad)

    def grads_of(which):
        kept, sent = attend_grads(
            m_orders[which],
            e_orders[which],
            normed_t,
            branch_t,
            projected_low,
            attended,
        )
        return kept, swap(sent, "dp", dp_bits[which][0])

    kept_one, got_one = grads_of(1)
    normed_t, got_zero = tie(normed_t, got_zero)
    mlp_zero = halve(add_low(kept_zero, got_zero), "dp", dp_bits[0][2:], 2)
    kept_zero, got_zero = grads_of(0)
    kept_zero, got_one = tie(kept_zero, got_one)
    attend_one = halve(add_low(kept_one, got_one), "dp", dp_bits[1][1:], 1)
    kept_zero, sent_zero = split(add_low(kept_zero, got_zero), 1)
    got_zero = swap(sent_zero, "dp", dp_bits[0][1])
    mlp_grad = reduce_mp(mlp_zero, mlp_one)

    latent_back = lax.all_to_all(latent_grad, "mp", split_axis=1, concat_axis=0, tiled=True)
    latent_back, kept_zero = tie(latent_back, kept_zero)
    attend_zero = halve(add_low(kept_zero, got_zero), "dp", dp_bits[0][2:], 1)
    attend_grad = reduce_mp(attend_zero, attend_one)
    back_within = pair_slot * dp_size + jnp.mod(my_place - starts[pair_peer], dp_size)
    back_slot = jnp.clip((starts[pair_peer] + back_within - my_place) // dp_size, 0, images - 1)
    back_patches = take_rows(latent_back, back_slot)
    got_patches = lax.all_to_all(back_patches, "dp", split_axis=0, concat_axis=0, tiled=True)
    slot_ids = jnp.arange(capacity)
    slot_live = slot_ids < my_count
    home_peer = dest_perm[jnp.mod(my_start + slot_ids, dp_size)]
    home_index = home_peer * slot_count + jnp.minimum(slot_ids // dp_size, slot_count - 1)
    patch_grad = jnp.where(slot_live[:, None, None], take_rows(got_patches, home_index), 0)

    modulation_grad = jnp.stack(
        [
            shift_one_grad[:, 0],
            scale_one_grad[:, 0],
            gate_one_grad,
            shift_two_grad[:, 0],
            scale_two_grad[:, 0],
            gate_two_grad,
        ],
        1,
    ).astype(bf16)
    packed = jnp.concatenate([modulation_grad.reshape(-1), gains_grad.astype(bf16).reshape(-1)])
    packed = xor_gather(packed, gather_bits)[0]
    mod_all = packed[:, : own * 6 * model_width].reshape(total_images, 6, model_width)
    gains_total = packed[:, own * 6 * model_width :].reshape(-1, 2, head_dim)
    gains_total = jnp.sum(gains_total.astype(f32), axis=0)
    gains_total = jnp.sum(
        jnp.where(order[:, None] == jnp.arange(head_dim)[None, :], gains_total[:, :, None], 0.0), axis=1
    )
    width_dp = model_width // dp_size
    width_mp = model_width // mp_size
    row0 = dp_index * width_dp
    silu_rows = lax.dynamic_slice_in_dim(silu_all, row0, width_dp, 1)
    mod_cols = lax.dynamic_slice_in_dim(mod_all, mp_index * width_mp, width_mp, 2)
    ada_grad = ein("id,ikc->dkc", silu_rows, mod_cols)
    ada_rows = lax.dynamic_slice_in_dim(ada_weight, row0, width_dp, 0)
    silu_grad = ein("ikc,dkc->id", mod_all, ada_rows)
    cond_rows = lax.dynamic_slice_in_dim(cond_all, row0, width_dp, 1)
    silu_val, silu_pull = jax.vjp(jax.nn.silu, cond_rows)
    condition_low = silu_pull(silu_grad)[0].astype(bf16)
    time_grad = ein("in,id->nd", bin_hot, condition_low)
    class_grad = ein("in,id->nd", label_hot, condition_low)

    expand_grad = mlp_grad[:2].swapaxes(0, 1)
    down_grad = mlp_grad[2].T
    out_grad = attend_grad[:, 3 * local_dim :].T
    qkv_grad = lax.dot_general(
        attend_grad[:, : 3 * local_dim],
        turn.astype(f32),
        (((1,), (0,)), ((), ())),
        precision=lax.Precision.HIGHEST,
        preferred_element_type=f32,
    )
    qkv_grad = qkv_grad.reshape(-1, 3, local_dim)
    return (
        result,
        patch_grad,
        time_grad,
        class_grad,
        ada_grad,
        qkv_grad,
        gains_total,
        out_grad,
        expand_grad,
        down_grad,
    )


def solution(mesh):
    in_specs = (
        P("dp", "mp", None),
        P("dp", "mp", None),
        P("dp"),
        P("dp"),
        P(),
        P(),
        P(),
        P(),
        P(),
        P(None, None, "mp"),
        P(),
        P("mp", None),
        P(None, None, "mp"),
        P("mp", None),
    )
    out_specs = (
        P("dp", "mp", None),
        P("dp", "mp", None),
        P(None, "dp"),
        P(None, "dp"),
        P("dp", None, "mp"),
        P("dp", None, "mp"),
        P(),
        P("mp", "dp"),
        P("dp", None, "mp"),
        P("mp", "dp"),
    )
    return jax.shard_map(shards, mesh=mesh, in_specs=in_specs, out_specs=out_specs, check_vma=False)
```

```python
import math

import jax
import jax.numpy as jnp
import numpy as np
from jax import lax
from jax.experimental import pallas as pl
from jax.experimental.pallas import tpu as pltpu
from jax.sharding import PartitionSpec as P

GRID = 16
NCLS = 1000
NBINS = 16

epsilon = 1e-06
rope_base = 10000.0
f32 = jnp.float32
bf16 = jnp.bfloat16


def feature_order(head_dim):
    quarter = head_dim // 4
    firsts = list(range(quarter)) + list(range(2 * quarter, 3 * quarter))
    cut = len(firsts) // 8 * 8
    seconds = [i + quarter for i in firsts]
    return firsts[:cut] + seconds[:cut] + firsts[cut:] + seconds[cut:], cut


def rope_tables(length, head_dim):
    quarter = head_dim // 4
    order, cut = feature_order(head_dim)
    position = jnp.arange(length)
    places = jnp.stack([position // GRID, position % GRID]).astype(f32)
    frequency = rope_base ** (-jnp.arange(quarter).astype(f32) / quarter)
    angle = (frequency[None, :, None] * places[:, None, :]).reshape(2 * quarter, length)
    cosine, sine = jnp.cos(angle), jnp.sin(angle)
    cos_tab = jnp.concatenate([cosine[:cut], cosine[:cut], cosine[cut:], cosine[cut:]])
    sin_tab = jnp.concatenate([-sine[:cut], sine[:cut], -sine[cut:], sine[cut:]])
    return cos_tab, sin_tab


def partner(values, cut):
    rest = values[2 * cut :]
    half = rest.shape[0] // 2
    return jnp.concatenate(
        [values[cut : 2 * cut], values[:cut], pltpu.roll(rest, half, 0)], axis=0
    )


def head_scale(values):
    return lax.rsqrt(jnp.mean(values * values, axis=0, keepdims=True) + epsilon)


def dot_00(a, b):
    return lax.dot_general(a, b, (((0,), (0,)), ((), ())), preferred_element_type=f32)


def dot_11(a, b):
    return lax.dot_general(a, b, (((1,), (1,)), ((), ())), preferred_element_type=f32)


def dot_10(a, b):
    return lax.dot_general(a, b, (((1,), (0,)), ((), ())), preferred_element_type=f32)


def softmax_first(scores):
    shifted = jnp.exp(scores - jnp.max(scores, axis=0, keepdims=True))
    return shifted * (1.0 / jnp.sum(shifted, axis=0, keepdims=True))


SHIFT_ONE, SCALE_ONE, GATE_ONE, SHIFT_TWO, SCALE_TWO, GATE_TWO, WEIGHT = range(7)


def row_of(mods_ref, which):
    return mods_ref[0, which : which + 1, :]


def rms(values):
    scale = lax.rsqrt(jnp.mean(values * values, -1, keepdims=True) + epsilon)
    return values * scale, scale


def rms_back(grad, unit, scale, scaling):
    grad = grad * (1.0 + scaling)
    return scale * (grad - unit * jnp.mean(grad * unit, -1, keepdims=True))


def row_sum(values):
    return jnp.sum(values, axis=0, keepdims=True)


def put_rows(sums_ref, rows):
    for which in range(sums_ref.shape[1]):
        value = rows.get(which, jnp.zeros((1, sums_ref.shape[2]), f32))
        sums_ref[0, which : which + 1, :] = value


def attend_kernel(
    latent_ref, mods_ref, w_ref, gains_ref, cos_ref, sin_ref,
    proj_ref, att_ref, out_ref, x_ref, xt_ref, middle_ref, two_ref, twot_ref,
):
    head_dim = gains_ref.shape[1]
    rows_all, length = att_ref.shape[1:]
    cut = feature_order(head_dim)[1]
    cos_tab, sin_tab = cos_ref[...], sin_ref[...]
    group, image = pl.program_id(0), pl.program_id(1)
    tokens = pl.ds(pl.multiple_of(image * length, length), length)

    @pl.when(group == 0)
    def _():
        unit = rms(latent_ref[...].astype(f32))[0]
        x = unit * (1.0 + row_of(mods_ref, SCALE_ONE)) + row_of(mods_ref, SHIFT_ONE)
        x = x.astype(bf16)
        x_ref[tokens, :] = x
        xt_ref[:, tokens] = x.T

    proj = dot_11(w_ref[0, : 3 * rows_all], x_ref[tokens, :])
    proj_ref[0] = proj
    outs = []
    for head in range(rows_all // head_dim):
        lows = []
        for kind in range(2):
            start = kind * rows_all + head * head_dim
            raw = proj[start : start + head_dim]
            scaled = raw * head_scale(raw) * gains_ref[kind]
            turned = scaled * cos_tab + partner(scaled, cut) * sin_tab
            lows.append(turned.astype(bf16))
        start = 2 * rows_all + head * head_dim
        value_low = proj[start : start + head_dim].astype(bf16)
        probs = softmax_first(dot_00(lows[1], lows[0]))
        outs.append(dot_10(value_low, probs.astype(bf16)))
    att = jnp.concatenate(outs, axis=0).astype(bf16)
    att_ref[0] = att
    part = dot_00(att, w_ref[0, 3 * rows_all :])
    add_rows(out_ref, part, group == 0, image, length)

    @pl.when(group == pl.num_programs(0) - 1)
    def _():
        middle = latent_ref[...].astype(f32) + row_of(mods_ref, GATE_ONE) * out_ref[tokens, :]
        middle_ref[tokens, :] = middle
        two = rms(middle)[0] * (1.0 + row_of(mods_ref, SCALE_TWO)) + row_of(mods_ref, SHIFT_TWO)
        two = two.astype(bf16)
        two_ref[tokens, :] = two
        twot_ref[:, tokens] = two.T


def finish_kernel(
    branch_ref, middle_ref, cot_ref, mods_ref, result_ref, low_ref, lowt_ref, sums_ref
):
    branch = branch_ref[...]
    gate = row_of(mods_ref, GATE_TWO)
    result_ref[...] = (middle_ref[...] + gate * branch).astype(bf16)
    cot = cot_ref[...].astype(f32) * row_of(mods_ref, WEIGHT)
    low = (gate * cot).astype(bf16)
    low_ref[...] = low
    lowt_ref[...] = low.T
    put_rows(sums_ref, {GATE_TWO: row_sum(cot * branch)})


def middle_kernel(
    one_ref, other_ref, middle_ref, branch_ref, cot_ref, mods_ref,
    grad_ref, low_ref, lowt_ref, sums_ref,
):
    grad = one_ref[...] + other_ref[...]
    unit, scale = rms(middle_ref[...])
    sums = {SHIFT_TWO: row_sum(grad), SCALE_TWO: row_sum(grad * unit)}
    cot = cot_ref[...].astype(f32) * row_of(mods_ref, WEIGHT)
    grad = cot + rms_back(grad, unit, scale, row_of(mods_ref, SCALE_TWO))
    grad_ref[...] = grad
    low = (row_of(mods_ref, GATE_ONE) * grad).astype(bf16)
    low_ref[...] = low
    lowt_ref[...] = low.T
    sums[GATE_ONE] = row_sum(grad * branch_ref[...])
    put_rows(sums_ref, sums)


def entry_kernel(grad_ref, latent_ref, middle_ref, mods_ref, out_ref, sums_ref):
    grad = grad_ref[...]
    unit, scale = rms(latent_ref[...].astype(f32))
    put_rows(sums_ref, {SHIFT_ONE: row_sum(grad), SCALE_ONE: row_sum(grad * unit)})
    grad = middle_ref[...] + rms_back(grad, unit, scale, row_of(mods_ref, SCALE_ONE))
    out_ref[...] = grad.astype(bf16)


def by_image(kernel, name, arrays, mods, outs):
    own, sums, width = mods.shape
    tokens = arrays[0].shape[0]
    length = tokens // own
    block = pl.BlockSpec((length, width), lambda i: (i, 0))
    turned = pl.BlockSpec((width, length), lambda i: (0, i))
    whole = pl.BlockSpec((1, sums, width), lambda i: (i, 0, 0))
    shapes = [
        jax.ShapeDtypeStruct((width, tokens), bf16)
        if out is True
        else jax.ShapeDtypeStruct((tokens, width), out)
        for out in outs
    ]
    return pl.pallas_call(
        kernel,
        grid=(own,),
        in_specs=[block] * len(arrays) + [whole],
        out_specs=[turned if out is True else block for out in outs] + [whole],
        out_shape=shapes + [jax.ShapeDtypeStruct(mods.shape, f32)],
        compiler_params=pltpu.CompilerParams(vmem_limit_bytes=48 << 20),
        cost_estimate=pl.CostEstimate(
            flops=10 * tokens * width,
            bytes_accessed=4 * tokens * width * (len(arrays) + len(outs)),
            transcendentals=0,
        ),
        name=name,
    )(*arrays, mods)


def add_rows(out_ref, part, first, index, length):
    rows = pl.ds(pl.multiple_of(index * length, length), length)

    @pl.when(first)
    def _():
        out_ref[rows, :] = part

    @pl.when(jnp.logical_not(first))
    def _():
        out_ref[rows, :] += part


def attend_back_kernel(
    proj_ref, low_ref, w_ref, gains_ref, cos_ref, sin_ref, out_ref, gain_grad_ref, x_grad_ref
):
    head_dim = gains_ref.shape[1]
    rows_all, length = proj_ref.shape[1] // 3, proj_ref.shape[2]
    cut = feature_order(head_dim)[1]
    cos_tab, sin_tab = cos_ref[...], sin_ref[...]

    @pl.when((pl.program_id(0) == 0) & (pl.program_id(1) == 0))
    def _():
        gain_grad_ref[...] = jnp.zeros_like(gain_grad_ref)

    outs = [[], [], []]
    cot_all = dot_11(w_ref[0, 3 * rows_all :], low_ref[...])
    for head in range(rows_all // head_dim):
        lows, units, scales = [], [], []
        for kind in range(2):
            start = kind * rows_all + head * head_dim
            raw = proj_ref[0, start : start + head_dim, :]
            scale = head_scale(raw)
            unit = raw * scale
            scaled = unit * gains_ref[kind]
            turned = scaled * cos_tab + partner(scaled, cut) * sin_tab
            lows.append(turned.astype(bf16))
            units.append(unit)
            scales.append(scale)
        start = 2 * rows_all + head * head_dim
        value_low = proj_ref[0, start : start + head_dim, :].astype(bf16)
        cot_low = cot_all[head * head_dim : (head + 1) * head_dim].astype(bf16)
        probs = softmax_first(dot_00(lows[1], lows[0]))
        prob_grad = dot_00(value_low, cot_low)
        outs[2].append(dot_11(cot_low, probs.astype(bf16)))
        mean = jnp.sum(probs * prob_grad, axis=0, keepdims=True)
        score_low = (probs * (prob_grad - mean)).astype(bf16)
        turned_grads = (dot_10(lows[1], score_low), dot_11(lows[0], score_low))
        for kind in range(2):
            grad = turned_grads[kind]
            grad = grad * cos_tab + partner(grad * sin_tab, cut)
            gain_grad_ref[kind] += grad * units[kind]
            grad = grad * gains_ref[kind]
            along = jnp.mean(grad * units[kind], axis=0, keepdims=True)
            outs[kind].append(scales[kind] * (grad - units[kind] * along))
    grads = jnp.concatenate(outs[0] + outs[1] + outs[2], axis=0).astype(bf16)
    out_ref[0] = grads
    part = dot_00(grads, w_ref[0, : 3 * rows_all])
    add_rows(x_grad_ref, part, pl.program_id(0) == 0, pl.program_id(1), length)


def attend_specs(groups, rows, own, length, width, head_dim):
    proj = pl.BlockSpec((1, 3 * rows, length), lambda g, i: (g, 0, i))
    att = pl.BlockSpec((1, rows, length), lambda g, i: (g, 0, i))
    x = pl.BlockSpec((length, width), lambda g, i: (i, 0))
    w = pl.BlockSpec((1, 4 * rows, width), lambda g, i: (g, 0, 0))
    gains = pl.BlockSpec((2, head_dim, 1), lambda g, i: (0, 0, 0))
    table = pl.BlockSpec((head_dim, length), lambda g, i: (0, 0))
    grads = pl.BlockSpec((2, head_dim, length), lambda g, i: (0, 0, 0))
    total = pl.BlockSpec((own * length, width), lambda g, i: (0, 0))
    return proj, att, x, w, gains, table, grads, total


def attend(latent, mods, weights, gains, tables, own):
    groups, rows, width = weights.shape[0], weights.shape[1] // 4, weights.shape[2]
    tokens = latent.shape[0]
    length, head_dim = tokens // own, gains.shape[1]
    proj_s, att_s, x_s, w_s, gains_s, table_s, _, total_s = attend_specs(
        groups, rows, own, length, width, head_dim
    )
    turned_s = pl.BlockSpec((width, tokens), lambda g, i: (0, 0))
    mods_s = pl.BlockSpec((1,) + mods.shape[1:], lambda g, i: (i, 0, 0))
    total, turned = (tokens, width), (width, tokens)
    return pl.pallas_call(
        attend_kernel,
        grid=(groups, own),
        in_specs=[x_s, mods_s, w_s, gains_s, table_s, table_s],
        out_specs=[proj_s, att_s, total_s, total_s, turned_s, total_s, total_s, turned_s],
        out_shape=[
            jax.ShapeDtypeStruct((groups, 3 * rows, tokens), f32),
            jax.ShapeDtypeStruct((groups, rows, tokens), bf16),
            jax.ShapeDtypeStruct(total, f32),
            jax.ShapeDtypeStruct(total, bf16),
            jax.ShapeDtypeStruct(turned, bf16),
            jax.ShapeDtypeStruct(total, f32),
            jax.ShapeDtypeStruct(total, bf16),
            jax.ShapeDtypeStruct(turned, bf16),
        ],
        compiler_params=pltpu.CompilerParams(vmem_limit_bytes=60 << 20),
        cost_estimate=pl.CostEstimate(
            flops=groups * rows * tokens * (4 * length + 8 * width),
            bytes_accessed=14 * groups * rows * tokens,
            transcendentals=groups * rows // head_dim * tokens * length,
        ),
        name="attend",
    )(latent, mods, weights, gains, *tables)


def attend_back(proj, low, weights, gains, tables, own):
    groups, rows, width = weights.shape[0], weights.shape[1] // 4, weights.shape[2]
    tokens = low.shape[0]
    length, head_dim = tokens // own, gains.shape[1]
    proj_s, _, x_s, w_s, gains_s, table_s, grads_s, total_s = attend_specs(
        groups, rows, own, length, width, head_dim
    )
    return pl.pallas_call(
        attend_back_kernel,
        grid=(groups, own),
        in_specs=[proj_s, x_s, w_s, gains_s, table_s, table_s],
        out_specs=[proj_s, grads_s, total_s],
        out_shape=[
            jax.ShapeDtypeStruct(proj.shape, bf16),
            jax.ShapeDtypeStruct((2, head_dim, length), f32),
            jax.ShapeDtypeStruct((tokens, width), f32),
        ],
        compiler_params=pltpu.CompilerParams(vmem_limit_bytes=56 << 20),
        cost_estimate=pl.CostEstimate(
            flops=groups * rows * tokens * (10 * length + 8 * width),
            bytes_accessed=18 * groups * rows * tokens,
            transcendentals=groups * rows // head_dim * tokens * length,
        ),
        name="attend_back",
    )(proj, low, weights, gains, *tables)


def sigmoid(values):
    return 1.0 / (1.0 + jnp.exp(-values))


def kind_of(w_ref, kind):
    pieces, _, rows, width = w_ref.shape[1:]
    return w_ref[0, :, kind].reshape(pieces * rows, width)


def mlp_kernel(x_ref, w_ref, save_ref, out_ref):
    first = pl.program_id(0) == 0
    x = x_ref[...]
    gate = dot_11(x, kind_of(w_ref, 0))
    up = dot_11(x, kind_of(w_ref, 1))
    save_ref[0, 0] = gate.astype(bf16)
    save_ref[0, 1] = up.astype(bf16)
    hidden = (gate * sigmoid(gate) * up).astype(bf16)
    part = dot_10(hidden, kind_of(w_ref, 2))
    add_rows(out_ref, part, first, 0, x.shape[0])


def mlp(x, weights):
    groups, pieces, _, rows, width = weights.shape
    units, tokens = pieces * rows, x.shape[0]
    return pl.pallas_call(
        mlp_kernel,
        grid=(groups,),
        in_specs=[
            pl.BlockSpec((tokens, width), lambda g: (0, 0)),
            pl.BlockSpec((1, pieces, 3, rows, width), lambda g: (g, 0, 0, 0, 0)),
        ],
        out_specs=[
            pl.BlockSpec((1, 2, tokens, units), lambda g: (g, 0, 0, 0)),
            pl.BlockSpec((tokens, width), lambda g: (0, 0)),
        ],
        out_shape=[
            jax.ShapeDtypeStruct((groups, 2, tokens, units), bf16),
            jax.ShapeDtypeStruct((tokens, width), f32),
        ],
        compiler_params=pltpu.CompilerParams(vmem_limit_bytes=60 << 20),
        cost_estimate=pl.CostEstimate(
            flops=6 * groups * units * tokens * width,
            bytes_accessed=4 * groups * units * tokens + 6 * groups * units * width,
            transcendentals=groups * units * tokens,
        ),
        name="mlp",
    )(x, weights)


def fill_rows(order_ref, source_ref, target_ref):
    blocks, rows = source_ref.shape[0], source_ref.shape[1]
    for place in range(blocks):
        target_ref[place * rows : (place + 1) * rows, :] = source_ref[order_ref[place]]


def mlp_back_kernel(
    m_ref, e_ref, xt_ref, lowt_ref, low_ref, save_ref, w_ref,
    keep_ref, send_ref, two_ref, xs, lows, parts,
):
    first = pl.program_id(0) == 0
    tokens, width = low_ref.shape
    step = math.gcd(tokens, 512)

    @pl.when(first)
    def _():
        fill_rows(e_ref, xt_ref, xs)
        fill_rows(e_ref, lowt_ref, lows)

    for index in range(tokens // step):
        rows = pl.ds(index * step, step)
        hidden_grad = dot_11(low_ref[rows, :], kind_of(w_ref, 2))
        gate = save_ref[0, 0, rows, :].astype(f32)
        up = save_ref[0, 1, rows, :].astype(f32)
        sig = sigmoid(gate)
        swish = gate * sig
        gate_low = (hidden_grad * up * (sig + swish * (1.0 - sig))).astype(bf16)
        up_low = (hidden_grad * swish).astype(bf16)
        parts[0, rows, :] = gate_low
        parts[1, rows, :] = up_low
        parts[2, rows, :] = (swish * up).astype(bf16)
        part = dot_10(gate_low, kind_of(w_ref, 0)) + dot_10(up_low, kind_of(w_ref, 1))
        add_rows(two_ref, part, first, index, step)

    half = width // 2
    for out_ref, rows in ((keep_ref, slice(0, half)), (send_ref, slice(half, width))):
        x_rows = xs[rows, :]
        for kind in range(2):
            out_ref[0, kind] = dot_10(x_rows, parts[kind]).astype(bf16)
        out_ref[0, 2] = dot_10(lows[rows, :], parts[2]).astype(bf16)


def mlp_back(m_order, e_order, xt, lowt, low, save, weights):
    _, pieces, _, rows, width = weights.shape
    units, tokens = pieces * rows, low.shape[0]
    blocks = m_order.shape[0]
    once = pl.Buffered(1)
    whole = lambda p, m, e: (0, 0)
    whole3 = lambda p, m, e: (0, 0, 0)
    half = jax.ShapeDtypeStruct((blocks, 3, width // 2, units), bf16)
    half_spec = pl.BlockSpec((1, 3, width // 2, units), lambda p, m, e: (p, 0, 0, 0))
    return pl.pallas_call(
        mlp_back_kernel,
        grid_spec=pltpu.PrefetchScalarGridSpec(
            num_scalar_prefetch=2,
            grid=(blocks,),
            in_specs=[
                pl.BlockSpec(xt.shape, whole3, pipeline_mode=once),
                pl.BlockSpec(lowt.shape, whole3, pipeline_mode=once),
                pl.BlockSpec((tokens, width), whole, pipeline_mode=once),
                pl.BlockSpec((1, 2, tokens, units), lambda p, m, e: (m[p], 0, 0, 0)),
                pl.BlockSpec((1, pieces, 3, rows, width), lambda p, m, e: (m[p], 0, 0, 0, 0)),
            ],
            out_specs=[half_spec, half_spec, pl.BlockSpec((tokens, width), whole)],
            scratch_shapes=[
                pltpu.VMEM((width, tokens), bf16),
                pltpu.VMEM((width, tokens), bf16),
                pltpu.VMEM((3, tokens, units), bf16),
            ],
        ),
        out_shape=[half, half, jax.ShapeDtypeStruct((tokens, width), f32)],
        compiler_params=pltpu.CompilerParams(vmem_limit_bytes=62 << 20),
        cost_estimate=pl.CostEstimate(
            flops=12 * blocks * units * tokens * width,
            bytes_accessed=4 * blocks * units * tokens + 12 * blocks * units * width,
            transcendentals=blocks * units * tokens,
        ),
        name="mlp_back",
    )(m_order, e_order, xt, lowt, low, save, weights)


def attend_grads_kernel(
    m_ref, e_ref, xt_ref, lowt_ref, proj_ref, att_ref, keep_ref, send_ref, xs, lows
):
    @pl.when(pl.program_id(0) == 0)
    def _():
        fill_rows(e_ref, xt_ref, xs)
        fill_rows(e_ref, lowt_ref, lows)

    width = xs.shape[0]
    half = width // 2
    columns = proj_ref.shape[1]

    for out_ref, rows in ((keep_ref, slice(0, half)), (send_ref, slice(half, width))):
        out_ref[0, :, :columns] = dot_11(xs[rows, :], proj_ref[0]).astype(bf16)
        out_ref[0, :, columns:] = dot_11(lows[rows, :], att_ref[0]).astype(bf16)


def attend_grads(m_order, e_order, xt, lowt, proj, att):
    rows, tokens = att.shape[1:]
    width = xt.shape[0] * xt.shape[1]
    blocks = m_order.shape[0]
    whole3 = lambda p, m, e: (0, 0, 0)
    half = jax.ShapeDtypeStruct((blocks, width // 2, 4 * rows), bf16)
    half_spec = pl.BlockSpec((1, width // 2, 4 * rows), lambda p, m, e: (p, 0, 0))
    return pl.pallas_call(
        attend_grads_kernel,
        grid_spec=pltpu.PrefetchScalarGridSpec(
            num_scalar_prefetch=2,
            grid=(blocks,),
            in_specs=[
                pl.BlockSpec(xt.shape, whole3, pipeline_mode=pl.Buffered(1)),
                pl.BlockSpec(lowt.shape, whole3, pipeline_mode=pl.Buffered(1)),
                pl.BlockSpec((1, 3 * rows, tokens), lambda p, m, e: (m[p], 0, 0)),
                pl.BlockSpec((1, rows, tokens), lambda p, m, e: (m[p], 0, 0)),
            ],
            out_specs=[half_spec, half_spec],
            scratch_shapes=[
                pltpu.VMEM((width, tokens), bf16),
                pltpu.VMEM((width, tokens), bf16),
            ],
        ),
        out_shape=[half, half],
        compiler_params=pltpu.CompilerParams(vmem_limit_bytes=56 << 20),
        cost_estimate=pl.CostEstimate(
            flops=8 * blocks * rows * tokens * width,
            bytes_accessed=8 * blocks * rows * (tokens + width),
            transcendentals=0,
        ),
        name="attend_grads",
    )(m_order, e_order, xt, lowt, proj, att)


def dot(a, b):
    return jnp.dot(a, b, preferred_element_type=f32)


def ein(spec, a, b):
    return jnp.einsum(spec, a, b, preferred_element_type=f32)


def gather_pieces(piece, mp_size):
    whole = lax.all_gather(piece, ("mp", "dp"), axis=0, tiled=False)
    return whole.reshape((mp_size, -1) + piece.shape)


def take_rows(values, index):
    return jnp.take(values, index, axis=0, mode="clip")


def bits_of(size):
    return [1 << i for i in range(size.bit_length() - 1)]


def swap(values, axis, bit):
    size = lax.axis_size(axis)
    return lax.ppermute(values, axis, [(i, i ^ bit) for i in range(size)])


def xor_gather(values, axes_bits):
    names = sorted({axis for axis, _ in axes_bits})
    places = [{name: 0 for name in names}]
    values = values[None]
    for axis, bit in axes_bits:
        values = jnp.concatenate([values, swap(values, axis, bit)], axis=0)
        places = places + [dict(place, **{axis: place[axis] ^ bit}) for place in places]
    return values, {name: [place[name] for place in places] for name in names}


def halving_order(bits):
    order = [0]
    for bit in reversed(bits):
        order = order + [place ^ bit for place in order]
    return order


def add_low(kept, received):
    return (kept.astype(f32) + received.astype(f32)).astype(bf16)


def tie(*values):
    return lax.optimization_barrier(values)


def split(values, dim):
    size = values.shape[dim] // 2
    return (
        lax.slice_in_dim(values, 0, size, axis=dim),
        lax.slice_in_dim(values, size, 2 * size, axis=dim),
    )


def halve(values, axis, bits, dim):
    for bit in bits:
        kept, sent = split(values, dim)
        values = add_low(kept, swap(sent, axis, bit))
    return values


def shards(
    patches,
    cotangent,
    time_bins,
    labels,
    image_counts,
    dest_perm,
    time_table,
    class_table,
    ada_weight,
    qkv_weight,
    norm_gains,
    out_weight,
    expand_weight,
    down_weight,
):
    dp_size = lax.axis_size("dp")
    mp_size = lax.axis_size("mp")
    capacity = patches.shape[0]
    slot_count = capacity // dp_size
    images = cotangent.shape[0]
    local_len = patches.shape[1]
    model_width = patches.shape[2]
    length = local_len * mp_size
    head_dim = norm_gains.shape[1]
    local_dim = out_weight.shape[0]
    unit_count = down_weight.shape[0]
    own = images // mp_size
    total_images = images * dp_size
    order = np.array(feature_order(head_dim)[0])
    columns = np.arange(4 * local_dim)
    places = columns // head_dim * head_dim + order[columns % head_dim]
    places = np.where(columns < 2 * local_dim, places, columns).astype(np.int32)
    tables = rope_tables(length, head_dim)
    gains_f = norm_gains.astype(f32)[:, order]
    gains_f = (gains_f * jnp.array([[head_dim ** (-0.5)], [1.0]], f32))[:, :, None]
    dp_index = lax.axis_index("dp")
    mp_index = lax.axis_index("mp")

    starts = jnp.cumsum(image_counts) - image_counts
    finish = starts + image_counts
    my_start = starts[dp_index]
    my_count = image_counts[dp_index]
    device_ids = jnp.arange(dp_size)
    matches = (dest_perm[:, None] == device_ids[None, :]).astype(jnp.int32)
    inverse = jnp.sum(device_ids[:, None] * matches, axis=0)
    my_place = inverse[dp_index]
    pair_ids = jnp.arange(dp_size * slot_count)
    pair_peer = pair_ids // slot_count
    pair_slot = pair_ids % slot_count
    send_index = pair_slot * dp_size + jnp.mod(inverse[pair_peer] - my_start, dp_size)
    send_index = jnp.minimum(send_index, capacity - 1)
    send_patches = take_rows(patches, send_index)
    info, info_places = xor_gather(
        jnp.stack([time_bins, labels]), [("dp", bit) for bit in bits_of(dp_size)]
    )
    qkv_weight, out_weight, expand_weight, down_weight, send_patches, info = tie(
        qkv_weight, out_weight, expand_weight, down_weight, send_patches, info
    )
    share = 4 * local_dim // dp_size
    spots = lax.dynamic_slice_in_dim(jnp.array(places), dp_index * share, share, 0)
    take_qkv = (spots[:, None] == jnp.arange(3 * local_dim)[None, :]).astype(bf16)
    take_out = (spots[:, None] - 3 * local_dim == jnp.arange(local_dim)[None, :]).astype(bf16)
    attend_piece = ein("rc,dc->rd", take_qkv, qkv_weight.reshape(model_width, -1))
    attend_piece = (attend_piece + dot(take_out, out_weight)).astype(bf16)
    share = unit_count // dp_size
    spots = dp_index * share + jnp.arange(share)
    take_units = (spots[:, None] == jnp.arange(unit_count)[None, :]).astype(bf16)
    mlp_piece = jnp.stack(
        [
            ein("rf,df->rd", take_units, expand_weight[:, 0]).astype(bf16),
            ein("rf,df->rd", take_units, expand_weight[:, 1]).astype(bf16),
            lax.dynamic_slice_in_dim(down_weight, dp_index * share, share, 0),
        ]
    )
    attend_full = gather_pieces(attend_piece, mp_size).reshape(mp_size, 4 * local_dim, -1)
    mlp_full = gather_pieces(mlp_piece, mp_size)
    if share % 16:
        mlp_full = mlp_full.swapaxes(1, 2).reshape(mp_size, 1, 3, unit_count, model_width)

    recv_patches = lax.all_to_all(send_patches, "dp", split_axis=0, concat_axis=0, tiled=True)
    info = info.swapaxes(0, 1).reshape(2, -1)
    info_owner = jnp.repeat(dp_index ^ jnp.array(info_places["dp"]), capacity)
    info_slot = jnp.tile(jnp.arange(capacity), dp_size)
    info_count = jnp.sum(
        jnp.where(info_owner[:, None] == device_ids[None, :], image_counts[None, :], 0), axis=1
    )
    live_all = info_slot < info_count
    bin_totals = jnp.sum(
        ((info[0][:, None] == jnp.arange(NBINS)[None, :]) & live_all[:, None]).astype(f32), axis=0
    )
    gather_bits = [("mp", bit) for bit in bits_of(mp_size)[::-1]]
    gather_bits = gather_bits + [("dp", bit) for bit in bits_of(dp_size)[::-1]]
    spread = {"dp": [0], "mp": [0]}
    for axis, bit in gather_bits:
        spread = {
            name: spread[name] + [place ^ (bit if name == axis else 0) for place in spread[name]]
            for name in spread
        }
    owner_all = jnp.repeat(dp_index ^ jnp.array(spread["dp"]), own)
    group_all = jnp.repeat(mp_index ^ jnp.array(spread["mp"]), own)
    row_all = group_all * own + jnp.tile(jnp.arange(own), dp_size * mp_size)
    place_all = jnp.sum(
        jnp.where(owner_all[:, None] == device_ids[None, :], inverse[None, :], 0), axis=1
    )
    rank_all = row_all * dp_size + place_all
    source_all = jnp.sum((finish[None, :] <= rank_all[:, None]).astype(jnp.int32), axis=1)
    start_all = jnp.sum(
        jnp.where(source_all[:, None] == device_ids[None, :], starts[None, :], 0), axis=1
    )
    slots_all = source_all * capacity + rank_all - start_all
    slot_hit = slots_all[:, None] == (info_owner * capacity + info_slot)[None, :]
    bins_all = jnp.sum(jnp.where(slot_hit, info[0][None, :], 0), axis=1)
    labels_all = jnp.sum(jnp.where(slot_hit, info[1][None, :], 0), axis=1)
    bin_hot = (bins_all[:, None] == jnp.arange(NBINS)[None, :])
    label_hot = (labels_all[:, None] == jnp.arange(NCLS)[None, :])
    weights_all = total_images / (NBINS * jnp.sum(bin_hot.astype(f32) * bin_totals[None, :], axis=1))
    bin_hot = bin_hot.astype(bf16)
    label_hot = label_hot.astype(bf16)
    cond_all = (dot(bin_hot, time_table) + dot(label_hot, class_table)).astype(bf16).astype(f32)
    silu_all = jax.nn.silu(cond_all).astype(bf16)
    silu_cond = silu_all[:own]
    weights = weights_all[:own]

    modulation = dot(silu_cond, ada_weight.reshape(model_width, 6 * model_width))
    mods = jnp.concatenate(
        [
            modulation.reshape(own, 6, model_width),
            jnp.broadcast_to(weights[:, None, None], (own, 1, model_width)),
            jnp.zeros((own, 1, model_width), f32),
        ],
        axis=1,
    )
    recv_patches, mods = tie(recv_patches, mods)

    rank_ids = jnp.arange(images) * dp_size + my_place
    source = jnp.sum((finish[None, :] <= rank_ids[:, None]).astype(jnp.int32), axis=1)
    within = rank_ids - starts[source]
    recv_index = source * slot_count + within // dp_size
    latent = take_rows(recv_patches, recv_index)
    latent = lax.all_to_all(latent, "mp", split_axis=0, concat_axis=1, tiled=True)
    latent = latent.reshape(-1, model_width)

    proj, attended, branch_one, normed, normed_t, middle, two, two_t = attend(
        latent, mods, attend_full, gains_f, tables, own
    )
    cotangent, attended = tie(cotangent, attended)
    cot = lax.all_to_all(cotangent, "mp", split_axis=0, concat_axis=1, tiled=True)
    cot = cot.reshape(-1, model_width)
    save, branch_two = mlp(two, mlp_full)
    result, down_low, down_t, sums_finish = by_image(
        finish_kernel, "finish", (branch_two, middle, cot), mods, (bf16, bf16, True)
    )
    result = result.reshape(own, length, model_width)
    result = lax.all_to_all(result, "mp", split_axis=1, concat_axis=0, tiled=True)

    dp_bits = bits_of(dp_size)
    dp_bits = (dp_bits, dp_bits[:1] + dp_bits[1:][::-1])
    mp_bits = bits_of(mp_size)
    e_orders = [(dp_index ^ jnp.array(halving_order(bits))).astype(jnp.int32) for bits in dp_bits]
    m_order = (mp_index ^ jnp.array(halving_order(mp_bits))).astype(jnp.int32)
    m_orders = (m_order[: mp_size // 2], m_order[mp_size // 2 :])

    def by_owner(values):
        return values.reshape(dp_size, model_width // dp_size, -1)

    two_t, down_t = by_owner(two_t), by_owner(down_t)
    kept_one, sent_one, two_one = mlp_back(
        m_orders[1], e_orders[1], two_t, down_t, down_low, save, mlp_full
    )
    got_one = swap(sent_one, "dp", dp_bits[1][0])
    kept_zero, sent_zero, two_zero = mlp_back(
        m_orders[0], e_orders[0], two_t, down_t, down_low, save, mlp_full
    )
    got_zero = swap(sent_zero, "dp", dp_bits[0][0])
    two_zero, got_one, result = tie(two_zero, got_one, result)
    kept_one, sent_one = split(add_low(kept_one, got_one), 2)
    got_one = swap(sent_one, "dp", dp_bits[1][1])
    middle_grad, branch_low, branch_t, sums_middle = by_image(
        middle_kernel,
        "middle",
        (two_zero, two_one, middle, branch_one, cot),
        mods,
        (f32, bf16, True),
    )
    branch_low, got_zero = tie(branch_low, got_zero)
    kept_zero, sent_zero = split(add_low(kept_zero, got_zero), 2)
    got_zero = swap(sent_zero, "dp", dp_bits[0][1])
    projected_low, gains_grad, normed_grad = attend_back(
        proj, branch_low, attend_full, gains_f, tables, own
    )
    gains_grad = jnp.sum(gains_grad, axis=2) * jnp.array([[head_dim ** (-0.5)], [1.0]], f32)
    projected_low, normed_grad, got_one, got_zero = tie(projected_low, normed_grad, got_one, got_zero)
    kept_one, sent_one = split(add_low(kept_one, got_one), 2)
    kept_zero, sent_zero = split(add_low(kept_zero, got_zero), 2)
    got_one = swap(sent_one, "dp", dp_bits[1][2])
    got_zero = swap(sent_zero, "dp", dp_bits[0][2])
    latent_grad, sums_entry = by_image(
        entry_kernel, "entry", (normed_grad, latent, middle_grad), mods, (bf16,)
    )
    latent_back = latent_grad.reshape(own, length, model_width)
    latent_back = lax.all_to_all(latent_back, "mp", split_axis=1, concat_axis=0, tiled=True)

    normed_t, latent_grad = tie(normed_t, latent_grad)
    normed_t, branch_t = by_owner(normed_t), by_owner(branch_t)

    def grads_of(which):
        kept, sent = attend_grads(
            m_orders[which],
            e_orders[which],
            normed_t,
            branch_t,
            projected_low,
            attended,
        )
        return kept, swap(sent, "dp", dp_bits[which][0])

    attend_one, attend_got_one = grads_of(1)
    attend_zero, attend_got_zero = grads_of(0)
    attend_zero, attend_got_one, got_one, got_zero = tie(
        attend_zero, attend_got_one, got_one, got_zero
    )
    mlp_one = halve(add_low(kept_one, got_one), "dp", dp_bits[1][3:], 2)
    mlp_zero = halve(add_low(kept_zero, got_zero), "dp", dp_bits[0][3:], 2)
    mlp_got = swap(mlp_one, "mp", mp_bits[0])
    attend_one, sent_one = split(add_low(attend_one, attend_got_one), 1)
    attend_zero, sent_zero = split(add_low(attend_zero, attend_got_zero), 1)
    attend_got_one = swap(sent_one, "dp", dp_bits[1][1])
    attend_got_zero = swap(sent_zero, "dp", dp_bits[0][1])

    modulation_grad = (sums_finish + sums_middle + sums_entry)[:, :6].astype(bf16)
    packed = jnp.concatenate([modulation_grad.reshape(-1), gains_grad.astype(bf16).reshape(-1)])
    packed = xor_gather(packed, gather_bits)[0]
    latent_back, packed, attend_got_one, attend_got_zero, mlp_got = tie(
        latent_back, packed, attend_got_one, attend_got_zero, mlp_got
    )
    attend_one = halve(add_low(attend_one, attend_got_one), "dp", dp_bits[1][2:], 1)
    attend_zero = halve(add_low(attend_zero, attend_got_zero), "dp", dp_bits[0][2:], 1)
    mlp_grad = halve(add_low(mlp_zero, mlp_got), "mp", mp_bits[1:], 0)[0].astype(f32)
    attend_grad = add_low(attend_zero, swap(attend_one, "mp", mp_bits[0]))
    attend_grad = halve(attend_grad, "mp", mp_bits[1:], 0)[0].astype(f32)

    back_within = pair_slot * dp_size + jnp.mod(my_place - starts[pair_peer], dp_size)
    back_valid = back_within < image_counts[pair_peer]
    back_slot = jnp.clip((starts[pair_peer] + back_within - my_place) // dp_size, 0, images - 1)
    back_slot = jnp.where(back_valid, back_slot, images)
    latent_back = jnp.pad(latent_back, ((0, 1), (0, 0), (0, 0)))
    back_patches = take_rows(latent_back, back_slot)
    got_patches = lax.all_to_all(back_patches, "dp", split_axis=0, concat_axis=0, tiled=True)
    slot_ids = jnp.arange(capacity)
    home_peer = dest_perm[jnp.mod(my_start + slot_ids, dp_size)]
    home_index = home_peer * slot_count + jnp.minimum(slot_ids // dp_size, slot_count - 1)
    patch_grad = take_rows(got_patches, home_index)

    mod_all = packed[:, : own * 6 * model_width].reshape(total_images, 6, model_width)
    gains_total = packed[:, own * 6 * model_width :].reshape(-1, 2, head_dim)
    gains_total = jnp.sum(gains_total.astype(f32), axis=0)
    gains_total = jnp.sum(
        jnp.where(order[:, None] == jnp.arange(head_dim)[None, :], gains_total[:, :, None], 0.0), axis=1
    )
    width_dp = model_width // dp_size
    width_mp = model_width // mp_size
    row0 = dp_index * width_dp
    silu_rows = lax.dynamic_slice_in_dim(silu_all, row0, width_dp, 1)
    mod_cols = lax.dynamic_slice_in_dim(mod_all, mp_index * width_mp, width_mp, 2)
    ada_grad = ein("id,ikc->dkc", silu_rows, mod_cols)
    ada_rows = lax.dynamic_slice_in_dim(ada_weight, row0, width_dp, 0)
    silu_grad = ein("ikc,dkc->id", mod_all, ada_rows)
    cond_rows = lax.dynamic_slice_in_dim(cond_all, row0, width_dp, 1)
    silu_val, silu_pull = jax.vjp(jax.nn.silu, cond_rows)
    condition_low = silu_pull(silu_grad)[0].astype(bf16)
    time_grad = ein("in,id->nd", bin_hot, condition_low)
    class_grad = ein("in,id->nd", label_hot, condition_low)

    expand_grad = mlp_grad[:2].swapaxes(0, 1)
    down_grad = mlp_grad[2].T
    out_grad = attend_grad[:, 3 * local_dim :].T
    qkv_grad = lax.dot_general(
        attend_grad[:, : 3 * local_dim],
        jnp.array(places[: 3 * local_dim, None] == columns[: 3 * local_dim], f32),
        (((1,), (0,)), ((), ())),
        precision=lax.Precision.HIGHEST,
        preferred_element_type=f32,
    )
    qkv_grad = qkv_grad.reshape(-1, 3, local_dim)
    return (
        result,
        patch_grad,
        time_grad,
        class_grad,
        ada_grad,
        qkv_grad,
        gains_total,
        out_grad,
        expand_grad,
        down_grad,
    )


def solution(mesh):
    in_specs = (
        P("dp", "mp", None),
        P("dp", "mp", None),
        P("dp"),
        P("dp"),
        P(),
        P(),
        P(),
        P(),
        P(),
        P(None, None, "mp"),
        P(),
        P("mp", None),
        P(None, None, "mp"),
        P("mp", None),
    )
    out_specs = (
        P("dp", "mp", None),
        P("dp", "mp", None),
        P(None, "dp"),
        P(None, "dp"),
        P("dp", None, "mp"),
        P("dp", None, "mp"),
        P(),
        P("mp", "dp"),
        P("dp", None, "mp"),
        P("mp", "dp"),
    )
    return jax.shard_map(shards, mesh=mesh, in_specs=in_specs, out_specs=out_specs, check_vma=False)
```

```python
import functools
import math

import jax
import jax.numpy as jnp
import numpy as np
from jax import lax
from jax.experimental import pallas as pl
from jax.experimental.pallas import tpu as pltpu
from jax.sharding import PartitionSpec as P

GRID = 16
NCLS = 1000
NBINS = 16

epsilon = 1e-06
rope_base = 10000.0
f32 = jnp.float32
bf16 = jnp.bfloat16


def feature_order(head_dim):
    quarter = head_dim // 4
    firsts = list(range(quarter)) + list(range(2 * quarter, 3 * quarter))
    cut = len(firsts) // 8 * 8
    seconds = [i + quarter for i in firsts]
    return firsts[:cut] + seconds[:cut] + firsts[cut:] + seconds[cut:], cut


def rope_tables(position, head_dim):
    quarter = head_dim // 4
    order, cut = feature_order(head_dim)
    places = jnp.stack([position // GRID, position % GRID]).astype(f32)
    frequency = rope_base ** (-jnp.arange(quarter).astype(f32) / quarter)
    angle = (frequency[None, :, None] * places[:, None, :]).reshape(2 * quarter, -1)
    cosine, sine = jnp.cos(angle), jnp.sin(angle)
    cos_tab = jnp.concatenate([cosine[:cut], cosine[:cut], cosine[cut:], cosine[cut:]])
    sin_tab = jnp.concatenate([-sine[:cut], sine[:cut], -sine[cut:], sine[cut:]])
    return cos_tab, sin_tab


def partner(values, cut):
    rest = values[2 * cut :]
    half = rest.shape[0] // 2
    return jnp.concatenate(
        [values[cut : 2 * cut], values[:cut], pltpu.roll(rest, half, 0)], axis=0
    )


def head_scale(values):
    return lax.rsqrt(jnp.mean(values * values, axis=0, keepdims=True) + epsilon)


def dot_00(a, b):
    return lax.dot_general(a, b, (((0,), (0,)), ((), ())), preferred_element_type=f32)


def dot_11(a, b):
    return lax.dot_general(a, b, (((1,), (1,)), ((), ())), preferred_element_type=f32)


def dot_10(a, b):
    return lax.dot_general(a, b, (((1,), (0,)), ((), ())), preferred_element_type=f32)


def softmax_first(scores):
    shifted = jnp.exp(scores - jnp.max(scores, axis=0, keepdims=True))
    return shifted * (1.0 / jnp.sum(shifted, axis=0, keepdims=True))


def lasting(microseconds):
    return pl.CostEstimate(
        flops=int(microseconds * 1.1e9), bytes_accessed=1 << 20, transcendentals=0
    )


SHIFT_ONE, SCALE_ONE, GATE_ONE, SHIFT_TWO, SCALE_TWO, GATE_TWO, WEIGHT = range(7)


def row_of(mods, which):
    return mods[which : which + 1, :]


def rms(values):
    scale = lax.rsqrt(jnp.mean(values * values, -1, keepdims=True) + epsilon)
    return values * scale, scale


def rms_back(grad, unit, scale, scaling):
    grad = grad * (1.0 + scaling)
    return scale * (grad - unit * jnp.mean(grad * unit, -1, keepdims=True))


def row_sum(values):
    return jnp.sum(values, axis=0, keepdims=True)


def put_rows(sums_ref, image, rows):
    for which in range(sums_ref.shape[1]):
        value = rows.get(which, jnp.zeros((1, sums_ref.shape[2]), f32))
        sums_ref[image, which : which + 1, :] = value


def chunk_rows(ref, image):
    return jnp.concatenate([ref[chunk, image] for chunk in range(ref.shape[0])], axis=0)


def put_chunks(ref, image, values):
    size = ref.shape[2]
    for chunk in range(ref.shape[0]):
        ref[chunk, image] = values[chunk * size : (chunk + 1) * size]


def attend_kernel(
    latent_ref, mods_ref, w_ref, wo_ref, gains_ref, cos_ref, sin_ref,
    proj_ref, att_ref, branch_ref, xt_ref, middle_ref, two_ref, twot_ref, x_ref,
):
    own = mods_ref.shape[0]
    head_dim = gains_ref.shape[1]
    rows_all = att_ref.shape[1]
    length = xt_ref.shape[1] // own
    heads = range(rows_all // head_dim)
    cut = feature_order(head_dim)[1]
    group = pl.program_id(0)

    def place(image):
        return pl.ds(pl.multiple_of(image * length, length), length)

    @pl.when(group == 0)
    def _():
        def entry(image, carry):
            mods = mods_ref[image]
            unit = rms(chunk_rows(latent_ref, image).astype(f32))[0]
            x = (unit * (1.0 + row_of(mods, SCALE_ONE)) + row_of(mods, SHIFT_ONE)).astype(bf16)
            x_ref[place(image), :] = x
            xt_ref[:, place(image)] = x.T
            return carry

        lax.fori_loop(0, own, entry, 0)

    proj_ref[0] = dot_11(w_ref[0, : 3 * rows_all], x_ref[...])

    def heads_of(image, carry):
        tokens = place(image)
        cos_tab, sin_tab = cos_ref[...], sin_ref[...]
        lows = [[], [], []]
        for kind in range(2):
            for head in heads:
                start = kind * rows_all + head * head_dim
                raw = proj_ref[0, start : start + head_dim, tokens]
                scaled = raw * head_scale(raw) * gains_ref[kind]
                turned = scaled * cos_tab + partner(scaled, cut) * sin_tab
                lows[kind].append(turned.astype(bf16))
        for head in heads:
            start = 2 * rows_all + head * head_dim
            lows[2].append(proj_ref[0, start : start + head_dim, tokens].astype(bf16))
        scores = [dot_00(lows[1][head], lows[0][head]) for head in heads]
        probs = [softmax_first(score).astype(bf16) for score in scores]
        outs = [dot_10(lows[2][head], probs[head]) for head in heads]
        att_ref[group, :, tokens] = jnp.concatenate(outs, axis=0).astype(bf16)
        return carry

    lax.fori_loop(0, own, heads_of, 0, unroll=True)

    @pl.when(group == pl.num_programs(0) - 1)
    def _():
        groups = att_ref.shape[0]

        def leave(image, carry):
            tokens = place(image)
            mods = mods_ref[image]
            att = att_ref[:, :, tokens].reshape(groups * rows_all, length)
            branch = dot_00(att, wo_ref[...].reshape(groups * rows_all, -1))
            branch_ref[tokens, :] = branch.astype(bf16)
            latent = chunk_rows(latent_ref, image).astype(f32)
            middle = latent + row_of(mods, GATE_ONE) * branch
            middle_ref[tokens, :] = middle
            two = rms(middle)[0] * (1.0 + row_of(mods, SCALE_TWO)) + row_of(mods, SHIFT_TWO)
            two = two.astype(bf16)
            two_ref[tokens, :] = two
            twot_ref[:, tokens] = two.T
            return carry

        lax.fori_loop(0, own, leave, 0)


def attend_back_kernel(
    latent_ref, proj_ref, low_ref, w_ref, gains_ref, cos_ref, sin_ref, grad_ref, mods_ref,
    out_ref, gain_grad_ref, sums_ref, chunks_ref, cot_ref,
):
    own = mods_ref.shape[0]
    head_dim = gains_ref.shape[1]
    rows_all, tokens_all = proj_ref.shape[1] // 3, proj_ref.shape[2]
    length = tokens_all // own
    heads = range(rows_all // head_dim)
    cut = feature_order(head_dim)[1]
    group = pl.program_id(0)

    def place(image):
        return pl.ds(pl.multiple_of(image * length, length), length)

    @pl.when(group == 0)
    def _():
        gain_grad_ref[...] = jnp.zeros_like(gain_grad_ref)

    cot_ref[...] = dot_11(w_ref[group, 3 * rows_all :], low_ref[...])

    def heads_of(image, carry):
        tokens = place(image)
        cos_tab, sin_tab = cos_ref[...], sin_ref[...]
        lows, units, scales = [[], [], []], [[], []], [[], []]
        for kind in range(2):
            for head in heads:
                start = kind * rows_all + head * head_dim
                raw = proj_ref[0, start : start + head_dim, tokens]
                scale = head_scale(raw)
                unit = raw * scale
                scaled = unit * gains_ref[kind]
                turned = scaled * cos_tab + partner(scaled, cut) * sin_tab
                lows[kind].append(turned.astype(bf16))
                units[kind].append(unit)
                scales[kind].append(scale)
        cots = []
        for head in heads:
            start = 2 * rows_all + head * head_dim
            lows[2].append(proj_ref[0, start : start + head_dim, tokens].astype(bf16))
            cots.append(cot_ref[head * head_dim : (head + 1) * head_dim, tokens].astype(bf16))
        scores = [dot_00(lows[1][head], lows[0][head]) for head in heads]
        prob_grads = [dot_00(lows[2][head], cots[head]) for head in heads]
        probs = [softmax_first(score) for score in scores]
        outs = [[], [], []]
        outs[2] = [dot_11(cots[head], probs[head].astype(bf16)) for head in heads]
        score_lows = []
        for head in heads:
            mean = jnp.sum(probs[head] * prob_grads[head], axis=0, keepdims=True)
            score_lows.append((probs[head] * (prob_grads[head] - mean)).astype(bf16))
        turned_grads = [
            [dot_10(lows[1][head], score_lows[head]) for head in heads],
            [dot_11(lows[0][head], score_lows[head]) for head in heads],
        ]
        for kind in range(2):
            total = 0.0
            for head in heads:
                grad, unit = turned_grads[kind][head], units[kind][head]
                grad = grad * cos_tab + partner(grad * sin_tab, cut)
                total = total + grad * unit
                grad = grad * gains_ref[kind]
                along = jnp.mean(grad * unit, axis=0, keepdims=True)
                outs[kind].append(scales[kind][head] * (grad - unit * along))
            gain_grad_ref[kind] += total
        grads = jnp.concatenate(outs[0] + outs[1] + outs[2], axis=0).astype(bf16)
        out_ref[group, :, tokens] = grads
        return carry

    lax.fori_loop(0, own, heads_of, 0, unroll=True)

    @pl.when(group == pl.num_programs(0) - 1)
    def _():
        def leave(image, carry):
            tokens = place(image)
            mods = mods_ref[image]
            grad = 0.0
            for other in range(out_ref.shape[0]):
                grad = grad + dot_00(out_ref[other, :, tokens], w_ref[other, : 3 * rows_all])
            unit, scale = rms(chunk_rows(latent_ref, image).astype(f32))
            sums = {SHIFT_ONE: row_sum(grad), SCALE_ONE: row_sum(grad * unit)}
            put_rows(sums_ref, image, sums)
            grad = grad_ref[tokens, :] + rms_back(grad, unit, scale, row_of(mods, SCALE_ONE))
            put_chunks(chunks_ref, image, grad.astype(bf16))
            return carry

        lax.fori_loop(0, own, leave, 0)


def whole_spec(shape):
    return pl.BlockSpec(shape, lambda g: (0,) * len(shape), pipeline_mode=pl.Buffered(1))


def attend(latent, mods, weights, gains, tables):
    groups, rows, width = weights.shape[0], weights.shape[1] // 4, weights.shape[2]
    own = mods.shape[0]
    length, head_dim = tables[0].shape[1], gains.shape[1]
    tokens = own * length
    total, turned = (tokens, width), (width, tokens)
    const = lambda shape: pl.BlockSpec(shape, lambda g: (0,) * len(shape))
    return pl.pallas_call(
        attend_kernel,
        grid=(groups,),
        in_specs=[
            whole_spec(latent.shape),
            whole_spec(mods.shape),
            pl.BlockSpec((1, 4 * rows, width), lambda g: (g, 0, 0)),
            pl.BlockSpec((groups, rows, width), lambda g: (0, 3, 0), pipeline_mode=pl.Buffered(1)),
            whole_spec(gains.shape),
            whole_spec(tables[0].shape),
            whole_spec(tables[0].shape),
        ],
        out_specs=[
            pl.BlockSpec((1, 3 * rows, tokens), lambda g: (g, 0, 0)),
            const((groups, rows, tokens)),
            const(total),
            const(turned),
            const(total),
            const(total),
            const(turned),
        ],
        out_shape=[
            jax.ShapeDtypeStruct((groups, 3 * rows, tokens), f32),
            jax.ShapeDtypeStruct((groups, rows, tokens), bf16),
            jax.ShapeDtypeStruct(total, bf16),
            jax.ShapeDtypeStruct(turned, bf16),
            jax.ShapeDtypeStruct(total, f32),
            jax.ShapeDtypeStruct(total, bf16),
            jax.ShapeDtypeStruct(turned, bf16),
        ],
        scratch_shapes=[pltpu.VMEM(total, bf16)],
        compiler_params=pltpu.CompilerParams(vmem_limit_bytes=62 << 20),
        cost_estimate=lasting(160),
        name="attend",
    )(latent, mods, weights, weights, gains, *tables)


def attend_back(latent, proj, low, weights, gains, tables, grad, mods):
    groups, rows, width = weights.shape[0], weights.shape[1] // 4, weights.shape[2]
    own = mods.shape[0]
    tokens = low.shape[0]
    length, head_dim = tokens // own, gains.shape[1]
    const = lambda shape: pl.BlockSpec(shape, lambda g: (0,) * len(shape))
    gain_shape = (2, head_dim, length)
    return pl.pallas_call(
        attend_back_kernel,
        grid=(groups,),
        in_specs=[
            whole_spec(latent.shape),
            pl.BlockSpec((1, 3 * rows, tokens), lambda g: (g, 0, 0)),
            whole_spec(low.shape),
            whole_spec(weights.shape),
            whole_spec(gains.shape),
            whole_spec(tables[0].shape),
            whole_spec(tables[0].shape),
            whole_spec(grad.shape),
            whole_spec(mods.shape),
        ],
        out_specs=[const(proj.shape), const(gain_shape), const(mods.shape), const(latent.shape)],
        out_shape=[
            jax.ShapeDtypeStruct(proj.shape, bf16),
            jax.ShapeDtypeStruct(gain_shape, f32),
            jax.ShapeDtypeStruct(mods.shape, f32),
            jax.ShapeDtypeStruct(latent.shape, bf16),
        ],
        scratch_shapes=[pltpu.VMEM((rows, tokens), f32)],
        compiler_params=pltpu.CompilerParams(vmem_limit_bytes=62 << 20),
        cost_estimate=lasting(160),
        name="attend_back",
    )(latent, proj, low, weights, gains, *tables, grad, mods)


def finish_kernel(
    branch_ref, middle_ref, cot_ref, mods_ref, low_ref, lowt_ref, chunks_ref, sums_ref
):
    branch, mods = branch_ref[...], mods_ref[0]
    gate = row_of(mods, GATE_TWO)
    result = (middle_ref[...] + gate * branch).astype(bf16)
    put_chunks(chunks_ref, 0, result)
    cot = chunk_rows(cot_ref, 0).astype(f32) * row_of(mods, WEIGHT)
    low = (gate * cot).astype(bf16)
    low_ref[...] = low
    lowt_ref[...] = low.T
    put_rows(sums_ref, 0, {GATE_TWO: row_sum(cot * branch)})


def middle_kernel(
    one_ref, other_ref, middle_ref, branch_ref, cot_ref, mods_ref,
    grad_ref, low_ref, lowt_ref, sums_ref,
):
    mods = mods_ref[0]
    grad = one_ref[...] + other_ref[...]
    unit, scale = rms(middle_ref[...])
    sums = {SHIFT_TWO: row_sum(grad), SCALE_TWO: row_sum(grad * unit)}
    cot = chunk_rows(cot_ref, 0).astype(f32) * row_of(mods, WEIGHT)
    grad = cot + rms_back(grad, unit, scale, row_of(mods, SCALE_TWO))
    grad_ref[...] = grad
    low = (row_of(mods, GATE_ONE) * grad).astype(bf16)
    low_ref[...] = low
    lowt_ref[...] = low.T
    sums[GATE_ONE] = row_sum(grad * branch_ref[...].astype(f32))
    put_rows(sums_ref, 0, sums)


def by_image(kernel, name, rows, chunks, mods, outs):
    own, sums, width = mods.shape
    tokens = rows[0].shape[0]
    length = tokens // own
    block = pl.BlockSpec((length, width), lambda i: (i, 0))
    turned = pl.BlockSpec((width, length), lambda i: (0, i))
    chunk = pl.BlockSpec((chunks.shape[0], 1) + chunks.shape[2:], lambda i: (0, i, 0, 0))
    whole = pl.BlockSpec((1, sums, width), lambda i: (i, 0, 0))
    specs, shapes = [], []
    for out in outs:
        if out is True:
            specs.append(turned)
            shapes.append(jax.ShapeDtypeStruct((width, tokens), bf16))
        elif out is False:
            specs.append(chunk)
            shapes.append(jax.ShapeDtypeStruct(chunks.shape, bf16))
        else:
            specs.append(block)
            shapes.append(jax.ShapeDtypeStruct((tokens, width), out))
    return pl.pallas_call(
        kernel,
        grid=(own,),
        in_specs=[block] * len(rows) + [chunk, whole],
        out_specs=specs + [whole],
        out_shape=shapes + [jax.ShapeDtypeStruct(mods.shape, f32)],
        compiler_params=pltpu.CompilerParams(vmem_limit_bytes=48 << 20),
        cost_estimate=lasting(30),
        name=name,
    )(*rows, chunks, mods)


def modulate_kernel(silu_ref, weight_ref, ada_ref, out_ref):
    own, kinds = out_ref.shape[0], ada_ref.shape[1]
    depth = ada_ref.shape[0]
    base = pl.program_id(0) * depth

    @pl.when(pl.program_id(0) == 0)
    def _():
        out_ref[...] = jnp.zeros_like(out_ref)
        for image in range(own):
            out_ref[image, WEIGHT : WEIGHT + 1, :] = jnp.full(
                (1, out_ref.shape[2]), weight_ref[image], f32
            )

    def step(index, totals):
        row = ada_ref[index].astype(f32)
        return tuple(
            total + silu_ref[image, base + index] * row for image, total in enumerate(totals)
        )

    start = tuple(out_ref[image, :kinds] for image in range(own))
    for image, total in enumerate(lax.fori_loop(0, depth, step, start, unroll=4)):
        out_ref[image, :kinds] = total


def modulate(silu, weight, ada):
    own, width = silu.shape
    depth = math.gcd(width, 144)
    return pl.pallas_call(
        modulate_kernel,
        grid=(width // depth,),
        in_specs=[
            pl.BlockSpec(memory_space=pltpu.SMEM),
            pl.BlockSpec(memory_space=pltpu.SMEM),
            pl.BlockSpec((depth,) + ada.shape[1:], lambda i: (i, 0, 0)),
        ],
        out_specs=pl.BlockSpec((own, 8, width), lambda i: (0, 0, 0)),
        out_shape=jax.ShapeDtypeStruct((own, 8, width), f32),
        compiler_params=pltpu.CompilerParams(vmem_limit_bytes=32 << 20),
        cost_estimate=lasting(100),
        name="modulate",
    )(silu.astype(f32), weight, ada)


def add_rows(out_ref, part, first, index, length):
    rows = pl.ds(pl.multiple_of(index * length, length), length)

    @pl.when(first)
    def _():
        out_ref[rows, :] = part

    @pl.when(jnp.logical_not(first))
    def _():
        out_ref[rows, :] += part


def sigmoid(values):
    return 1.0 / (1.0 + jnp.exp(-values))


def mlp_kernel(count, e_ref, x_ref, *refs):
    first = pl.program_id(0) == 0
    save_ref, out_ref, w_ref = refs[count:]
    size = refs[0].shape[2]
    for index, ref in enumerate(refs[:count]):
        rows = pl.ds(pl.multiple_of(e_ref[index] * size, size), size)
        for kind in range(3):
            w_ref[0, kind, rows, :] = ref[0, kind]
    x = x_ref[...]
    gate = dot_11(x, w_ref[0, 0])
    up = dot_11(x, w_ref[0, 1])
    save_ref[0, 0] = gate.astype(bf16)
    save_ref[0, 1] = up.astype(bf16)
    hidden = (gate * sigmoid(gate) * up).astype(bf16)
    part = dot_10(hidden, w_ref[0, 2])
    add_rows(out_ref, part, first, 0, x.shape[0])


def mlp(x, order, pieces):
    groups, _, size, width = pieces[0].shape
    units, tokens = size * len(pieces), x.shape[0]
    return pl.pallas_call(
        functools.partial(mlp_kernel, len(pieces)),
        grid_spec=pltpu.PrefetchScalarGridSpec(
            num_scalar_prefetch=1,
            grid=(groups,),
            in_specs=[pl.BlockSpec((tokens, width), lambda g, e: (0, 0), pipeline_mode=pl.Buffered(1))]
            + [pl.BlockSpec((1, 3, size, width), lambda g, e: (g, 0, 0, 0))] * len(pieces),
            out_specs=[
                pl.BlockSpec((1, 2, tokens, units), lambda g, e: (g, 0, 0, 0)),
                pl.BlockSpec((tokens, width), lambda g, e: (0, 0)),
                pl.BlockSpec((1, 3, units, width), lambda g, e: (g, 0, 0, 0)),
            ],
        ),
        out_shape=[
            jax.ShapeDtypeStruct((groups, 2, tokens, units), bf16),
            jax.ShapeDtypeStruct((tokens, width), f32),
            jax.ShapeDtypeStruct((groups, 3, units, width), bf16),
        ],
        compiler_params=pltpu.CompilerParams(vmem_limit_bytes=62 << 20),
        cost_estimate=lasting(120),
        name="mlp",
    )(order, x, *pieces)


def fill_rows(order_ref, source_ref, target_ref):
    blocks, rows = source_ref.shape[0], source_ref.shape[1]
    for place in range(blocks):
        target_ref[place * rows : (place + 1) * rows, :] = source_ref[order_ref[place]]


def mlp_back_kernel(
    e_ref, xt_ref, lowt_ref, low_ref, save_ref, w_ref,
    keep_ref, send_ref, two_ref, xs, lows, parts,
):
    first = pl.program_id(0) == 0
    tokens, width = low_ref.shape
    step = math.gcd(tokens, 512)

    @pl.when(first)
    def _():
        fill_rows(e_ref, xt_ref, xs)
        fill_rows(e_ref, lowt_ref, lows)

    for index in range(tokens // step):
        rows = pl.ds(index * step, step)
        hidden_grad = dot_11(low_ref[rows, :], w_ref[0, 2])
        gate = save_ref[0, 0, rows, :].astype(f32)
        up = save_ref[0, 1, rows, :].astype(f32)
        sig = sigmoid(gate)
        swish = gate * sig
        gate_low = (hidden_grad * up * (sig + swish * (1.0 - sig))).astype(bf16)
        up_low = (hidden_grad * swish).astype(bf16)
        parts[0, rows, :] = gate_low
        parts[1, rows, :] = up_low
        parts[2, rows, :] = (swish * up).astype(bf16)
        part = dot_10(gate_low, w_ref[0, 0]) + dot_10(up_low, w_ref[0, 1])
        add_rows(two_ref, part, first, index, step)

    half = width // 2
    for out_ref, rows in ((keep_ref, slice(0, half)), (send_ref, slice(half, width))):
        x_rows = xs[rows, :]
        for kind in range(2):
            out_ref[0, kind] = dot_10(x_rows, parts[kind]).astype(bf16)
        out_ref[0, 2] = dot_10(lows[rows, :], parts[2]).astype(bf16)


def mlp_back(which, e_order, xt, lowt, low, save, weights):
    groups, _, units, width = weights.shape
    tokens = low.shape[0]
    blocks = groups // 2
    base = which * blocks
    once = pl.Buffered(1)
    whole = lambda p, e: (0, 0)
    whole3 = lambda p, e: (0, 0, 0)
    half = jax.ShapeDtypeStruct((blocks, 3, width // 2, units), bf16)
    half_spec = pl.BlockSpec((1, 3, width // 2, units), lambda p, e: (p, 0, 0, 0))
    return pl.pallas_call(
        mlp_back_kernel,
        grid_spec=pltpu.PrefetchScalarGridSpec(
            num_scalar_prefetch=1,
            grid=(blocks,),
            in_specs=[
                pl.BlockSpec(xt.shape, whole3, pipeline_mode=once),
                pl.BlockSpec(lowt.shape, whole3, pipeline_mode=once),
                pl.BlockSpec((tokens, width), whole, pipeline_mode=once),
                pl.BlockSpec((1, 2, tokens, units), lambda p, e: (base + p, 0, 0, 0)),
                pl.BlockSpec((1, 3, units, width), lambda p, e: (base + p, 0, 0, 0)),
            ],
            out_specs=[half_spec, half_spec, pl.BlockSpec((tokens, width), whole)],
            scratch_shapes=[
                pltpu.VMEM((width, tokens), bf16),
                pltpu.VMEM((width, tokens), bf16),
                pltpu.VMEM((3, tokens, units), bf16),
            ],
        ),
        out_shape=[half, half, jax.ShapeDtypeStruct((tokens, width), f32)],
        compiler_params=pltpu.CompilerParams(vmem_limit_bytes=62 << 20),
        cost_estimate=lasting(150),
        name="mlp_back",
    )(e_order, xt, lowt, low, save, weights)


def attend_grads_kernel(
    m_ref, e_ref, xt_ref, lowt_ref, proj_ref, att_ref, keep_ref, send_ref, xs, lows
):
    @pl.when(pl.program_id(0) == 0)
    def _():
        fill_rows(e_ref, xt_ref, xs)
        fill_rows(e_ref, lowt_ref, lows)

    width = xs.shape[0]
    half = width // 2
    columns = proj_ref.shape[1]

    for out_ref, rows in ((keep_ref, slice(0, half)), (send_ref, slice(half, width))):
        out_ref[0, :, :columns] = dot_11(xs[rows, :], proj_ref[0]).astype(bf16)
        out_ref[0, :, columns:] = dot_11(lows[rows, :], att_ref[0]).astype(bf16)


def attend_grads(m_order, e_order, xt, lowt, proj, att, microseconds):
    rows, tokens = att.shape[1:]
    width = xt.shape[0] * xt.shape[1]
    blocks = m_order.shape[0]
    whole3 = lambda p, m, e: (0, 0, 0)
    half = jax.ShapeDtypeStruct((blocks, width // 2, 4 * rows), bf16)
    half_spec = pl.BlockSpec((1, width // 2, 4 * rows), lambda p, m, e: (p, 0, 0))
    return pl.pallas_call(
        attend_grads_kernel,
        grid_spec=pltpu.PrefetchScalarGridSpec(
            num_scalar_prefetch=2,
            grid=(blocks,),
            in_specs=[
                pl.BlockSpec(xt.shape, whole3, pipeline_mode=pl.Buffered(1)),
                pl.BlockSpec(lowt.shape, whole3, pipeline_mode=pl.Buffered(1)),
                pl.BlockSpec((1, 3 * rows, tokens), lambda p, m, e: (m[p], 0, 0)),
                pl.BlockSpec((1, rows, tokens), lambda p, m, e: (m[p], 0, 0)),
            ],
            out_specs=[half_spec, half_spec],
            scratch_shapes=[
                pltpu.VMEM((width, tokens), bf16),
                pltpu.VMEM((width, tokens), bf16),
            ],
        ),
        out_shape=[half, half],
        compiler_params=pltpu.CompilerParams(vmem_limit_bytes=56 << 20),
        cost_estimate=lasting(microseconds),
        name="attend_grads",
    )(m_order, e_order, xt, lowt, proj, att)


def dot(a, b):
    return jnp.dot(a, b, preferred_element_type=f32)


def ein(spec, a, b):
    return jnp.einsum(spec, a, b, preferred_element_type=f32)


def gather_pieces(piece, mp_size):
    whole = lax.all_gather(piece, ("mp", "dp"), axis=0, tiled=False)
    return whole.reshape((mp_size, -1) + piece.shape)


def take_rows(values, index):
    return jnp.take(values, index, axis=0, mode="clip")


def bits_of(size):
    return [1 << i for i in range(size.bit_length() - 1)]


def swap(values, axis, bit):
    size = lax.axis_size(axis)
    return lax.ppermute(values, axis, [(i, i ^ bit) for i in range(size)])


def xor_gather(values, axes_bits):
    names = sorted({axis for axis, _ in axes_bits})
    places = [{name: 0 for name in names}]
    values = values[None]
    for axis, bit in axes_bits:
        values = jnp.concatenate([values, swap(values, axis, bit)], axis=0)
        places = places + [dict(place, **{axis: place[axis] ^ bit}) for place in places]
    return values, {name: [place[name] for place in places] for name in names}


def halving_order(bits):
    order = [0]
    for bit in reversed(bits):
        order = order + [place ^ bit for place in order]
    return order


def add_low(kept, received):
    return (kept.astype(f32) + received.astype(f32)).astype(bf16)


def tie(*values):
    return lax.optimization_barrier(values)


def split(values, dim):
    size = values.shape[dim] // 2
    return (
        lax.slice_in_dim(values, 0, size, axis=dim),
        lax.slice_in_dim(values, size, 2 * size, axis=dim),
    )


def halve(values, axis, bits, dim):
    for bit in bits:
        kept, sent = split(values, dim)
        values = add_low(kept, swap(sent, axis, bit))
    return values


def shards(
    patches,
    cotangent,
    time_bins,
    labels,
    image_counts,
    dest_perm,
    time_table,
    class_table,
    ada_weight,
    qkv_weight,
    norm_gains,
    out_weight,
    expand_weight,
    down_weight,
):
    dp_size = lax.axis_size("dp")
    mp_size = lax.axis_size("mp")
    capacity = patches.shape[0]
    slot_count = capacity // dp_size
    images = cotangent.shape[0]
    local_len = patches.shape[1]
    model_width = patches.shape[2]
    length = local_len * mp_size
    head_dim = norm_gains.shape[1]
    local_dim = out_weight.shape[0]
    unit_count = down_weight.shape[0]
    own = images // mp_size
    total_images = images * dp_size
    order = np.array(feature_order(head_dim)[0])
    columns = np.arange(4 * local_dim)
    places = columns // head_dim * head_dim + order[columns % head_dim]
    places = np.where(columns < 2 * local_dim, places, columns).astype(np.int32)
    gains_f = norm_gains.astype(f32)[:, order]
    gains_f = (gains_f * jnp.array([[head_dim ** (-0.5)], [1.0]], f32))[:, :, None]
    dp_index = lax.axis_index("dp")
    mp_index = lax.axis_index("mp")
    dp_bits = bits_of(dp_size)
    dp_bits = (dp_bits, dp_bits[:1] + dp_bits[1:][::-1])
    mp_bits = bits_of(mp_size)

    tables = rope_tables(jnp.arange(length), head_dim)

    def turn(chunks):
        return lax.all_to_all(chunks, "mp", split_axis=0, concat_axis=0, tiled=True)

    starts = jnp.cumsum(image_counts) - image_counts
    finish = starts + image_counts
    my_start = starts[dp_index]
    my_count = image_counts[dp_index]
    device_ids = jnp.arange(dp_size)
    matches = (dest_perm[:, None] == device_ids[None, :]).astype(jnp.int32)
    inverse = jnp.sum(device_ids[:, None] * matches, axis=0)
    my_place = inverse[dp_index]
    pair_ids = jnp.arange(dp_size * slot_count)
    pair_peer = pair_ids // slot_count
    pair_slot = pair_ids % slot_count
    send_index = pair_slot * dp_size + jnp.mod(inverse[pair_peer] - my_start, dp_size)
    send_index = jnp.minimum(send_index, capacity - 1)
    send_patches = take_rows(patches, send_index)
    info, info_places = xor_gather(
        jnp.stack([time_bins, labels]), [("dp", bit) for bit in bits_of(dp_size)]
    )
    qkv_weight, out_weight, expand_weight, down_weight, send_patches, info = tie(
        qkv_weight, out_weight, expand_weight, down_weight, send_patches, info
    )
    share = 4 * local_dim // dp_size
    spots = lax.dynamic_slice_in_dim(jnp.array(places), dp_index * share, share, 0)
    take_qkv = (spots[:, None] == jnp.arange(3 * local_dim)[None, :]).astype(bf16)
    take_out = (spots[:, None] - 3 * local_dim == jnp.arange(local_dim)[None, :]).astype(bf16)
    attend_piece = ein("rc,dc->rd", take_qkv, qkv_weight.reshape(model_width, -1))
    attend_piece = (attend_piece + dot(take_out, out_weight)).astype(bf16)
    share = unit_count // dp_size
    spots = dp_index * share + jnp.arange(share)
    take_units = (spots[:, None] == jnp.arange(unit_count)[None, :]).astype(bf16)
    mlp_piece = jnp.stack(
        [
            ein("rf,df->rd", take_units, expand_weight[:, 0]).astype(bf16),
            ein("rf,df->rd", take_units, expand_weight[:, 1]).astype(bf16),
            lax.dynamic_slice_in_dim(down_weight, dp_index * share, share, 0),
        ]
    )
    attend_full = gather_pieces(attend_piece, mp_size).reshape(mp_size, 4 * local_dim, -1)
    by_permutes = share % 32 == 0 and dp_size == 8 and mp_size == 4
    if by_permutes:
        mlp_near = mlp_piece[None]
        far_near = swap(mlp_near, "mp", 2)
    else:
        mlp_full = gather_pieces(mlp_piece, mp_size)
        mlp_full = mlp_full.swapaxes(1, 2).reshape(mp_size, 3, unit_count, model_width)
        mlp_pieces = [mlp_full[mp_index ^ jnp.array(halving_order(mp_bits))]]
        mlp_order = jnp.zeros((1,), jnp.int32)

    recv_patches = lax.all_to_all(send_patches, "dp", split_axis=0, concat_axis=0, tiled=True)
    info = info.swapaxes(0, 1).reshape(2, -1)
    info_owner = jnp.repeat(dp_index ^ jnp.array(info_places["dp"]), capacity)
    info_slot = jnp.tile(jnp.arange(capacity), dp_size)
    info_count = jnp.sum(
        jnp.where(info_owner[:, None] == device_ids[None, :], image_counts[None, :], 0), axis=1
    )
    live_all = info_slot < info_count
    bin_totals = jnp.sum(
        ((info[0][:, None] == jnp.arange(NBINS)[None, :]) & live_all[:, None]).astype(f32), axis=0
    )
    gather_bits = [("mp", bit) for bit in bits_of(mp_size)[::-1]]
    gather_bits = gather_bits + [("dp", bit) for bit in bits_of(dp_size)[::-1]]
    spread = {"dp": [0], "mp": [0]}
    for axis, bit in gather_bits:
        spread = {
            name: spread[name] + [place ^ (bit if name == axis else 0) for place in spread[name]]
            for name in spread
        }
    owner_all = jnp.repeat(dp_index ^ jnp.array(spread["dp"]), own)
    group_all = jnp.repeat(mp_index ^ jnp.array(spread["mp"]), own)
    row_all = group_all * own + jnp.tile(jnp.arange(own), dp_size * mp_size)
    place_all = jnp.sum(
        jnp.where(owner_all[:, None] == device_ids[None, :], inverse[None, :], 0), axis=1
    )
    rank_all = row_all * dp_size + place_all
    source_all = jnp.sum((finish[None, :] <= rank_all[:, None]).astype(jnp.int32), axis=1)
    start_all = jnp.sum(
        jnp.where(source_all[:, None] == device_ids[None, :], starts[None, :], 0), axis=1
    )
    slots_all = source_all * capacity + rank_all - start_all
    slot_hit = slots_all[:, None] == (info_owner * capacity + info_slot)[None, :]
    bins_all = jnp.sum(jnp.where(slot_hit, info[0][None, :], 0), axis=1)
    labels_all = jnp.sum(jnp.where(slot_hit, info[1][None, :], 0), axis=1)
    bin_hot = (bins_all[:, None] == jnp.arange(NBINS)[None, :])
    label_hot = (labels_all[:, None] == jnp.arange(NCLS)[None, :])
    weights_all = total_images / (NBINS * jnp.sum(bin_hot.astype(f32) * bin_totals[None, :], axis=1))
    bin_hot = bin_hot.astype(bf16)
    label_hot = label_hot.astype(bf16)
    cond_all = (dot(bin_hot, time_table) + dot(label_hot, class_table)).astype(bf16).astype(f32)
    silu_all = jax.nn.silu(cond_all).astype(bf16)
    silu_cond = silu_all[:own]
    weights = weights_all[:own]

    if by_permutes:
        silu_cond, far_near = tie(silu_cond, far_near)
        mlp_near = jnp.concatenate([mlp_near, far_near], axis=0)
        far_near = swap(mlp_near, "mp", 1)
    mods = modulate(silu_cond, weights, ada_weight)
    recv_patches, mods = tie(recv_patches, mods)

    rank_ids = jnp.arange(images) * dp_size + my_place
    source = jnp.sum((finish[None, :] <= rank_ids[:, None]).astype(jnp.int32), axis=1)
    within = rank_ids - starts[source]
    recv_index = source * slot_count + within // dp_size
    latent = take_rows(recv_patches, recv_index).reshape(mp_size, own, local_len, model_width)
    latent = turn(latent)
    if by_permutes:
        mlp_near = jnp.concatenate([mlp_near, far_near], axis=0)
        halves = split(mlp_near, 2)
        orders = ((2, 4), (4, 2))
        got = [swap(halves[half], "dp", orders[half][0]) for half in range(2)]
        latent, got[0], got[1] = tie(latent, got[0], got[1])
        halves = [jnp.stack([halves[half], got[half]]) for half in range(2)]
        got = [swap(halves[half], "dp", orders[half][1]) for half in range(2)]

    proj, attended, branch_one, normed_t, middle, two, two_t = attend(
        latent, mods, attend_full, gains_f, tables
    )
    cotangent, attended = tie(cotangent, attended)
    cot = turn(cotangent.reshape(mp_size, own, local_len, model_width))
    if by_permutes:
        mlp_pieces, mlp_order = [], []
        for half in range(2):
            first, second = orders[half]
            parts = {0: halves[half][0], first: halves[half][1]}
            parts.update({second: got[half][0], first ^ second: got[half][1]})
            for near, part in parts.items():
                mlp_pieces += [part, swap(part, "dp", 1)]
                mlp_order += [(dp_index ^ near) * 2 + half, (dp_index ^ near ^ 1) * 2 + half]
        mlp_order = jnp.stack(mlp_order).astype(jnp.int32)
    save, branch_two, mlp_full = mlp(two, mlp_order, mlp_pieces)
    down_low, down_t, result, sums_finish = by_image(
        finish_kernel, "finish", (branch_two, middle), cot, mods, (bf16, True, False)
    )
    result = turn(result)

    e_orders = [(dp_index ^ jnp.array(halving_order(bits))).astype(jnp.int32) for bits in dp_bits]
    m_order = (mp_index ^ jnp.array(halving_order(mp_bits))).astype(jnp.int32)
    m_orders = (m_order[: mp_size // 2], m_order[mp_size // 2 :])

    def by_owner(values):
        return values.reshape(dp_size, model_width // dp_size, -1)

    two_t, down_t = by_owner(two_t), by_owner(down_t)
    kept_one, sent_one, two_one = mlp_back(
        1, e_orders[1], two_t, down_t, down_low, save, mlp_full
    )
    got_one = swap(sent_one, "dp", dp_bits[1][0])
    kept_zero, sent_zero, two_zero = mlp_back(
        0, e_orders[0], two_t, down_t, down_low, save, mlp_full
    )
    got_zero = swap(sent_zero, "dp", dp_bits[0][0])
    two_zero, got_one, result = tie(two_zero, got_one, result)
    kept_one, sent_one = split(add_low(kept_one, got_one), 2)
    got_one = swap(sent_one, "dp", dp_bits[1][1])
    middle_grad, branch_low, branch_t, sums_middle = by_image(
        middle_kernel,
        "middle",
        (two_zero, two_one, middle, branch_one),
        cot,
        mods,
        (f32, bf16, True),
    )
    branch_low, got_zero = tie(branch_low, got_zero)
    kept_zero, sent_zero = split(add_low(kept_zero, got_zero), 2)
    got_zero = swap(sent_zero, "dp", dp_bits[0][1])
    projected_low, gains_grad, sums_entry, latent_back = attend_back(
        latent, proj, branch_low, attend_full, gains_f, tables, middle_grad, mods
    )
    gains_grad = jnp.sum(gains_grad, axis=2) * jnp.array([[head_dim ** (-0.5)], [1.0]], f32)
    projected_low, got_one, got_zero = tie(projected_low, got_one, got_zero)
    kept_one, sent_one = split(add_low(kept_one, got_one), 2)
    kept_zero, sent_zero = split(add_low(kept_zero, got_zero), 2)
    got_one = swap(sent_one, "dp", dp_bits[1][2])
    got_zero = swap(sent_zero, "dp", dp_bits[0][2])
    latent_back = turn(latent_back)

    normed_t, branch_t = by_owner(normed_t), by_owner(branch_t)

    def grads_of(which):
        kept, sent = attend_grads(
            m_orders[which],
            e_orders[which],
            normed_t,
            branch_t,
            projected_low,
            attended,
            200 if which else 5,
        )
        return kept, swap(sent, "dp", dp_bits[which][0])

    attend_one, attend_got_one = grads_of(1)
    attend_zero, attend_got_zero = grads_of(0)
    attend_zero, attend_got_one, got_one, got_zero = tie(
        attend_zero, attend_got_one, got_one, got_zero
    )
    mlp_one = halve(add_low(kept_one, got_one), "dp", dp_bits[1][3:], 2)
    mlp_zero = halve(add_low(kept_zero, got_zero), "dp", dp_bits[0][3:], 2)
    mlp_got = swap(mlp_one, "mp", mp_bits[0])
    attend_one, sent_one = split(add_low(attend_one, attend_got_one), 1)
    attend_zero, sent_zero = split(add_low(attend_zero, attend_got_zero), 1)
    attend_got_one = swap(sent_one, "dp", dp_bits[1][1])
    attend_got_zero = swap(sent_zero, "dp", dp_bits[0][1])

    packed = sums_finish + sums_middle + sums_entry
    gains_row = jnp.pad(gains_grad.reshape(1, 1, -1), ((0, own - 1), (7, 0), (0, model_width - 2 * head_dim)))
    packed = jnp.where(jnp.arange(8)[:, None] == 7, gains_row, packed).astype(bf16)
    packed = xor_gather(packed, gather_bits)[0]
    latent_back, attend_got_one, attend_got_zero, mlp_got = tie(
        latent_back, attend_got_one, attend_got_zero, mlp_got
    )
    attend_one = halve(add_low(attend_one, attend_got_one), "dp", dp_bits[1][2:], 1)
    attend_zero = halve(add_low(attend_zero, attend_got_zero), "dp", dp_bits[0][2:], 1)
    mlp_grad = halve(add_low(mlp_zero, mlp_got), "mp", mp_bits[1:], 0)[0].astype(f32)
    attend_grad = add_low(attend_zero, swap(attend_one, "mp", mp_bits[0]))
    attend_grad = halve(attend_grad, "mp", mp_bits[1:], 0)[0].astype(f32)

    back_within = pair_slot * dp_size + jnp.mod(my_place - starts[pair_peer], dp_size)
    back_valid = back_within < image_counts[pair_peer]
    back_slot = jnp.clip((starts[pair_peer] + back_within - my_place) // dp_size, 0, images - 1)
    back_slot = jnp.where(back_valid, back_slot, images)
    empty = jnp.zeros((1, local_len, model_width), bf16)
    latent_back = latent_back.reshape(images, local_len, model_width)
    latent_back = jnp.concatenate([latent_back, empty], axis=0)
    back_patches = take_rows(latent_back, back_slot)
    got_patches = lax.all_to_all(back_patches, "dp", split_axis=0, concat_axis=0, tiled=True)
    slot_ids = jnp.arange(capacity)
    home_peer = dest_perm[jnp.mod(my_start + slot_ids, dp_size)]
    home_index = home_peer * slot_count + jnp.minimum(slot_ids // dp_size, slot_count - 1)
    patch_grad = take_rows(got_patches, home_index)

    packed = packed.reshape(total_images, 8, model_width)
    mod_all = packed[:, :6]
    gains_total = packed.reshape(-1, own, 8, model_width)[:, 0, 7, : 2 * head_dim]
    gains_total = jnp.sum(gains_total.astype(f32), axis=0).reshape(2, head_dim)
    gains_total = jnp.sum(
        jnp.where(order[:, None] == jnp.arange(head_dim)[None, :], gains_total[:, :, None], 0.0), axis=1
    )
    width_dp = model_width // dp_size
    width_mp = model_width // mp_size
    row0 = dp_index * width_dp
    silu_rows = lax.dynamic_slice_in_dim(silu_all, row0, width_dp, 1)
    mod_cols = lax.dynamic_slice_in_dim(mod_all, mp_index * width_mp, width_mp, 2)
    ada_grad = ein("id,ikc->dkc", silu_rows, mod_cols)
    ada_rows = lax.dynamic_slice_in_dim(ada_weight, row0, width_dp, 0)
    silu_grad = ein("ikc,dkc->id", mod_all, ada_rows)
    cond_rows = lax.dynamic_slice_in_dim(cond_all, row0, width_dp, 1)
    silu_val, silu_pull = jax.vjp(jax.nn.silu, cond_rows)
    condition_low = silu_pull(silu_grad)[0].astype(bf16)
    time_grad = ein("in,id->nd", bin_hot, condition_low)
    class_grad = ein("in,id->nd", label_hot, condition_low)

    expand_grad = mlp_grad[:2].swapaxes(0, 1)
    down_grad = mlp_grad[2].T
    out_grad = attend_grad[:, 3 * local_dim :].T
    qkv_grad = lax.dot_general(
        attend_grad[:, : 3 * local_dim],
        jnp.array(places[: 3 * local_dim, None] == columns[: 3 * local_dim], f32),
        (((1,), (0,)), ((), ())),
        precision=lax.Precision.HIGHEST,
        preferred_element_type=f32,
    )
    qkv_grad = qkv_grad.reshape(-1, 3, local_dim)
    return (
        result.reshape(images, local_len, model_width),
        patch_grad,
        time_grad,
        class_grad,
        ada_grad,
        qkv_grad,
        gains_total,
        out_grad,
        expand_grad,
        down_grad,
    )


def solution(mesh):
    in_specs = (
        P("dp", "mp", None),
        P("dp", "mp", None),
        P("dp"),
        P("dp"),
        P(),
        P(),
        P(),
        P(),
        P(),
        P(None, None, "mp"),
        P(),
        P("mp", None),
        P(None, None, "mp"),
        P("mp", None),
    )
    out_specs = (
        P("dp", "mp", None),
        P("dp", "mp", None),
        P(None, "dp"),
        P(None, "dp"),
        P("dp", None, "mp"),
        P("dp", None, "mp"),
        P(),
        P("mp", "dp"),
        P("dp", None, "mp"),
        P("mp", "dp"),
    )
    return jax.shard_map(shards, mesh=mesh, in_specs=in_specs, out_specs=out_specs, check_vma=False)
```

```python
import functools
import math

import jax
import jax.numpy as jnp
import numpy as np
from jax import lax
from jax.experimental import pallas as pl
from jax.experimental.pallas import tpu as pltpu
from jax.sharding import PartitionSpec as P

GRID = 16
NCLS = 1000
NBINS = 16

epsilon = 1e-06
rope_base = 10000.0
f32 = jnp.float32
bf16 = jnp.bfloat16


def feature_order(head_dim):
    quarter = head_dim // 4
    firsts = list(range(quarter)) + list(range(2 * quarter, 3 * quarter))
    cut = len(firsts) // 8 * 8
    seconds = [i + quarter for i in firsts]
    return firsts[:cut] + seconds[:cut] + firsts[cut:] + seconds[cut:], cut


def rope_tables(position, head_dim):
    quarter = head_dim // 4
    order, cut = feature_order(head_dim)
    places = jnp.stack([position // GRID, position % GRID]).astype(f32)
    frequency = rope_base ** (-jnp.arange(quarter).astype(f32) / quarter)
    angle = (frequency[None, :, None] * places[:, None, :]).reshape(2 * quarter, -1)
    cosine, sine = jnp.cos(angle), jnp.sin(angle)
    cos_tab = jnp.concatenate([cosine[:cut], cosine[:cut], cosine[cut:], cosine[cut:]])
    sin_tab = jnp.concatenate([-sine[:cut], sine[:cut], -sine[cut:], sine[cut:]])
    return cos_tab, sin_tab


def partner(values, cut):
    rest = values[2 * cut :]
    half = rest.shape[0] // 2
    return jnp.concatenate(
        [values[cut : 2 * cut], values[:cut], pltpu.roll(rest, half, 0)], axis=0
    )


def head_scale(values):
    return lax.rsqrt(jnp.mean(values * values, axis=0, keepdims=True) + epsilon)


def dot_00(a, b):
    return lax.dot_general(a, b, (((0,), (0,)), ((), ())), preferred_element_type=f32)


def dot_11(a, b):
    return lax.dot_general(a, b, (((1,), (1,)), ((), ())), preferred_element_type=f32)


def dot_10(a, b):
    return lax.dot_general(a, b, (((1,), (0,)), ((), ())), preferred_element_type=f32)


def softmax_first(scores):
    shifted = jnp.exp(scores - jnp.max(scores, axis=0, keepdims=True))
    return shifted * (1.0 / jnp.sum(shifted, axis=0, keepdims=True))


def lasting(microseconds):
    return pl.CostEstimate(
        flops=int(microseconds * 1.1e9), bytes_accessed=1 << 20, transcendentals=0
    )


SHIFT_ONE, SCALE_ONE, GATE_ONE, SHIFT_TWO, SCALE_TWO, GATE_TWO, WEIGHT = range(7)


def row_of(mods, which):
    return mods[which : which + 1, :]


def rms(values):
    scale = lax.rsqrt(jnp.mean(values * values, -1, keepdims=True) + epsilon)
    return values * scale, scale


def rms_back(grad, unit, scale, scaling):
    grad = grad * (1.0 + scaling)
    return scale * (grad - unit * jnp.mean(grad * unit, -1, keepdims=True))


def row_sum(values):
    return jnp.sum(values, axis=0, keepdims=True)


def put_rows(sums_ref, image, rows):
    for which in range(sums_ref.shape[1]):
        value = rows.get(which, jnp.zeros((1, sums_ref.shape[2]), f32))
        sums_ref[image, which : which + 1, :] = value


def chunk_rows(ref, image):
    return jnp.concatenate([ref[chunk, image] for chunk in range(ref.shape[0])], axis=0)


def put_chunks(ref, image, values):
    size = ref.shape[2]
    for chunk in range(ref.shape[0]):
        ref[chunk, image] = values[chunk * size : (chunk + 1) * size]


def attend_kernel(
    latent_ref, mods_ref, w_ref, wo_ref, gains_ref, cos_ref, sin_ref,
    proj_ref, att_ref, branch_ref, xt_ref, middle_ref, two_ref, twot_ref, x_ref,
):
    own = mods_ref.shape[0]
    head_dim = gains_ref.shape[1]
    rows_all = att_ref.shape[1]
    length = xt_ref.shape[1] // own
    heads = range(rows_all // head_dim)
    cut = feature_order(head_dim)[1]
    group = pl.program_id(0)

    def place(image):
        return pl.ds(pl.multiple_of(image * length, length), length)

    @pl.when(group == 0)
    def _():
        def entry(image, carry):
            mods = mods_ref[image]
            unit = rms(chunk_rows(latent_ref, image).astype(f32))[0]
            x = (unit * (1.0 + row_of(mods, SCALE_ONE)) + row_of(mods, SHIFT_ONE)).astype(bf16)
            x_ref[place(image), :] = x
            xt_ref[:, place(image)] = x.T
            return carry

        lax.fori_loop(0, own, entry, 0)

    proj_ref[0] = dot_11(w_ref[0, : 3 * rows_all], x_ref[...])

    def heads_of(image, carry):
        tokens = place(image)
        cos_tab, sin_tab = cos_ref[...], sin_ref[...]
        lows = [[], [], []]
        for kind in range(2):
            for head in heads:
                start = kind * rows_all + head * head_dim
                raw = proj_ref[0, start : start + head_dim, tokens]
                scaled = raw * head_scale(raw) * gains_ref[kind]
                turned = scaled * cos_tab + partner(scaled, cut) * sin_tab
                lows[kind].append(turned.astype(bf16))
        for head in heads:
            start = 2 * rows_all + head * head_dim
            lows[2].append(proj_ref[0, start : start + head_dim, tokens].astype(bf16))
        scores = [dot_00(lows[1][head], lows[0][head]) for head in heads]
        probs = [softmax_first(score).astype(bf16) for score in scores]
        outs = [dot_10(lows[2][head], probs[head]) for head in heads]
        att_ref[group, :, tokens] = jnp.concatenate(outs, axis=0).astype(bf16)
        return carry

    lax.fori_loop(0, own, heads_of, 0, unroll=True)

    @pl.when(group == pl.num_programs(0) - 1)
    def _():
        groups = att_ref.shape[0]

        def leave(image, carry):
            tokens = place(image)
            mods = mods_ref[image]
            att = att_ref[:, :, tokens].reshape(groups * rows_all, length)
            branch = dot_00(att, wo_ref[...].reshape(groups * rows_all, -1))
            branch_ref[tokens, :] = branch.astype(bf16)
            latent = chunk_rows(latent_ref, image).astype(f32)
            middle = latent + row_of(mods, GATE_ONE) * branch
            middle_ref[tokens, :] = middle
            two = rms(middle)[0] * (1.0 + row_of(mods, SCALE_TWO)) + row_of(mods, SHIFT_TWO)
            two = two.astype(bf16)
            two_ref[tokens, :] = two
            twot_ref[:, tokens] = two.T
            return carry

        lax.fori_loop(0, own, leave, 0)


def attend_back_kernel(
    latent_ref, proj_ref, low_ref, w_ref, gains_ref, cos_ref, sin_ref, grad_ref, mods_ref,
    out_ref, gain_grad_ref, sums_ref, chunks_ref, cot_ref,
):
    own = mods_ref.shape[0]
    head_dim = gains_ref.shape[1]
    rows_all, tokens_all = proj_ref.shape[1] // 3, proj_ref.shape[2]
    length = tokens_all // own
    heads = range(rows_all // head_dim)
    cut = feature_order(head_dim)[1]
    group = pl.program_id(0)

    def place(image):
        return pl.ds(pl.multiple_of(image * length, length), length)

    @pl.when(group == 0)
    def _():
        gain_grad_ref[...] = jnp.zeros_like(gain_grad_ref)

    cot_ref[...] = dot_11(w_ref[group, 3 * rows_all :], low_ref[...])

    def heads_of(image, carry):
        tokens = place(image)
        cos_tab, sin_tab = cos_ref[...], sin_ref[...]
        lows, units, scales = [[], [], []], [[], []], [[], []]
        for kind in range(2):
            for head in heads:
                start = kind * rows_all + head * head_dim
                raw = proj_ref[0, start : start + head_dim, tokens]
                scale = head_scale(raw)
                unit = raw * scale
                scaled = unit * gains_ref[kind]
                turned = scaled * cos_tab + partner(scaled, cut) * sin_tab
                lows[kind].append(turned.astype(bf16))
                units[kind].append(unit)
                scales[kind].append(scale)
        cots = []
        for head in heads:
            start = 2 * rows_all + head * head_dim
            lows[2].append(proj_ref[0, start : start + head_dim, tokens].astype(bf16))
            cots.append(cot_ref[head * head_dim : (head + 1) * head_dim, tokens].astype(bf16))
        scores = [dot_00(lows[1][head], lows[0][head]) for head in heads]
        prob_grads = [dot_00(lows[2][head], cots[head]) for head in heads]
        probs = [softmax_first(score) for score in scores]
        outs = [[], [], []]
        outs[2] = [dot_11(cots[head], probs[head].astype(bf16)) for head in heads]
        score_lows = []
        for head in heads:
            mean = jnp.sum(probs[head] * prob_grads[head], axis=0, keepdims=True)
            score_lows.append((probs[head] * (prob_grads[head] - mean)).astype(bf16))
        turned_grads = [
            [dot_10(lows[1][head], score_lows[head]) for head in heads],
            [dot_11(lows[0][head], score_lows[head]) for head in heads],
        ]
        for kind in range(2):
            total = 0.0
            for head in heads:
                grad, unit = turned_grads[kind][head], units[kind][head]
                grad = grad * cos_tab + partner(grad * sin_tab, cut)
                total = total + grad * unit
                grad = grad * gains_ref[kind]
                along = jnp.mean(grad * unit, axis=0, keepdims=True)
                outs[kind].append(scales[kind][head] * (grad - unit * along))
            gain_grad_ref[kind] += total
        grads = jnp.concatenate(outs[0] + outs[1] + outs[2], axis=0).astype(bf16)
        out_ref[group, :, tokens] = grads
        return carry

    lax.fori_loop(0, own, heads_of, 0, unroll=True)

    @pl.when(group == pl.num_programs(0) - 1)
    def _():
        def leave(image, carry):
            tokens = place(image)
            mods = mods_ref[image]
            grad = 0.0
            for other in range(out_ref.shape[0]):
                grad = grad + dot_00(out_ref[other, :, tokens], w_ref[other, : 3 * rows_all])
            unit, scale = rms(chunk_rows(latent_ref, image).astype(f32))
            sums = {SHIFT_ONE: row_sum(grad), SCALE_ONE: row_sum(grad * unit)}
            put_rows(sums_ref, image, sums)
            grad = grad_ref[tokens, :] + rms_back(grad, unit, scale, row_of(mods, SCALE_ONE))
            put_chunks(chunks_ref, image, grad.astype(bf16))
            return carry

        lax.fori_loop(0, own, leave, 0)


def whole_spec(shape):
    return pl.BlockSpec(shape, lambda g: (0,) * len(shape), pipeline_mode=pl.Buffered(1))


def attend(latent, mods, weights, gains, tables):
    groups, rows, width = weights.shape[0], weights.shape[1] // 4, weights.shape[2]
    own = mods.shape[0]
    length, head_dim = tables[0].shape[1], gains.shape[1]
    tokens = own * length
    total, turned = (tokens, width), (width, tokens)
    const = lambda shape: pl.BlockSpec(shape, lambda g: (0,) * len(shape))
    return pl.pallas_call(
        attend_kernel,
        grid=(groups,),
        in_specs=[
            whole_spec(latent.shape),
            whole_spec(mods.shape),
            pl.BlockSpec((1, 4 * rows, width), lambda g: (g, 0, 0)),
            pl.BlockSpec((groups, rows, width), lambda g: (0, 3, 0), pipeline_mode=pl.Buffered(1)),
            whole_spec(gains.shape),
            whole_spec(tables[0].shape),
            whole_spec(tables[0].shape),
        ],
        out_specs=[
            pl.BlockSpec((1, 3 * rows, tokens), lambda g: (g, 0, 0)),
            const((groups, rows, tokens)),
            const(total),
            const(turned),
            const(total),
            const(total),
            const(turned),
        ],
        out_shape=[
            jax.ShapeDtypeStruct((groups, 3 * rows, tokens), f32),
            jax.ShapeDtypeStruct((groups, rows, tokens), bf16),
            jax.ShapeDtypeStruct(total, bf16),
            jax.ShapeDtypeStruct(turned, bf16),
            jax.ShapeDtypeStruct(total, f32),
            jax.ShapeDtypeStruct(total, bf16),
            jax.ShapeDtypeStruct(turned, bf16),
        ],
        scratch_shapes=[pltpu.VMEM(total, bf16)],
        compiler_params=pltpu.CompilerParams(vmem_limit_bytes=62 << 20),
        cost_estimate=lasting(160),
        name="attend",
    )(latent, mods, weights, weights, gains, *tables)


def attend_back(latent, proj, low, weights, gains, tables, grad, mods):
    groups, rows, width = weights.shape[0], weights.shape[1] // 4, weights.shape[2]
    own = mods.shape[0]
    tokens = low.shape[0]
    length, head_dim = tokens // own, gains.shape[1]
    const = lambda shape: pl.BlockSpec(shape, lambda g: (0,) * len(shape))
    gain_shape = (2, head_dim, length)
    return pl.pallas_call(
        attend_back_kernel,
        grid=(groups,),
        in_specs=[
            whole_spec(latent.shape),
            pl.BlockSpec((1, 3 * rows, tokens), lambda g: (g, 0, 0)),
            whole_spec(low.shape),
            whole_spec(weights.shape),
            whole_spec(gains.shape),
            whole_spec(tables[0].shape),
            whole_spec(tables[0].shape),
            whole_spec(grad.shape),
            whole_spec(mods.shape),
        ],
        out_specs=[const(proj.shape), const(gain_shape), const(mods.shape), const(latent.shape)],
        out_shape=[
            jax.ShapeDtypeStruct(proj.shape, bf16),
            jax.ShapeDtypeStruct(gain_shape, f32),
            jax.ShapeDtypeStruct(mods.shape, f32),
            jax.ShapeDtypeStruct(latent.shape, bf16),
        ],
        scratch_shapes=[pltpu.VMEM((rows, tokens), f32)],
        compiler_params=pltpu.CompilerParams(vmem_limit_bytes=62 << 20),
        cost_estimate=lasting(160),
        name="attend_back",
    )(latent, proj, low, weights, gains, *tables, grad, mods)


def finish_kernel(
    branch_ref, middle_ref, cot_ref, mods_ref, low_ref, lowt_ref, chunks_ref, sums_ref
):
    branch, mods = branch_ref[...], mods_ref[0]
    gate = row_of(mods, GATE_TWO)
    result = (middle_ref[...] + gate * branch).astype(bf16)
    put_chunks(chunks_ref, 0, result)
    cot = chunk_rows(cot_ref, 0).astype(f32) * row_of(mods, WEIGHT)
    low = (gate * cot).astype(bf16)
    low_ref[...] = low
    lowt_ref[...] = low.T
    put_rows(sums_ref, 0, {GATE_TWO: row_sum(cot * branch)})


def middle_kernel(
    one_ref, other_ref, middle_ref, branch_ref, cot_ref, mods_ref,
    grad_ref, low_ref, lowt_ref, sums_ref,
):
    mods = mods_ref[0]
    grad = one_ref[...] + other_ref[...]
    unit, scale = rms(middle_ref[...])
    sums = {SHIFT_TWO: row_sum(grad), SCALE_TWO: row_sum(grad * unit)}
    cot = chunk_rows(cot_ref, 0).astype(f32) * row_of(mods, WEIGHT)
    grad = cot + rms_back(grad, unit, scale, row_of(mods, SCALE_TWO))
    grad_ref[...] = grad
    low = (row_of(mods, GATE_ONE) * grad).astype(bf16)
    low_ref[...] = low
    lowt_ref[...] = low.T
    sums[GATE_ONE] = row_sum(grad * branch_ref[...].astype(f32))
    put_rows(sums_ref, 0, sums)


def by_image(kernel, name, rows, chunks, mods, outs):
    own, sums, width = mods.shape
    tokens = rows[0].shape[0]
    length = tokens // own
    block = pl.BlockSpec((length, width), lambda i: (i, 0))
    turned = pl.BlockSpec((width, length), lambda i: (0, i))
    chunk = pl.BlockSpec((chunks.shape[0], 1) + chunks.shape[2:], lambda i: (0, i, 0, 0))
    whole = pl.BlockSpec((1, sums, width), lambda i: (i, 0, 0))
    specs, shapes = [], []
    for out in outs:
        if out is True:
            specs.append(turned)
            shapes.append(jax.ShapeDtypeStruct((width, tokens), bf16))
        elif out is False:
            specs.append(chunk)
            shapes.append(jax.ShapeDtypeStruct(chunks.shape, bf16))
        else:
            specs.append(block)
            shapes.append(jax.ShapeDtypeStruct((tokens, width), out))
    return pl.pallas_call(
        kernel,
        grid=(own,),
        in_specs=[block] * len(rows) + [chunk, whole],
        out_specs=specs + [whole],
        out_shape=shapes + [jax.ShapeDtypeStruct(mods.shape, f32)],
        compiler_params=pltpu.CompilerParams(vmem_limit_bytes=48 << 20),
        cost_estimate=lasting(30),
        name=name,
    )(*rows, chunks, mods)


def modulate_kernel(silu_ref, ada_ref, out_ref):
    out_ref[0] = dot_10(silu_ref[...], ada_ref[0])


def modulate(silu, ada):
    kinds, width = ada.shape[:2]
    return pl.pallas_call(
        modulate_kernel,
        grid=(kinds,),
        in_specs=[
            pl.BlockSpec(silu.shape, lambda k: (0, 0)),
            pl.BlockSpec((1, width, width), lambda k: (k, 0, 0)),
        ],
        out_specs=pl.BlockSpec((1,) + silu.shape, lambda k: (k, 0, 0)),
        out_shape=jax.ShapeDtypeStruct((kinds,) + silu.shape, f32),
        compiler_params=pltpu.CompilerParams(vmem_limit_bytes=32 << 20),
        cost_estimate=lasting(60),
        name="modulate",
    )(silu, ada)


def add_rows(out_ref, part, first, index, length):
    rows = pl.ds(pl.multiple_of(index * length, length), length)

    @pl.when(first)
    def _():
        out_ref[rows, :] = part

    @pl.when(jnp.logical_not(first))
    def _():
        out_ref[rows, :] += part


def sigmoid(values):
    return 1.0 / (1.0 + jnp.exp(-values))


def mlp_kernel(count, e_ref, x_ref, *refs):
    first = pl.program_id(0) == 0
    save_ref, out_ref, w_ref = refs[count:]
    size = refs[0].shape[2]
    for index, ref in enumerate(refs[:count]):
        rows = pl.ds(pl.multiple_of(e_ref[index] * size, size), size)
        for kind in range(3):
            w_ref[0, kind, rows, :] = ref[0, kind]
    x = x_ref[...]
    gate = dot_11(x, w_ref[0, 0])
    up = dot_11(x, w_ref[0, 1])
    save_ref[0, 0] = gate.astype(bf16)
    save_ref[0, 1] = up.astype(bf16)
    hidden = (gate * sigmoid(gate) * up).astype(bf16)
    part = dot_10(hidden, w_ref[0, 2])
    add_rows(out_ref, part, first, 0, x.shape[0])


def mlp(x, order, pieces):
    groups, _, size, width = pieces[0].shape
    units, tokens = size * len(pieces), x.shape[0]
    return pl.pallas_call(
        functools.partial(mlp_kernel, len(pieces)),
        grid_spec=pltpu.PrefetchScalarGridSpec(
            num_scalar_prefetch=1,
            grid=(groups,),
            in_specs=[pl.BlockSpec((tokens, width), lambda g, e: (0, 0), pipeline_mode=pl.Buffered(1))]
            + [pl.BlockSpec((1, 3, size, width), lambda g, e: (g, 0, 0, 0))] * len(pieces),
            out_specs=[
                pl.BlockSpec((1, 2, tokens, units), lambda g, e: (g, 0, 0, 0)),
                pl.BlockSpec((tokens, width), lambda g, e: (0, 0)),
                pl.BlockSpec((1, 3, units, width), lambda g, e: (g, 0, 0, 0)),
            ],
        ),
        out_shape=[
            jax.ShapeDtypeStruct((groups, 2, tokens, units), bf16),
            jax.ShapeDtypeStruct((tokens, width), f32),
            jax.ShapeDtypeStruct((groups, 3, units, width), bf16),
        ],
        compiler_params=pltpu.CompilerParams(vmem_limit_bytes=62 << 20),
        cost_estimate=lasting(120),
        name="mlp",
    )(order, x, *pieces)


def fill_rows(order_ref, source_ref, target_ref):
    blocks, rows = source_ref.shape[0], source_ref.shape[1]
    for place in range(blocks):
        target_ref[place * rows : (place + 1) * rows, :] = source_ref[order_ref[place]]


def mlp_back_kernel(
    e_ref, xt_ref, lowt_ref, low_ref, save_ref, w_ref,
    keep_ref, send_ref, two_ref, xs, lows, parts,
):
    first = pl.program_id(0) == 0
    tokens, width = low_ref.shape
    step = math.gcd(tokens, 512)

    @pl.when(first)
    def _():
        fill_rows(e_ref, xt_ref, xs)
        fill_rows(e_ref, lowt_ref, lows)

    for index in range(tokens // step):
        rows = pl.ds(index * step, step)
        hidden_grad = dot_11(low_ref[rows, :], w_ref[0, 2])
        gate = save_ref[0, 0, rows, :].astype(f32)
        up = save_ref[0, 1, rows, :].astype(f32)
        sig = sigmoid(gate)
        swish = gate * sig
        gate_low = (hidden_grad * up * (sig + swish * (1.0 - sig))).astype(bf16)
        up_low = (hidden_grad * swish).astype(bf16)
        parts[0, rows, :] = gate_low
        parts[1, rows, :] = up_low
        parts[2, rows, :] = (swish * up).astype(bf16)
        part = dot_10(gate_low, w_ref[0, 0]) + dot_10(up_low, w_ref[0, 1])
        add_rows(two_ref, part, first, index, step)

    half = width // 2
    for out_ref, rows in ((keep_ref, slice(0, half)), (send_ref, slice(half, width))):
        x_rows = xs[rows, :]
        for kind in range(2):
            out_ref[0, kind] = dot_10(x_rows, parts[kind]).astype(bf16)
        out_ref[0, 2] = dot_10(lows[rows, :], parts[2]).astype(bf16)


def mlp_back(which, e_order, xt, lowt, low, save, weights):
    groups, _, units, width = weights.shape
    tokens = low.shape[0]
    blocks = groups // 2
    base = which * blocks
    once = pl.Buffered(1)
    whole = lambda p, e: (0, 0)
    whole3 = lambda p, e: (0, 0, 0)
    half = jax.ShapeDtypeStruct((blocks, 3, width // 2, units), bf16)
    half_spec = pl.BlockSpec((1, 3, width // 2, units), lambda p, e: (p, 0, 0, 0))
    return pl.pallas_call(
        mlp_back_kernel,
        grid_spec=pltpu.PrefetchScalarGridSpec(
            num_scalar_prefetch=1,
            grid=(blocks,),
            in_specs=[
                pl.BlockSpec(xt.shape, whole3, pipeline_mode=once),
                pl.BlockSpec(lowt.shape, whole3, pipeline_mode=once),
                pl.BlockSpec((tokens, width), whole, pipeline_mode=once),
                pl.BlockSpec((1, 2, tokens, units), lambda p, e: (base + p, 0, 0, 0)),
                pl.BlockSpec((1, 3, units, width), lambda p, e: (base + p, 0, 0, 0)),
            ],
            out_specs=[half_spec, half_spec, pl.BlockSpec((tokens, width), whole)],
            scratch_shapes=[
                pltpu.VMEM((width, tokens), bf16),
                pltpu.VMEM((width, tokens), bf16),
                pltpu.VMEM((3, tokens, units), bf16),
            ],
        ),
        out_shape=[half, half, jax.ShapeDtypeStruct((tokens, width), f32)],
        compiler_params=pltpu.CompilerParams(vmem_limit_bytes=62 << 20),
        cost_estimate=lasting(150),
        name="mlp_back",
    )(e_order, xt, lowt, low, save, weights)


def attend_grads_kernel(
    m_ref, e_ref, xt_ref, lowt_ref, proj_ref, att_ref, keep_ref, send_ref, xs, lows
):
    @pl.when(pl.program_id(0) == 0)
    def _():
        fill_rows(e_ref, xt_ref, xs)
        fill_rows(e_ref, lowt_ref, lows)

    width = xs.shape[0]
    half = width // 2
    columns = proj_ref.shape[1]

    for out_ref, rows in ((keep_ref, slice(0, half)), (send_ref, slice(half, width))):
        out_ref[0, :, :columns] = dot_11(xs[rows, :], proj_ref[0]).astype(bf16)
        out_ref[0, :, columns:] = dot_11(lows[rows, :], att_ref[0]).astype(bf16)


def attend_grads(m_order, e_order, xt, lowt, proj, att, microseconds):
    rows, tokens = att.shape[1:]
    width = xt.shape[0] * xt.shape[1]
    blocks = m_order.shape[0]
    whole3 = lambda p, m, e: (0, 0, 0)
    half = jax.ShapeDtypeStruct((blocks, width // 2, 4 * rows), bf16)
    half_spec = pl.BlockSpec((1, width // 2, 4 * rows), lambda p, m, e: (p, 0, 0))
    return pl.pallas_call(
        attend_grads_kernel,
        grid_spec=pltpu.PrefetchScalarGridSpec(
            num_scalar_prefetch=2,
            grid=(blocks,),
            in_specs=[
                pl.BlockSpec(xt.shape, whole3, pipeline_mode=pl.Buffered(1)),
                pl.BlockSpec(lowt.shape, whole3, pipeline_mode=pl.Buffered(1)),
                pl.BlockSpec((1, 3 * rows, tokens), lambda p, m, e: (m[p], 0, 0)),
                pl.BlockSpec((1, rows, tokens), lambda p, m, e: (m[p], 0, 0)),
            ],
            out_specs=[half_spec, half_spec],
            scratch_shapes=[
                pltpu.VMEM((width, tokens), bf16),
                pltpu.VMEM((width, tokens), bf16),
            ],
        ),
        out_shape=[half, half],
        compiler_params=pltpu.CompilerParams(vmem_limit_bytes=56 << 20),
        cost_estimate=lasting(microseconds),
        name="attend_grads",
    )(m_order, e_order, xt, lowt, proj, att)


def dot(a, b):
    return jnp.dot(a, b, preferred_element_type=f32)


def ein(spec, a, b):
    return jnp.einsum(spec, a, b, preferred_element_type=f32)


def gather_pieces(piece, mp_size):
    whole = lax.all_gather(piece, ("mp", "dp"), axis=0, tiled=False)
    return whole.reshape((mp_size, -1) + piece.shape)


def take_rows(values, index):
    return jnp.take(values, index, axis=0, mode="clip")


def bits_of(size):
    return [1 << i for i in range(size.bit_length() - 1)]


def swap(values, axis, bit):
    size = lax.axis_size(axis)
    return lax.ppermute(values, axis, [(i, i ^ bit) for i in range(size)])


def xor_gather(values, axes_bits):
    names = sorted({axis for axis, _ in axes_bits})
    places = [{name: 0 for name in names}]
    values = values[None]
    for axis, bit in axes_bits:
        values = jnp.concatenate([values, swap(values, axis, bit)], axis=0)
        places = places + [dict(place, **{axis: place[axis] ^ bit}) for place in places]
    return values, {name: [place[name] for place in places] for name in names}


def halving_order(bits):
    order = [0]
    for bit in reversed(bits):
        order = order + [place ^ bit for place in order]
    return order


def add_low(kept, received):
    return (kept.astype(f32) + received.astype(f32)).astype(bf16)


def tie(*values):
    return lax.optimization_barrier(values)


def split(values, dim):
    size = values.shape[dim] // 2
    return (
        lax.slice_in_dim(values, 0, size, axis=dim),
        lax.slice_in_dim(values, size, 2 * size, axis=dim),
    )


def halve(values, axis, bits, dim):
    for bit in bits:
        kept, sent = split(values, dim)
        values = add_low(kept, swap(sent, axis, bit))
    return values


def shards(
    patches,
    cotangent,
    time_bins,
    labels,
    image_counts,
    dest_perm,
    time_table,
    class_table,
    ada_weight,
    qkv_weight,
    norm_gains,
    out_weight,
    expand_weight,
    down_weight,
):
    dp_size = lax.axis_size("dp")
    mp_size = lax.axis_size("mp")
    capacity = patches.shape[0]
    slot_count = capacity // dp_size
    images = cotangent.shape[0]
    local_len = patches.shape[1]
    model_width = patches.shape[2]
    length = local_len * mp_size
    head_dim = norm_gains.shape[1]
    local_dim = out_weight.shape[0]
    unit_count = down_weight.shape[0]
    own = images // mp_size
    total_images = images * dp_size
    order = np.array(feature_order(head_dim)[0])
    columns = np.arange(4 * local_dim)
    places = columns // head_dim * head_dim + order[columns % head_dim]
    places = np.where(columns < 2 * local_dim, places, columns).astype(np.int32)
    gains_f = norm_gains.astype(f32)[:, order]
    gains_f = (gains_f * jnp.array([[head_dim ** (-0.5)], [1.0]], f32))[:, :, None]
    dp_index = lax.axis_index("dp")
    mp_index = lax.axis_index("mp")
    dp_bits = bits_of(dp_size)
    dp_bits = (dp_bits, dp_bits[:1] + dp_bits[1:][::-1])
    mp_bits = bits_of(mp_size)

    tables = rope_tables(jnp.arange(length), head_dim)

    def turn(chunks):
        return lax.all_to_all(chunks, "mp", split_axis=0, concat_axis=0, tiled=True)

    starts = jnp.cumsum(image_counts) - image_counts
    finish = starts + image_counts
    my_start = starts[dp_index]
    my_count = image_counts[dp_index]
    device_ids = jnp.arange(dp_size)
    matches = (dest_perm[:, None] == device_ids[None, :]).astype(jnp.int32)
    inverse = jnp.sum(device_ids[:, None] * matches, axis=0)
    my_place = inverse[dp_index]
    pair_ids = jnp.arange(dp_size * slot_count)
    pair_peer = pair_ids // slot_count
    pair_slot = pair_ids % slot_count
    send_index = pair_slot * dp_size + jnp.mod(inverse[pair_peer] - my_start, dp_size)
    send_index = jnp.minimum(send_index, capacity - 1)
    send_patches = take_rows(patches, send_index)
    info, info_places = xor_gather(
        jnp.stack([time_bins, labels]), [("dp", bit) for bit in bits_of(dp_size)]
    )
    qkv_weight, out_weight, expand_weight, down_weight, send_patches, info = tie(
        qkv_weight, out_weight, expand_weight, down_weight, send_patches, info
    )
    share = 4 * local_dim // dp_size
    spots = lax.dynamic_slice_in_dim(jnp.array(places), dp_index * share, share, 0)
    take_qkv = (spots[:, None] == jnp.arange(3 * local_dim)[None, :]).astype(bf16)
    take_out = (spots[:, None] - 3 * local_dim == jnp.arange(local_dim)[None, :]).astype(bf16)
    attend_piece = dot(take_qkv, qkv_weight.transpose(1, 2, 0).reshape(-1, model_width))
    attend_piece = (attend_piece + dot(take_out, out_weight)).astype(bf16)
    share = unit_count // dp_size
    spots = dp_index * share + jnp.arange(share)
    take_units = (spots[:, None] == jnp.arange(unit_count)[None, :]).astype(bf16)
    mlp_piece = jnp.stack(
        [
            ein("rf,df->rd", take_units, expand_weight[:, 0]).astype(bf16),
            ein("rf,df->rd", take_units, expand_weight[:, 1]).astype(bf16),
            lax.dynamic_slice_in_dim(down_weight, dp_index * share, share, 0),
        ]
    )
    attend_full = gather_pieces(attend_piece, mp_size).reshape(mp_size, 4 * local_dim, -1)
    by_permutes = share % 32 == 0 and dp_size == 8 and mp_size == 4
    if by_permutes:
        mlp_near = mlp_piece[None]
        far_near = swap(mlp_near, "mp", 2)
    else:
        mlp_full = gather_pieces(mlp_piece, mp_size)
        mlp_full = mlp_full.swapaxes(1, 2).reshape(mp_size, 3, unit_count, model_width)
        mlp_pieces = [mlp_full[mp_index ^ jnp.array(halving_order(mp_bits))]]
        mlp_order = jnp.zeros((1,), jnp.int32)

    recv_patches = lax.all_to_all(send_patches, "dp", split_axis=0, concat_axis=0, tiled=True)
    info = info.swapaxes(0, 1).reshape(2, -1)
    info_owner = jnp.repeat(dp_index ^ jnp.array(info_places["dp"]), capacity)
    info_slot = jnp.tile(jnp.arange(capacity), dp_size)
    info_count = jnp.sum(
        jnp.where(info_owner[:, None] == device_ids[None, :], image_counts[None, :], 0), axis=1
    )
    live_all = info_slot < info_count
    bin_totals = jnp.sum(
        ((info[0][:, None] == jnp.arange(NBINS)[None, :]) & live_all[:, None]).astype(f32), axis=0
    )
    gather_bits = [("mp", bit) for bit in bits_of(mp_size)[::-1]]
    gather_bits = gather_bits + [("dp", bit) for bit in bits_of(dp_size)[::-1]]
    spread = {"dp": [0], "mp": [0]}
    for axis, bit in gather_bits:
        spread = {
            name: spread[name] + [place ^ (bit if name == axis else 0) for place in spread[name]]
            for name in spread
        }
    owner_all = jnp.repeat(dp_index ^ jnp.array(spread["dp"]), own)
    group_all = jnp.repeat(mp_index ^ jnp.array(spread["mp"]), own)
    row_all = group_all * own + jnp.tile(jnp.arange(own), dp_size * mp_size)
    place_all = jnp.sum(
        jnp.where(owner_all[:, None] == device_ids[None, :], inverse[None, :], 0), axis=1
    )
    rank_all = row_all * dp_size + place_all
    source_all = jnp.sum((finish[None, :] <= rank_all[:, None]).astype(jnp.int32), axis=1)
    start_all = jnp.sum(
        jnp.where(source_all[:, None] == device_ids[None, :], starts[None, :], 0), axis=1
    )
    slots_all = source_all * capacity + rank_all - start_all
    slot_hit = slots_all[:, None] == (info_owner * capacity + info_slot)[None, :]
    bins_all = jnp.sum(jnp.where(slot_hit, info[0][None, :], 0), axis=1)
    labels_all = jnp.sum(jnp.where(slot_hit, info[1][None, :], 0), axis=1)
    bin_hot = (bins_all[:, None] == jnp.arange(NBINS)[None, :])
    label_hot = (labels_all[:, None] == jnp.arange(NCLS)[None, :])
    weights_all = total_images / (NBINS * jnp.sum(bin_hot.astype(f32) * bin_totals[None, :], axis=1))
    bin_hot = bin_hot.astype(bf16)
    label_hot = label_hot.astype(bf16)
    cond_all = (dot(bin_hot, time_table) + dot(label_hot, class_table)).astype(bf16).astype(f32)
    silu_all = jax.nn.silu(cond_all).astype(bf16)
    silu_cond = silu_all[:own]
    weights = weights_all[:own]

    if by_permutes:
        silu_cond, far_near = tie(silu_cond, far_near)
        mlp_near = jnp.concatenate([mlp_near, far_near], axis=0)
        far_near = swap(mlp_near, "mp", 1)
    ada_kinds = ada_weight.swapaxes(0, 1)
    modulation = modulate(jnp.pad(silu_cond, ((0, -own % 16), (0, 0))), ada_kinds)[:, :own]
    mods = jnp.concatenate(
        [
            modulation.swapaxes(0, 1),
            jnp.broadcast_to(weights[:, None, None], (own, 1, model_width)),
            jnp.zeros((own, 1, model_width), f32),
        ],
        axis=1,
    )
    if by_permutes:
        recv_patches, mods, far_near = tie(recv_patches, mods, far_near)
    else:
        recv_patches, mods = tie(recv_patches, mods)

    rank_ids = jnp.arange(images) * dp_size + my_place
    source = jnp.sum((finish[None, :] <= rank_ids[:, None]).astype(jnp.int32), axis=1)
    within = rank_ids - starts[source]
    recv_index = source * slot_count + within // dp_size
    latent = take_rows(recv_patches, recv_index).reshape(mp_size, own, local_len, model_width)
    latent = turn(latent)
    if by_permutes:
        mlp_near = jnp.concatenate([mlp_near, far_near], axis=0)
        halves = split(mlp_near, 2)
        orders = ((2, 4), (4, 2))
        got = [swap(halves[half], "dp", orders[half][0]) for half in range(2)]
        latent, got[0], got[1] = tie(latent, got[0], got[1])
        firsts = [(halves[half], got[half]) for half in range(2)]
        got = [swap(jnp.stack(firsts[half]), "dp", orders[half][1]) for half in range(2)]

    proj, attended, branch_one, normed_t, middle, two, two_t = attend(
        latent, mods, attend_full, gains_f, tables
    )
    cotangent, attended = tie(cotangent, attended)
    cot = turn(cotangent.reshape(mp_size, own, local_len, model_width))
    if by_permutes:
        got[0], got[1], attended = tie(got[0], got[1], attended)
        mlp_pieces, mlp_order = [], []
        for half in range(2):
            first, second = orders[half]
            parts = {0: firsts[half][0], first: firsts[half][1]}
            parts.update({second: got[half][0], first ^ second: got[half][1]})
            for near, part in parts.items():
                mlp_pieces += [part, swap(part, "dp", 1)]
                mlp_order += [(dp_index ^ near) * 2 + half, (dp_index ^ near ^ 1) * 2 + half]
        mlp_order = jnp.stack(mlp_order).astype(jnp.int32)
    save, branch_two, mlp_full = mlp(two, mlp_order, mlp_pieces)
    down_low, down_t, result, sums_finish = by_image(
        finish_kernel, "finish", (branch_two, middle), cot, mods, (bf16, True, False)
    )
    result = turn(result)

    e_orders = [(dp_index ^ jnp.array(halving_order(bits))).astype(jnp.int32) for bits in dp_bits]
    m_order = (mp_index ^ jnp.array(halving_order(mp_bits))).astype(jnp.int32)
    m_orders = (m_order[: mp_size // 2], m_order[mp_size // 2 :])

    def by_owner(values):
        return values.reshape(dp_size, model_width // dp_size, -1)

    two_t, down_t = by_owner(two_t), by_owner(down_t)
    kept_one, sent_one, two_one = mlp_back(
        1, e_orders[1], two_t, down_t, down_low, save, mlp_full
    )
    got_one = swap(sent_one, "dp", dp_bits[1][0])
    kept_zero, sent_zero, two_zero = mlp_back(
        0, e_orders[0], two_t, down_t, down_low, save, mlp_full
    )
    got_zero = swap(sent_zero, "dp", dp_bits[0][0])
    two_zero, got_one, result = tie(two_zero, got_one, result)
    kept_one, sent_one = split(add_low(kept_one, got_one), 2)
    got_one = swap(sent_one, "dp", dp_bits[1][1])
    middle_grad, branch_low, branch_t, sums_middle = by_image(
        middle_kernel,
        "middle",
        (two_zero, two_one, middle, branch_one),
        cot,
        mods,
        (f32, bf16, True),
    )
    branch_low, got_zero = tie(branch_low, got_zero)
    kept_zero, sent_zero = split(add_low(kept_zero, got_zero), 2)
    got_zero = swap(sent_zero, "dp", dp_bits[0][1])
    projected_low, gains_grad, sums_entry, latent_back = attend_back(
        latent, proj, branch_low, attend_full, gains_f, tables, middle_grad, mods
    )
    gains_grad = jnp.sum(gains_grad, axis=2) * jnp.array([[head_dim ** (-0.5)], [1.0]], f32)
    projected_low, got_one, got_zero = tie(projected_low, got_one, got_zero)
    kept_one, sent_one = split(add_low(kept_one, got_one), 2)
    kept_zero, sent_zero = split(add_low(kept_zero, got_zero), 2)
    got_one = swap(sent_one, "dp", dp_bits[1][2])
    got_zero = swap(sent_zero, "dp", dp_bits[0][2])
    latent_back = turn(latent_back)

    normed_t, branch_t = by_owner(normed_t), by_owner(branch_t)

    def grads_of(which):
        kept, sent = attend_grads(
            m_orders[which],
            e_orders[which],
            normed_t,
            branch_t,
            projected_low,
            attended,
            200 if which else 5,
        )
        return kept, swap(sent, "dp", dp_bits[which][0])

    attend_one, attend_got_one = grads_of(1)
    attend_zero, attend_got_zero = grads_of(0)
    mlp_one = halve(add_low(kept_one, got_one), "dp", dp_bits[1][3:], 2)
    mlp_zero = halve(add_low(kept_zero, got_zero), "dp", dp_bits[0][3:], 2)
    attend_one = add_low(attend_one, attend_got_one)
    attend_zero = add_low(attend_zero, attend_got_zero)
    latent_back, attend_one, attend_zero, mlp_one, mlp_zero = tie(
        latent_back, attend_one, attend_zero, mlp_one, mlp_zero
    )
    attend_one, sent_one = split(attend_one, 1)
    attend_zero, sent_zero = split(attend_zero, 1)
    attend_got_one = swap(sent_one, "dp", dp_bits[1][1])
    attend_got_zero = swap(sent_zero, "dp", dp_bits[0][1])
    mlp_got = swap(mlp_one, "mp", mp_bits[0])

    back_within = pair_slot * dp_size + jnp.mod(my_place - starts[pair_peer], dp_size)
    back_valid = back_within < image_counts[pair_peer]
    back_slot = jnp.clip((starts[pair_peer] + back_within - my_place) // dp_size, 0, images - 1)
    back_slot = jnp.where(back_valid, back_slot, images)
    empty = jnp.zeros((1, local_len, model_width), bf16)
    latent_back = latent_back.reshape(images, local_len, model_width)
    latent_back = jnp.concatenate([latent_back, empty], axis=0)
    back_patches = take_rows(latent_back, back_slot)

    packed = sums_finish + sums_middle + sums_entry
    gains_row = jnp.pad(gains_grad.reshape(1, 1, -1), ((0, own - 1), (7, 0), (0, model_width - 2 * head_dim)))
    packed = jnp.where(jnp.arange(8)[:, None] == 7, gains_row, packed).astype(bf16)
    packed, back_patches = tie(packed, back_patches)
    packed = xor_gather(packed, gather_bits)[0]
    got_patches = lax.all_to_all(back_patches, "dp", split_axis=0, concat_axis=0, tiled=True)
    slot_ids = jnp.arange(capacity)
    home_peer = dest_perm[jnp.mod(my_start + slot_ids, dp_size)]
    home_index = home_peer * slot_count + jnp.minimum(slot_ids // dp_size, slot_count - 1)
    patch_grad = take_rows(got_patches, home_index)

    packed = packed.reshape(total_images, 8, model_width)
    mod_all = packed[:, :6]
    gains_total = packed.reshape(-1, own, 8, model_width)[:, 0, 7, : 2 * head_dim]
    gains_total = jnp.sum(gains_total.astype(f32), axis=0).reshape(2, head_dim)
    gains_total = jnp.sum(
        jnp.where(order[:, None] == jnp.arange(head_dim)[None, :], gains_total[:, :, None], 0.0), axis=1
    )
    width_dp = model_width // dp_size
    width_mp = model_width // mp_size
    row0 = dp_index * width_dp
    silu_rows = lax.dynamic_slice_in_dim(silu_all, row0, width_dp, 1)
    mod_cols = lax.dynamic_slice_in_dim(mod_all, mp_index * width_mp, width_mp, 2)
    ada_grad = ein("id,ikc->dkc", silu_rows, mod_cols)
    ada_rows = lax.dynamic_slice_in_dim(ada_kinds, row0, width_dp, 1)
    silu_grad = ein("ikc,kdc->id", mod_all, ada_rows)
    cond_rows = lax.dynamic_slice_in_dim(cond_all, row0, width_dp, 1)
    silu_val, silu_pull = jax.vjp(jax.nn.silu, cond_rows)
    condition_low = silu_pull(silu_grad)[0].astype(bf16)
    time_grad = ein("in,id->nd", bin_hot, condition_low)
    class_grad = ein("in,id->nd", label_hot, condition_low)

    attend_one = halve(add_low(attend_one, attend_got_one), "dp", dp_bits[1][2:], 1)
    attend_zero = halve(add_low(attend_zero, attend_got_zero), "dp", dp_bits[0][2:], 1)
    mlp_grad = halve(add_low(mlp_zero, mlp_got), "mp", mp_bits[1:], 0)[0].astype(f32)
    attend_grad = add_low(attend_zero, swap(attend_one, "mp", mp_bits[0]))
    attend_grad = halve(attend_grad, "mp", mp_bits[1:], 0)[0].astype(f32)

    expand_grad = mlp_grad[:2].swapaxes(0, 1)
    down_grad = mlp_grad[2].T
    out_grad = attend_grad[:, 3 * local_dim :].T
    qkv_grad = lax.dot_general(
        attend_grad[:, : 3 * local_dim],
        jnp.array(places[: 3 * local_dim, None] == columns[: 3 * local_dim], f32),
        (((1,), (0,)), ((), ())),
        precision=lax.Precision.HIGHEST,
        preferred_element_type=f32,
    )
    qkv_grad = qkv_grad.reshape(-1, 3, local_dim)
    return (
        result.reshape(images, local_len, model_width),
        patch_grad,
        time_grad,
        class_grad,
        ada_grad,
        qkv_grad,
        gains_total,
        out_grad,
        expand_grad,
        down_grad,
    )


def solution(mesh):
    in_specs = (
        P("dp", "mp", None),
        P("dp", "mp", None),
        P("dp"),
        P("dp"),
        P(),
        P(),
        P(),
        P(),
        P(),
        P(None, None, "mp"),
        P(),
        P("mp", None),
        P(None, None, "mp"),
        P("mp", None),
    )
    out_specs = (
        P("dp", "mp", None),
        P("dp", "mp", None),
        P(None, "dp"),
        P(None, "dp"),
        P("dp", None, "mp"),
        P("dp", None, "mp"),
        P(),
        P("mp", "dp"),
        P("dp", None, "mp"),
        P("mp", "dp"),
    )
    return jax.shard_map(shards, mesh=mesh, in_specs=in_specs, out_specs=out_specs, check_vma=False)
```

```python
import functools
import math

import jax
import jax.numpy as jnp
import numpy as np
from jax import lax
from jax.experimental import pallas as pl
from jax.experimental.pallas import tpu as pltpu
from jax.sharding import PartitionSpec as P

GRID = 16
NCLS = 1000
NBINS = 16

epsilon = 1e-06
rope_base = 10000.0
f32 = jnp.float32
bf16 = jnp.bfloat16


def feature_order(head_dim):
    quarter = head_dim // 4
    firsts = list(range(quarter)) + list(range(2 * quarter, 3 * quarter))
    cut = len(firsts) // 8 * 8
    seconds = [i + quarter for i in firsts]
    return firsts[:cut] + seconds[:cut] + firsts[cut:] + seconds[cut:], cut


def rope_tables(position, head_dim):
    quarter = head_dim // 4
    order, cut = feature_order(head_dim)
    places = jnp.stack([position // GRID, position % GRID]).astype(f32)
    frequency = rope_base ** (-jnp.arange(quarter).astype(f32) / quarter)
    angle = (frequency[None, :, None] * places[:, None, :]).reshape(2 * quarter, -1)
    cosine, sine = jnp.cos(angle), jnp.sin(angle)
    cos_tab = jnp.concatenate([cosine[:cut], cosine[:cut], cosine[cut:], cosine[cut:]])
    sin_tab = jnp.concatenate([-sine[:cut], sine[:cut], -sine[cut:], sine[cut:]])
    return cos_tab, sin_tab


def partner(values, cut):
    rest = values[2 * cut :]
    half = rest.shape[0] // 2
    return jnp.concatenate(
        [values[cut : 2 * cut], values[:cut], pltpu.roll(rest, half, 0)], axis=0
    )


def head_scale(values):
    return lax.rsqrt(jnp.mean(values * values, axis=0, keepdims=True) + epsilon)


def dot_00(a, b):
    return lax.dot_general(a, b, (((0,), (0,)), ((), ())), preferred_element_type=f32)


def dot_11(a, b):
    return lax.dot_general(a, b, (((1,), (1,)), ((), ())), preferred_element_type=f32)


def dot_10(a, b):
    return lax.dot_general(a, b, (((1,), (0,)), ((), ())), preferred_element_type=f32)


def softmax_first(scores):
    shifted = jnp.exp(scores - jnp.max(scores, axis=0, keepdims=True))
    return shifted * (1.0 / jnp.sum(shifted, axis=0, keepdims=True))


def lasting(microseconds):
    return pl.CostEstimate(
        flops=int(microseconds * 1.1e9), bytes_accessed=1 << 20, transcendentals=0
    )


SHIFT_ONE, SCALE_ONE, GATE_ONE, SHIFT_TWO, SCALE_TWO, GATE_TWO, WEIGHT = range(7)


def row_of(mods, which):
    return mods[which : which + 1, :]


def rms(values):
    scale = lax.rsqrt(jnp.mean(values * values, -1, keepdims=True) + epsilon)
    return values * scale, scale


def rms_back(grad, unit, scale, scaling):
    grad = grad * (1.0 + scaling)
    return scale * (grad - unit * jnp.mean(grad * unit, -1, keepdims=True))


def row_sum(values):
    return jnp.sum(values, axis=0, keepdims=True)


def put_rows(sums_ref, image, rows):
    for which in range(sums_ref.shape[1]):
        value = rows.get(which, jnp.zeros((1, sums_ref.shape[2]), f32))
        sums_ref[image, which : which + 1, :] = value


def chunk_rows(ref, image):
    return jnp.concatenate([ref[chunk, image] for chunk in range(ref.shape[0])], axis=0)


def put_chunks(ref, image, values):
    size = ref.shape[2]
    for chunk in range(ref.shape[0]):
        ref[chunk, image] = values[chunk * size : (chunk + 1) * size]


def attend_kernel(
    latent_ref, mods_ref, w_ref, wo_ref, gains_ref, cos_ref, sin_ref,
    proj_ref, att_ref, branch_ref, xt_ref, middle_ref, two_ref, twot_ref, x_ref,
):
    own = mods_ref.shape[0]
    head_dim = gains_ref.shape[1]
    rows_all = att_ref.shape[1]
    length = xt_ref.shape[1] // own
    heads = range(rows_all // head_dim)
    cut = feature_order(head_dim)[1]
    group = pl.program_id(0)

    def place(image):
        return pl.ds(pl.multiple_of(image * length, length), length)

    @pl.when(group == 0)
    def _():
        def entry(image, carry):
            mods = mods_ref[image]
            unit = rms(chunk_rows(latent_ref, image).astype(f32))[0]
            x = (unit * (1.0 + row_of(mods, SCALE_ONE)) + row_of(mods, SHIFT_ONE)).astype(bf16)
            x_ref[place(image), :] = x
            xt_ref[:, place(image)] = x.T
            return carry

        lax.fori_loop(0, own, entry, 0)

    proj_ref[0] = dot_11(w_ref[0, : 3 * rows_all], x_ref[...])

    def heads_of(image, carry):
        tokens = place(image)
        cos_tab, sin_tab = cos_ref[...], sin_ref[...]
        lows = [[], [], []]
        for kind in range(2):
            for head in heads:
                start = kind * rows_all + head * head_dim
                raw = proj_ref[0, start : start + head_dim, tokens]
                scaled = raw * head_scale(raw) * gains_ref[kind]
                turned = scaled * cos_tab + partner(scaled, cut) * sin_tab
                lows[kind].append(turned.astype(bf16))
        for head in heads:
            start = 2 * rows_all + head * head_dim
            lows[2].append(proj_ref[0, start : start + head_dim, tokens].astype(bf16))
        scores = [dot_00(lows[1][head], lows[0][head]) for head in heads]
        probs = [softmax_first(score).astype(bf16) for score in scores]
        outs = [dot_10(lows[2][head], probs[head]) for head in heads]
        att_ref[group, :, tokens] = jnp.concatenate(outs, axis=0).astype(bf16)
        return carry

    lax.fori_loop(0, own, heads_of, 0, unroll=True)

    @pl.when(group == pl.num_programs(0) - 1)
    def _():
        groups = att_ref.shape[0]

        def leave(image, carry):
            tokens = place(image)
            mods = mods_ref[image]
            att = att_ref[:, :, tokens].reshape(groups * rows_all, length)
            branch = dot_00(att, wo_ref[...].reshape(groups * rows_all, -1))
            branch_ref[tokens, :] = branch.astype(bf16)
            latent = chunk_rows(latent_ref, image).astype(f32)
            middle = latent + row_of(mods, GATE_ONE) * branch
            middle_ref[tokens, :] = middle
            two = rms(middle)[0] * (1.0 + row_of(mods, SCALE_TWO)) + row_of(mods, SHIFT_TWO)
            two = two.astype(bf16)
            two_ref[tokens, :] = two
            twot_ref[:, tokens] = two.T
            return carry

        lax.fori_loop(0, own, leave, 0)


def attend_back_kernel(
    latent_ref, proj_ref, low_ref, w_ref, gains_ref, cos_ref, sin_ref, grad_ref, mods_ref,
    out_ref, gain_grad_ref, sums_ref, chunks_ref, cot_ref,
):
    own = mods_ref.shape[0]
    head_dim = gains_ref.shape[1]
    rows_all, tokens_all = proj_ref.shape[1] // 3, proj_ref.shape[2]
    length = tokens_all // own
    heads = range(rows_all // head_dim)
    cut = feature_order(head_dim)[1]
    group = pl.program_id(0)

    def place(image):
        return pl.ds(pl.multiple_of(image * length, length), length)

    @pl.when(group == 0)
    def _():
        gain_grad_ref[...] = jnp.zeros_like(gain_grad_ref)

    cot_ref[...] = dot_11(w_ref[group, 3 * rows_all :], low_ref[...])

    def heads_of(image, carry):
        tokens = place(image)
        cos_tab, sin_tab = cos_ref[...], sin_ref[...]
        lows, units, scales = [[], [], []], [[], []], [[], []]
        for kind in range(2):
            for head in heads:
                start = kind * rows_all + head * head_dim
                raw = proj_ref[0, start : start + head_dim, tokens]
                scale = head_scale(raw)
                unit = raw * scale
                scaled = unit * gains_ref[kind]
                turned = scaled * cos_tab + partner(scaled, cut) * sin_tab
                lows[kind].append(turned.astype(bf16))
                units[kind].append(unit)
                scales[kind].append(scale)
        cots = []
        for head in heads:
            start = 2 * rows_all + head * head_dim
            lows[2].append(proj_ref[0, start : start + head_dim, tokens].astype(bf16))
            cots.append(cot_ref[head * head_dim : (head + 1) * head_dim, tokens].astype(bf16))
        scores = [dot_00(lows[1][head], lows[0][head]) for head in heads]
        prob_grads = [dot_00(lows[2][head], cots[head]) for head in heads]
        probs = [softmax_first(score) for score in scores]
        outs = [[], [], []]
        outs[2] = [dot_11(cots[head], probs[head].astype(bf16)) for head in heads]
        score_lows = []
        for head in heads:
            mean = jnp.sum(probs[head] * prob_grads[head], axis=0, keepdims=True)
            score_lows.append((probs[head] * (prob_grads[head] - mean)).astype(bf16))
        turned_grads = [
            [dot_10(lows[1][head], score_lows[head]) for head in heads],
            [dot_11(lows[0][head], score_lows[head]) for head in heads],
        ]
        for kind in range(2):
            total = 0.0
            for head in heads:
                grad, unit = turned_grads[kind][head], units[kind][head]
                grad = grad * cos_tab + partner(grad * sin_tab, cut)
                total = total + grad * unit
                grad = grad * gains_ref[kind]
                along = jnp.mean(grad * unit, axis=0, keepdims=True)
                outs[kind].append(scales[kind][head] * (grad - unit * along))
            gain_grad_ref[kind] += total
        grads = jnp.concatenate(outs[0] + outs[1] + outs[2], axis=0).astype(bf16)
        out_ref[group, :, tokens] = grads
        return carry

    lax.fori_loop(0, own, heads_of, 0, unroll=True)

    @pl.when(group == pl.num_programs(0) - 1)
    def _():
        def leave(image, carry):
            tokens = place(image)
            mods = mods_ref[image]
            grad = 0.0
            for other in range(out_ref.shape[0]):
                grad = grad + dot_00(out_ref[other, :, tokens], w_ref[other, : 3 * rows_all])
            unit, scale = rms(chunk_rows(latent_ref, image).astype(f32))
            sums = {SHIFT_ONE: row_sum(grad), SCALE_ONE: row_sum(grad * unit)}
            put_rows(sums_ref, image, sums)
            grad = grad_ref[tokens, :] + rms_back(grad, unit, scale, row_of(mods, SCALE_ONE))
            put_chunks(chunks_ref, image, grad.astype(bf16))
            return carry

        lax.fori_loop(0, own, leave, 0)


def whole_spec(shape):
    return pl.BlockSpec(shape, lambda g: (0,) * len(shape), pipeline_mode=pl.Buffered(1))


def attend(latent, mods, weights, gains, tables):
    groups, rows, width = weights.shape[0], weights.shape[1] // 4, weights.shape[2]
    own = mods.shape[0]
    length, head_dim = tables[0].shape[1], gains.shape[1]
    tokens = own * length
    total, turned = (tokens, width), (width, tokens)
    const = lambda shape: pl.BlockSpec(shape, lambda g: (0,) * len(shape))
    return pl.pallas_call(
        attend_kernel,
        grid=(groups,),
        in_specs=[
            whole_spec(latent.shape),
            whole_spec(mods.shape),
            pl.BlockSpec((1, 4 * rows, width), lambda g: (g, 0, 0)),
            pl.BlockSpec((groups, rows, width), lambda g: (0, 3, 0), pipeline_mode=pl.Buffered(1)),
            whole_spec(gains.shape),
            whole_spec(tables[0].shape),
            whole_spec(tables[0].shape),
        ],
        out_specs=[
            pl.BlockSpec((1, 3 * rows, tokens), lambda g: (g, 0, 0)),
            const((groups, rows, tokens)),
            const(total),
            const(turned),
            const(total),
            const(total),
            const(turned),
        ],
        out_shape=[
            jax.ShapeDtypeStruct((groups, 3 * rows, tokens), f32),
            jax.ShapeDtypeStruct((groups, rows, tokens), bf16),
            jax.ShapeDtypeStruct(total, bf16),
            jax.ShapeDtypeStruct(turned, bf16),
            jax.ShapeDtypeStruct(total, f32),
            jax.ShapeDtypeStruct(total, bf16),
            jax.ShapeDtypeStruct(turned, bf16),
        ],
        scratch_shapes=[pltpu.VMEM(total, bf16)],
        compiler_params=pltpu.CompilerParams(vmem_limit_bytes=62 << 20),
        cost_estimate=lasting(160),
        name="attend",
    )(latent, mods, weights, weights, gains, *tables)


def attend_back(latent, proj, low, weights, gains, tables, grad, mods):
    groups, rows, width = weights.shape[0], weights.shape[1] // 4, weights.shape[2]
    own = mods.shape[0]
    tokens = low.shape[0]
    length, head_dim = tokens // own, gains.shape[1]
    const = lambda shape: pl.BlockSpec(shape, lambda g: (0,) * len(shape))
    gain_shape = (2, head_dim, length)
    return pl.pallas_call(
        attend_back_kernel,
        grid=(groups,),
        in_specs=[
            whole_spec(latent.shape),
            pl.BlockSpec((1, 3 * rows, tokens), lambda g: (g, 0, 0)),
            whole_spec(low.shape),
            whole_spec(weights.shape),
            whole_spec(gains.shape),
            whole_spec(tables[0].shape),
            whole_spec(tables[0].shape),
            whole_spec(grad.shape),
            whole_spec(mods.shape),
        ],
        out_specs=[const(proj.shape), const(gain_shape), const(mods.shape), const(latent.shape)],
        out_shape=[
            jax.ShapeDtypeStruct(proj.shape, bf16),
            jax.ShapeDtypeStruct(gain_shape, f32),
            jax.ShapeDtypeStruct(mods.shape, f32),
            jax.ShapeDtypeStruct(latent.shape, bf16),
        ],
        scratch_shapes=[pltpu.VMEM((rows, tokens), f32)],
        compiler_params=pltpu.CompilerParams(vmem_limit_bytes=62 << 20),
        cost_estimate=lasting(160),
        name="attend_back",
    )(latent, proj, low, weights, gains, *tables, grad, mods)


def finish_kernel(
    branch_ref, middle_ref, cot_ref, mods_ref, low_ref, lowt_ref, chunks_ref, sums_ref
):
    branch, mods = branch_ref[...], mods_ref[0]
    gate = row_of(mods, GATE_TWO)
    result = (middle_ref[...] + gate * branch).astype(bf16)
    put_chunks(chunks_ref, 0, result)
    cot = chunk_rows(cot_ref, 0).astype(f32) * row_of(mods, WEIGHT)
    low = (gate * cot).astype(bf16)
    low_ref[...] = low
    lowt_ref[...] = low.T
    put_rows(sums_ref, 0, {GATE_TWO: row_sum(cot * branch)})


def middle_kernel(
    one_ref, other_ref, middle_ref, branch_ref, cot_ref, mods_ref,
    grad_ref, low_ref, lowt_ref, sums_ref,
):
    mods = mods_ref[0]
    grad = one_ref[...] + other_ref[...]
    unit, scale = rms(middle_ref[...])
    sums = {SHIFT_TWO: row_sum(grad), SCALE_TWO: row_sum(grad * unit)}
    cot = chunk_rows(cot_ref, 0).astype(f32) * row_of(mods, WEIGHT)
    grad = cot + rms_back(grad, unit, scale, row_of(mods, SCALE_TWO))
    grad_ref[...] = grad
    low = (row_of(mods, GATE_ONE) * grad).astype(bf16)
    low_ref[...] = low
    lowt_ref[...] = low.T
    sums[GATE_ONE] = row_sum(grad * branch_ref[...].astype(f32))
    put_rows(sums_ref, 0, sums)


def by_image(kernel, name, microseconds, rows, chunks, mods, outs):
    own, sums, width = mods.shape
    tokens = rows[0].shape[0]
    length = tokens // own
    block = pl.BlockSpec((length, width), lambda i: (i, 0))
    turned = pl.BlockSpec((width, length), lambda i: (0, i))
    chunk = pl.BlockSpec((chunks.shape[0], 1) + chunks.shape[2:], lambda i: (0, i, 0, 0))
    whole = pl.BlockSpec((1, sums, width), lambda i: (i, 0, 0))
    specs, shapes = [], []
    for out in outs:
        if out is True:
            specs.append(turned)
            shapes.append(jax.ShapeDtypeStruct((width, tokens), bf16))
        elif out is False:
            specs.append(chunk)
            shapes.append(jax.ShapeDtypeStruct(chunks.shape, bf16))
        else:
            specs.append(block)
            shapes.append(jax.ShapeDtypeStruct((tokens, width), out))
    return pl.pallas_call(
        kernel,
        grid=(own,),
        in_specs=[block] * len(rows) + [chunk, whole],
        out_specs=specs + [whole],
        out_shape=shapes + [jax.ShapeDtypeStruct(mods.shape, f32)],
        compiler_params=pltpu.CompilerParams(vmem_limit_bytes=48 << 20),
        cost_estimate=lasting(microseconds),
        name=name,
    )(*rows, chunks, mods)


def modulate_kernel(silu_ref, ada_ref, out_ref):
    out_ref[0] = dot_10(silu_ref[...], ada_ref[0])


def modulate(silu, ada):
    kinds, width = ada.shape[:2]
    return pl.pallas_call(
        modulate_kernel,
        grid=(kinds,),
        in_specs=[
            pl.BlockSpec(silu.shape, lambda k: (0, 0)),
            pl.BlockSpec((1, width, width), lambda k: (k, 0, 0)),
        ],
        out_specs=pl.BlockSpec((1,) + silu.shape, lambda k: (k, 0, 0)),
        out_shape=jax.ShapeDtypeStruct((kinds,) + silu.shape, f32),
        compiler_params=pltpu.CompilerParams(vmem_limit_bytes=32 << 20),
        cost_estimate=lasting(60),
        name="modulate",
    )(silu, ada)


def add_rows(out_ref, part, first, index, length):
    rows = pl.ds(pl.multiple_of(index * length, length), length)

    @pl.when(first)
    def _():
        out_ref[rows, :] = part

    @pl.when(jnp.logical_not(first))
    def _():
        out_ref[rows, :] += part


def sigmoid(values):
    return 1.0 / (1.0 + jnp.exp(-values))


def mlp_kernel(count, e_ref, x_ref, *refs):
    first = pl.program_id(0) == 0
    save_ref, out_ref, w_ref = refs[count:]
    unit = min(ref.shape[2] for ref in refs[:count])
    for index, ref in enumerate(refs[:count]):
        rows = pl.ds(pl.multiple_of(e_ref[index] * unit, unit), ref.shape[2])
        for kind in range(3):
            w_ref[0, kind, rows, :] = ref[0, kind]
    x = x_ref[...]
    gate = dot_11(x, w_ref[0, 0])
    up = dot_11(x, w_ref[0, 1])
    save_ref[0, 0] = gate.astype(bf16)
    save_ref[0, 1] = up.astype(bf16)
    hidden = (gate * sigmoid(gate) * up).astype(bf16)
    part = dot_10(hidden, w_ref[0, 2])
    add_rows(out_ref, part, first, 0, x.shape[0])


def mlp(x, order, pieces):
    groups, _, _, width = pieces[0].shape
    units, tokens = sum(piece.shape[2] for piece in pieces), x.shape[0]
    return pl.pallas_call(
        functools.partial(mlp_kernel, len(pieces)),
        grid_spec=pltpu.PrefetchScalarGridSpec(
            num_scalar_prefetch=1,
            grid=(groups,),
            in_specs=[pl.BlockSpec((tokens, width), lambda g, e: (0, 0), pipeline_mode=pl.Buffered(1))]
            + [pl.BlockSpec((1,) + piece.shape[1:], lambda g, e: (g, 0, 0, 0)) for piece in pieces],
            out_specs=[
                pl.BlockSpec((1, 2, tokens, units), lambda g, e: (g, 0, 0, 0)),
                pl.BlockSpec((tokens, width), lambda g, e: (0, 0)),
                pl.BlockSpec((1, 3, units, width), lambda g, e: (g, 0, 0, 0)),
            ],
        ),
        out_shape=[
            jax.ShapeDtypeStruct((groups, 2, tokens, units), bf16),
            jax.ShapeDtypeStruct((tokens, width), f32),
            jax.ShapeDtypeStruct((groups, 3, units, width), bf16),
        ],
        compiler_params=pltpu.CompilerParams(vmem_limit_bytes=62 << 20),
        cost_estimate=lasting(120),
        name="mlp",
    )(order, x, *pieces)


def fill_rows(order_ref, source_ref, target_ref, base=0):
    blocks, rows = source_ref.shape[0], source_ref.shape[1]
    for place in range(blocks):
        target_ref[place * rows : (place + 1) * rows, :] = source_ref[order_ref[base + place]]


def mlp_back_kernel(
    e_ref, xt_ref, lowt_ref, low_ref, save_ref, w_ref,
    keep_ref, send_ref, two_ref, xs, lows, parts,
):
    first = pl.program_id(0) == 0
    tokens, width = low_ref.shape
    step = math.gcd(tokens, 512)

    @pl.when(first)
    def _():
        fill_rows(e_ref, xt_ref, xs)
        fill_rows(e_ref, lowt_ref, lows)

    for index in range(tokens // step):
        rows = pl.ds(index * step, step)
        hidden_grad = dot_11(low_ref[rows, :], w_ref[0, 2])
        gate = save_ref[0, 0, rows, :].astype(f32)
        up = save_ref[0, 1, rows, :].astype(f32)
        sig = sigmoid(gate)
        swish = gate * sig
        gate_low = (hidden_grad * up * (sig + swish * (1.0 - sig))).astype(bf16)
        up_low = (hidden_grad * swish).astype(bf16)
        parts[0, rows, :] = gate_low
        parts[1, rows, :] = up_low
        parts[2, rows, :] = (swish * up).astype(bf16)
        part = dot_10(gate_low, w_ref[0, 0]) + dot_10(up_low, w_ref[0, 1])
        add_rows(two_ref, part, first, index, step)

    half = width // 2
    for out_ref, rows in ((keep_ref, slice(0, half)), (send_ref, slice(half, width))):
        x_rows = xs[rows, :]
        for kind in range(2):
            out_ref[0, kind] = dot_10(x_rows, parts[kind]).astype(bf16)
        out_ref[0, 2] = dot_10(lows[rows, :], parts[2]).astype(bf16)


def mlp_back(which, e_order, xt, lowt, low, save, weights):
    groups, _, units, width = weights.shape
    tokens = low.shape[0]
    blocks = groups // 2
    base = which * blocks
    once = pl.Buffered(1)
    whole = lambda p, e: (0, 0)
    whole3 = lambda p, e: (0, 0, 0)
    half = jax.ShapeDtypeStruct((blocks, 3, width // 2, units), bf16)
    half_spec = pl.BlockSpec((1, 3, width // 2, units), lambda p, e: (p, 0, 0, 0))
    return pl.pallas_call(
        mlp_back_kernel,
        grid_spec=pltpu.PrefetchScalarGridSpec(
            num_scalar_prefetch=1,
            grid=(blocks,),
            in_specs=[
                pl.BlockSpec(xt.shape, whole3, pipeline_mode=once),
                pl.BlockSpec(lowt.shape, whole3, pipeline_mode=once),
                pl.BlockSpec((tokens, width), whole, pipeline_mode=once),
                pl.BlockSpec((1, 2, tokens, units), lambda p, e: (base + p, 0, 0, 0)),
                pl.BlockSpec((1, 3, units, width), lambda p, e: (base + p, 0, 0, 0)),
            ],
            out_specs=[half_spec, half_spec, pl.BlockSpec((tokens, width), whole)],
            scratch_shapes=[
                pltpu.VMEM((width, tokens), bf16),
                pltpu.VMEM((width, tokens), bf16),
                pltpu.VMEM((3, tokens, units), bf16),
            ],
        ),
        out_shape=[half, half, jax.ShapeDtypeStruct((tokens, width), f32)],
        compiler_params=pltpu.CompilerParams(vmem_limit_bytes=62 << 20),
        cost_estimate=lasting(150),
        name="mlp_back",
    )(e_order, xt, lowt, low, save, weights)


def attend_grads_kernel(
    m_ref, e_ref, xt_ref, lowt_ref, proj_ref, att_ref, keep_ref, send_ref, xs, lows
):
    first = pl.num_programs(0) // 2 == pl.program_id(0)
    base = jnp.where(first, xt_ref.shape[0], 0)

    @pl.when(first | (pl.program_id(0) == 0))
    def _():
        fill_rows(e_ref, xt_ref, xs, base)
        fill_rows(e_ref, lowt_ref, lows, base)

    width = xs.shape[0]
    half = width // 2
    columns = proj_ref.shape[1]

    for out_ref, rows in ((keep_ref, slice(0, half)), (send_ref, slice(half, width))):
        out_ref[0, :, :columns] = dot_11(xs[rows, :], proj_ref[0]).astype(bf16)
        out_ref[0, :, columns:] = dot_11(lows[rows, :], att_ref[0]).astype(bf16)


def attend_grads(m_order, e_orders, xt, lowt, proj, att):
    rows, tokens = att.shape[1:]
    width = xt.shape[0] * xt.shape[1]
    blocks = m_order.shape[0]
    whole3 = lambda p, m, e: (0, 0, 0)
    half = jax.ShapeDtypeStruct((blocks, width // 2, 4 * rows), bf16)
    half_spec = pl.BlockSpec((1, width // 2, 4 * rows), lambda p, m, e: (p, 0, 0))
    return pl.pallas_call(
        attend_grads_kernel,
        grid_spec=pltpu.PrefetchScalarGridSpec(
            num_scalar_prefetch=2,
            grid=(blocks,),
            in_specs=[
                pl.BlockSpec(xt.shape, whole3, pipeline_mode=pl.Buffered(1)),
                pl.BlockSpec(lowt.shape, whole3, pipeline_mode=pl.Buffered(1)),
                pl.BlockSpec((1, 3 * rows, tokens), lambda p, m, e: (m[p], 0, 0)),
                pl.BlockSpec((1, rows, tokens), lambda p, m, e: (m[p], 0, 0)),
            ],
            out_specs=[half_spec, half_spec],
            scratch_shapes=[
                pltpu.VMEM((width, tokens), bf16),
                pltpu.VMEM((width, tokens), bf16),
            ],
        ),
        out_shape=[half, half],
        compiler_params=pltpu.CompilerParams(vmem_limit_bytes=56 << 20),
        cost_estimate=lasting(200),
        name="attend_grads",
    )(m_order, e_orders, xt, lowt, proj, att)


def dot(a, b):
    return jnp.dot(a, b, preferred_element_type=f32)


def ein(spec, a, b):
    return jnp.einsum(spec, a, b, preferred_element_type=f32)


def gather_pieces(piece, mp_size):
    whole = lax.all_gather(piece, ("mp", "dp"), axis=0, tiled=False)
    return whole.reshape((mp_size, -1) + piece.shape)


def take_rows(values, index):
    return jnp.take(values, index, axis=0, mode="clip")


def bits_of(size):
    return [1 << i for i in range(size.bit_length() - 1)]


def swap(values, axis, bit):
    size = lax.axis_size(axis)
    return lax.ppermute(values, axis, [(i, i ^ bit) for i in range(size)])


def xor_gather(values, axes_bits):
    names = sorted({axis for axis, _ in axes_bits})
    places = [{name: 0 for name in names}]
    values = values[None]
    for axis, bit in axes_bits:
        values = jnp.concatenate([values, swap(values, axis, bit)], axis=0)
        places = places + [dict(place, **{axis: place[axis] ^ bit}) for place in places]
    return values, {name: [place[name] for place in places] for name in names}


def halving_order(bits):
    order = [0]
    for bit in reversed(bits):
        order = order + [place ^ bit for place in order]
    return order


def add_low(kept, received):
    return (kept.astype(f32) + received.astype(f32)).astype(bf16)


def tie(*values):
    return lax.optimization_barrier(values)


def split(values, dim):
    size = values.shape[dim] // 2
    return (
        lax.slice_in_dim(values, 0, size, axis=dim),
        lax.slice_in_dim(values, size, 2 * size, axis=dim),
    )


def halve(values, axis, bits, dim):
    for bit in bits:
        kept, sent = split(values, dim)
        values = add_low(kept, swap(sent, axis, bit))
    return values


def shards(
    patches,
    cotangent,
    time_bins,
    labels,
    image_counts,
    dest_perm,
    time_table,
    class_table,
    ada_weight,
    qkv_weight,
    norm_gains,
    out_weight,
    expand_weight,
    down_weight,
):
    dp_size = lax.axis_size("dp")
    mp_size = lax.axis_size("mp")
    capacity = patches.shape[0]
    slot_count = capacity // dp_size
    images = cotangent.shape[0]
    local_len = patches.shape[1]
    model_width = patches.shape[2]
    length = local_len * mp_size
    head_dim = norm_gains.shape[1]
    local_dim = out_weight.shape[0]
    unit_count = down_weight.shape[0]
    own = images // mp_size
    total_images = images * dp_size
    order = np.array(feature_order(head_dim)[0])
    columns = np.arange(4 * local_dim)
    places = columns // head_dim * head_dim + order[columns % head_dim]
    places = np.where(columns < 2 * local_dim, places, columns).astype(np.int32)
    gains_f = norm_gains.astype(f32)[:, order]
    gains_f = (gains_f * jnp.array([[head_dim ** (-0.5)], [1.0]], f32))[:, :, None]
    dp_index = lax.axis_index("dp")
    mp_index = lax.axis_index("mp")
    dp_bits = bits_of(dp_size)
    dp_bits = (dp_bits, dp_bits[:1] + dp_bits[1:][::-1])
    mp_bits = bits_of(mp_size)

    tables = rope_tables(jnp.arange(length), head_dim)

    def turn(chunks):
        return lax.all_to_all(chunks, "mp", split_axis=0, concat_axis=0, tiled=True)

    starts = jnp.cumsum(image_counts) - image_counts
    finish = starts + image_counts
    my_start = starts[dp_index]
    my_count = image_counts[dp_index]
    device_ids = jnp.arange(dp_size)
    matches = (dest_perm[:, None] == device_ids[None, :]).astype(jnp.int32)
    inverse = jnp.sum(device_ids[:, None] * matches, axis=0)
    my_place = inverse[dp_index]
    pair_ids = jnp.arange(dp_size * slot_count)
    pair_peer = pair_ids // slot_count
    pair_slot = pair_ids % slot_count
    send_index = pair_slot * dp_size + jnp.mod(inverse[pair_peer] - my_start, dp_size)
    send_index = jnp.minimum(send_index, capacity - 1)
    send_patches = take_rows(patches, send_index)
    info, info_places = xor_gather(
        jnp.stack([time_bins, labels]), [("dp", bit) for bit in bits_of(dp_size)]
    )
    qkv_weight, out_weight, expand_weight, down_weight, send_patches, info = tie(
        qkv_weight, out_weight, expand_weight, down_weight, send_patches, info
    )
    share = 4 * local_dim // dp_size
    spots = lax.dynamic_slice_in_dim(jnp.array(places), dp_index * share, share, 0)
    take_qkv = (spots[:, None] == jnp.arange(3 * local_dim)[None, :]).astype(bf16)
    take_out = (spots[:, None] - 3 * local_dim == jnp.arange(local_dim)[None, :]).astype(bf16)
    attend_piece = dot(take_qkv, qkv_weight.transpose(1, 2, 0).reshape(-1, model_width))
    attend_piece = (attend_piece + dot(take_out, out_weight)).astype(bf16)
    share = unit_count // dp_size
    spots = dp_index * share + jnp.arange(share)
    take_units = (spots[:, None] == jnp.arange(unit_count)[None, :]).astype(bf16)
    mlp_piece = jnp.stack(
        [
            ein("rf,df->rd", take_units, expand_weight[:, 0]).astype(bf16),
            ein("rf,df->rd", take_units, expand_weight[:, 1]).astype(bf16),
            lax.dynamic_slice_in_dim(down_weight, dp_index * share, share, 0),
        ]
    )
    attend_full = gather_pieces(attend_piece, mp_size).reshape(mp_size, 4 * local_dim, -1)
    by_permutes = share % 32 == 0 and dp_size == 8 and mp_size == 4
    if by_permutes:
        mlp_near = mlp_piece[None]
        far_near = swap(mlp_near, "mp", 2)
    else:
        mlp_full = gather_pieces(mlp_piece, mp_size)
        mlp_full = mlp_full.swapaxes(1, 2).reshape(mp_size, 3, unit_count, model_width)
        mlp_pieces = [mlp_full[mp_index ^ jnp.array(halving_order(mp_bits))]]
        mlp_order = jnp.zeros((1,), jnp.int32)

    recv_patches = lax.all_to_all(send_patches, "dp", split_axis=0, concat_axis=0, tiled=True)
    info = info.swapaxes(0, 1).reshape(2, -1)
    info_owner = jnp.repeat(dp_index ^ jnp.array(info_places["dp"]), capacity)
    info_slot = jnp.tile(jnp.arange(capacity), dp_size)
    info_count = jnp.sum(
        jnp.where(info_owner[:, None] == device_ids[None, :], image_counts[None, :], 0), axis=1
    )
    live_all = info_slot < info_count
    bin_totals = jnp.sum(
        ((info[0][:, None] == jnp.arange(NBINS)[None, :]) & live_all[:, None]).astype(f32), axis=0
    )
    gather_bits = [("dp", bit) for bit in bits_of(dp_size)]
    gather_bits = gather_bits + [("mp", bit) for bit in bits_of(mp_size)[::-1]]
    spread = {"dp": [0], "mp": [0]}
    for axis, bit in gather_bits:
        spread = {
            name: spread[name] + [place ^ (bit if name == axis else 0) for place in spread[name]]
            for name in spread
        }
    owner_all = jnp.repeat(dp_index ^ jnp.array(spread["dp"]), own)
    group_all = jnp.repeat(mp_index ^ jnp.array(spread["mp"]), own)
    row_all = group_all * own + jnp.tile(jnp.arange(own), dp_size * mp_size)
    place_all = jnp.sum(
        jnp.where(owner_all[:, None] == device_ids[None, :], inverse[None, :], 0), axis=1
    )
    rank_all = row_all * dp_size + place_all
    source_all = jnp.sum((finish[None, :] <= rank_all[:, None]).astype(jnp.int32), axis=1)
    start_all = jnp.sum(
        jnp.where(source_all[:, None] == device_ids[None, :], starts[None, :], 0), axis=1
    )
    slots_all = source_all * capacity + rank_all - start_all
    slot_hit = slots_all[:, None] == (info_owner * capacity + info_slot)[None, :]
    bins_all = jnp.sum(jnp.where(slot_hit, info[0][None, :], 0), axis=1)
    labels_all = jnp.sum(jnp.where(slot_hit, info[1][None, :], 0), axis=1)
    bin_hot = (bins_all[:, None] == jnp.arange(NBINS)[None, :])
    label_hot = (labels_all[:, None] == jnp.arange(NCLS)[None, :])
    weights_all = total_images / (NBINS * jnp.sum(bin_hot.astype(f32) * bin_totals[None, :], axis=1))
    bin_hot = bin_hot.astype(bf16)
    label_hot = label_hot.astype(bf16)
    cond_all = (dot(bin_hot, time_table) + dot(label_hot, class_table)).astype(bf16).astype(f32)
    silu_all = jax.nn.silu(cond_all).astype(bf16)
    silu_cond = silu_all[:own]
    weights = weights_all[:own]

    if by_permutes:
        silu_cond, far_near = tie(silu_cond, far_near)
        mlp_near = jnp.concatenate([mlp_near, far_near], axis=0)
        far_near = swap(mlp_near, "mp", 1)
    ada_kinds = ada_weight.swapaxes(0, 1)
    modulation = modulate(jnp.pad(silu_cond, ((0, -own % 16), (0, 0))), ada_kinds)[:, :own]
    mods = jnp.concatenate(
        [
            modulation.swapaxes(0, 1),
            jnp.broadcast_to(weights[:, None, None], (own, 1, model_width)),
            jnp.zeros((own, 1, model_width), f32),
        ],
        axis=1,
    )
    if by_permutes:
        recv_patches, mods, far_near = tie(recv_patches, mods, far_near)
    else:
        recv_patches, mods = tie(recv_patches, mods)

    rank_ids = jnp.arange(images) * dp_size + my_place
    source = jnp.sum((finish[None, :] <= rank_ids[:, None]).astype(jnp.int32), axis=1)
    within = rank_ids - starts[source]
    recv_index = source * slot_count + within // dp_size
    latent = take_rows(recv_patches, recv_index).reshape(mp_size, own, local_len, model_width)
    latent = turn(latent)
    if by_permutes:
        mlp_near = jnp.concatenate([mlp_near, far_near], axis=0)
        halves = split(mlp_near, 2)
        orders = ((2, 4), (4, 2))
        parts = [{bit: swap(halves[half], "dp", bit) for bit in orders[half]} for half in range(2)]
        cored = swap(mlp_near, "dp", 1)
        latent, parts[0][2], parts[1][4], cored = tie(latent, parts[0][2], parts[1][4], cored)
        got = [swap(parts[half][orders[half][0]], "dp", orders[half][1]) for half in range(2)]

    cotangent, latent = tie(cotangent, latent)
    proj, attended, branch_one, normed_t, middle, two, two_t = attend(
        latent, mods, attend_full, gains_f, tables
    )
    cot = turn(cotangent.reshape(mp_size, own, local_len, model_width))
    if by_permutes:
        got[0], got[1], attended = tie(got[0], got[1], attended)
        mlp_pieces, mlp_order = [mlp_near, cored], [dp_index * 2, (dp_index ^ 1) * 2]
        for half in range(2):
            parts[half][6] = got[half]
            for near, part in parts[half].items():
                mlp_pieces += [part, swap(part, "dp", 1)]
                mlp_order += [(dp_index ^ near) * 2 + half, (dp_index ^ near ^ 1) * 2 + half]
        mlp_order = jnp.stack(mlp_order).astype(jnp.int32)
    two, cot = tie(two, cot)
    save, branch_two, mlp_full = mlp(two, mlp_order, mlp_pieces)
    down_low, down_t, result, sums_finish = by_image(
        finish_kernel, "finish", 30, (branch_two, middle), cot, mods, (bf16, True, False)
    )
    result = turn(result)

    e_orders = [(dp_index ^ jnp.array(halving_order(bits))).astype(jnp.int32) for bits in dp_bits]
    m_order = (mp_index ^ jnp.array(halving_order(mp_bits))).astype(jnp.int32)

    def by_owner(values):
        return values.reshape(dp_size, model_width // dp_size, -1)

    two_t, down_t = by_owner(two_t), by_owner(down_t)
    kept_one, sent_one, two_one = mlp_back(
        1, e_orders[1], two_t, down_t, down_low, save, mlp_full
    )
    got_one = swap(sent_one, "dp", dp_bits[1][0])
    kept_zero, sent_zero, two_zero = mlp_back(
        0, e_orders[0], two_t, down_t, down_low, save, mlp_full
    )
    got_zero = swap(sent_zero, "dp", dp_bits[0][0])
    kept_one, kept_zero = add_low(kept_one, got_one), add_low(kept_zero, got_zero)
    two_zero, kept_one, kept_zero = tie(two_zero, kept_one, kept_zero)
    kept_one, sent_one = split(kept_one, 2)
    kept_zero, sent_zero = split(kept_zero, 2)
    got_one = swap(sent_one, "dp", dp_bits[1][1])
    got_zero = swap(sent_zero, "dp", dp_bits[0][1])
    middle_grad, branch_low, branch_t, sums_middle = by_image(
        middle_kernel,
        "middle",
        1,
        (two_zero, two_one, middle, branch_one),
        cot,
        mods,
        (f32, bf16, True),
    )
    branch_low, result = tie(branch_low, result)
    projected_low, gains_grad, sums_entry, latent_back = attend_back(
        latent, proj, branch_low, attend_full, gains_f, tables, middle_grad, mods
    )
    gains_grad = jnp.sum(gains_grad, axis=2) * jnp.array([[head_dim ** (-0.5)], [1.0]], f32)
    projected_low, got_one, got_zero = tie(projected_low, got_one, got_zero)
    kept_one, kept_zero = add_low(kept_one, got_one), add_low(kept_zero, got_zero)
    normed_t, kept_one, kept_zero = tie(normed_t, kept_one, kept_zero)
    kept_one, sent_one = split(kept_one, 2)
    kept_zero, sent_zero = split(kept_zero, 2)
    got_one = swap(sent_one, "dp", dp_bits[1][2])
    got_zero = swap(sent_zero, "dp", dp_bits[0][2])
    latent_back = turn(latent_back)

    normed_t, branch_t = by_owner(normed_t), by_owner(branch_t)

    attend_kept, attend_sent = attend_grads(
        m_order, jnp.concatenate(e_orders), normed_t, branch_t, projected_low, attended
    )
    attend_got = swap(attend_sent, "dp", dp_bits[0][0])
    attend_kept, got_one, got_zero = tie(attend_kept, got_one, got_zero)

    packed = sums_finish + sums_middle + sums_entry
    gains_row = jnp.pad(gains_grad.reshape(1, 1, -1), ((0, own - 1), (7, 0), (0, model_width - 2 * head_dim)))
    packed = jnp.where(jnp.arange(8)[:, None] == 7, gains_row, packed).astype(bf16)
    packed = packed[None]
    got_packed = swap(packed, *gather_bits[0])

    def more(after):
        nonlocal packed, got_packed, stage
        after, got_packed = tie(after, got_packed)
        packed = jnp.concatenate([packed, got_packed], axis=0)
        stage += 1
        if stage < len(gather_bits):
            got_packed = swap(packed, *gather_bits[stage])
        return after

    stage = 0
    attend_kept = more(attend_kept)
    attend_sum = more(add_low(attend_kept, attend_got))
    mlp_one = halve(add_low(kept_one, got_one), "dp", dp_bits[1][3:], 2)
    mlp_zero = halve(add_low(kept_zero, got_zero), "dp", dp_bits[0][3:], 2)
    mlp_one = more(mlp_one)
    attend_zero, attend_one = split(attend_sum, 0)
    latent_back, attend_one, attend_zero = tie(latent_back, attend_one, attend_zero)
    attend_one, sent_one = split(attend_one, 1)
    attend_zero, sent_zero = split(attend_zero, 1)
    attend_got_one = swap(sent_one, "dp", dp_bits[1][1])
    attend_got_zero = swap(sent_zero, "dp", dp_bits[0][1])
    mlp_got = swap(mlp_one, "mp", mp_bits[0])

    back_within = pair_slot * dp_size + jnp.mod(my_place - starts[pair_peer], dp_size)
    back_valid = back_within < image_counts[pair_peer]
    back_slot = jnp.clip((starts[pair_peer] + back_within - my_place) // dp_size, 0, images - 1)
    back_slot = jnp.where(back_valid, back_slot, images)
    empty = jnp.zeros((1, local_len, model_width), bf16)
    latent_back = latent_back.reshape(images, local_len, model_width)
    latent_back = jnp.concatenate([latent_back, empty], axis=0)
    back_patches = take_rows(latent_back, back_slot)

    got_patches = lax.all_to_all(back_patches, "dp", split_axis=0, concat_axis=0, tiled=True)
    slot_ids = jnp.arange(capacity)
    home_peer = dest_perm[jnp.mod(my_start + slot_ids, dp_size)]
    home_index = home_peer * slot_count + jnp.minimum(slot_ids // dp_size, slot_count - 1)
    patch_grad = take_rows(got_patches, home_index)

    while stage < len(gather_bits):
        mlp_zero = more(mlp_zero)
    packed = packed.reshape(total_images, 8, model_width)
    mod_all = packed[:, :6]
    gains_total = packed.reshape(-1, own, 8, model_width)[:, 0, 7, : 2 * head_dim]
    gains_total = jnp.sum(gains_total.astype(f32), axis=0).reshape(2, head_dim)
    gains_total = jnp.sum(
        jnp.where(order[:, None] == jnp.arange(head_dim)[None, :], gains_total[:, :, None], 0.0), axis=1
    )
    width_dp = model_width // dp_size
    width_mp = model_width // mp_size
    row0 = dp_index * width_dp
    silu_rows = lax.dynamic_slice_in_dim(silu_all, row0, width_dp, 1)
    mod_cols = lax.dynamic_slice_in_dim(mod_all, mp_index * width_mp, width_mp, 2)
    ada_grad = ein("id,ikc->dkc", silu_rows, mod_cols)
    ada_rows = lax.dynamic_slice_in_dim(ada_kinds, row0, width_dp, 1)
    silu_grad = ein("ikc,kdc->id", mod_all, ada_rows)
    cond_rows = lax.dynamic_slice_in_dim(cond_all, row0, width_dp, 1)
    silu_val, silu_pull = jax.vjp(jax.nn.silu, cond_rows)
    condition_low = silu_pull(silu_grad)[0].astype(bf16)
    time_grad = ein("in,id->nd", bin_hot, condition_low)
    class_grad = ein("in,id->nd", label_hot, condition_low)

    attend_one = halve(add_low(attend_one, attend_got_one), "dp", dp_bits[1][2:], 1)
    attend_zero = halve(add_low(attend_zero, attend_got_zero), "dp", dp_bits[0][2:], 1)
    mlp_grad = halve(add_low(mlp_zero, mlp_got), "mp", mp_bits[1:], 0)[0].astype(f32)
    attend_grad = add_low(attend_zero, swap(attend_one, "mp", mp_bits[0]))
    attend_grad = halve(attend_grad, "mp", mp_bits[1:], 0)[0].astype(f32)

    expand_grad = mlp_grad[:2].swapaxes(0, 1)
    down_grad = mlp_grad[2].T
    out_grad = attend_grad[:, 3 * local_dim :].T
    qkv_grad = lax.dot_general(
        attend_grad[:, : 3 * local_dim],
        jnp.array(places[: 3 * local_dim, None] == columns[: 3 * local_dim], f32),
        (((1,), (0,)), ((), ())),
        precision=lax.Precision.HIGHEST,
        preferred_element_type=f32,
    )
    qkv_grad = qkv_grad.reshape(-1, 3, local_dim)
    return (
        result.reshape(images, local_len, model_width),
        patch_grad,
        time_grad,
        class_grad,
        ada_grad,
        qkv_grad,
        gains_total,
        out_grad,
        expand_grad,
        down_grad,
    )


def solution(mesh):
    in_specs = (
        P("dp", "mp", None),
        P("dp", "mp", None),
        P("dp"),
        P("dp"),
        P(),
        P(),
        P(),
        P(),
        P(),
        P(None, None, "mp"),
        P(),
        P("mp", None),
        P(None, None, "mp"),
        P("mp", None),
    )
    out_specs = (
        P("dp", "mp", None),
        P("dp", "mp", None),
        P(None, "dp"),
        P(None, "dp"),
        P("dp", None, "mp"),
        P("dp", None, "mp"),
        P(),
        P("mp", "dp"),
        P("dp", None, "mp"),
        P("mp", "dp"),
    )
    return jax.shard_map(shards, mesh=mesh, in_specs=in_specs, out_specs=out_specs, check_vma=False)
```

```python
import functools
import math

import jax
import jax.numpy as jnp
import numpy as np
from jax import lax
from jax.experimental import pallas as pl
from jax.experimental.pallas import tpu as pltpu
from jax.sharding import PartitionSpec as P

GRID = 16
NCLS = 1000
NBINS = 16

epsilon = 1e-06
rope_base = 10000.0
f32 = jnp.float32
bf16 = jnp.bfloat16


def feature_order(head_dim):
    quarter = head_dim // 4
    firsts = list(range(quarter)) + list(range(2 * quarter, 3 * quarter))
    cut = len(firsts) // 8 * 8
    seconds = [i + quarter for i in firsts]
    return firsts[:cut] + seconds[:cut] + firsts[cut:] + seconds[cut:], cut


def rope_tables(position, head_dim):
    quarter = head_dim // 4
    order, cut = feature_order(head_dim)
    places = jnp.stack([position // GRID, position % GRID]).astype(f32)
    frequency = rope_base ** (-jnp.arange(quarter).astype(f32) / quarter)
    angle = (frequency[None, :, None] * places[:, None, :]).reshape(2 * quarter, -1)
    cosine, sine = jnp.cos(angle), jnp.sin(angle)
    cos_tab = jnp.concatenate([cosine[:cut], cosine[:cut], cosine[cut:], cosine[cut:]])
    sin_tab = jnp.concatenate([-sine[:cut], sine[:cut], -sine[cut:], sine[cut:]])
    return cos_tab, sin_tab


def partner(values, cut):
    rest = values[2 * cut :]
    half = rest.shape[0] // 2
    return jnp.concatenate(
        [values[cut : 2 * cut], values[:cut], pltpu.roll(rest, half, 0)], axis=0
    )


def head_scale(values):
    return lax.rsqrt(jnp.mean(values * values, axis=0, keepdims=True) + epsilon)


def dot_00(a, b):
    return lax.dot_general(a, b, (((0,), (0,)), ((), ())), preferred_element_type=f32)


def dot_11(a, b):
    return lax.dot_general(a, b, (((1,), (1,)), ((), ())), preferred_element_type=f32)


def dot_10(a, b):
    return lax.dot_general(a, b, (((1,), (0,)), ((), ())), preferred_element_type=f32)


def softmax_first(scores):
    shifted = jnp.exp(scores - jnp.max(scores, axis=0, keepdims=True))
    return shifted * (1.0 / jnp.sum(shifted, axis=0, keepdims=True))


def lasting(microseconds):
    return pl.CostEstimate(
        flops=int(microseconds * 1.1e9), bytes_accessed=1 << 10, transcendentals=0
    )


SHIFT_ONE, SCALE_ONE, GATE_ONE, SHIFT_TWO, SCALE_TWO, GATE_TWO, WEIGHT = range(7)


def row_of(mods, which):
    return mods[which : which + 1, :]


def rms(values):
    scale = lax.rsqrt(jnp.mean(values * values, -1, keepdims=True) + epsilon)
    return values * scale, scale


def rms_back(grad, unit, scale, scaling):
    grad = grad * (1.0 + scaling)
    return scale * (grad - unit * jnp.mean(grad * unit, -1, keepdims=True))


def row_sum(values):
    return jnp.sum(values, axis=0, keepdims=True)


def put_rows(sums_ref, image, rows):
    for which in range(sums_ref.shape[1]):
        value = rows.get(which, jnp.zeros((1, sums_ref.shape[2]), f32))
        sums_ref[image, which : which + 1, :] = value


def chunk_rows(ref, image):
    return jnp.concatenate([ref[chunk, image] for chunk in range(ref.shape[0])], axis=0)


def put_chunks(ref, image, values):
    size = ref.shape[2]
    for chunk in range(ref.shape[0]):
        ref[chunk, image] = values[chunk * size : (chunk + 1) * size]


def attend_kernel(
    latent_ref, mods_ref, w_ref, wo_ref, gains_ref, cos_ref, sin_ref,
    proj_ref, att_ref, branch_ref, xt_ref, middle_ref, two_ref, twot_ref, x_ref,
):
    own = mods_ref.shape[0]
    head_dim = gains_ref.shape[1]
    rows_all = att_ref.shape[1]
    length = xt_ref.shape[1] // own
    heads = range(rows_all // head_dim)
    cut = feature_order(head_dim)[1]
    group = pl.program_id(0)

    def place(image):
        return pl.ds(pl.multiple_of(image * length, length), length)

    @pl.when(group == 0)
    def _():
        def entry(image, carry):
            mods = mods_ref[image]
            unit = rms(chunk_rows(latent_ref, image).astype(f32))[0]
            x = (unit * (1.0 + row_of(mods, SCALE_ONE)) + row_of(mods, SHIFT_ONE)).astype(bf16)
            x_ref[place(image), :] = x
            xt_ref[:, place(image)] = x.T
            return carry

        lax.fori_loop(0, own, entry, 0)

    proj_ref[0] = dot_11(w_ref[0, : 3 * rows_all], x_ref[...])

    def heads_of(image, carry):
        tokens = place(image)
        cos_tab, sin_tab = cos_ref[...], sin_ref[...]
        lows = [[], [], []]
        for kind in range(2):
            for head in heads:
                start = kind * rows_all + head * head_dim
                raw = proj_ref[0, start : start + head_dim, tokens]
                scaled = raw * head_scale(raw) * gains_ref[kind]
                turned = scaled * cos_tab + partner(scaled, cut) * sin_tab
                lows[kind].append(turned.astype(bf16))
        for head in heads:
            start = 2 * rows_all + head * head_dim
            lows[2].append(proj_ref[0, start : start + head_dim, tokens].astype(bf16))
        scores = [dot_00(lows[1][head], lows[0][head]) for head in heads]
        probs = [softmax_first(score).astype(bf16) for score in scores]
        outs = [dot_10(lows[2][head], probs[head]) for head in heads]
        att_ref[group, :, tokens] = jnp.concatenate(outs, axis=0).astype(bf16)
        return carry

    lax.fori_loop(0, own, heads_of, 0, unroll=True)

    @pl.when(group == pl.num_programs(0) - 1)
    def _():
        groups = att_ref.shape[0]

        def leave(image, carry):
            tokens = place(image)
            mods = mods_ref[image]
            att = att_ref[:, :, tokens].reshape(groups * rows_all, length)
            branch = dot_00(att, wo_ref[...].reshape(groups * rows_all, -1))
            branch_ref[tokens, :] = branch.astype(bf16)
            latent = chunk_rows(latent_ref, image).astype(f32)
            middle = latent + row_of(mods, GATE_ONE) * branch
            middle_ref[tokens, :] = middle
            two = rms(middle)[0] * (1.0 + row_of(mods, SCALE_TWO)) + row_of(mods, SHIFT_TWO)
            two = two.astype(bf16)
            two_ref[tokens, :] = two
            twot_ref[:, tokens] = two.T
            return carry

        lax.fori_loop(0, own, leave, 0)


def attend_back_kernel(
    latent_ref, proj_ref, low_ref, w_ref, gains_ref, cos_ref, sin_ref, grad_ref, mods_ref,
    out_ref, gain_grad_ref, sums_ref, chunks_ref, cot_ref,
):
    own = mods_ref.shape[0]
    head_dim = gains_ref.shape[1]
    rows_all, tokens_all = proj_ref.shape[1] // 3, proj_ref.shape[2]
    length = tokens_all // own
    heads = range(rows_all // head_dim)
    cut = feature_order(head_dim)[1]
    group = pl.program_id(0)

    def place(image):
        return pl.ds(pl.multiple_of(image * length, length), length)

    @pl.when(group == 0)
    def _():
        gain_grad_ref[...] = jnp.zeros_like(gain_grad_ref)

    cot_ref[...] = dot_11(w_ref[group, 3 * rows_all :], low_ref[...])

    def heads_of(image, carry):
        tokens = place(image)
        cos_tab, sin_tab = cos_ref[...], sin_ref[...]
        lows, units, scales = [[], [], []], [[], []], [[], []]
        for kind in range(2):
            for head in heads:
                start = kind * rows_all + head * head_dim
                raw = proj_ref[0, start : start + head_dim, tokens]
                scale = head_scale(raw)
                unit = raw * scale
                scaled = unit * gains_ref[kind]
                turned = scaled * cos_tab + partner(scaled, cut) * sin_tab
                lows[kind].append(turned.astype(bf16))
                units[kind].append(unit)
                scales[kind].append(scale)
        cots = []
        for head in heads:
            start = 2 * rows_all + head * head_dim
            lows[2].append(proj_ref[0, start : start + head_dim, tokens].astype(bf16))
            cots.append(cot_ref[head * head_dim : (head + 1) * head_dim, tokens].astype(bf16))
        scores = [dot_00(lows[1][head], lows[0][head]) for head in heads]
        prob_grads = [dot_00(lows[2][head], cots[head]) for head in heads]
        probs = [softmax_first(score) for score in scores]
        outs = [[], [], []]
        outs[2] = [dot_11(cots[head], probs[head].astype(bf16)) for head in heads]
        score_lows = []
        for head in heads:
            mean = jnp.sum(probs[head] * prob_grads[head], axis=0, keepdims=True)
            score_lows.append((probs[head] * (prob_grads[head] - mean)).astype(bf16))
        turned_grads = [
            [dot_10(lows[1][head], score_lows[head]) for head in heads],
            [dot_11(lows[0][head], score_lows[head]) for head in heads],
        ]
        for kind in range(2):
            total = 0.0
            for head in heads:
                grad, unit = turned_grads[kind][head], units[kind][head]
                grad = grad * cos_tab + partner(grad * sin_tab, cut)
                total = total + grad * unit
                grad = grad * gains_ref[kind]
                along = jnp.mean(grad * unit, axis=0, keepdims=True)
                outs[kind].append(scales[kind][head] * (grad - unit * along))
            gain_grad_ref[kind] += total
        grads = jnp.concatenate(outs[0] + outs[1] + outs[2], axis=0).astype(bf16)
        out_ref[group, :, tokens] = grads
        return carry

    lax.fori_loop(0, own, heads_of, 0, unroll=True)

    @pl.when(group == pl.num_programs(0) - 1)
    def _():
        def leave(image, carry):
            tokens = place(image)
            mods = mods_ref[image]
            grad = 0.0
            for other in range(out_ref.shape[0]):
                grad = grad + dot_00(out_ref[other, :, tokens], w_ref[other, : 3 * rows_all])
            unit, scale = rms(chunk_rows(latent_ref, image).astype(f32))
            sums = {SHIFT_ONE: row_sum(grad), SCALE_ONE: row_sum(grad * unit)}
            put_rows(sums_ref, image, sums)
            grad = grad_ref[tokens, :] + rms_back(grad, unit, scale, row_of(mods, SCALE_ONE))
            put_chunks(chunks_ref, image, grad.astype(bf16))
            return carry

        lax.fori_loop(0, own, leave, 0)


def whole_spec(shape):
    return pl.BlockSpec(shape, lambda g: (0,) * len(shape), pipeline_mode=pl.Buffered(1))


def attend(latent, mods, weights, gains, tables):
    groups, rows, width = weights.shape[0], weights.shape[1] // 4, weights.shape[2]
    own = mods.shape[0]
    length, head_dim = tables[0].shape[1], gains.shape[1]
    tokens = own * length
    total, turned = (tokens, width), (width, tokens)
    const = lambda shape: pl.BlockSpec(shape, lambda g: (0,) * len(shape))
    return pl.pallas_call(
        attend_kernel,
        grid=(groups,),
        in_specs=[
            whole_spec(latent.shape),
            whole_spec(mods.shape),
            pl.BlockSpec((1, 4 * rows, width), lambda g: (g, 0, 0)),
            pl.BlockSpec((groups, rows, width), lambda g: (0, 3, 0), pipeline_mode=pl.Buffered(1)),
            whole_spec(gains.shape),
            whole_spec(tables[0].shape),
            whole_spec(tables[0].shape),
        ],
        out_specs=[
            pl.BlockSpec((1, 3 * rows, tokens), lambda g: (g, 0, 0)),
            const((groups, rows, tokens)),
            const(total),
            const(turned),
            const(total),
            const(total),
            const(turned),
        ],
        out_shape=[
            jax.ShapeDtypeStruct((groups, 3 * rows, tokens), f32),
            jax.ShapeDtypeStruct((groups, rows, tokens), bf16),
            jax.ShapeDtypeStruct(total, bf16),
            jax.ShapeDtypeStruct(turned, bf16),
            jax.ShapeDtypeStruct(total, f32),
            jax.ShapeDtypeStruct(total, bf16),
            jax.ShapeDtypeStruct(turned, bf16),
        ],
        scratch_shapes=[pltpu.VMEM(total, bf16)],
        compiler_params=pltpu.CompilerParams(vmem_limit_bytes=62 << 20),
        cost_estimate=lasting(160),
        name="attend",
    )(latent, mods, weights, weights, gains, *tables)


def attend_back(latent, proj, low, weights, gains, tables, grad, mods):
    groups, rows, width = weights.shape[0], weights.shape[1] // 4, weights.shape[2]
    own = mods.shape[0]
    tokens = low.shape[0]
    length, head_dim = tokens // own, gains.shape[1]
    const = lambda shape: pl.BlockSpec(shape, lambda g: (0,) * len(shape))
    gain_shape = (2, head_dim, length)
    return pl.pallas_call(
        attend_back_kernel,
        grid=(groups,),
        in_specs=[
            whole_spec(latent.shape),
            pl.BlockSpec((1, 3 * rows, tokens), lambda g: (g, 0, 0)),
            whole_spec(low.shape),
            whole_spec(weights.shape),
            whole_spec(gains.shape),
            whole_spec(tables[0].shape),
            whole_spec(tables[0].shape),
            whole_spec(grad.shape),
            whole_spec(mods.shape),
        ],
        out_specs=[const(proj.shape), const(gain_shape), const(mods.shape), const(latent.shape)],
        out_shape=[
            jax.ShapeDtypeStruct(proj.shape, bf16),
            jax.ShapeDtypeStruct(gain_shape, f32),
            jax.ShapeDtypeStruct(mods.shape, f32),
            jax.ShapeDtypeStruct(latent.shape, bf16),
        ],
        scratch_shapes=[pltpu.VMEM((rows, tokens), f32)],
        compiler_params=pltpu.CompilerParams(vmem_limit_bytes=62 << 20),
        cost_estimate=lasting(1),
        name="attend_back",
    )(latent, proj, low, weights, gains, *tables, grad, mods)


def finish_kernel(
    branch_ref, middle_ref, cot_ref, mods_ref, low_ref, lowt_ref, chunks_ref, sums_ref
):
    branch, mods = branch_ref[...], mods_ref[0]
    gate = row_of(mods, GATE_TWO)
    result = (middle_ref[...] + gate * branch).astype(bf16)
    put_chunks(chunks_ref, 0, result)
    cot = chunk_rows(cot_ref, 0).astype(f32) * row_of(mods, WEIGHT)
    low = (gate * cot).astype(bf16)
    low_ref[...] = low
    lowt_ref[...] = low.T
    put_rows(sums_ref, 0, {GATE_TWO: row_sum(cot * branch)})


def middle_kernel(
    one_ref, other_ref, middle_ref, branch_ref, cot_ref, mods_ref,
    grad_ref, low_ref, lowt_ref, sums_ref,
):
    mods = mods_ref[0]
    grad = one_ref[...] + other_ref[...]
    unit, scale = rms(middle_ref[...])
    sums = {SHIFT_TWO: row_sum(grad), SCALE_TWO: row_sum(grad * unit)}
    cot = chunk_rows(cot_ref, 0).astype(f32) * row_of(mods, WEIGHT)
    grad = cot + rms_back(grad, unit, scale, row_of(mods, SCALE_TWO))
    grad_ref[...] = grad
    low = (row_of(mods, GATE_ONE) * grad).astype(bf16)
    low_ref[...] = low
    lowt_ref[...] = low.T
    sums[GATE_ONE] = row_sum(grad * branch_ref[...].astype(f32))
    put_rows(sums_ref, 0, sums)


def by_image(kernel, name, microseconds, rows, chunks, mods, outs):
    own, sums, width = mods.shape
    tokens = rows[0].shape[0]
    length = tokens // own
    block = pl.BlockSpec((length, width), lambda i: (i, 0))
    turned = pl.BlockSpec((width, length), lambda i: (0, i))
    chunk = pl.BlockSpec((chunks.shape[0], 1) + chunks.shape[2:], lambda i: (0, i, 0, 0))
    whole = pl.BlockSpec((1, sums, width), lambda i: (i, 0, 0))
    specs, shapes = [], []
    for out in outs:
        if out is True:
            specs.append(turned)
            shapes.append(jax.ShapeDtypeStruct((width, tokens), bf16))
        elif out is False:
            specs.append(chunk)
            shapes.append(jax.ShapeDtypeStruct(chunks.shape, bf16))
        else:
            specs.append(block)
            shapes.append(jax.ShapeDtypeStruct((tokens, width), out))
    return pl.pallas_call(
        kernel,
        grid=(own,),
        in_specs=[block] * len(rows) + [chunk, whole],
        out_specs=specs + [whole],
        out_shape=shapes + [jax.ShapeDtypeStruct(mods.shape, f32)],
        compiler_params=pltpu.CompilerParams(vmem_limit_bytes=48 << 20),
        cost_estimate=lasting(microseconds),
        name=name,
    )(*rows, chunks, mods)


def modulate_kernel(silu_ref, ada_ref, out_ref):
    out_ref[0] = dot_10(silu_ref[...], ada_ref[0])


def modulate(silu, ada):
    kinds, width = ada.shape[:2]
    return pl.pallas_call(
        modulate_kernel,
        grid=(kinds,),
        in_specs=[
            pl.BlockSpec(silu.shape, lambda k: (0, 0)),
            pl.BlockSpec((1, width, width), lambda k: (k, 0, 0)),
        ],
        out_specs=pl.BlockSpec((1,) + silu.shape, lambda k: (k, 0, 0)),
        out_shape=jax.ShapeDtypeStruct((kinds,) + silu.shape, f32),
        compiler_params=pltpu.CompilerParams(vmem_limit_bytes=32 << 20),
        cost_estimate=lasting(60),
        name="modulate",
    )(silu, ada)


def add_rows(out_ref, part, first, index, length):
    rows = pl.ds(pl.multiple_of(index * length, length), length)

    @pl.when(first)
    def _():
        out_ref[rows, :] = part

    @pl.when(jnp.logical_not(first))
    def _():
        out_ref[rows, :] += part


def sigmoid(values):
    return 1.0 / (1.0 + jnp.exp(-values))


def mlp_kernel(count, e_ref, x_ref, *refs):
    first = pl.program_id(0) == 0
    save_ref, out_ref, w_ref = refs[count:]
    unit = min(ref.shape[2] for ref in refs[:count])
    for index, ref in enumerate(refs[:count]):
        rows = pl.ds(pl.multiple_of(e_ref[index] * unit, unit), ref.shape[2])
        for kind in range(3):
            w_ref[0, kind, rows, :] = ref[0, kind]
    x = x_ref[...]
    gate = dot_11(x, w_ref[0, 0])
    up = dot_11(x, w_ref[0, 1])
    save_ref[0, 0] = gate.astype(bf16)
    save_ref[0, 1] = up.astype(bf16)
    hidden = (gate * sigmoid(gate) * up).astype(bf16)
    part = dot_10(hidden, w_ref[0, 2])
    add_rows(out_ref, part, first, 0, x.shape[0])


def mlp(x, order, pieces):
    groups, _, _, width = pieces[0].shape
    units, tokens = sum(piece.shape[2] for piece in pieces), x.shape[0]
    return pl.pallas_call(
        functools.partial(mlp_kernel, len(pieces)),
        grid_spec=pltpu.PrefetchScalarGridSpec(
            num_scalar_prefetch=1,
            grid=(groups,),
            in_specs=[pl.BlockSpec((tokens, width), lambda g, e: (0, 0), pipeline_mode=pl.Buffered(1))]
            + [pl.BlockSpec((1,) + piece.shape[1:], lambda g, e: (g, 0, 0, 0)) for piece in pieces],
            out_specs=[
                pl.BlockSpec((1, 2, tokens, units), lambda g, e: (g, 0, 0, 0)),
                pl.BlockSpec((tokens, width), lambda g, e: (0, 0)),
                pl.BlockSpec((1, 3, units, width), lambda g, e: (g, 0, 0, 0)),
            ],
        ),
        out_shape=[
            jax.ShapeDtypeStruct((groups, 2, tokens, units), bf16),
            jax.ShapeDtypeStruct((tokens, width), f32),
            jax.ShapeDtypeStruct((groups, 3, units, width), bf16),
        ],
        compiler_params=pltpu.CompilerParams(vmem_limit_bytes=62 << 20),
        cost_estimate=lasting(1),
        name="mlp",
    )(order, x, *pieces)


def fill_rows(order_ref, source_ref, target_ref, base=0):
    blocks, rows = source_ref.shape[0], source_ref.shape[1]
    for place in range(blocks):
        target_ref[place * rows : (place + 1) * rows, :] = source_ref[order_ref[base + place]]


def mlp_back_kernel(
    e_ref, xt_ref, lowt_ref, low_ref, save_ref, w_ref,
    keep_ref, send_ref, two_ref, xs, lows, parts,
):
    first = pl.program_id(0) == 0
    tokens, width = low_ref.shape
    step = math.gcd(tokens, 512)

    @pl.when(first)
    def _():
        fill_rows(e_ref, xt_ref, xs)
        fill_rows(e_ref, lowt_ref, lows)

    for index in range(tokens // step):
        rows = pl.ds(index * step, step)
        hidden_grad = dot_11(low_ref[rows, :], w_ref[0, 2])
        gate = save_ref[0, 0, rows, :].astype(f32)
        up = save_ref[0, 1, rows, :].astype(f32)
        sig = sigmoid(gate)
        swish = gate * sig
        gate_low = (hidden_grad * up * (sig + swish * (1.0 - sig))).astype(bf16)
        up_low = (hidden_grad * swish).astype(bf16)
        parts[0, rows, :] = gate_low
        parts[1, rows, :] = up_low
        parts[2, rows, :] = (swish * up).astype(bf16)
        part = dot_10(gate_low, w_ref[0, 0]) + dot_10(up_low, w_ref[0, 1])
        add_rows(two_ref, part, first, index, step)

    half = width // 2
    for out_ref, rows in ((keep_ref, slice(0, half)), (send_ref, slice(half, width))):
        x_rows = xs[rows, :]
        for kind in range(2):
            out_ref[0, kind] = dot_10(x_rows, parts[kind]).astype(bf16)
        out_ref[0, 2] = dot_10(lows[rows, :], parts[2]).astype(bf16)


def mlp_back(which, e_order, xt, lowt, low, save, weights):
    groups, _, units, width = weights.shape
    tokens = low.shape[0]
    blocks = groups // 2
    base = which * blocks
    once = pl.Buffered(1)
    whole = lambda p, e: (0, 0)
    whole3 = lambda p, e: (0, 0, 0)
    half = jax.ShapeDtypeStruct((blocks, 3, width // 2, units), bf16)
    half_spec = pl.BlockSpec((1, 3, width // 2, units), lambda p, e: (p, 0, 0, 0))
    return pl.pallas_call(
        mlp_back_kernel,
        grid_spec=pltpu.PrefetchScalarGridSpec(
            num_scalar_prefetch=1,
            grid=(blocks,),
            in_specs=[
                pl.BlockSpec(xt.shape, whole3, pipeline_mode=once),
                pl.BlockSpec(lowt.shape, whole3, pipeline_mode=once),
                pl.BlockSpec((tokens, width), whole, pipeline_mode=once),
                pl.BlockSpec((1, 2, tokens, units), lambda p, e: (base + p, 0, 0, 0)),
                pl.BlockSpec((1, 3, units, width), lambda p, e: (base + p, 0, 0, 0)),
            ],
            out_specs=[half_spec, half_spec, pl.BlockSpec((tokens, width), whole)],
            scratch_shapes=[
                pltpu.VMEM((width, tokens), bf16),
                pltpu.VMEM((width, tokens), bf16),
                pltpu.VMEM((3, tokens, units), bf16),
            ],
        ),
        out_shape=[half, half, jax.ShapeDtypeStruct((tokens, width), f32)],
        compiler_params=pltpu.CompilerParams(vmem_limit_bytes=62 << 20),
        cost_estimate=lasting(150),
        name="mlp_back",
    )(e_order, xt, lowt, low, save, weights)


def attend_grads_kernel(
    m_ref, e_ref, xt_ref, lowt_ref, proj_ref, att_ref, keep_ref, send_ref, xs, lows
):
    first = pl.num_programs(0) // 2 == pl.program_id(0)
    base = jnp.where(first, xt_ref.shape[0], 0)

    @pl.when(first | (pl.program_id(0) == 0))
    def _():
        fill_rows(e_ref, xt_ref, xs, base)
        fill_rows(e_ref, lowt_ref, lows, base)

    width = xs.shape[0]
    half = width // 2
    columns = proj_ref.shape[1]

    for out_ref, rows in ((keep_ref, slice(0, half)), (send_ref, slice(half, width))):
        out_ref[0, :, :columns] = dot_11(xs[rows, :], proj_ref[0]).astype(bf16)
        out_ref[0, :, columns:] = dot_11(lows[rows, :], att_ref[0]).astype(bf16)


def attend_grads(m_order, e_orders, xt, lowt, proj, att):
    rows, tokens = att.shape[1:]
    width = xt.shape[0] * xt.shape[1]
    blocks = m_order.shape[0]
    whole3 = lambda p, m, e: (0, 0, 0)
    half = jax.ShapeDtypeStruct((blocks, width // 2, 4 * rows), bf16)
    half_spec = pl.BlockSpec((1, width // 2, 4 * rows), lambda p, m, e: (p, 0, 0))
    return pl.pallas_call(
        attend_grads_kernel,
        grid_spec=pltpu.PrefetchScalarGridSpec(
            num_scalar_prefetch=2,
            grid=(blocks,),
            in_specs=[
                pl.BlockSpec(xt.shape, whole3, pipeline_mode=pl.Buffered(1)),
                pl.BlockSpec(lowt.shape, whole3, pipeline_mode=pl.Buffered(1)),
                pl.BlockSpec((1, 3 * rows, tokens), lambda p, m, e: (m[p], 0, 0)),
                pl.BlockSpec((1, rows, tokens), lambda p, m, e: (m[p], 0, 0)),
            ],
            out_specs=[half_spec, half_spec],
            scratch_shapes=[
                pltpu.VMEM((width, tokens), bf16),
                pltpu.VMEM((width, tokens), bf16),
            ],
        ),
        out_shape=[half, half],
        compiler_params=pltpu.CompilerParams(vmem_limit_bytes=56 << 20),
        cost_estimate=lasting(200),
        name="attend_grads",
    )(m_order, e_orders, xt, lowt, proj, att)


def dot(a, b):
    return jnp.dot(a, b, preferred_element_type=f32)


def ein(spec, a, b):
    return jnp.einsum(spec, a, b, preferred_element_type=f32)


def gather_pieces(piece, mp_size):
    whole = lax.all_gather(piece, ("mp", "dp"), axis=0, tiled=False)
    return whole.reshape((mp_size, -1) + piece.shape)


def take_rows(values, index):
    return jnp.take(values, index, axis=0, mode="clip")


def bits_of(size):
    return [1 << i for i in range(size.bit_length() - 1)]


def swap(values, axis, bit):
    size = lax.axis_size(axis)
    return lax.ppermute(values, axis, [(i, i ^ bit) for i in range(size)])


def xor_gather(values, axes_bits):
    names = sorted({axis for axis, _ in axes_bits})
    places = [{name: 0 for name in names}]
    values = values[None]
    for axis, bit in axes_bits:
        values = jnp.concatenate([values, swap(values, axis, bit)], axis=0)
        places = places + [dict(place, **{axis: place[axis] ^ bit}) for place in places]
    return values, {name: [place[name] for place in places] for name in names}


def halving_order(bits):
    order = [0]
    for bit in reversed(bits):
        order = order + [place ^ bit for place in order]
    return order


def add_low(kept, received):
    return (kept.astype(f32) + received.astype(f32)).astype(bf16)


def sum_halves_kernel(kept_ref, got_ref, first_ref, second_ref):
    total = (kept_ref[0].astype(f32) + got_ref[0].astype(f32)).astype(bf16)
    half = first_ref.shape[1]
    first_ref[0] = total[:half]
    second_ref[0] = total[half:]


def sum_halves(kept, got):
    rows, columns = kept.shape[-2:]
    if rows % 32:
        return split(add_low(kept, got), kept.ndim - 2)
    shape = kept.shape[:-2] + (rows // 2, columns)
    kept, got = kept.reshape(-1, rows, columns), got.reshape(-1, rows, columns)
    whole = pl.BlockSpec((1, rows, columns), lambda i: (i, 0, 0))
    half = pl.BlockSpec((1, rows // 2, columns), lambda i: (i, 0, 0))
    halves = pl.pallas_call(
        sum_halves_kernel,
        grid=(kept.shape[0],),
        in_specs=[whole, whole],
        out_specs=[half, half],
        out_shape=[jax.ShapeDtypeStruct((kept.shape[0], rows // 2, columns), bf16)] * 2,
        compiler_params=pltpu.CompilerParams(vmem_limit_bytes=32 << 20),
        cost_estimate=lasting(0),
        name="sum_halves",
    )(kept, got)
    return halves[0].reshape(shape), halves[1].reshape(shape)


def tie(*values):
    return lax.optimization_barrier(values)


def split(values, dim):
    size = values.shape[dim] // 2
    return (
        lax.slice_in_dim(values, 0, size, axis=dim),
        lax.slice_in_dim(values, size, 2 * size, axis=dim),
    )


def halve(values, axis, bits, dim):
    for bit in bits:
        kept, sent = split(values, dim)
        values = add_low(kept, swap(sent, axis, bit))
    return values


def shards(
    patches,
    cotangent,
    time_bins,
    labels,
    image_counts,
    dest_perm,
    time_table,
    class_table,
    ada_weight,
    qkv_weight,
    norm_gains,
    out_weight,
    expand_weight,
    down_weight,
):
    dp_size = lax.axis_size("dp")
    mp_size = lax.axis_size("mp")
    capacity = patches.shape[0]
    slot_count = capacity // dp_size
    images = cotangent.shape[0]
    local_len = patches.shape[1]
    model_width = patches.shape[2]
    length = local_len * mp_size
    head_dim = norm_gains.shape[1]
    local_dim = out_weight.shape[0]
    unit_count = down_weight.shape[0]
    own = images // mp_size
    total_images = images * dp_size
    order = np.array(feature_order(head_dim)[0])
    columns = np.arange(4 * local_dim)
    places = columns // head_dim * head_dim + order[columns % head_dim]
    places = np.where(columns < 2 * local_dim, places, columns).astype(np.int32)
    gains_f = norm_gains.astype(f32)[:, order]
    gains_f = (gains_f * jnp.array([[head_dim ** (-0.5)], [1.0]], f32))[:, :, None]
    dp_index = lax.axis_index("dp")
    mp_index = lax.axis_index("mp")
    dp_bits = bits_of(dp_size)
    dp_bits = (dp_bits, dp_bits[:1] + dp_bits[1:][::-1])
    mp_bits = bits_of(mp_size)

    tables = rope_tables(jnp.arange(length), head_dim)

    def turn(chunks):
        return lax.all_to_all(chunks, "mp", split_axis=0, concat_axis=0, tiled=True)

    starts = jnp.cumsum(image_counts) - image_counts
    finish = starts + image_counts
    my_start = starts[dp_index]
    my_count = image_counts[dp_index]
    device_ids = jnp.arange(dp_size)
    matches = (dest_perm[:, None] == device_ids[None, :]).astype(jnp.int32)
    inverse = jnp.sum(device_ids[:, None] * matches, axis=0)
    my_place = inverse[dp_index]
    pair_ids = jnp.arange(dp_size * slot_count)
    pair_peer = pair_ids // slot_count
    pair_slot = pair_ids % slot_count
    send_index = pair_slot * dp_size + jnp.mod(inverse[pair_peer] - my_start, dp_size)
    send_index = jnp.minimum(send_index, capacity - 1)
    send_patches = take_rows(patches, send_index)
    info, info_places = xor_gather(
        jnp.stack([time_bins, labels]), [("dp", bit) for bit in bits_of(dp_size)]
    )
    qkv_weight, out_weight, expand_weight, down_weight, send_patches, info = tie(
        qkv_weight, out_weight, expand_weight, down_weight, send_patches, info
    )
    share = 4 * local_dim // dp_size
    spots = lax.dynamic_slice_in_dim(jnp.array(places), dp_index * share, share, 0)
    take_qkv = (spots[:, None] == jnp.arange(3 * local_dim)[None, :]).astype(bf16)
    take_out = (spots[:, None] - 3 * local_dim == jnp.arange(local_dim)[None, :]).astype(bf16)
    attend_piece = dot(take_qkv, qkv_weight.transpose(1, 2, 0).reshape(-1, model_width))
    attend_piece = (attend_piece + dot(take_out, out_weight)).astype(bf16)
    share = unit_count // dp_size
    spots = dp_index * share + jnp.arange(share)
    take_units = (spots[:, None] == jnp.arange(unit_count)[None, :]).astype(bf16)
    mlp_piece = jnp.stack(
        [
            ein("rf,df->rd", take_units, expand_weight[:, 0]).astype(bf16),
            ein("rf,df->rd", take_units, expand_weight[:, 1]).astype(bf16),
            lax.dynamic_slice_in_dim(down_weight, dp_index * share, share, 0),
        ]
    )
    attend_full = gather_pieces(attend_piece, mp_size).reshape(mp_size, 4 * local_dim, -1)
    by_permutes = share % 32 == 0 and dp_size == 8 and mp_size == 4
    if by_permutes:
        mlp_near = mlp_piece[None]
        far_near = swap(mlp_near, "mp", 2)
    else:
        mlp_full = gather_pieces(mlp_piece, mp_size)
        mlp_full = mlp_full.swapaxes(1, 2).reshape(mp_size, 3, unit_count, model_width)
        mlp_pieces = [mlp_full[mp_index ^ jnp.array(halving_order(mp_bits))]]
        mlp_order = jnp.zeros((1,), jnp.int32)

    recv_patches = lax.all_to_all(send_patches, "dp", split_axis=0, concat_axis=0, tiled=True)
    info = info.swapaxes(0, 1).reshape(2, -1)
    info_owner = jnp.repeat(dp_index ^ jnp.array(info_places["dp"]), capacity)
    info_slot = jnp.tile(jnp.arange(capacity), dp_size)
    info_count = jnp.sum(
        jnp.where(info_owner[:, None] == device_ids[None, :], image_counts[None, :], 0), axis=1
    )
    live_all = info_slot < info_count
    bin_totals = jnp.sum(
        ((info[0][:, None] == jnp.arange(NBINS)[None, :]) & live_all[:, None]).astype(f32), axis=0
    )
    gather_bits = [("dp", bit) for bit in bits_of(dp_size)]
    gather_bits = gather_bits + [("mp", bit) for bit in bits_of(mp_size)[::-1]]
    spread = {"dp": [0], "mp": [0]}
    for axis, bit in gather_bits:
        spread = {
            name: spread[name] + [place ^ (bit if name == axis else 0) for place in spread[name]]
            for name in spread
        }
    owner_all = jnp.repeat(dp_index ^ jnp.array(spread["dp"]), own)
    group_all = jnp.repeat(mp_index ^ jnp.array(spread["mp"]), own)
    row_all = group_all * own + jnp.tile(jnp.arange(own), dp_size * mp_size)
    place_all = jnp.sum(
        jnp.where(owner_all[:, None] == device_ids[None, :], inverse[None, :], 0), axis=1
    )
    rank_all = row_all * dp_size + place_all
    source_all = jnp.sum((finish[None, :] <= rank_all[:, None]).astype(jnp.int32), axis=1)
    start_all = jnp.sum(
        jnp.where(source_all[:, None] == device_ids[None, :], starts[None, :], 0), axis=1
    )
    slots_all = source_all * capacity + rank_all - start_all
    slot_hit = slots_all[:, None] == (info_owner * capacity + info_slot)[None, :]
    bins_all = jnp.sum(jnp.where(slot_hit, info[0][None, :], 0), axis=1)
    labels_all = jnp.sum(jnp.where(slot_hit, info[1][None, :], 0), axis=1)
    bin_hot = (bins_all[:, None] == jnp.arange(NBINS)[None, :])
    label_hot = (labels_all[:, None] == jnp.arange(NCLS)[None, :])
    weights_all = total_images / (NBINS * jnp.sum(bin_hot.astype(f32) * bin_totals[None, :], axis=1))
    bin_hot = bin_hot.astype(bf16)
    label_hot = label_hot.astype(bf16)
    cond_all = (dot(bin_hot, time_table) + dot(label_hot, class_table)).astype(bf16).astype(f32)
    silu_all = jax.nn.silu(cond_all).astype(bf16)
    silu_cond = silu_all[:own]
    weights = weights_all[:own]

    if by_permutes:
        silu_cond, far_near = tie(silu_cond, far_near)
        mlp_near = jnp.concatenate([mlp_near, far_near], axis=0)
        far_near = swap(mlp_near, "mp", 1)
    ada_kinds = ada_weight.swapaxes(0, 1)
    modulation = modulate(jnp.pad(silu_cond, ((0, -own % 16), (0, 0))), ada_kinds)[:, :own]
    mods = jnp.concatenate(
        [
            modulation.swapaxes(0, 1),
            jnp.broadcast_to(weights[:, None, None], (own, 1, model_width)),
            jnp.zeros((own, 1, model_width), f32),
        ],
        axis=1,
    )
    recv_patches, mods = tie(recv_patches, mods)

    rank_ids = jnp.arange(images) * dp_size + my_place
    source = jnp.sum((finish[None, :] <= rank_ids[:, None]).astype(jnp.int32), axis=1)
    within = rank_ids - starts[source]
    recv_index = source * slot_count + within // dp_size
    latent = take_rows(recv_patches, recv_index).reshape(mp_size, own, local_len, model_width)
    if by_permutes:
        far_near, _ = tie(far_near, latent)
    latent = turn(latent)
    if by_permutes:
        mlp_near = jnp.concatenate([mlp_near, far_near], axis=0)
        halves = split(mlp_near, 2)
        orders = ((2, 4), (4, 2))
        parts = [{bit: swap(halves[half], "dp", bit) for bit in orders[half]} for half in range(2)]
        cored = swap(mlp_near, "dp", 1)
        latent, parts[0][2], parts[1][4], cored = tie(latent, parts[0][2], parts[1][4], cored)
        got = [swap(parts[half][orders[half][0]], "dp", orders[half][1]) for half in range(2)]

    cotangent, latent = tie(cotangent, latent)
    proj, attended, branch_one, normed_t, middle, two, two_t = attend(
        latent, mods, attend_full, gains_f, tables
    )
    cot = turn(cotangent.reshape(mp_size, own, local_len, model_width))
    if by_permutes:
        got[0], got[1], attended = tie(got[0], got[1], attended)
        mlp_pieces, mlp_order = [mlp_near, cored], [dp_index * 2, (dp_index ^ 1) * 2]
        for half in range(2):
            parts[half][6] = got[half]
            for near, part in parts[half].items():
                mlp_pieces += [part, swap(part, "dp", 1)]
                mlp_order += [(dp_index ^ near) * 2 + half, (dp_index ^ near ^ 1) * 2 + half]
        mlp_order = jnp.stack(mlp_order).astype(jnp.int32)
    save, branch_two, mlp_full = mlp(two, mlp_order, mlp_pieces)
    branch_two, cot = tie(branch_two, cot)
    down_low, down_t, result, sums_finish = by_image(
        finish_kernel, "finish", 1, (branch_two, middle), cot, mods, (bf16, True, False)
    )
    result = turn(result)

    e_orders = [(dp_index ^ jnp.array(halving_order(bits))).astype(jnp.int32) for bits in dp_bits]
    m_order = (mp_index ^ jnp.array(halving_order(mp_bits))).astype(jnp.int32)

    def by_owner(values):
        return values.reshape(dp_size, model_width // dp_size, -1)

    two_t, down_t = by_owner(two_t), by_owner(down_t)
    kept_one, sent_one, two_one = mlp_back(
        1, e_orders[1], two_t, down_t, down_low, save, mlp_full
    )
    got_one = swap(sent_one, "dp", dp_bits[1][0])
    kept_zero, sent_zero, two_zero = mlp_back(
        0, e_orders[0], two_t, down_t, down_low, save, mlp_full
    )
    got_zero = swap(sent_zero, "dp", dp_bits[0][0])
    kept_one, sent_one = sum_halves(kept_one, got_one)
    kept_zero, sent_zero = sum_halves(kept_zero, got_zero)
    two_zero, kept_one, kept_zero, result = tie(two_zero, kept_one, kept_zero, result)
    got_one = swap(sent_one, "dp", dp_bits[1][1])
    got_zero = swap(sent_zero, "dp", dp_bits[0][1])
    middle_grad, branch_low, branch_t, sums_middle = by_image(
        middle_kernel,
        "middle",
        100,
        (two_zero, two_one, middle, branch_one),
        cot,
        mods,
        (f32, bf16, True),
    )
    projected_low, gains_grad, sums_entry, latent_back = attend_back(
        latent, proj, branch_low, attend_full, gains_f, tables, middle_grad, mods
    )
    gains_grad = jnp.sum(gains_grad, axis=2) * jnp.array([[head_dim ** (-0.5)], [1.0]], f32)
    projected_low, got_one, got_zero = tie(projected_low, got_one, got_zero)
    kept_one, sent_one = sum_halves(kept_one, got_one)
    kept_zero, sent_zero = sum_halves(kept_zero, got_zero)
    normed_t, kept_one, kept_zero = tie(normed_t, kept_one, kept_zero)
    got_one = swap(sent_one, "dp", dp_bits[1][2])
    got_zero = swap(sent_zero, "dp", dp_bits[0][2])
    latent_back = turn(latent_back)

    normed_t, branch_t = by_owner(normed_t), by_owner(branch_t)

    attend_kept, attend_sent = attend_grads(
        m_order, jnp.concatenate(e_orders), normed_t, branch_t, projected_low, attended
    )
    attend_got = swap(attend_sent, "dp", dp_bits[0][0])
    attend_kept, got_one, got_zero = tie(attend_kept, got_one, got_zero)

    packed = sums_finish + sums_middle + sums_entry
    gains_row = jnp.pad(gains_grad.reshape(1, 1, -1), ((0, own - 1), (7, 0), (0, model_width - 2 * head_dim)))
    packed = jnp.where(jnp.arange(8)[:, None] == 7, gains_row, packed).astype(bf16)
    packed = packed[None]
    got_packed = swap(packed, *gather_bits[0])

    def more(after):
        nonlocal packed, got_packed, stage
        after, got_packed = tie(after, got_packed)
        packed = jnp.concatenate([packed, got_packed], axis=0)
        stage += 1
        if stage < len(gather_bits):
            got_packed = swap(packed, *gather_bits[stage])
        return after

    stage = 0
    attend_kept = more(attend_kept)
    halves = sum_halves(attend_kept, attend_got)
    (attend_zero, attend_one), (sent_zero, sent_one) = split(halves[0], 0), split(halves[1], 0)
    attend_got_one = swap(sent_one, "dp", dp_bits[1][1])
    attend_got_zero = swap(sent_zero, "dp", dp_bits[0][1])
    latent_back, attend_one, attend_zero = tie(latent_back, attend_one, attend_zero)

    back_within = pair_slot * dp_size + jnp.mod(my_place - starts[pair_peer], dp_size)
    back_valid = back_within < image_counts[pair_peer]
    back_slot = jnp.clip((starts[pair_peer] + back_within - my_place) // dp_size, 0, images - 1)
    back_slot = jnp.where(back_valid, back_slot, images)
    empty = jnp.zeros((1, local_len, model_width), bf16)
    latent_back = latent_back.reshape(images, local_len, model_width)
    latent_back = jnp.concatenate([latent_back, empty], axis=0)
    back_patches = take_rows(latent_back, back_slot)

    got_packed, _ = tie(got_packed, back_patches)
    got_patches = lax.all_to_all(back_patches, "dp", split_axis=0, concat_axis=0, tiled=True)
    slot_ids = jnp.arange(capacity)
    home_peer = dest_perm[jnp.mod(my_start + slot_ids, dp_size)]
    home_index = home_peer * slot_count + jnp.minimum(slot_ids // dp_size, slot_count - 1)
    patch_grad = take_rows(got_patches, home_index)

    mlp_one = more(halve(add_low(kept_one, got_one), "dp", dp_bits[1][3:], 2))
    mlp_zero = more(halve(add_low(kept_zero, got_zero), "dp", dp_bits[0][3:], 2))
    mlp_got = swap(mlp_one, "mp", mp_bits[0])
    attend_one, sent_one = sum_halves(attend_one, attend_got_one)
    attend_zero, sent_zero = sum_halves(attend_zero, attend_got_zero)
    attend_got_one = swap(sent_one, "dp", dp_bits[1][2])
    attend_got_zero = swap(sent_zero, "dp", dp_bits[0][2])
    while stage < len(gather_bits):
        mlp_zero = more(mlp_zero)
    packed = packed.reshape(total_images, 8, model_width)
    mod_all = packed[:, :6]
    gains_total = packed.reshape(-1, own, 8, model_width)[:, 0, 7, : 2 * head_dim]
    gains_total = jnp.sum(gains_total.astype(f32), axis=0).reshape(2, head_dim)
    gains_total = jnp.sum(
        jnp.where(order[:, None] == jnp.arange(head_dim)[None, :], gains_total[:, :, None], 0.0), axis=1
    )
    width_dp = model_width // dp_size
    width_mp = model_width // mp_size
    row0 = dp_index * width_dp
    silu_rows = lax.dynamic_slice_in_dim(silu_all, row0, width_dp, 1)
    mod_cols = lax.dynamic_slice_in_dim(mod_all, mp_index * width_mp, width_mp, 2)
    ada_grad = ein("id,ikc->dkc", silu_rows, mod_cols)
    ada_rows = lax.dynamic_slice_in_dim(ada_kinds, row0, width_dp, 1)
    silu_grad = ein("ikc,kdc->id", mod_all, ada_rows)
    cond_rows = lax.dynamic_slice_in_dim(cond_all, row0, width_dp, 1)
    silu_val, silu_pull = jax.vjp(jax.nn.silu, cond_rows)
    condition_low = silu_pull(silu_grad)[0].astype(bf16)
    time_grad = ein("in,id->nd", bin_hot, condition_low)
    class_grad = ein("in,id->nd", label_hot, condition_low)

    attend_one = halve(add_low(attend_one, attend_got_one), "dp", dp_bits[1][3:], 1)
    attend_zero = halve(add_low(attend_zero, attend_got_zero), "dp", dp_bits[0][3:], 1)
    mlp_grad = halve(add_low(mlp_zero, mlp_got), "mp", mp_bits[1:], 0)[0].astype(f32)
    attend_grad = add_low(attend_zero, swap(attend_one, "mp", mp_bits[0]))
    attend_grad = halve(attend_grad, "mp", mp_bits[1:], 0)[0].astype(f32)

    expand_grad = mlp_grad[:2].swapaxes(0, 1)
    down_grad = mlp_grad[2].T
    out_grad = attend_grad[:, 3 * local_dim :].T
    qkv_grad = lax.dot_general(
        attend_grad[:, : 3 * local_dim],
        jnp.array(places[: 3 * local_dim, None] == columns[: 3 * local_dim], f32),
        (((1,), (0,)), ((), ())),
        precision=lax.Precision.HIGHEST,
        preferred_element_type=f32,
    )
    qkv_grad = qkv_grad.reshape(-1, 3, local_dim)
    return (
        result.reshape(images, local_len, model_width),
        patch_grad,
        time_grad,
        class_grad,
        ada_grad,
        qkv_grad,
        gains_total,
        out_grad,
        expand_grad,
        down_grad,
    )


def solution(mesh):
    in_specs = (
        P("dp", "mp", None),
        P("dp", "mp", None),
        P("dp"),
        P("dp"),
        P(),
        P(),
        P(),
        P(),
        P(),
        P(None, None, "mp"),
        P(),
        P("mp", None),
        P(None, None, "mp"),
        P("mp", None),
    )
    out_specs = (
        P("dp", "mp", None),
        P("dp", "mp", None),
        P(None, "dp"),
        P(None, "dp"),
        P("dp", None, "mp"),
        P("dp", None, "mp"),
        P(),
        P("mp", "dp"),
        P("dp", None, "mp"),
        P("mp", "dp"),
    )
    return jax.shard_map(shards, mesh=mesh, in_specs=in_specs, out_specs=out_specs, check_vma=False)
```

```python
import functools
import math

import jax
import jax.numpy as jnp
import numpy as np
from jax import lax
from jax.experimental import pallas as pl
from jax.experimental.pallas import tpu as pltpu
from jax.sharding import PartitionSpec as P

GRID = 16
NCLS = 1000
NBINS = 16

epsilon = 1e-06
rope_base = 10000.0
f32 = jnp.float32
bf16 = jnp.bfloat16


def feature_order(head_dim):
    quarter = head_dim // 4
    firsts = list(range(quarter)) + list(range(2 * quarter, 3 * quarter))
    cut = len(firsts) // 8 * 8
    seconds = [i + quarter for i in firsts]
    return firsts[:cut] + seconds[:cut] + firsts[cut:] + seconds[cut:], cut


def rope_tables(position, head_dim):
    quarter = head_dim // 4
    order, cut = feature_order(head_dim)
    places = jnp.stack([position // GRID, position % GRID]).astype(f32)
    frequency = rope_base ** (-jnp.arange(quarter).astype(f32) / quarter)
    angle = (frequency[None, :, None] * places[:, None, :]).reshape(2 * quarter, -1)
    cosine, sine = jnp.cos(angle), jnp.sin(angle)
    cos_tab = jnp.concatenate([cosine[:cut], cosine[:cut], cosine[cut:], cosine[cut:]])
    sin_tab = jnp.concatenate([-sine[:cut], sine[:cut], -sine[cut:], sine[cut:]])
    return cos_tab, sin_tab


def partner(values, cut):
    rest = values[2 * cut :]
    half = rest.shape[0] // 2
    return jnp.concatenate(
        [values[cut : 2 * cut], values[:cut], pltpu.roll(rest, half, 0)], axis=0
    )


def head_scale(values):
    return lax.rsqrt(jnp.mean(values * values, axis=0, keepdims=True) + epsilon)


def dot_00(a, b):
    return lax.dot_general(a, b, (((0,), (0,)), ((), ())), preferred_element_type=f32)


def dot_11(a, b):
    return lax.dot_general(a, b, (((1,), (1,)), ((), ())), preferred_element_type=f32)


def dot_10(a, b):
    return lax.dot_general(a, b, (((1,), (0,)), ((), ())), preferred_element_type=f32)


def softmax_first(scores):
    shifted = jnp.exp(scores - jnp.max(scores, axis=0, keepdims=True))
    return shifted * (1.0 / jnp.sum(shifted, axis=0, keepdims=True))


def lasting(microseconds):
    return pl.CostEstimate(
        flops=int(microseconds * 1.1e9), bytes_accessed=1 << 10, transcendentals=0
    )


SHIFT_ONE, SCALE_ONE, GATE_ONE, SHIFT_TWO, SCALE_TWO, GATE_TWO, WEIGHT = range(7)


def row_of(mods, which):
    return mods[which : which + 1, :]


def rms(values):
    scale = lax.rsqrt(jnp.mean(values * values, -1, keepdims=True) + epsilon)
    return values * scale, scale


def rms_back(grad, unit, scale, scaling):
    grad = grad * (1.0 + scaling)
    return scale * (grad - unit * jnp.mean(grad * unit, -1, keepdims=True))


def row_sum(values):
    return jnp.sum(values, axis=0, keepdims=True)


def put_rows(sums_ref, image, rows):
    for which in range(sums_ref.shape[1]):
        value = rows.get(which, jnp.zeros((1, sums_ref.shape[2]), f32))
        sums_ref[image, which : which + 1, :] = value


def chunk_rows(ref, image):
    return jnp.concatenate([ref[chunk, image] for chunk in range(ref.shape[0])], axis=0)


def put_chunks(ref, image, values):
    size = ref.shape[2]
    for chunk in range(ref.shape[0]):
        ref[chunk, image] = values[chunk * size : (chunk + 1) * size]


def attend_kernel(
    latent_ref, mods_ref, w_ref, wo_ref, gains_ref, cos_ref, sin_ref,
    proj_ref, att_ref, branch_ref, xt_ref, middle_ref, two_ref, twot_ref, x_ref,
):
    own = mods_ref.shape[0]
    head_dim = gains_ref.shape[1]
    rows_all = att_ref.shape[1]
    length = xt_ref.shape[1] // own
    heads = range(rows_all // head_dim)
    cut = feature_order(head_dim)[1]
    group = pl.program_id(0)

    def place(image):
        return pl.ds(pl.multiple_of(image * length, length), length)

    @pl.when(group == 0)
    def _():
        def entry(image, carry):
            mods = mods_ref[image]
            unit = rms(chunk_rows(latent_ref, image).astype(f32))[0]
            x = (unit * (1.0 + row_of(mods, SCALE_ONE)) + row_of(mods, SHIFT_ONE)).astype(bf16)
            x_ref[place(image), :] = x
            xt_ref[:, place(image)] = x.T
            return carry

        lax.fori_loop(0, own, entry, 0)

    proj_ref[0] = dot_11(w_ref[0, : 3 * rows_all], x_ref[...])

    def heads_of(image, carry):
        tokens = place(image)
        cos_tab, sin_tab = cos_ref[...], sin_ref[...]
        lows = [[], [], []]
        for kind in range(2):
            for head in heads:
                start = kind * rows_all + head * head_dim
                raw = proj_ref[0, start : start + head_dim, tokens]
                scaled = raw * head_scale(raw) * gains_ref[kind]
                turned = scaled * cos_tab + partner(scaled, cut) * sin_tab
                lows[kind].append(turned.astype(bf16))
        for head in heads:
            start = 2 * rows_all + head * head_dim
            lows[2].append(proj_ref[0, start : start + head_dim, tokens].astype(bf16))
        scores = [dot_00(lows[1][head], lows[0][head]) for head in heads]
        probs = [softmax_first(score).astype(bf16) for score in scores]
        outs = [dot_10(lows[2][head], probs[head]) for head in heads]
        att_ref[group, :, tokens] = jnp.concatenate(outs, axis=0).astype(bf16)
        return carry

    lax.fori_loop(0, own, heads_of, 0, unroll=True)

    @pl.when(group == pl.num_programs(0) - 1)
    def _():
        groups = att_ref.shape[0]

        def leave(image, carry):
            tokens = place(image)
            mods = mods_ref[image]
            att = att_ref[:, :, tokens].reshape(groups * rows_all, length)
            branch = dot_00(att, wo_ref[...].reshape(groups * rows_all, -1))
            branch_ref[tokens, :] = branch.astype(bf16)
            latent = chunk_rows(latent_ref, image).astype(f32)
            middle = latent + row_of(mods, GATE_ONE) * branch
            middle_ref[tokens, :] = middle
            two = rms(middle)[0] * (1.0 + row_of(mods, SCALE_TWO)) + row_of(mods, SHIFT_TWO)
            two = two.astype(bf16)
            two_ref[tokens, :] = two
            twot_ref[:, tokens] = two.T
            return carry

        lax.fori_loop(0, own, leave, 0)


def attend_back_kernel(
    latent_ref, proj_ref, low_ref, w_ref, gains_ref, cos_ref, sin_ref, grad_ref, mods_ref,
    out_ref, gain_grad_ref, sums_ref, chunks_ref, cot_ref,
):
    own = mods_ref.shape[0]
    head_dim = gains_ref.shape[1]
    rows_all, tokens_all = proj_ref.shape[1] // 3, proj_ref.shape[2]
    length = tokens_all // own
    heads = range(rows_all // head_dim)
    cut = feature_order(head_dim)[1]
    group = pl.program_id(0)

    def place(image):
        return pl.ds(pl.multiple_of(image * length, length), length)

    @pl.when(group == 0)
    def _():
        gain_grad_ref[...] = jnp.zeros_like(gain_grad_ref)

    cot_ref[...] = dot_11(w_ref[group, 3 * rows_all :], low_ref[...])

    def heads_of(image, carry):
        tokens = place(image)
        cos_tab, sin_tab = cos_ref[...], sin_ref[...]
        lows, units, scales = [[], [], []], [[], []], [[], []]
        for kind in range(2):
            for head in heads:
                start = kind * rows_all + head * head_dim
                raw = proj_ref[0, start : start + head_dim, tokens]
                scale = head_scale(raw)
                unit = raw * scale
                scaled = unit * gains_ref[kind]
                turned = scaled * cos_tab + partner(scaled, cut) * sin_tab
                lows[kind].append(turned.astype(bf16))
                units[kind].append(unit)
                scales[kind].append(scale)
        cots = []
        for head in heads:
            start = 2 * rows_all + head * head_dim
            lows[2].append(proj_ref[0, start : start + head_dim, tokens].astype(bf16))
            cots.append(cot_ref[head * head_dim : (head + 1) * head_dim, tokens].astype(bf16))
        scores = [dot_00(lows[1][head], lows[0][head]) for head in heads]
        prob_grads = [dot_00(lows[2][head], cots[head]) for head in heads]
        probs = [softmax_first(score) for score in scores]
        outs = [[], [], []]
        outs[2] = [dot_11(cots[head], probs[head].astype(bf16)) for head in heads]
        score_lows = []
        for head in heads:
            mean = jnp.sum(probs[head] * prob_grads[head], axis=0, keepdims=True)
            score_lows.append((probs[head] * (prob_grads[head] - mean)).astype(bf16))
        turned_grads = [
            [dot_10(lows[1][head], score_lows[head]) for head in heads],
            [dot_11(lows[0][head], score_lows[head]) for head in heads],
        ]
        for kind in range(2):
            total = 0.0
            for head in heads:
                grad, unit = turned_grads[kind][head], units[kind][head]
                grad = grad * cos_tab + partner(grad * sin_tab, cut)
                total = total + grad * unit
                grad = grad * gains_ref[kind]
                along = jnp.mean(grad * unit, axis=0, keepdims=True)
                outs[kind].append(scales[kind][head] * (grad - unit * along))
            gain_grad_ref[kind] += total
        grads = jnp.concatenate(outs[0] + outs[1] + outs[2], axis=0).astype(bf16)
        out_ref[group, :, tokens] = grads
        return carry

    lax.fori_loop(0, own, heads_of, 0, unroll=True)

    @pl.when(group == pl.num_programs(0) - 1)
    def _():
        def leave(image, carry):
            tokens = place(image)
            mods = mods_ref[image]
            grad = 0.0
            for other in range(out_ref.shape[0]):
                grad = grad + dot_00(out_ref[other, :, tokens], w_ref[other, : 3 * rows_all])
            unit, scale = rms(chunk_rows(latent_ref, image).astype(f32))
            sums = {SHIFT_ONE: row_sum(grad), SCALE_ONE: row_sum(grad * unit)}
            put_rows(sums_ref, image, sums)
            grad = grad_ref[tokens, :] + rms_back(grad, unit, scale, row_of(mods, SCALE_ONE))
            put_chunks(chunks_ref, image, grad.astype(bf16))
            return carry

        lax.fori_loop(0, own, leave, 0)


def whole_spec(shape):
    return pl.BlockSpec(shape, lambda g: (0,) * len(shape), pipeline_mode=pl.Buffered(1))


def attend(latent, mods, weights, gains, tables):
    groups, rows, width = weights.shape[0], weights.shape[1] // 4, weights.shape[2]
    own = mods.shape[0]
    length, head_dim = tables[0].shape[1], gains.shape[1]
    tokens = own * length
    total, turned = (tokens, width), (width, tokens)
    const = lambda shape: pl.BlockSpec(shape, lambda g: (0,) * len(shape))
    return pl.pallas_call(
        attend_kernel,
        grid=(groups,),
        in_specs=[
            whole_spec(latent.shape),
            whole_spec(mods.shape),
            pl.BlockSpec((1, 4 * rows, width), lambda g: (g, 0, 0)),
            pl.BlockSpec((groups, rows, width), lambda g: (0, 3, 0), pipeline_mode=pl.Buffered(1)),
            whole_spec(gains.shape),
            whole_spec(tables[0].shape),
            whole_spec(tables[0].shape),
        ],
        out_specs=[
            pl.BlockSpec((1, 3 * rows, tokens), lambda g: (g, 0, 0)),
            const((groups, rows, tokens)),
            const(total),
            const(turned),
            const(total),
            const(total),
            const(turned),
        ],
        out_shape=[
            jax.ShapeDtypeStruct((groups, 3 * rows, tokens), f32),
            jax.ShapeDtypeStruct((groups, rows, tokens), bf16),
            jax.ShapeDtypeStruct(total, bf16),
            jax.ShapeDtypeStruct(turned, bf16),
            jax.ShapeDtypeStruct(total, f32),
            jax.ShapeDtypeStruct(total, bf16),
            jax.ShapeDtypeStruct(turned, bf16),
        ],
        scratch_shapes=[pltpu.VMEM(total, bf16)],
        compiler_params=pltpu.CompilerParams(vmem_limit_bytes=62 << 20),
        cost_estimate=lasting(160),
        name="attend",
    )(latent, mods, weights, weights, gains, *tables)


def attend_back(latent, proj, low, weights, gains, tables, grad, mods):
    groups, rows, width = weights.shape[0], weights.shape[1] // 4, weights.shape[2]
    own = mods.shape[0]
    tokens = low.shape[0]
    length, head_dim = tokens // own, gains.shape[1]
    const = lambda shape: pl.BlockSpec(shape, lambda g: (0,) * len(shape))
    gain_shape = (2, head_dim, length)
    return pl.pallas_call(
        attend_back_kernel,
        grid=(groups,),
        in_specs=[
            whole_spec(latent.shape),
            pl.BlockSpec((1, 3 * rows, tokens), lambda g: (g, 0, 0)),
            whole_spec(low.shape),
            whole_spec(weights.shape),
            whole_spec(gains.shape),
            whole_spec(tables[0].shape),
            whole_spec(tables[0].shape),
            whole_spec(grad.shape),
            whole_spec(mods.shape),
        ],
        out_specs=[const(proj.shape), const(gain_shape), const(mods.shape), const(latent.shape)],
        out_shape=[
            jax.ShapeDtypeStruct(proj.shape, bf16),
            jax.ShapeDtypeStruct(gain_shape, f32),
            jax.ShapeDtypeStruct(mods.shape, f32),
            jax.ShapeDtypeStruct(latent.shape, bf16),
        ],
        scratch_shapes=[pltpu.VMEM((rows, tokens), f32)],
        compiler_params=pltpu.CompilerParams(vmem_limit_bytes=62 << 20),
        cost_estimate=lasting(1),
        name="attend_back",
    )(latent, proj, low, weights, gains, *tables, grad, mods)


def finish_kernel(
    branch_ref, middle_ref, cot_ref, mods_ref, low_ref, lowt_ref, chunks_ref, sums_ref
):
    branch, mods = branch_ref[...], mods_ref[0]
    gate = row_of(mods, GATE_TWO)
    result = (middle_ref[...] + gate * branch).astype(bf16)
    put_chunks(chunks_ref, 0, result)
    cot = chunk_rows(cot_ref, 0).astype(f32) * row_of(mods, WEIGHT)
    low = (gate * cot).astype(bf16)
    low_ref[...] = low
    lowt_ref[...] = low.T
    put_rows(sums_ref, 0, {GATE_TWO: row_sum(cot * branch)})


def middle_kernel(
    one_ref, other_ref, middle_ref, branch_ref, cot_ref, mods_ref,
    grad_ref, low_ref, lowt_ref, sums_ref,
):
    mods = mods_ref[0]
    grad = one_ref[...] + other_ref[...]
    unit, scale = rms(middle_ref[...])
    sums = {SHIFT_TWO: row_sum(grad), SCALE_TWO: row_sum(grad * unit)}
    cot = chunk_rows(cot_ref, 0).astype(f32) * row_of(mods, WEIGHT)
    grad = cot + rms_back(grad, unit, scale, row_of(mods, SCALE_TWO))
    grad_ref[...] = grad
    low = (row_of(mods, GATE_ONE) * grad).astype(bf16)
    low_ref[...] = low
    lowt_ref[...] = low.T
    sums[GATE_ONE] = row_sum(grad * branch_ref[...].astype(f32))
    put_rows(sums_ref, 0, sums)


def by_image(kernel, name, microseconds, rows, chunks, mods, outs):
    own, sums, width = mods.shape
    tokens = rows[0].shape[0]
    length = tokens // own
    block = pl.BlockSpec((length, width), lambda i: (i, 0))
    turned = pl.BlockSpec((width, length), lambda i: (0, i))
    chunk = pl.BlockSpec((chunks.shape[0], 1) + chunks.shape[2:], lambda i: (0, i, 0, 0))
    whole = pl.BlockSpec((1, sums, width), lambda i: (i, 0, 0))
    specs, shapes = [], []
    for out in outs:
        if out is True:
            specs.append(turned)
            shapes.append(jax.ShapeDtypeStruct((width, tokens), bf16))
        elif out is False:
            specs.append(chunk)
            shapes.append(jax.ShapeDtypeStruct(chunks.shape, bf16))
        else:
            specs.append(block)
            shapes.append(jax.ShapeDtypeStruct((tokens, width), out))
    return pl.pallas_call(
        kernel,
        grid=(own,),
        in_specs=[block] * len(rows) + [chunk, whole],
        out_specs=specs + [whole],
        out_shape=shapes + [jax.ShapeDtypeStruct(mods.shape, f32)],
        compiler_params=pltpu.CompilerParams(vmem_limit_bytes=60 << 20),
        cost_estimate=lasting(microseconds),
        name=name,
    )(*rows, chunks, mods)


def modulate_kernel(silu_ref, ada_ref, out_ref):
    out_ref[0] = dot_10(silu_ref[...], ada_ref[0])


def modulate(silu, ada):
    kinds, width = ada.shape[:2]
    return pl.pallas_call(
        modulate_kernel,
        grid=(kinds,),
        in_specs=[
            pl.BlockSpec(silu.shape, lambda k: (0, 0)),
            pl.BlockSpec((1, width, width), lambda k: (k, 0, 0)),
        ],
        out_specs=pl.BlockSpec((1,) + silu.shape, lambda k: (k, 0, 0)),
        out_shape=jax.ShapeDtypeStruct((kinds,) + silu.shape, f32),
        compiler_params=pltpu.CompilerParams(vmem_limit_bytes=60 << 20),
        cost_estimate=lasting(60),
        name="modulate",
    )(silu, ada)


def add_rows(out_ref, part, first, index, length):
    rows = pl.ds(pl.multiple_of(index * length, length), length)

    @pl.when(first)
    def _():
        out_ref[rows, :] = part

    @pl.when(jnp.logical_not(first))
    def _():
        out_ref[rows, :] += part


def sigmoid(values):
    return 1.0 / (1.0 + jnp.exp(-values))


def mlp_kernel(count, e_ref, x_ref, *refs):
    first = pl.program_id(0) == 0
    save_ref, out_ref, w_ref = refs[count:]
    unit = min(ref.shape[2] for ref in refs[:count])
    for index, ref in enumerate(refs[:count]):
        rows = pl.ds(pl.multiple_of(e_ref[index] * unit, unit), ref.shape[2])
        for kind in range(3):
            w_ref[0, kind, rows, :] = ref[0, kind]
    x = x_ref[...]
    gate = dot_11(x, w_ref[0, 0])
    up = dot_11(x, w_ref[0, 1])
    save_ref[0, 0] = gate.astype(bf16)
    save_ref[0, 1] = up.astype(bf16)
    hidden = (gate * sigmoid(gate) * up).astype(bf16)
    part = dot_10(hidden, w_ref[0, 2])
    add_rows(out_ref, part, first, 0, x.shape[0])


def mlp(x, order, pieces):
    groups, _, _, width = pieces[0].shape
    units, tokens = sum(piece.shape[2] for piece in pieces), x.shape[0]
    return pl.pallas_call(
        functools.partial(mlp_kernel, len(pieces)),
        grid_spec=pltpu.PrefetchScalarGridSpec(
            num_scalar_prefetch=1,
            grid=(groups,),
            in_specs=[pl.BlockSpec((tokens, width), lambda g, e: (0, 0), pipeline_mode=pl.Buffered(1))]
            + [pl.BlockSpec((1,) + piece.shape[1:], lambda g, e: (g, 0, 0, 0)) for piece in pieces],
            out_specs=[
                pl.BlockSpec((1, 2, tokens, units), lambda g, e: (g, 0, 0, 0)),
                pl.BlockSpec((tokens, width), lambda g, e: (0, 0)),
                pl.BlockSpec((1, 3, units, width), lambda g, e: (g, 0, 0, 0)),
            ],
        ),
        out_shape=[
            jax.ShapeDtypeStruct((groups, 2, tokens, units), bf16),
            jax.ShapeDtypeStruct((tokens, width), f32),
            jax.ShapeDtypeStruct((groups, 3, units, width), bf16),
        ],
        compiler_params=pltpu.CompilerParams(vmem_limit_bytes=62 << 20),
        cost_estimate=lasting(1),
        name="mlp",
    )(order, x, *pieces)


def fill_rows(order_ref, source_ref, target_ref, base=0):
    blocks, rows = source_ref.shape[0], source_ref.shape[1]
    for place in range(blocks):
        target_ref[place * rows : (place + 1) * rows, :] = source_ref[order_ref[base + place]]


def mlp_back_kernel(
    e_ref, xt_ref, lowt_ref, low_ref, save_ref, w_ref,
    keep_ref, send_ref, two_ref, xs, lows, parts,
):
    first = pl.program_id(0) == 0
    tokens, width = low_ref.shape
    step = math.gcd(tokens, 512)

    @pl.when(first)
    def _():
        fill_rows(e_ref, xt_ref, xs)
        fill_rows(e_ref, lowt_ref, lows)

    for index in range(tokens // step):
        rows = pl.ds(index * step, step)
        hidden_grad = dot_11(low_ref[rows, :], w_ref[0, 2])
        gate = save_ref[0, 0, rows, :].astype(f32)
        up = save_ref[0, 1, rows, :].astype(f32)
        sig = sigmoid(gate)
        swish = gate * sig
        gate_low = (hidden_grad * up * (sig + swish * (1.0 - sig))).astype(bf16)
        up_low = (hidden_grad * swish).astype(bf16)
        parts[0, rows, :] = gate_low
        parts[1, rows, :] = up_low
        parts[2, rows, :] = (swish * up).astype(bf16)
        part = dot_10(gate_low, w_ref[0, 0]) + dot_10(up_low, w_ref[0, 1])
        add_rows(two_ref, part, first, index, step)

    half = width // 2
    for out_ref, rows in ((keep_ref, slice(0, half)), (send_ref, slice(half, width))):
        x_rows = xs[rows, :]
        for kind in range(2):
            out_ref[0, kind] = dot_10(x_rows, parts[kind]).astype(bf16)
        out_ref[0, 2] = dot_10(lows[rows, :], parts[2]).astype(bf16)


def mlp_back(which, e_order, xt, lowt, low, save, weights):
    groups, _, units, width = weights.shape
    tokens = low.shape[0]
    blocks = groups // 2
    base = which * blocks
    once = pl.Buffered(1)
    whole = lambda p, e: (0, 0)
    whole3 = lambda p, e: (0, 0, 0)
    half = jax.ShapeDtypeStruct((blocks, 3, width // 2, units), bf16)
    half_spec = pl.BlockSpec((1, 3, width // 2, units), lambda p, e: (p, 0, 0, 0))
    return pl.pallas_call(
        mlp_back_kernel,
        grid_spec=pltpu.PrefetchScalarGridSpec(
            num_scalar_prefetch=1,
            grid=(blocks,),
            in_specs=[
                pl.BlockSpec(xt.shape, whole3, pipeline_mode=once),
                pl.BlockSpec(lowt.shape, whole3, pipeline_mode=once),
                pl.BlockSpec((tokens, width), whole, pipeline_mode=once),
                pl.BlockSpec((1, 2, tokens, units), lambda p, e: (base + p, 0, 0, 0)),
                pl.BlockSpec((1, 3, units, width), lambda p, e: (base + p, 0, 0, 0)),
            ],
            out_specs=[half_spec, half_spec, pl.BlockSpec((tokens, width), whole)],
            scratch_shapes=[
                pltpu.VMEM((width, tokens), bf16),
                pltpu.VMEM((width, tokens), bf16),
                pltpu.VMEM((3, tokens, units), bf16),
            ],
        ),
        out_shape=[half, half, jax.ShapeDtypeStruct((tokens, width), f32)],
        compiler_params=pltpu.CompilerParams(vmem_limit_bytes=62 << 20),
        cost_estimate=lasting(150),
        name="mlp_back",
    )(e_order, xt, lowt, low, save, weights)


def attend_grads_kernel(
    m_ref, e_ref, xt_ref, lowt_ref, proj_ref, att_ref, keep_ref, send_ref, xs, lows
):
    first = pl.num_programs(0) // 2 == pl.program_id(0)
    base = jnp.where(first, xt_ref.shape[0], 0)

    @pl.when(first | (pl.program_id(0) == 0))
    def _():
        fill_rows(e_ref, xt_ref, xs, base)
        fill_rows(e_ref, lowt_ref, lows, base)

    width = xs.shape[0]
    half = width // 2
    columns = proj_ref.shape[1]

    for out_ref, rows in ((keep_ref, slice(0, half)), (send_ref, slice(half, width))):
        out_ref[0, :, :columns] = dot_11(xs[rows, :], proj_ref[0]).astype(bf16)
        out_ref[0, :, columns:] = dot_11(lows[rows, :], att_ref[0]).astype(bf16)


def attend_grads(m_order, e_orders, xt, lowt, proj, att):
    rows, tokens = att.shape[1:]
    width = xt.shape[0] * xt.shape[1]
    blocks = m_order.shape[0]
    whole3 = lambda p, m, e: (0, 0, 0)
    half = jax.ShapeDtypeStruct((blocks, width // 2, 4 * rows), bf16)
    half_spec = pl.BlockSpec((1, width // 2, 4 * rows), lambda p, m, e: (p, 0, 0))
    return pl.pallas_call(
        attend_grads_kernel,
        grid_spec=pltpu.PrefetchScalarGridSpec(
            num_scalar_prefetch=2,
            grid=(blocks,),
            in_specs=[
                pl.BlockSpec(xt.shape, whole3, pipeline_mode=pl.Buffered(1)),
                pl.BlockSpec(lowt.shape, whole3, pipeline_mode=pl.Buffered(1)),
                pl.BlockSpec((1, 3 * rows, tokens), lambda p, m, e: (m[p], 0, 0)),
                pl.BlockSpec((1, rows, tokens), lambda p, m, e: (m[p], 0, 0)),
            ],
            out_specs=[half_spec, half_spec],
            scratch_shapes=[
                pltpu.VMEM((width, tokens), bf16),
                pltpu.VMEM((width, tokens), bf16),
            ],
        ),
        out_shape=[half, half],
        compiler_params=pltpu.CompilerParams(vmem_limit_bytes=56 << 20),
        cost_estimate=lasting(0),
        name="attend_grads",
    )(m_order, e_orders, xt, lowt, proj, att)


def dot(a, b):
    return jnp.dot(a, b, preferred_element_type=f32)


def ein(spec, a, b):
    return jnp.einsum(spec, a, b, preferred_element_type=f32)


def gather_pieces(piece, mp_size):
    whole = lax.all_gather(piece, ("mp", "dp"), axis=0, tiled=False)
    return whole.reshape((mp_size, -1) + piece.shape)


def take_rows(values, index):
    return values.at[index].get(mode="promise_in_bounds")


def sum_quarters_kernel(kept_ref, got_ref, *out_refs):
    total = (kept_ref[0].astype(f32) + got_ref[0].astype(f32)).astype(bf16)
    half = total.shape[0] // 2
    later = pl.program_id(0) >= pl.num_programs(0) // 2

    @pl.when(jnp.logical_not(later))
    def _():
        out_refs[0][0] = total[:half]
        out_refs[1][0] = total[half:]

    @pl.when(later)
    def _():
        out_refs[2][0] = total[:half]
        out_refs[3][0] = total[half:]


def sum_quarters(kept, got):
    groups, rows, columns = kept.shape
    if rows % 32:
        halves = split(add_low(kept, got), 0)
        return split(halves[0], 1) + split(halves[1], 1)
    part = groups // 2
    whole = pl.BlockSpec((1, rows, columns), lambda i: (i, 0, 0))
    block = (1, rows // 2, columns)
    early = pl.BlockSpec(block, lambda i: (jnp.minimum(i, part - 1), 0, 0))
    late = pl.BlockSpec(block, lambda i: (jnp.maximum(i - part, 0), 0, 0))
    return pl.pallas_call(
        sum_quarters_kernel,
        grid=(groups,),
        in_specs=[whole, whole],
        out_specs=[early, early, late, late],
        out_shape=[jax.ShapeDtypeStruct((part, rows // 2, columns), bf16)] * 4,
        compiler_params=pltpu.CompilerParams(vmem_limit_bytes=60 << 20),
        cost_estimate=lasting(0),
        name="sum_quarters",
    )(kept, got)


def whole_arrays(kernel, name, microseconds, shape, *arrays):
    specs = [pl.BlockSpec(array.shape, functools.partial(lambda n: (0,) * n, array.ndim)) for array in arrays]
    return pl.pallas_call(
        kernel,
        in_specs=specs,
        out_specs=pl.BlockSpec(shape, lambda: (0,) * len(shape)),
        out_shape=jax.ShapeDtypeStruct(shape, bf16),
        compiler_params=pltpu.CompilerParams(vmem_limit_bytes=60 << 20),
        cost_estimate=lasting(microseconds),
        name=name,
    )(*arrays)


def append_zero_kernel(value_ref, out_ref):
    count = value_ref.shape[0]
    out_ref[:count] = value_ref[...]
    out_ref[count:] = jnp.zeros_like(out_ref[count:])


def append_zero(values, microseconds):
    shape = (values.shape[0] + 1,) + values.shape[1:]
    return whole_arrays(append_zero_kernel, "append_zero", microseconds, shape, values)


def append_kernel(one_ref, other_ref, out_ref):
    count = one_ref.shape[0]
    out_ref[:count] = one_ref[...]
    out_ref[count:] = other_ref[...]


def append(one, other, microseconds):
    shape = (2 * one.shape[0],) + one.shape[1:]
    return whole_arrays(append_kernel, "append", microseconds, shape, one, other)


def bits_of(size):
    return [1 << i for i in range(size.bit_length() - 1)]


def swap(values, axis, bit):
    size = lax.axis_size(axis)
    return lax.ppermute(values, axis, [(i, i ^ bit) for i in range(size)])


def xor_gather(values, axes_bits):
    names = sorted({axis for axis, _ in axes_bits})
    places = [{name: 0 for name in names}]
    values = values[None]
    for axis, bit in axes_bits:
        values = jnp.concatenate([values, swap(values, axis, bit)], axis=0)
        places = places + [dict(place, **{axis: place[axis] ^ bit}) for place in places]
    return values, {name: [place[name] for place in places] for name in names}


def halving_order(bits):
    order = [0]
    for bit in reversed(bits):
        order = order + [place ^ bit for place in order]
    return order


def add_low(kept, received):
    return (kept.astype(f32) + received.astype(f32)).astype(bf16)


def sum_halves_kernel(kept_ref, got_ref, first_ref, second_ref):
    total = (kept_ref[0].astype(f32) + got_ref[0].astype(f32)).astype(bf16)
    half = first_ref.shape[1]
    first_ref[0] = total[:half]
    second_ref[0] = total[half:]


def sum_halves(kept, got, microseconds=0):
    rows, columns = kept.shape[-2:]
    if rows % 32:
        return split(add_low(kept, got), kept.ndim - 2)
    shape = kept.shape[:-2] + (rows // 2, columns)
    kept, got = kept.reshape(-1, rows, columns), got.reshape(-1, rows, columns)
    whole = pl.BlockSpec((1, rows, columns), lambda i: (i, 0, 0))
    half = pl.BlockSpec((1, rows // 2, columns), lambda i: (i, 0, 0))
    halves = pl.pallas_call(
        sum_halves_kernel,
        grid=(kept.shape[0],),
        in_specs=[whole, whole],
        out_specs=[half, half],
        out_shape=[jax.ShapeDtypeStruct((kept.shape[0], rows // 2, columns), bf16)] * 2,
        compiler_params=pltpu.CompilerParams(vmem_limit_bytes=60 << 20),
        cost_estimate=lasting(microseconds),
        name="sum_halves",
    )(kept, got)
    return halves[0].reshape(shape), halves[1].reshape(shape)


def tie(*values):
    return lax.optimization_barrier(values)


def split(values, dim):
    size = values.shape[dim] // 2
    return (
        lax.slice_in_dim(values, 0, size, axis=dim),
        lax.slice_in_dim(values, size, 2 * size, axis=dim),
    )


def halve(values, axis, bits, dim):
    for bit in bits:
        kept, sent = split(values, dim)
        values = add_low(kept, swap(sent, axis, bit))
    return values


def shards(
    patches,
    cotangent,
    time_bins,
    labels,
    image_counts,
    dest_perm,
    time_table,
    class_table,
    ada_weight,
    qkv_weight,
    norm_gains,
    out_weight,
    expand_weight,
    down_weight,
):
    dp_size = lax.axis_size("dp")
    mp_size = lax.axis_size("mp")
    capacity = patches.shape[0]
    slot_count = capacity // dp_size
    images = cotangent.shape[0]
    local_len = patches.shape[1]
    model_width = patches.shape[2]
    length = local_len * mp_size
    head_dim = norm_gains.shape[1]
    local_dim = out_weight.shape[0]
    unit_count = down_weight.shape[0]
    own = images // mp_size
    total_images = images * dp_size
    order = np.array(feature_order(head_dim)[0])
    columns = np.arange(4 * local_dim)
    places = columns // head_dim * head_dim + order[columns % head_dim]
    places = np.where(columns < 2 * local_dim, places, columns).astype(np.int32)
    gains_f = norm_gains.astype(f32)[:, order]
    gains_f = (gains_f * jnp.array([[head_dim ** (-0.5)], [1.0]], f32))[:, :, None]
    dp_index = lax.axis_index("dp")
    mp_index = lax.axis_index("mp")
    dp_bits = bits_of(dp_size)
    dp_bits = (dp_bits, dp_bits[:1] + dp_bits[1:][::-1])
    mp_bits = bits_of(mp_size)

    tables = rope_tables(jnp.arange(length), head_dim)

    def turn(chunks):
        return lax.all_to_all(chunks, "mp", split_axis=0, concat_axis=0, tiled=True)

    starts = jnp.cumsum(image_counts) - image_counts
    finish = starts + image_counts
    my_start = starts[dp_index]
    my_count = image_counts[dp_index]
    device_ids = jnp.arange(dp_size)
    matches = (dest_perm[:, None] == device_ids[None, :]).astype(jnp.int32)
    inverse = jnp.sum(device_ids[:, None] * matches, axis=0)
    my_place = inverse[dp_index]
    pair_ids = jnp.arange(dp_size * slot_count)
    pair_peer = pair_ids // slot_count
    pair_slot = pair_ids % slot_count
    send_index = pair_slot * dp_size + jnp.mod(inverse[pair_peer] - my_start, dp_size)
    send_index = jnp.minimum(send_index, capacity - 1)
    send_patches = take_rows(patches, send_index)
    info, info_places = xor_gather(
        jnp.stack([time_bins, labels]), [("dp", bit) for bit in bits_of(dp_size)]
    )
    send_patches, info = tie(send_patches, info)
    share = 4 * local_dim // dp_size
    spots = lax.dynamic_slice_in_dim(jnp.array(places), dp_index * share, share, 0)
    take_qkv = (spots[:, None] == jnp.arange(3 * local_dim)[None, :]).astype(bf16)
    take_out = (spots[:, None] - 3 * local_dim == jnp.arange(local_dim)[None, :]).astype(bf16)
    attend_piece = dot(take_qkv, qkv_weight.transpose(1, 2, 0).reshape(-1, model_width))
    attend_piece = (attend_piece + dot(take_out, out_weight)).astype(bf16)
    share = unit_count // dp_size
    spots = dp_index * share + jnp.arange(share)
    take_units = (spots[:, None] == jnp.arange(unit_count)[None, :]).astype(bf16)
    mlp_piece = jnp.stack(
        [
            ein("rf,df->rd", take_units, expand_weight[:, 0]).astype(bf16),
            ein("rf,df->rd", take_units, expand_weight[:, 1]).astype(bf16),
            lax.dynamic_slice_in_dim(down_weight, dp_index * share, share, 0),
        ]
    )
    attend_full = gather_pieces(attend_piece, mp_size).reshape(mp_size, 4 * local_dim, -1)
    by_permutes = share % 32 == 0 and dp_size == 8 and mp_size == 4
    if by_permutes:
        mlp_near = mlp_piece[None]
        far_near = swap(mlp_near, "mp", 2)
    else:
        mlp_full = gather_pieces(mlp_piece, mp_size)
        mlp_full = mlp_full.swapaxes(1, 2).reshape(mp_size, 3, unit_count, model_width)
        mlp_pieces = [mlp_full[mp_index ^ jnp.array(halving_order(mp_bits))]]
        mlp_order = jnp.zeros((1,), jnp.int32)

    recv_patches = lax.all_to_all(send_patches, "dp", split_axis=0, concat_axis=0, tiled=True)
    info = info.swapaxes(0, 1).reshape(2, -1)
    info_owner = jnp.repeat(dp_index ^ jnp.array(info_places["dp"]), capacity)
    info_slot = jnp.tile(jnp.arange(capacity), dp_size)
    info_count = jnp.sum(
        jnp.where(info_owner[:, None] == device_ids[None, :], image_counts[None, :], 0), axis=1
    )
    live_all = info_slot < info_count
    bin_totals = jnp.sum(
        ((info[0][:, None] == jnp.arange(NBINS)[None, :]) & live_all[:, None]).astype(f32), axis=0
    )
    gather_bits = [("mp", bit) for bit in mp_bits[::-1]]
    gather_bits = gather_bits + [("dp", bit) for bit in dp_bits[0][1:] + dp_bits[0][:1]]
    spread = {"dp": [0], "mp": [0]}
    for axis, bit in gather_bits:
        spread = {
            name: spread[name] + [place ^ (bit if name == axis else 0) for place in spread[name]]
            for name in spread
        }
    owner_all = jnp.repeat(dp_index ^ jnp.array(spread["dp"]), own)
    group_all = jnp.repeat(mp_index ^ jnp.array(spread["mp"]), own)
    row_all = group_all * own + jnp.tile(jnp.arange(own), dp_size * mp_size)
    place_all = jnp.sum(
        jnp.where(owner_all[:, None] == device_ids[None, :], inverse[None, :], 0), axis=1
    )
    rank_all = row_all * dp_size + place_all
    source_all = jnp.sum((finish[None, :] <= rank_all[:, None]).astype(jnp.int32), axis=1)
    start_all = jnp.sum(
        jnp.where(source_all[:, None] == device_ids[None, :], starts[None, :], 0), axis=1
    )
    slots_all = source_all * capacity + rank_all - start_all
    slot_hit = slots_all[:, None] == (info_owner * capacity + info_slot)[None, :]
    bins_all = jnp.sum(jnp.where(slot_hit, info[0][None, :], 0), axis=1)
    labels_all = jnp.sum(jnp.where(slot_hit, info[1][None, :], 0), axis=1)
    bin_hot = (bins_all[:, None] == jnp.arange(NBINS)[None, :])
    label_hot = (labels_all[:, None] == jnp.arange(NCLS)[None, :])
    weights_all = total_images / (NBINS * jnp.sum(bin_hot.astype(f32) * bin_totals[None, :], axis=1))
    bin_hot = bin_hot.astype(bf16)
    label_hot = label_hot.astype(bf16)
    cond_all = (dot(bin_hot, time_table) + dot(label_hot, class_table)).astype(bf16).astype(f32)
    silu_all = jax.nn.silu(cond_all).astype(bf16)
    silu_cond = silu_all[:own]
    weights = weights_all[:own]

    if by_permutes:
        silu_cond, far_near = tie(silu_cond, far_near)
        mlp_near = jnp.concatenate([mlp_near, far_near], axis=0)
        far_near = swap(mlp_near, "mp", 1)
    ada_kinds = ada_weight.swapaxes(0, 1)
    modulation = modulate(jnp.pad(silu_cond, ((0, -own % 16), (0, 0))), ada_kinds)[:, :own]
    mods = jnp.concatenate(
        [
            modulation.swapaxes(0, 1),
            jnp.broadcast_to(weights[:, None, None], (own, 1, model_width)),
            jnp.zeros((own, 1, model_width), f32),
        ],
        axis=1,
    )
    back_within = pair_slot * dp_size + jnp.mod(my_place - starts[pair_peer], dp_size)
    back_valid = back_within < image_counts[pair_peer]
    back_slot = jnp.clip((starts[pair_peer] + back_within - my_place) // dp_size, 0, images - 1)
    back_slot = jnp.where(back_valid, back_slot, images)
    slot_ids = jnp.arange(capacity)
    home_peer = dest_perm[jnp.mod(my_start + slot_ids, dp_size)]
    home_index = home_peer * slot_count + jnp.minimum(slot_ids // dp_size, slot_count - 1)
    recv_patches, mods, back_slot, home_index = tie(recv_patches, mods, back_slot, home_index)

    rank_ids = jnp.arange(images) * dp_size + my_place
    source = jnp.sum((finish[None, :] <= rank_ids[:, None]).astype(jnp.int32), axis=1)
    within = rank_ids - starts[source]
    recv_index = source * slot_count + within // dp_size
    latent = take_rows(recv_patches, recv_index).reshape(mp_size, own, local_len, model_width)
    if by_permutes:
        far_near, _ = tie(far_near, latent)
    latent = turn(latent)
    if by_permutes:
        mlp_near = jnp.concatenate([mlp_near, far_near], axis=0)
        halves = split(mlp_near, 2)
        orders = ((2, 4), (4, 2))
        parts = [{bit: swap(halves[half], "dp", bit) for bit in orders[half]} for half in range(2)]
        cored = swap(mlp_near, "dp", 1)
        latent, parts[0][2], parts[1][4], cored = tie(latent, parts[0][2], parts[1][4], cored)
        got = [swap(parts[half][orders[half][0]], "dp", orders[half][1]) for half in range(2)]

    cotangent, latent = tie(cotangent, latent)
    proj, attended, branch_one, normed_t, middle, two, two_t = attend(
        latent, mods, attend_full, gains_f, tables
    )
    cot = turn(cotangent.reshape(mp_size, own, local_len, model_width))
    if by_permutes:
        got[0], got[1], attended = tie(got[0], got[1], attended)
        mlp_pieces, mlp_order = [mlp_near, cored], [dp_index * 2, (dp_index ^ 1) * 2]
        for half in range(2):
            parts[half][6] = got[half]
            for near, part in parts[half].items():
                mlp_pieces += [part, swap(part, "dp", 1)]
                mlp_order += [(dp_index ^ near) * 2 + half, (dp_index ^ near ^ 1) * 2 + half]
        mlp_order = jnp.stack(mlp_order).astype(jnp.int32)
    save, branch_two, mlp_full = mlp(two, mlp_order, mlp_pieces)
    branch_two, cot = tie(branch_two, cot)
    down_low, down_t, result, sums_finish = by_image(
        finish_kernel, "finish", 1, (branch_two, middle), cot, mods, (bf16, True, False)
    )
    result = turn(result)

    e_orders = [(dp_index ^ jnp.array(halving_order(bits))).astype(jnp.int32) for bits in dp_bits]
    m_order = (mp_index ^ jnp.array(halving_order(mp_bits))).astype(jnp.int32)

    def by_owner(values):
        return values.reshape(dp_size, model_width // dp_size, -1)

    two_t, down_t = by_owner(two_t), by_owner(down_t)
    kept_one, sent_one, two_one = mlp_back(
        1, e_orders[1], two_t, down_t, down_low, save, mlp_full
    )
    got_one = swap(sent_one, "dp", dp_bits[1][0])
    kept_zero, sent_zero, two_zero = mlp_back(
        0, e_orders[0], two_t, down_t, down_low, save, mlp_full
    )
    got_zero = swap(sent_zero, "dp", dp_bits[0][0])
    kept_one, sent_one = sum_halves(kept_one, got_one)
    kept_zero, sent_zero = sum_halves(kept_zero, got_zero)
    two_zero, kept_one, kept_zero = tie(two_zero, kept_one, kept_zero)
    got_one = swap(sent_one, "dp", dp_bits[1][1])
    got_zero = swap(sent_zero, "dp", dp_bits[0][1])
    middle_grad, branch_low, branch_t, sums_middle = by_image(
        middle_kernel,
        "middle",
        100,
        (two_zero, two_one, middle, branch_one),
        cot,
        mods,
        (f32, bf16, True),
    )
    projected_low, gains_grad, sums_entry, latent_back = attend_back(
        latent, proj, branch_low, attend_full, gains_f, tables, middle_grad, mods
    )
    gains_grad = jnp.sum(gains_grad, axis=2) * jnp.array([[head_dim ** (-0.5)], [1.0]], f32)
    projected_low, got_one, got_zero = tie(projected_low, got_one, got_zero)
    packed = sums_finish + sums_middle + sums_entry
    gains_row = jnp.pad(gains_grad.reshape(1, 1, -1), ((0, own - 1), (7, 0), (0, model_width - 2 * head_dim)))
    packed = jnp.where(jnp.arange(8)[:, None] == 7, gains_row, packed).astype(bf16)
    packed = packed[None]
    stage, got_packed = 0, swap(packed, *gather_bits[0])

    def more(after, microseconds=0):
        nonlocal packed, got_packed, stage
        after, got_packed = tie(after, got_packed)
        packed = append(packed, got_packed, microseconds)
        stage += 1
        if stage < len(gather_bits):
            got_packed = swap(packed, *gather_bits[stage])
        return after

    kept_one, sent_one = sum_halves(kept_one, got_one, 200)
    kept_one = more(kept_one)
    latent_back, packed = tie(latent_back, packed)
    kept_zero, sent_zero = sum_halves(kept_zero, got_zero, 200)
    normed_t, kept_one, kept_zero, result = tie(normed_t, kept_one, kept_zero, result)
    got_one = swap(sent_one, "dp", dp_bits[1][2])
    got_zero = swap(sent_zero, "dp", dp_bits[0][2])
    latent_back = turn(latent_back)

    normed_t, branch_t = by_owner(normed_t), by_owner(branch_t)

    attend_kept, attend_sent = attend_grads(
        m_order, jnp.concatenate(e_orders), normed_t, branch_t, projected_low, attended
    )
    attend_got = swap(attend_sent, "dp", dp_bits[0][0])

    attend_kept, got_one, got_zero, latent_back, got_packed = tie(
        attend_kept, got_one, got_zero, latent_back, got_packed
    )
    attend_kept = more(attend_kept, 200)
    attend_got, packed = tie(attend_got, packed)
    attend_zero, sent_zero, attend_one, sent_one = sum_quarters(attend_kept, attend_got)
    mlp_one = halve(add_low(kept_one, got_one), "dp", dp_bits[1][3:], 2)
    mlp_zero = halve(add_low(kept_zero, got_zero), "dp", dp_bits[0][3:], 2)
    mlp_got = swap(mlp_one, "mp", mp_bits[0])

    latent_back, attend_zero, attend_one = tie(latent_back, attend_zero, attend_one)
    latent_back = append_zero(latent_back.reshape(images, local_len, model_width), 200)
    back_patches = take_rows(latent_back, back_slot)
    attend_got_one = swap(sent_one, "dp", dp_bits[1][1])
    attend_got_zero = swap(sent_zero, "dp", dp_bits[0][1])
    attend_zero = more(attend_zero)
    back_patches, attend_zero, attend_one = tie(back_patches, attend_zero, attend_one)
    attend_zero = more(attend_zero)
    attend_one, sent_one = sum_halves(attend_one, attend_got_one)
    attend_zero, sent_zero = sum_halves(attend_zero, attend_got_zero)
    back_patches, sent_one, sent_zero = tie(back_patches, sent_one, sent_zero)
    got_patches = lax.all_to_all(back_patches, "dp", split_axis=0, concat_axis=0, tiled=True)
    patch_grad = take_rows(got_patches, home_index)
    attend_got_one = swap(sent_one, "dp", dp_bits[1][2])
    attend_got_zero = swap(sent_zero, "dp", dp_bits[0][2])
    while stage < len(gather_bits):
        mlp_zero = more(mlp_zero)
    packed = packed.reshape(total_images, 8, model_width)
    mod_all = packed[:, :6]
    gains_total = packed.reshape(-1, own, 8, model_width)[:, 0, 7, : 2 * head_dim]
    gains_total = jnp.sum(gains_total.astype(f32), axis=0).reshape(2, head_dim)
    gains_total = jnp.sum(
        jnp.where(order[:, None] == jnp.arange(head_dim)[None, :], gains_total[:, :, None], 0.0), axis=1
    )
    width_dp = model_width // dp_size
    width_mp = model_width // mp_size
    row0 = dp_index * width_dp
    silu_rows = lax.dynamic_slice_in_dim(silu_all, row0, width_dp, 1)
    mod_cols = lax.dynamic_slice_in_dim(mod_all, mp_index * width_mp, width_mp, 2)
    ada_grad = ein("id,ikc->dkc", silu_rows, mod_cols)
    ada_rows = lax.dynamic_slice_in_dim(ada_kinds, row0, width_dp, 1)
    silu_grad = ein("ikc,kdc->id", mod_all, ada_rows)
    cond_rows = lax.dynamic_slice_in_dim(cond_all, row0, width_dp, 1)
    silu_val, silu_pull = jax.vjp(jax.nn.silu, cond_rows)
    condition_low = silu_pull(silu_grad)[0].astype(bf16)
    time_grad = ein("in,id->nd", bin_hot, condition_low)
    class_grad = ein("in,id->nd", label_hot, condition_low)

    attend_one = halve(add_low(attend_one, attend_got_one), "dp", dp_bits[1][3:], 1)
    attend_zero = halve(add_low(attend_zero, attend_got_zero), "dp", dp_bits[0][3:], 1)
    mlp_grad = halve(add_low(mlp_zero, mlp_got), "mp", mp_bits[1:], 0)[0].astype(f32)
    attend_grad = add_low(attend_zero, swap(attend_one, "mp", mp_bits[0]))
    attend_grad = halve(attend_grad, "mp", mp_bits[1:], 0)[0].astype(f32)

    expand_grad = mlp_grad[:2].swapaxes(0, 1)
    down_grad = mlp_grad[2].T
    out_grad = attend_grad[:, 3 * local_dim :].T
    qkv_grad = lax.dot_general(
        attend_grad[:, : 3 * local_dim],
        jnp.array(places[: 3 * local_dim, None] == columns[: 3 * local_dim], f32),
        (((1,), (0,)), ((), ())),
        precision=lax.Precision.HIGHEST,
        preferred_element_type=f32,
    )
    qkv_grad = qkv_grad.reshape(-1, 3, local_dim)
    return (
        result.reshape(images, local_len, model_width),
        patch_grad,
        time_grad,
        class_grad,
        ada_grad,
        qkv_grad,
        gains_total,
        out_grad,
        expand_grad,
        down_grad,
    )


def solution(mesh):
    in_specs = (
        P("dp", "mp", None),
        P("dp", "mp", None),
        P("dp"),
        P("dp"),
        P(),
        P(),
        P(),
        P(),
        P(),
        P(None, None, "mp"),
        P(),
        P("mp", None),
        P(None, None, "mp"),
        P("mp", None),
    )
    out_specs = (
        P("dp", "mp", None),
        P("dp", "mp", None),
        P(None, "dp"),
        P(None, "dp"),
        P("dp", None, "mp"),
        P("dp", None, "mp"),
        P(),
        P("mp", "dp"),
        P("dp", None, "mp"),
        P("mp", "dp"),
    )
    return jax.shard_map(shards, mesh=mesh, in_specs=in_specs, out_specs=out_specs, check_vma=False)
```

```python
import functools
import math

import jax
import jax.numpy as jnp
import numpy as np
from jax import lax
from jax.experimental import pallas as pl
from jax.experimental.pallas import tpu as pltpu
from jax.sharding import PartitionSpec as P

GRID = 16
NCLS = 1000
NBINS = 16

epsilon = 1e-06
rope_base = 10000.0
f32 = jnp.float32
bf16 = jnp.bfloat16


def feature_order(head_dim):
    quarter = head_dim // 4
    firsts = list(range(quarter)) + list(range(2 * quarter, 3 * quarter))
    cut = len(firsts) // 8 * 8
    seconds = [i + quarter for i in firsts]
    return firsts[:cut] + seconds[:cut] + firsts[cut:] + seconds[cut:], cut


def rope_tables(position, head_dim):
    quarter = head_dim // 4
    order, cut = feature_order(head_dim)
    places = jnp.stack([position // GRID, position % GRID]).astype(f32)
    frequency = rope_base ** (-jnp.arange(quarter).astype(f32) / quarter)
    angle = (frequency[None, :, None] * places[:, None, :]).reshape(2 * quarter, -1)
    cosine, sine = jnp.cos(angle), jnp.sin(angle)
    cos_tab = jnp.concatenate([cosine[:cut], cosine[:cut], cosine[cut:], cosine[cut:]])
    sin_tab = jnp.concatenate([-sine[:cut], sine[:cut], -sine[cut:], sine[cut:]])
    return cos_tab, sin_tab


def partner(values, cut):
    rest = values[2 * cut :]
    half = rest.shape[0] // 2
    return jnp.concatenate(
        [values[cut : 2 * cut], values[:cut], pltpu.roll(rest, half, 0)], axis=0
    )


def head_scale(values):
    return lax.rsqrt(jnp.mean(values * values, axis=0, keepdims=True) + epsilon)


def dot_00(a, b):
    return lax.dot_general(a, b, (((0,), (0,)), ((), ())), preferred_element_type=f32)


def dot_11(a, b):
    return lax.dot_general(a, b, (((1,), (1,)), ((), ())), preferred_element_type=f32)


def dot_10(a, b):
    return lax.dot_general(a, b, (((1,), (0,)), ((), ())), preferred_element_type=f32)


def softmax_first(scores):
    shifted = jnp.exp(scores - jnp.max(scores, axis=0, keepdims=True))
    return shifted * (1.0 / jnp.sum(shifted, axis=0, keepdims=True))


def lasting(microseconds):
    return pl.CostEstimate(
        flops=int(microseconds * 1.1e9), bytes_accessed=1 << 10, transcendentals=0
    )


SHIFT_ONE, SCALE_ONE, GATE_ONE, SHIFT_TWO, SCALE_TWO, GATE_TWO, WEIGHT = range(7)


def row_of(mods, which):
    return mods[which : which + 1, :]


def rms(values):
    scale = lax.rsqrt(jnp.mean(values * values, -1, keepdims=True) + epsilon)
    return values * scale, scale


def rms_back(grad, unit, scale, scaling):
    grad = grad * (1.0 + scaling)
    return scale * (grad - unit * jnp.mean(grad * unit, -1, keepdims=True))


def row_sum(values):
    return jnp.sum(values, axis=0, keepdims=True)


def put_rows(sums_ref, image, rows):
    for which in range(sums_ref.shape[1]):
        value = rows.get(which, jnp.zeros((1, sums_ref.shape[2]), f32))
        sums_ref[image, which : which + 1, :] = value


def chunk_rows(ref, image):
    return jnp.concatenate([ref[chunk, image] for chunk in range(ref.shape[0])], axis=0)


def put_chunks(ref, image, values):
    size = ref.shape[2]
    for chunk in range(ref.shape[0]):
        ref[chunk, image] = values[chunk * size : (chunk + 1) * size]


def attend_kernel(
    latent_ref, mods_ref, w_ref, wo_ref, gains_ref, cos_ref, sin_ref,
    proj_ref, att_ref, branch_ref, xt_ref, middle_ref, two_ref, twot_ref, x_ref,
):
    own = mods_ref.shape[0]
    head_dim = gains_ref.shape[1]
    rows_all = att_ref.shape[1]
    length = xt_ref.shape[1] // own
    heads = range(rows_all // head_dim)
    cut = feature_order(head_dim)[1]
    group = pl.program_id(0)

    def place(image):
        return pl.ds(pl.multiple_of(image * length, length), length)

    @pl.when(group == 0)
    def _():
        def entry(image, carry):
            mods = mods_ref[image]
            unit = rms(chunk_rows(latent_ref, image).astype(f32))[0]
            x = (unit * (1.0 + row_of(mods, SCALE_ONE)) + row_of(mods, SHIFT_ONE)).astype(bf16)
            x_ref[place(image), :] = x
            xt_ref[:, place(image)] = x.T
            return carry

        lax.fori_loop(0, own, entry, 0)

    proj_ref[0] = dot_11(w_ref[0, : 3 * rows_all], x_ref[...])

    def heads_of(image, carry):
        tokens = place(image)
        cos_tab, sin_tab = cos_ref[...], sin_ref[...]
        lows = [[], [], []]
        for kind in range(2):
            for head in heads:
                start = kind * rows_all + head * head_dim
                raw = proj_ref[0, start : start + head_dim, tokens]
                scaled = raw * head_scale(raw) * gains_ref[kind]
                turned = scaled * cos_tab + partner(scaled, cut) * sin_tab
                lows[kind].append(turned.astype(bf16))
        for head in heads:
            start = 2 * rows_all + head * head_dim
            lows[2].append(proj_ref[0, start : start + head_dim, tokens].astype(bf16))
        scores = [dot_00(lows[1][head], lows[0][head]) for head in heads]
        probs = [softmax_first(score).astype(bf16) for score in scores]
        outs = [dot_10(lows[2][head], probs[head]) for head in heads]
        att_ref[group, :, tokens] = jnp.concatenate(outs, axis=0).astype(bf16)
        return carry

    lax.fori_loop(0, own, heads_of, 0, unroll=True)

    @pl.when(group == pl.num_programs(0) - 1)
    def _():
        groups = att_ref.shape[0]

        def leave(image, carry):
            tokens = place(image)
            mods = mods_ref[image]
            att = att_ref[:, :, tokens].reshape(groups * rows_all, length)
            branch = dot_00(att, wo_ref[...].reshape(groups * rows_all, -1))
            branch_ref[tokens, :] = branch.astype(bf16)
            latent = chunk_rows(latent_ref, image).astype(f32)
            middle = latent + row_of(mods, GATE_ONE) * branch
            middle_ref[tokens, :] = middle
            two = rms(middle)[0] * (1.0 + row_of(mods, SCALE_TWO)) + row_of(mods, SHIFT_TWO)
            two = two.astype(bf16)
            two_ref[tokens, :] = two
            twot_ref[:, tokens] = two.T
            return carry

        lax.fori_loop(0, own, leave, 0)


def attend_back_kernel(
    latent_ref, proj_ref, low_ref, w_ref, gains_ref, cos_ref, sin_ref, grad_ref, mods_ref,
    out_ref, gain_grad_ref, sums_ref, chunks_ref, cot_ref,
):
    own = mods_ref.shape[0]
    head_dim = gains_ref.shape[1]
    rows_all, tokens_all = proj_ref.shape[1] // 3, proj_ref.shape[2]
    length = tokens_all // own
    heads = range(rows_all // head_dim)
    cut = feature_order(head_dim)[1]
    group = pl.program_id(0)

    def place(image):
        return pl.ds(pl.multiple_of(image * length, length), length)

    @pl.when(group == 0)
    def _():
        gain_grad_ref[...] = jnp.zeros_like(gain_grad_ref)

    cot_ref[...] = dot_11(w_ref[group, 3 * rows_all :], low_ref[...])

    def heads_of(image, carry):
        tokens = place(image)
        cos_tab, sin_tab = cos_ref[...], sin_ref[...]
        lows, units, scales = [[], [], []], [[], []], [[], []]
        for kind in range(2):
            for head in heads:
                start = kind * rows_all + head * head_dim
                raw = proj_ref[0, start : start + head_dim, tokens]
                scale = head_scale(raw)
                unit = raw * scale
                scaled = unit * gains_ref[kind]
                turned = scaled * cos_tab + partner(scaled, cut) * sin_tab
                lows[kind].append(turned.astype(bf16))
                units[kind].append(unit)
                scales[kind].append(scale)
        cots = []
        for head in heads:
            start = 2 * rows_all + head * head_dim
            lows[2].append(proj_ref[0, start : start + head_dim, tokens].astype(bf16))
            cots.append(cot_ref[head * head_dim : (head + 1) * head_dim, tokens].astype(bf16))
        scores = [dot_00(lows[1][head], lows[0][head]) for head in heads]
        prob_grads = [dot_00(lows[2][head], cots[head]) for head in heads]
        probs = [softmax_first(score) for score in scores]
        outs = [[], [], []]
        outs[2] = [dot_11(cots[head], probs[head].astype(bf16)) for head in heads]
        score_lows = []
        for head in heads:
            mean = jnp.sum(probs[head] * prob_grads[head], axis=0, keepdims=True)
            score_lows.append((probs[head] * (prob_grads[head] - mean)).astype(bf16))
        turned_grads = [
            [dot_10(lows[1][head], score_lows[head]) for head in heads],
            [dot_11(lows[0][head], score_lows[head]) for head in heads],
        ]
        for kind in range(2):
            total = 0.0
            for head in heads:
                grad, unit = turned_grads[kind][head], units[kind][head]
                grad = grad * cos_tab + partner(grad * sin_tab, cut)
                total = total + grad * unit
                grad = grad * gains_ref[kind]
                along = jnp.mean(grad * unit, axis=0, keepdims=True)
                outs[kind].append(scales[kind][head] * (grad - unit * along))
            gain_grad_ref[kind] += total
        grads = jnp.concatenate(outs[0] + outs[1] + outs[2], axis=0).astype(bf16)
        out_ref[group, :, tokens] = grads
        return carry

    lax.fori_loop(0, own, heads_of, 0, unroll=True)

    @pl.when(group == pl.num_programs(0) - 1)
    def _():
        def leave(image, carry):
            tokens = place(image)
            mods = mods_ref[image]
            grad = 0.0
            for other in range(out_ref.shape[0]):
                grad = grad + dot_00(out_ref[other, :, tokens], w_ref[other, : 3 * rows_all])
            unit, scale = rms(chunk_rows(latent_ref, image).astype(f32))
            sums = {SHIFT_ONE: row_sum(grad), SCALE_ONE: row_sum(grad * unit)}
            put_rows(sums_ref, image, sums)
            grad = grad_ref[tokens, :] + rms_back(grad, unit, scale, row_of(mods, SCALE_ONE))
            put_chunks(chunks_ref, image, grad.astype(bf16))
            return carry

        lax.fori_loop(0, own, leave, 0)


def whole_spec(shape):
    return pl.BlockSpec(shape, lambda g: (0,) * len(shape), pipeline_mode=pl.Buffered(1))


def attend(latent, mods, weights, gains, tables):
    groups, rows, width = weights.shape[0], weights.shape[1] // 4, weights.shape[2]
    own = mods.shape[0]
    length, head_dim = tables[0].shape[1], gains.shape[1]
    tokens = own * length
    total, turned = (tokens, width), (width, tokens)
    const = lambda shape: pl.BlockSpec(shape, lambda g: (0,) * len(shape))
    return pl.pallas_call(
        attend_kernel,
        grid=(groups,),
        in_specs=[
            whole_spec(latent.shape),
            whole_spec(mods.shape),
            pl.BlockSpec((1, 4 * rows, width), lambda g: (g, 0, 0)),
            pl.BlockSpec((groups, rows, width), lambda g: (0, 3, 0), pipeline_mode=pl.Buffered(1)),
            whole_spec(gains.shape),
            whole_spec(tables[0].shape),
            whole_spec(tables[0].shape),
        ],
        out_specs=[
            pl.BlockSpec((1, 3 * rows, tokens), lambda g: (g, 0, 0)),
            const((groups, rows, tokens)),
            const(total),
            const(turned),
            const(total),
            const(total),
            const(turned),
        ],
        out_shape=[
            jax.ShapeDtypeStruct((groups, 3 * rows, tokens), f32),
            jax.ShapeDtypeStruct((groups, rows, tokens), bf16),
            jax.ShapeDtypeStruct(total, bf16),
            jax.ShapeDtypeStruct(turned, bf16),
            jax.ShapeDtypeStruct(total, f32),
            jax.ShapeDtypeStruct(total, bf16),
            jax.ShapeDtypeStruct(turned, bf16),
        ],
        scratch_shapes=[pltpu.VMEM(total, bf16)],
        compiler_params=pltpu.CompilerParams(vmem_limit_bytes=62 << 20),
        cost_estimate=lasting(160),
        name="attend",
    )(latent, mods, weights, weights, gains, *tables)


def attend_back(latent, proj, low, weights, gains, tables, grad, mods):
    groups, rows, width = weights.shape[0], weights.shape[1] // 4, weights.shape[2]
    own = mods.shape[0]
    tokens = low.shape[0]
    length, head_dim = tokens // own, gains.shape[1]
    const = lambda shape: pl.BlockSpec(shape, lambda g: (0,) * len(shape))
    gain_shape = (2, head_dim, length)
    return pl.pallas_call(
        attend_back_kernel,
        grid=(groups,),
        in_specs=[
            whole_spec(latent.shape),
            pl.BlockSpec((1, 3 * rows, tokens), lambda g: (g, 0, 0)),
            whole_spec(low.shape),
            whole_spec(weights.shape),
            whole_spec(gains.shape),
            whole_spec(tables[0].shape),
            whole_spec(tables[0].shape),
            whole_spec(grad.shape),
            whole_spec(mods.shape),
        ],
        out_specs=[const(proj.shape), const(gain_shape), const(mods.shape), const(latent.shape)],
        out_shape=[
            jax.ShapeDtypeStruct(proj.shape, bf16),
            jax.ShapeDtypeStruct(gain_shape, f32),
            jax.ShapeDtypeStruct(mods.shape, f32),
            jax.ShapeDtypeStruct(latent.shape, bf16),
        ],
        scratch_shapes=[pltpu.VMEM((rows, tokens), f32)],
        compiler_params=pltpu.CompilerParams(vmem_limit_bytes=62 << 20),
        cost_estimate=lasting(1),
        name="attend_back",
    )(latent, proj, low, weights, gains, *tables, grad, mods)


def finish_kernel(
    branch_ref, middle_ref, cot_ref, mods_ref, low_ref, lowt_ref, chunks_ref, sums_ref
):
    branch, mods = branch_ref[...], mods_ref[0]
    gate = row_of(mods, GATE_TWO)
    result = (middle_ref[...] + gate * branch).astype(bf16)
    put_chunks(chunks_ref, 0, result)
    cot = chunk_rows(cot_ref, 0).astype(f32) * row_of(mods, WEIGHT)
    low = (gate * cot).astype(bf16)
    low_ref[...] = low
    lowt_ref[...] = low.T
    put_rows(sums_ref, 0, {GATE_TWO: row_sum(cot * branch)})


def middle_kernel(
    one_ref, other_ref, middle_ref, branch_ref, cot_ref, mods_ref,
    grad_ref, low_ref, lowt_ref, sums_ref,
):
    mods = mods_ref[0]
    grad = one_ref[...] + other_ref[...]
    unit, scale = rms(middle_ref[...])
    sums = {SHIFT_TWO: row_sum(grad), SCALE_TWO: row_sum(grad * unit)}
    cot = chunk_rows(cot_ref, 0).astype(f32) * row_of(mods, WEIGHT)
    grad = cot + rms_back(grad, unit, scale, row_of(mods, SCALE_TWO))
    grad_ref[...] = grad
    low = (row_of(mods, GATE_ONE) * grad).astype(bf16)
    low_ref[...] = low
    lowt_ref[...] = low.T
    sums[GATE_ONE] = row_sum(grad * branch_ref[...].astype(f32))
    put_rows(sums_ref, 0, sums)


def by_image(kernel, name, microseconds, rows, chunks, mods, outs):
    own, sums, width = mods.shape
    tokens = rows[0].shape[0]
    length = tokens // own
    block = pl.BlockSpec((length, width), lambda i: (i, 0))
    turned = pl.BlockSpec((width, length), lambda i: (0, i))
    chunk = pl.BlockSpec((chunks.shape[0], 1) + chunks.shape[2:], lambda i: (0, i, 0, 0))
    whole = pl.BlockSpec((1, sums, width), lambda i: (i, 0, 0))
    specs, shapes = [], []
    for out in outs:
        if out is True:
            specs.append(turned)
            shapes.append(jax.ShapeDtypeStruct((width, tokens), bf16))
        elif out is False:
            specs.append(chunk)
            shapes.append(jax.ShapeDtypeStruct(chunks.shape, bf16))
        else:
            specs.append(block)
            shapes.append(jax.ShapeDtypeStruct((tokens, width), out))
    return pl.pallas_call(
        kernel,
        grid=(own,),
        in_specs=[block] * len(rows) + [chunk, whole],
        out_specs=specs + [whole],
        out_shape=shapes + [jax.ShapeDtypeStruct(mods.shape, f32)],
        compiler_params=pltpu.CompilerParams(vmem_limit_bytes=60 << 20),
        cost_estimate=lasting(microseconds),
        name=name,
    )(*rows, chunks, mods)


def modulate_kernel(silu_ref, ada_ref, out_ref):
    out_ref[0] = dot_10(silu_ref[...], ada_ref[0])


def modulate(silu, ada):
    kinds, width = ada.shape[:2]
    return pl.pallas_call(
        modulate_kernel,
        grid=(kinds,),
        in_specs=[
            pl.BlockSpec(silu.shape, lambda k: (0, 0)),
            pl.BlockSpec((1, width, width), lambda k: (k, 0, 0)),
        ],
        out_specs=pl.BlockSpec((1,) + silu.shape, lambda k: (k, 0, 0)),
        out_shape=jax.ShapeDtypeStruct((kinds,) + silu.shape, f32),
        compiler_params=pltpu.CompilerParams(vmem_limit_bytes=60 << 20),
        cost_estimate=lasting(0),
        name="modulate",
    )(silu, ada)


def add_rows(out_ref, part, first, index, length):
    rows = pl.ds(pl.multiple_of(index * length, length), length)

    @pl.when(first)
    def _():
        out_ref[rows, :] = part

    @pl.when(jnp.logical_not(first))
    def _():
        out_ref[rows, :] += part


def sigmoid(values):
    return 1.0 / (1.0 + jnp.exp(-values))


def mlp_kernel(count, e_ref, x_ref, *refs):
    first = pl.program_id(0) == 0
    save_ref, out_ref, w_ref = refs[count:]
    unit = min(ref.shape[2] for ref in refs[:count])
    for index, ref in enumerate(refs[:count]):
        rows = pl.ds(pl.multiple_of(e_ref[index] * unit, unit), ref.shape[2])
        for kind in range(3):
            w_ref[0, kind, rows, :] = ref[0, kind]
    x = x_ref[...]
    gate = dot_11(x, w_ref[0, 0])
    up = dot_11(x, w_ref[0, 1])
    save_ref[0, 0] = gate.astype(bf16)
    save_ref[0, 1] = up.astype(bf16)
    hidden = (gate * sigmoid(gate) * up).astype(bf16)
    part = dot_10(hidden, w_ref[0, 2])
    add_rows(out_ref, part, first, 0, x.shape[0])


def mlp(x, order, pieces):
    groups, _, _, width = pieces[0].shape
    units, tokens = sum(piece.shape[2] for piece in pieces), x.shape[0]
    return pl.pallas_call(
        functools.partial(mlp_kernel, len(pieces)),
        grid_spec=pltpu.PrefetchScalarGridSpec(
            num_scalar_prefetch=1,
            grid=(groups,),
            in_specs=[pl.BlockSpec((tokens, width), lambda g, e: (0, 0), pipeline_mode=pl.Buffered(1))]
            + [pl.BlockSpec((1,) + piece.shape[1:], lambda g, e: (g, 0, 0, 0)) for piece in pieces],
            out_specs=[
                pl.BlockSpec((1, 2, tokens, units), lambda g, e: (g, 0, 0, 0)),
                pl.BlockSpec((tokens, width), lambda g, e: (0, 0)),
                pl.BlockSpec((1, 3, units, width), lambda g, e: (g, 0, 0, 0)),
            ],
        ),
        out_shape=[
            jax.ShapeDtypeStruct((groups, 2, tokens, units), bf16),
            jax.ShapeDtypeStruct((tokens, width), f32),
            jax.ShapeDtypeStruct((groups, 3, units, width), bf16),
        ],
        compiler_params=pltpu.CompilerParams(vmem_limit_bytes=62 << 20),
        cost_estimate=lasting(1),
        name="mlp",
    )(order, x, *pieces)


def fill_rows(order_ref, source_ref, target_ref, base=0):
    blocks, rows = source_ref.shape[0], source_ref.shape[1]
    for place in range(blocks):
        target_ref[place * rows : (place + 1) * rows, :] = source_ref[order_ref[base + place]]


def mlp_back_kernel(
    e_ref, xt_ref, lowt_ref, low_ref, save_ref, w_ref,
    keep_ref, send_ref, two_ref, xs, lows, parts,
):
    first = pl.program_id(0) == 0
    tokens, width = low_ref.shape
    step = math.gcd(tokens, 512)

    @pl.when(first)
    def _():
        fill_rows(e_ref, xt_ref, xs)
        fill_rows(e_ref, lowt_ref, lows)

    for index in range(tokens // step):
        rows = pl.ds(index * step, step)
        hidden_grad = dot_11(low_ref[rows, :], w_ref[0, 2])
        gate = save_ref[0, 0, rows, :].astype(f32)
        up = save_ref[0, 1, rows, :].astype(f32)
        sig = sigmoid(gate)
        swish = gate * sig
        gate_low = (hidden_grad * up * (sig + swish * (1.0 - sig))).astype(bf16)
        up_low = (hidden_grad * swish).astype(bf16)
        parts[0, rows, :] = gate_low
        parts[1, rows, :] = up_low
        parts[2, rows, :] = (swish * up).astype(bf16)
        part = dot_10(gate_low, w_ref[0, 0]) + dot_10(up_low, w_ref[0, 1])
        add_rows(two_ref, part, first, index, step)

    half = width // 2
    for out_ref, rows in ((keep_ref, slice(0, half)), (send_ref, slice(half, width))):
        x_rows = xs[rows, :]
        for kind in range(2):
            out_ref[0, kind] = dot_10(x_rows, parts[kind]).astype(bf16)
        out_ref[0, 2] = dot_10(lows[rows, :], parts[2]).astype(bf16)


def mlp_back(which, e_order, xt, lowt, low, save, weights):
    groups, _, units, width = weights.shape
    tokens = low.shape[0]
    blocks = groups // 2
    base = which * blocks
    once = pl.Buffered(1)
    whole = lambda p, e: (0, 0)
    whole3 = lambda p, e: (0, 0, 0)
    half = jax.ShapeDtypeStruct((blocks, 3, width // 2, units), bf16)
    half_spec = pl.BlockSpec((1, 3, width // 2, units), lambda p, e: (p, 0, 0, 0))
    return pl.pallas_call(
        mlp_back_kernel,
        grid_spec=pltpu.PrefetchScalarGridSpec(
            num_scalar_prefetch=1,
            grid=(blocks,),
            in_specs=[
                pl.BlockSpec(xt.shape, whole3, pipeline_mode=once),
                pl.BlockSpec(lowt.shape, whole3, pipeline_mode=once),
                pl.BlockSpec((tokens, width), whole, pipeline_mode=once),
                pl.BlockSpec((1, 2, tokens, units), lambda p, e: (base + p, 0, 0, 0)),
                pl.BlockSpec((1, 3, units, width), lambda p, e: (base + p, 0, 0, 0)),
            ],
            out_specs=[half_spec, half_spec, pl.BlockSpec((tokens, width), whole)],
            scratch_shapes=[
                pltpu.VMEM((width, tokens), bf16),
                pltpu.VMEM((width, tokens), bf16),
                pltpu.VMEM((3, tokens, units), bf16),
            ],
        ),
        out_shape=[half, half, jax.ShapeDtypeStruct((tokens, width), f32)],
        compiler_params=pltpu.CompilerParams(vmem_limit_bytes=62 << 20),
        cost_estimate=lasting(150),
        name="mlp_back",
    )(e_order, xt, lowt, low, save, weights)


def attend_grads_kernel(
    m_ref, e_ref, xt_ref, lowt_ref, proj_ref, att_ref, keep_ref, send_ref, xs, lows
):
    first = pl.num_programs(0) // 2 == pl.program_id(0)
    base = jnp.where(first, xt_ref.shape[0], 0)

    @pl.when(first | (pl.program_id(0) == 0))
    def _():
        fill_rows(e_ref, xt_ref, xs, base)
        fill_rows(e_ref, lowt_ref, lows, base)

    width = xs.shape[0]
    half = width // 2
    columns = proj_ref.shape[1]

    for out_ref, rows in ((keep_ref, slice(0, half)), (send_ref, slice(half, width))):
        out_ref[0, :, :columns] = dot_11(xs[rows, :], proj_ref[0]).astype(bf16)
        out_ref[0, :, columns:] = dot_11(lows[rows, :], att_ref[0]).astype(bf16)


def attend_grads(m_order, e_orders, xt, lowt, proj, att):
    rows, tokens = att.shape[1:]
    width = xt.shape[0] * xt.shape[1]
    blocks = m_order.shape[0]
    whole3 = lambda p, m, e: (0, 0, 0)
    half = jax.ShapeDtypeStruct((blocks, width // 2, 4 * rows), bf16)
    half_spec = pl.BlockSpec((1, width // 2, 4 * rows), lambda p, m, e: (p, 0, 0))
    return pl.pallas_call(
        attend_grads_kernel,
        grid_spec=pltpu.PrefetchScalarGridSpec(
            num_scalar_prefetch=2,
            grid=(blocks,),
            in_specs=[
                pl.BlockSpec(xt.shape, whole3, pipeline_mode=pl.Buffered(1)),
                pl.BlockSpec(lowt.shape, whole3, pipeline_mode=pl.Buffered(1)),
                pl.BlockSpec((1, 3 * rows, tokens), lambda p, m, e: (m[p], 0, 0)),
                pl.BlockSpec((1, rows, tokens), lambda p, m, e: (m[p], 0, 0)),
            ],
            out_specs=[half_spec, half_spec],
            scratch_shapes=[
                pltpu.VMEM((width, tokens), bf16),
                pltpu.VMEM((width, tokens), bf16),
            ],
        ),
        out_shape=[half, half],
        compiler_params=pltpu.CompilerParams(vmem_limit_bytes=56 << 20),
        cost_estimate=lasting(0),
        name="attend_grads",
    )(m_order, e_orders, xt, lowt, proj, att)


def dot(a, b):
    return jnp.dot(a, b, preferred_element_type=f32)


def ein(spec, a, b):
    return jnp.einsum(spec, a, b, preferred_element_type=f32)


def gather_pieces(piece, mp_size):
    whole = lax.all_gather(piece, ("mp", "dp"), axis=0, tiled=False)
    return whole.reshape((mp_size, -1) + piece.shape)


def take_rows(values, index):
    return values.at[index].get(mode="promise_in_bounds")


def sum_quarters_kernel(kept_ref, got_ref, *out_refs):
    total = (kept_ref[0].astype(f32) + got_ref[0].astype(f32)).astype(bf16)
    half = total.shape[0] // 2
    later = pl.program_id(0) >= pl.num_programs(0) // 2

    @pl.when(jnp.logical_not(later))
    def _():
        out_refs[0][0] = total[:half]
        out_refs[1][0] = total[half:]

    @pl.when(later)
    def _():
        out_refs[2][0] = total[:half]
        out_refs[3][0] = total[half:]


def sum_quarters(kept, got):
    groups, rows, columns = kept.shape
    if rows % 32:
        halves = split(add_low(kept, got), 0)
        return split(halves[0], 1) + split(halves[1], 1)
    part = groups // 2
    whole = pl.BlockSpec((1, rows, columns), lambda i: (i, 0, 0))
    block = (1, rows // 2, columns)
    early = pl.BlockSpec(block, lambda i: (jnp.minimum(i, part - 1), 0, 0))
    late = pl.BlockSpec(block, lambda i: (jnp.maximum(i - part, 0), 0, 0))
    return pl.pallas_call(
        sum_quarters_kernel,
        grid=(groups,),
        in_specs=[whole, whole],
        out_specs=[early, early, late, late],
        out_shape=[jax.ShapeDtypeStruct((part, rows // 2, columns), bf16)] * 4,
        compiler_params=pltpu.CompilerParams(vmem_limit_bytes=60 << 20),
        cost_estimate=lasting(0),
        name="sum_quarters",
    )(kept, got)


def whole_arrays(kernel, name, microseconds, shape, *arrays):
    specs = [pl.BlockSpec(array.shape, functools.partial(lambda n: (0,) * n, array.ndim)) for array in arrays]
    return pl.pallas_call(
        kernel,
        in_specs=specs,
        out_specs=pl.BlockSpec(shape, lambda: (0,) * len(shape)),
        out_shape=jax.ShapeDtypeStruct(shape, arrays[0].dtype),
        compiler_params=pltpu.CompilerParams(vmem_limit_bytes=60 << 20),
        cost_estimate=lasting(microseconds),
        name=name,
    )(*arrays)


def append_zero_kernel(value_ref, out_ref):
    count = value_ref.shape[0]
    out_ref[:count] = value_ref[...]
    out_ref[count:] = jnp.zeros_like(out_ref[count:])


def append_zero(values, microseconds):
    shape = (values.shape[0] + 1,) + values.shape[1:]
    return whole_arrays(append_zero_kernel, "append_zero", microseconds, shape, values)


def append_kernel(one_ref, other_ref, out_ref):
    count = one_ref.shape[0]
    out_ref[:count] = one_ref[...]
    out_ref[count:] = other_ref[...]


def append(one, other, microseconds):
    shape = (2 * one.shape[0],) + one.shape[1:]
    return whole_arrays(append_kernel, "append", microseconds, shape, one, other)


def bits_of(size):
    return [1 << i for i in range(size.bit_length() - 1)]


def swap(values, axis, bit):
    size = lax.axis_size(axis)
    return lax.ppermute(values, axis, [(i, i ^ bit) for i in range(size)])


def halving_order(bits):
    order = [0]
    for bit in reversed(bits):
        order = order + [place ^ bit for place in order]
    return order


def add_low(kept, received):
    return (kept.astype(f32) + received.astype(f32)).astype(bf16)


def sum_halves_kernel(kept_ref, got_ref, first_ref, second_ref):
    total = (kept_ref[0].astype(f32) + got_ref[0].astype(f32)).astype(bf16)
    half = first_ref.shape[1]
    first_ref[0] = total[:half]
    second_ref[0] = total[half:]


def sum_halves(kept, got, microseconds=0):
    rows, columns = kept.shape[-2:]
    if rows % 32:
        return split(add_low(kept, got), kept.ndim - 2)
    shape = kept.shape[:-2] + (rows // 2, columns)
    kept, got = kept.reshape(-1, rows, columns), got.reshape(-1, rows, columns)
    whole = pl.BlockSpec((1, rows, columns), lambda i: (i, 0, 0))
    half = pl.BlockSpec((1, rows // 2, columns), lambda i: (i, 0, 0))
    halves = pl.pallas_call(
        sum_halves_kernel,
        grid=(kept.shape[0],),
        in_specs=[whole, whole],
        out_specs=[half, half],
        out_shape=[jax.ShapeDtypeStruct((kept.shape[0], rows // 2, columns), bf16)] * 2,
        compiler_params=pltpu.CompilerParams(vmem_limit_bytes=60 << 20),
        cost_estimate=lasting(microseconds),
        name="sum_halves",
    )(kept, got)
    return halves[0].reshape(shape), halves[1].reshape(shape)


def tie(*values):
    return lax.optimization_barrier(values)


def split(values, dim):
    size = values.shape[dim] // 2
    return (
        lax.slice_in_dim(values, 0, size, axis=dim),
        lax.slice_in_dim(values, size, 2 * size, axis=dim),
    )


def halve(values, axis, bits, dim):
    for bit in bits:
        kept, sent = split(values, dim)
        values = add_low(kept, swap(sent, axis, bit))
    return values


def shards(
    patches,
    cotangent,
    time_bins,
    labels,
    image_counts,
    dest_perm,
    time_table,
    class_table,
    ada_weight,
    qkv_weight,
    norm_gains,
    out_weight,
    expand_weight,
    down_weight,
):
    dp_size = lax.axis_size("dp")
    mp_size = lax.axis_size("mp")
    capacity = patches.shape[0]
    slot_count = capacity // dp_size
    images = cotangent.shape[0]
    local_len = patches.shape[1]
    model_width = patches.shape[2]
    length = local_len * mp_size
    head_dim = norm_gains.shape[1]
    local_dim = out_weight.shape[0]
    unit_count = down_weight.shape[0]
    own = images // mp_size
    total_images = images * dp_size
    order = np.array(feature_order(head_dim)[0])
    columns = np.arange(4 * local_dim)
    places = columns // head_dim * head_dim + order[columns % head_dim]
    places = np.where(columns < 2 * local_dim, places, columns).astype(np.int32)
    gains_f = norm_gains.astype(f32)[:, order]
    gains_f = (gains_f * jnp.array([[head_dim ** (-0.5)], [1.0]], f32))[:, :, None]
    dp_index = lax.axis_index("dp")
    mp_index = lax.axis_index("mp")
    dp_bits = bits_of(dp_size)
    dp_bits = (dp_bits, dp_bits[:1] + dp_bits[1:][::-1])
    mp_bits = bits_of(mp_size)

    tables = rope_tables(jnp.arange(length), head_dim)

    def turn(chunks):
        return lax.all_to_all(chunks, "mp", split_axis=0, concat_axis=0, tiled=True)

    starts = jnp.cumsum(image_counts) - image_counts
    finish = starts + image_counts
    my_start = starts[dp_index]
    my_count = image_counts[dp_index]
    device_ids = jnp.arange(dp_size)
    matches = (dest_perm[:, None] == device_ids[None, :]).astype(jnp.int32)
    inverse = jnp.sum(device_ids[:, None] * matches, axis=0)
    my_place = inverse[dp_index]
    pair_ids = jnp.arange(dp_size * slot_count)
    pair_peer = pair_ids // slot_count
    pair_slot = pair_ids % slot_count
    send_index = pair_slot * dp_size + jnp.mod(inverse[pair_peer] - my_start, dp_size)
    send_index = jnp.minimum(send_index, capacity - 1)
    send_patches = take_rows(patches, send_index)
    share = 4 * local_dim // dp_size
    spots = lax.dynamic_slice_in_dim(jnp.array(places), dp_index * share, share, 0)
    take_qkv = (spots[:, None] == jnp.arange(3 * local_dim)[None, :]).astype(bf16)
    take_out = (spots[:, None] - 3 * local_dim == jnp.arange(local_dim)[None, :]).astype(bf16)
    attend_piece = dot(take_qkv, qkv_weight.transpose(1, 2, 0).reshape(-1, model_width))
    attend_piece = (attend_piece + dot(take_out, out_weight)).astype(bf16)
    share = unit_count // dp_size
    spots = dp_index * share + jnp.arange(share)
    take_units = (spots[:, None] == jnp.arange(unit_count)[None, :]).astype(bf16)
    expand_kinds = tie(expand_weight.swapaxes(0, 1))[0]
    mlp_piece = jnp.stack(
        [
            dot_11(take_units, expand_kinds[0]).astype(bf16),
            dot_11(take_units, expand_kinds[1]).astype(bf16),
            lax.dynamic_slice_in_dim(down_weight, dp_index * share, share, 0),
        ]
    )
    info = jnp.stack([time_bins, labels])[None]
    info_places = [0]
    for bit in bits_of(dp_size):
        got_info = swap(info, "dp", bit)
        if bit * 2 == dp_size:
            send_patches, got_info, attend_piece = tie(send_patches, got_info, attend_piece)
        info = append(info, got_info, 200)
        info_places = info_places + [place ^ bit for place in info_places]
    attend_full = gather_pieces(attend_piece, mp_size).reshape(mp_size, 4 * local_dim, -1)
    by_permutes = share % 32 == 0 and dp_size == 8 and mp_size == 4
    if by_permutes:
        mlp_near = mlp_piece[None]
        far_near = swap(mlp_near, "mp", 2)
    else:
        mlp_full = gather_pieces(mlp_piece, mp_size)
        mlp_full = mlp_full.swapaxes(1, 2).reshape(mp_size, 3, unit_count, model_width)
        mlp_pieces = [mlp_full[mp_index ^ jnp.array(halving_order(mp_bits))]]
        mlp_order = jnp.zeros((1,), jnp.int32)

    recv_patches = lax.all_to_all(send_patches, "dp", split_axis=0, concat_axis=0, tiled=True)
    info = info.swapaxes(0, 1).reshape(2, -1)
    info_owner = jnp.repeat(dp_index ^ jnp.array(info_places), capacity)
    info_slot = jnp.tile(jnp.arange(capacity), dp_size)
    info_count = jnp.sum(
        jnp.where(info_owner[:, None] == device_ids[None, :], image_counts[None, :], 0), axis=1
    )
    live_all = info_slot < info_count
    bin_totals = jnp.sum(
        ((info[0][:, None] == jnp.arange(NBINS)[None, :]) & live_all[:, None]).astype(f32), axis=0
    )
    gather_bits = [("mp", bit) for bit in mp_bits[::-1]]
    gather_bits = gather_bits + [("dp", bit) for bit in dp_bits[0][1:] + dp_bits[0][:1]]
    spread = {"dp": [0], "mp": [0]}
    for axis, bit in gather_bits:
        spread = {
            name: spread[name] + [place ^ (bit if name == axis else 0) for place in spread[name]]
            for name in spread
        }
    owner_all = jnp.repeat(dp_index ^ jnp.array(spread["dp"]), own)
    group_all = jnp.repeat(mp_index ^ jnp.array(spread["mp"]), own)
    row_all = group_all * own + jnp.tile(jnp.arange(own), dp_size * mp_size)
    place_all = jnp.sum(
        jnp.where(owner_all[:, None] == device_ids[None, :], inverse[None, :], 0), axis=1
    )
    rank_all = row_all * dp_size + place_all
    source_all = jnp.sum((finish[None, :] <= rank_all[:, None]).astype(jnp.int32), axis=1)
    start_all = jnp.sum(
        jnp.where(source_all[:, None] == device_ids[None, :], starts[None, :], 0), axis=1
    )
    slots_all = source_all * capacity + rank_all - start_all
    slot_hit = slots_all[:, None] == (info_owner * capacity + info_slot)[None, :]
    bins_all = jnp.sum(jnp.where(slot_hit, info[0][None, :], 0), axis=1)
    labels_all = jnp.sum(jnp.where(slot_hit, info[1][None, :], 0), axis=1)
    bin_hot = (bins_all[:, None] == jnp.arange(NBINS)[None, :])
    label_hot = (labels_all[:, None] == jnp.arange(NCLS)[None, :])
    weights_all = total_images / (NBINS * jnp.sum(bin_hot.astype(f32) * bin_totals[None, :], axis=1))
    bin_hot = bin_hot.astype(bf16)
    label_hot = label_hot.astype(bf16)
    cond_all = (dot(bin_hot, time_table) + dot(label_hot, class_table)).astype(bf16).astype(f32)
    silu_all = jax.nn.silu(cond_all).astype(bf16)
    silu_cond = silu_all[:own]
    weights = weights_all[:own]

    if by_permutes:
        silu_cond, far_near = tie(silu_cond, far_near)
        mlp_near = jnp.concatenate([mlp_near, far_near], axis=0)
        far_near = swap(mlp_near, "mp", 1)
    ada_kinds = ada_weight.swapaxes(0, 1)
    modulation = modulate(jnp.pad(silu_cond, ((0, -own % 16), (0, 0))), ada_kinds)[:, :own]
    mods = jnp.concatenate(
        [
            modulation.swapaxes(0, 1),
            jnp.broadcast_to(weights[:, None, None], (own, 1, model_width)),
            jnp.zeros((own, 1, model_width), f32),
        ],
        axis=1,
    )
    mods, starts, image_counts, dest_perm, my_place = tie(mods, starts, image_counts, dest_perm, my_place)
    back_within = pair_slot * dp_size + jnp.mod(my_place - starts[pair_peer], dp_size)
    back_valid = back_within < image_counts[pair_peer]
    back_slot = jnp.clip((starts[pair_peer] + back_within - my_place) // dp_size, 0, images - 1)
    back_slot = jnp.where(back_valid, back_slot, images)
    slot_ids = jnp.arange(capacity)
    home_peer = dest_perm[jnp.mod(my_start + slot_ids, dp_size)]
    home_index = home_peer * slot_count + jnp.minimum(slot_ids // dp_size, slot_count - 1)
    recv_patches, mods, back_slot, home_index = tie(recv_patches, mods, back_slot, home_index)

    rank_ids = jnp.arange(images) * dp_size + my_place
    source = jnp.sum((finish[None, :] <= rank_ids[:, None]).astype(jnp.int32), axis=1)
    within = rank_ids - starts[source]
    recv_index = source * slot_count + within // dp_size
    latent = take_rows(recv_patches, recv_index).reshape(mp_size, own, local_len, model_width)
    if by_permutes:
        far_near, _ = tie(far_near, latent)
    latent = turn(latent)
    if by_permutes:
        mlp_near = jnp.concatenate([mlp_near, far_near], axis=0)
        halves = split(mlp_near, 2)
        orders = ((2, 4), (4, 2))
        parts = [{bit: swap(halves[half], "dp", bit) for bit in orders[half]} for half in range(2)]
        cored = swap(mlp_near, "dp", 1)
        latent, parts[0][2], parts[1][4], cored = tie(latent, parts[0][2], parts[1][4], cored)
        got = [swap(parts[half][orders[half][0]], "dp", orders[half][1]) for half in range(2)]

    cotangent, latent = tie(cotangent, latent)
    proj, attended, branch_one, normed_t, middle, two, two_t = attend(
        latent, mods, attend_full, gains_f, tables
    )
    cot = turn(cotangent.reshape(mp_size, own, local_len, model_width))
    if by_permutes:
        got[0], got[1], attended = tie(got[0], got[1], attended)
        mlp_pieces, mlp_order = [mlp_near, cored], [dp_index * 2, (dp_index ^ 1) * 2]
        for half in range(2):
            parts[half][6] = got[half]
            for near, part in parts[half].items():
                mlp_pieces += [part, swap(part, "dp", 1)]
                mlp_order += [(dp_index ^ near) * 2 + half, (dp_index ^ near ^ 1) * 2 + half]
        mlp_order = jnp.stack(mlp_order).astype(jnp.int32)
    save, branch_two, mlp_full = mlp(two, mlp_order, mlp_pieces)
    branch_two, cot = tie(branch_two, cot)
    down_low, down_t, result, sums_finish = by_image(
        finish_kernel, "finish", 1, (branch_two, middle), cot, mods, (bf16, True, False)
    )
    result = turn(result)

    e_orders = [(dp_index ^ jnp.array(halving_order(bits))).astype(jnp.int32) for bits in dp_bits]
    m_order = (mp_index ^ jnp.array(halving_order(mp_bits))).astype(jnp.int32)

    def by_owner(values):
        return values.reshape(dp_size, model_width // dp_size, -1)

    two_t, down_t = by_owner(two_t), by_owner(down_t)
    kept_one, sent_one, two_one = mlp_back(
        1, e_orders[1], two_t, down_t, down_low, save, mlp_full
    )
    got_one = swap(sent_one, "dp", dp_bits[1][0])
    kept_zero, sent_zero, two_zero = mlp_back(
        0, e_orders[0], two_t, down_t, down_low, save, mlp_full
    )
    got_zero = swap(sent_zero, "dp", dp_bits[0][0])
    kept_one, sent_one = sum_halves(kept_one, got_one)
    kept_zero, sent_zero = sum_halves(kept_zero, got_zero)
    two_zero, kept_one, kept_zero = tie(two_zero, kept_one, kept_zero)
    got_one = swap(sent_one, "dp", dp_bits[1][1])
    got_zero = swap(sent_zero, "dp", dp_bits[0][1])
    middle_grad, branch_low, branch_t, sums_middle = by_image(
        middle_kernel,
        "middle",
        100,
        (two_zero, two_one, middle, branch_one),
        cot,
        mods,
        (f32, bf16, True),
    )
    projected_low, gains_grad, sums_entry, latent_back = attend_back(
        latent, proj, branch_low, attend_full, gains_f, tables, middle_grad, mods
    )
    gains_grad = jnp.sum(gains_grad, axis=2) * jnp.array([[head_dim ** (-0.5)], [1.0]], f32)
    projected_low, got_one, got_zero = tie(projected_low, got_one, got_zero)
    packed = sums_finish + sums_middle + sums_entry
    gains_row = jnp.pad(gains_grad.reshape(1, 1, -1), ((0, own - 1), (7, 0), (0, model_width - 2 * head_dim)))
    packed = jnp.where(jnp.arange(8)[:, None] == 7, gains_row, packed).astype(bf16)
    packed = packed[None]
    stage, got_packed = 0, swap(packed, *gather_bits[0])

    def more(after, microseconds=0):
        nonlocal packed, got_packed, stage
        after, got_packed = tie(after, got_packed)
        packed = append(packed, got_packed, microseconds)
        stage += 1
        if stage < len(gather_bits):
            got_packed = swap(packed, *gather_bits[stage])
        return after

    kept_one, sent_one = sum_halves(kept_one, got_one, 200)
    kept_one = more(kept_one)
    kept_one, kept_zero = tie(kept_one, kept_zero)
    kept_zero, sent_zero = sum_halves(kept_zero, got_zero)
    normed_t, kept_one, kept_zero, result = tie(normed_t, kept_one, kept_zero, result)
    got_one = swap(sent_one, "dp", dp_bits[1][2])
    got_zero = swap(sent_zero, "dp", dp_bits[0][2])
    latent_back = turn(latent_back)

    normed_t, branch_t = by_owner(normed_t), by_owner(branch_t)

    attend_kept, attend_sent = attend_grads(
        m_order, jnp.concatenate(e_orders), normed_t, branch_t, projected_low, attended
    )
    attend_got = swap(attend_sent, "dp", dp_bits[0][0])

    attend_kept, got_one, got_zero, latent_back, got_packed = tie(
        attend_kept, got_one, got_zero, latent_back, got_packed
    )
    attend_kept = more(attend_kept, 200)
    attend_got, packed = tie(attend_got, packed)
    attend_zero, sent_zero, attend_one, sent_one = sum_quarters(attend_kept, attend_got)
    mlp_one = halve(add_low(kept_one, got_one), "dp", dp_bits[1][3:], 2)
    mlp_zero = halve(add_low(kept_zero, got_zero), "dp", dp_bits[0][3:], 2)
    mlp_got = swap(mlp_one, "mp", mp_bits[0])

    latent_back, attend_zero, attend_one = tie(latent_back, attend_zero, attend_one)
    latent_back = append_zero(latent_back.reshape(images, local_len, model_width), 200)
    back_patches = take_rows(latent_back, back_slot)
    attend_got_one = swap(sent_one, "dp", dp_bits[1][1])
    attend_got_zero = swap(sent_zero, "dp", dp_bits[0][1])
    back_patches, attend_zero, attend_one = tie(back_patches, attend_zero, attend_one)
    attend_zero = more(attend_zero)
    attend_one, sent_one = sum_halves(attend_one, attend_got_one)
    attend_zero, sent_zero = sum_halves(attend_zero, attend_got_zero)
    back_patches, sent_one, sent_zero, mlp_zero = tie(back_patches, sent_one, sent_zero, mlp_zero)
    got_patches = lax.all_to_all(back_patches, "dp", split_axis=0, concat_axis=0, tiled=True)
    patch_grad = take_rows(got_patches, home_index)
    attend_got_one = swap(sent_one, "dp", dp_bits[1][2])
    attend_got_zero = swap(sent_zero, "dp", dp_bits[0][2])
    while stage < len(gather_bits):
        mlp_zero = more(mlp_zero)
    packed = packed.reshape(total_images, 8, model_width)
    mod_all = packed[:, :6]
    gains_total = packed.reshape(-1, own, 8, model_width)[:, 0, 7, : 2 * head_dim]
    gains_total = jnp.sum(gains_total.astype(f32), axis=0).reshape(2, head_dim)
    gains_total = jnp.sum(
        jnp.where(order[:, None] == jnp.arange(head_dim)[None, :], gains_total[:, :, None], 0.0), axis=1
    )
    width_dp = model_width // dp_size
    width_mp = model_width // mp_size
    row0 = dp_index * width_dp
    silu_rows = lax.dynamic_slice_in_dim(silu_all, row0, width_dp, 1)
    mod_cols = lax.dynamic_slice_in_dim(mod_all, mp_index * width_mp, width_mp, 2)
    ada_grad = ein("id,ikc->dkc", silu_rows, mod_cols)
    ada_rows = lax.dynamic_slice_in_dim(ada_kinds, row0, width_dp, 1)
    silu_grad = ein("ikc,kdc->id", mod_all, ada_rows)
    cond_rows = lax.dynamic_slice_in_dim(cond_all, row0, width_dp, 1)
    silu_val, silu_pull = jax.vjp(jax.nn.silu, cond_rows)
    condition_low = silu_pull(silu_grad)[0].astype(bf16)
    time_grad = ein("in,id->nd", bin_hot, condition_low)
    class_grad = ein("in,id->nd", label_hot, condition_low)

    attend_one = halve(add_low(attend_one, attend_got_one), "dp", dp_bits[1][3:], 1)
    attend_zero = halve(add_low(attend_zero, attend_got_zero), "dp", dp_bits[0][3:], 1)
    mlp_grad = halve(add_low(mlp_zero, mlp_got), "mp", mp_bits[1:], 0)[0].astype(f32)
    attend_grad = add_low(attend_zero, swap(attend_one, "mp", mp_bits[0]))
    attend_grad = halve(attend_grad, "mp", mp_bits[1:], 0)[0].astype(f32)

    expand_grad = mlp_grad[:2].swapaxes(0, 1)
    down_grad = mlp_grad[2].T
    out_grad = attend_grad[:, 3 * local_dim :].T
    qkv_grad = lax.dot_general(
        attend_grad[:, : 3 * local_dim],
        jnp.array(places[: 3 * local_dim, None] == columns[: 3 * local_dim], f32),
        (((1,), (0,)), ((), ())),
        precision=lax.Precision.HIGHEST,
        preferred_element_type=f32,
    )
    qkv_grad = qkv_grad.reshape(-1, 3, local_dim)
    return (
        result.reshape(images, local_len, model_width),
        patch_grad,
        time_grad,
        class_grad,
        ada_grad,
        qkv_grad,
        gains_total,
        out_grad,
        expand_grad,
        down_grad,
    )


def solution(mesh):
    in_specs = (
        P("dp", "mp", None),
        P("dp", "mp", None),
        P("dp"),
        P("dp"),
        P(),
        P(),
        P(),
        P(),
        P(),
        P(None, None, "mp"),
        P(),
        P("mp", None),
        P(None, None, "mp"),
        P("mp", None),
    )
    out_specs = (
        P("dp", "mp", None),
        P("dp", "mp", None),
        P(None, "dp"),
        P(None, "dp"),
        P("dp", None, "mp"),
        P("dp", None, "mp"),
        P(),
        P("mp", "dp"),
        P("dp", None, "mp"),
        P("mp", "dp"),
    )
    return jax.shard_map(shards, mesh=mesh, in_specs=in_specs, out_specs=out_specs, check_vma=False)
```

```python
import functools
import math

import jax
import jax.numpy as jnp
import numpy as np
from jax import lax
from jax.experimental import pallas as pl
from jax.experimental.pallas import tpu as pltpu
from jax.sharding import PartitionSpec as P

GRID = 16
NCLS = 1000
NBINS = 16

epsilon = 1e-06
rope_base = 10000.0
f32 = jnp.float32
bf16 = jnp.bfloat16


def feature_order(head_dim):
    quarter = head_dim // 4
    firsts = list(range(quarter)) + list(range(2 * quarter, 3 * quarter))
    cut = len(firsts) // 8 * 8
    seconds = [i + quarter for i in firsts]
    return firsts[:cut] + seconds[:cut] + firsts[cut:] + seconds[cut:], cut


def rope_tables(position, head_dim):
    quarter = head_dim // 4
    order, cut = feature_order(head_dim)
    places = jnp.stack([position // GRID, position % GRID]).astype(f32)
    frequency = rope_base ** (-jnp.arange(quarter).astype(f32) / quarter)
    angle = (frequency[None, :, None] * places[:, None, :]).reshape(2 * quarter, -1)
    cosine, sine = jnp.cos(angle), jnp.sin(angle)
    cos_tab = jnp.concatenate([cosine[:cut], cosine[:cut], cosine[cut:], cosine[cut:]])
    sin_tab = jnp.concatenate([-sine[:cut], sine[:cut], -sine[cut:], sine[cut:]])
    return cos_tab, sin_tab


def partner(values, cut):
    rest = values[2 * cut :]
    half = rest.shape[0] // 2
    return jnp.concatenate(
        [values[cut : 2 * cut], values[:cut], pltpu.roll(rest, half, 0)], axis=0
    )


def head_scale(values):
    return lax.rsqrt(jnp.mean(values * values, axis=0, keepdims=True) + epsilon)


def dot_00(a, b):
    return lax.dot_general(a, b, (((0,), (0,)), ((), ())), preferred_element_type=f32)


def dot_11(a, b):
    return lax.dot_general(a, b, (((1,), (1,)), ((), ())), preferred_element_type=f32)


def dot_10(a, b):
    return lax.dot_general(a, b, (((1,), (0,)), ((), ())), preferred_element_type=f32)


def softmax_first(scores):
    shifted = jnp.exp(scores - jnp.max(scores, axis=0, keepdims=True))
    return shifted * (1.0 / jnp.sum(shifted, axis=0, keepdims=True))


def lasting(microseconds):
    return pl.CostEstimate(
        flops=int(microseconds * 1.1e9), bytes_accessed=1 << 10, transcendentals=0
    )


SHIFT_ONE, SCALE_ONE, GATE_ONE, SHIFT_TWO, SCALE_TWO, GATE_TWO, WEIGHT = range(7)


def row_of(mods, which):
    return mods[which : which + 1, :]


def rms(values):
    scale = lax.rsqrt(jnp.mean(values * values, -1, keepdims=True) + epsilon)
    return values * scale, scale


def rms_back(grad, unit, scale, scaling):
    grad = grad * (1.0 + scaling)
    return scale * (grad - unit * jnp.mean(grad * unit, -1, keepdims=True))


def row_sum(values):
    return jnp.sum(values, axis=0, keepdims=True)


def put_rows(sums_ref, image, rows):
    for which in range(sums_ref.shape[1]):
        value = rows.get(which, jnp.zeros((1, sums_ref.shape[2]), f32))
        sums_ref[image, which : which + 1, :] = value


def chunk_rows(ref, image):
    return jnp.concatenate([ref[chunk, image] for chunk in range(ref.shape[0])], axis=0)


def put_chunks(ref, image, values):
    size = ref.shape[2]
    for chunk in range(ref.shape[0]):
        ref[chunk, image] = values[chunk * size : (chunk + 1) * size]


def attend_kernel(
    latent_ref, mods_ref, w_ref, wo_ref, gains_ref, cos_ref, sin_ref,
    proj_ref, att_ref, branch_ref, xt_ref, middle_ref, two_ref, twot_ref, x_ref,
):
    own = mods_ref.shape[0]
    head_dim = gains_ref.shape[1]
    rows_all = att_ref.shape[1]
    length = xt_ref.shape[1] // own
    heads = range(rows_all // head_dim)
    cut = feature_order(head_dim)[1]
    group = pl.program_id(0)

    def place(image):
        return pl.ds(pl.multiple_of(image * length, length), length)

    @pl.when(group == 0)
    def _():
        def entry(image, carry):
            mods = mods_ref[image]
            unit = rms(chunk_rows(latent_ref, image).astype(f32))[0]
            x = (unit * (1.0 + row_of(mods, SCALE_ONE)) + row_of(mods, SHIFT_ONE)).astype(bf16)
            x_ref[place(image), :] = x
            xt_ref[:, place(image)] = x.T
            return carry

        lax.fori_loop(0, own, entry, 0)

    proj_ref[0] = dot_11(w_ref[0, : 3 * rows_all], x_ref[...])

    def heads_of(image, carry):
        tokens = place(image)
        cos_tab, sin_tab = cos_ref[...], sin_ref[...]
        lows = [[], [], []]
        for kind in range(2):
            for head in heads:
                start = kind * rows_all + head * head_dim
                raw = proj_ref[0, start : start + head_dim, tokens]
                scaled = raw * head_scale(raw) * gains_ref[kind]
                turned = scaled * cos_tab + partner(scaled, cut) * sin_tab
                lows[kind].append(turned.astype(bf16))
        for head in heads:
            start = 2 * rows_all + head * head_dim
            lows[2].append(proj_ref[0, start : start + head_dim, tokens].astype(bf16))
        scores = [dot_00(lows[1][head], lows[0][head]) for head in heads]
        probs = [softmax_first(score).astype(bf16) for score in scores]
        outs = [dot_10(lows[2][head], probs[head]) for head in heads]
        att_ref[group, :, tokens] = jnp.concatenate(outs, axis=0).astype(bf16)
        return carry

    lax.fori_loop(0, own, heads_of, 0, unroll=True)

    @pl.when(group == pl.num_programs(0) - 1)
    def _():
        groups = att_ref.shape[0]

        def leave(image, carry):
            tokens = place(image)
            mods = mods_ref[image]
            att = att_ref[:, :, tokens].reshape(groups * rows_all, length)
            branch = dot_00(att, wo_ref[...].reshape(groups * rows_all, -1))
            branch_ref[tokens, :] = branch.astype(bf16)
            latent = chunk_rows(latent_ref, image).astype(f32)
            middle = latent + row_of(mods, GATE_ONE) * branch
            middle_ref[tokens, :] = middle
            two = rms(middle)[0] * (1.0 + row_of(mods, SCALE_TWO)) + row_of(mods, SHIFT_TWO)
            two = two.astype(bf16)
            two_ref[tokens, :] = two
            twot_ref[:, tokens] = two.T
            return carry

        lax.fori_loop(0, own, leave, 0)


def attend_back_kernel(
    latent_ref, proj_ref, low_ref, w_ref, gains_ref, cos_ref, sin_ref, grad_ref, mods_ref,
    out_ref, gain_grad_ref, sums_ref, chunks_ref, cot_ref,
):
    own = mods_ref.shape[0]
    head_dim = gains_ref.shape[1]
    rows_all, tokens_all = proj_ref.shape[1] // 3, proj_ref.shape[2]
    length = tokens_all // own
    heads = range(rows_all // head_dim)
    cut = feature_order(head_dim)[1]
    group = pl.program_id(0)

    def place(image):
        return pl.ds(pl.multiple_of(image * length, length), length)

    @pl.when(group == 0)
    def _():
        gain_grad_ref[...] = jnp.zeros_like(gain_grad_ref)

    cot_ref[...] = dot_11(w_ref[group, 3 * rows_all :], low_ref[...])

    def heads_of(image, carry):
        tokens = place(image)
        cos_tab, sin_tab = cos_ref[...], sin_ref[...]
        lows, units, scales = [[], [], []], [[], []], [[], []]
        for kind in range(2):
            for head in heads:
                start = kind * rows_all + head * head_dim
                raw = proj_ref[0, start : start + head_dim, tokens]
                scale = head_scale(raw)
                unit = raw * scale
                scaled = unit * gains_ref[kind]
                turned = scaled * cos_tab + partner(scaled, cut) * sin_tab
                lows[kind].append(turned.astype(bf16))
                units[kind].append(unit)
                scales[kind].append(scale)
        cots = []
        for head in heads:
            start = 2 * rows_all + head * head_dim
            lows[2].append(proj_ref[0, start : start + head_dim, tokens].astype(bf16))
            cots.append(cot_ref[head * head_dim : (head + 1) * head_dim, tokens].astype(bf16))
        scores = [dot_00(lows[1][head], lows[0][head]) for head in heads]
        prob_grads = [dot_00(lows[2][head], cots[head]) for head in heads]
        probs = [softmax_first(score) for score in scores]
        outs = [[], [], []]
        outs[2] = [dot_11(cots[head], probs[head].astype(bf16)) for head in heads]
        score_lows = []
        for head in heads:
            mean = jnp.sum(probs[head] * prob_grads[head], axis=0, keepdims=True)
            score_lows.append((probs[head] * (prob_grads[head] - mean)).astype(bf16))
        turned_grads = [
            [dot_10(lows[1][head], score_lows[head]) for head in heads],
            [dot_11(lows[0][head], score_lows[head]) for head in heads],
        ]
        for kind in range(2):
            total = 0.0
            for head in heads:
                grad, unit = turned_grads[kind][head], units[kind][head]
                grad = grad * cos_tab + partner(grad * sin_tab, cut)
                total = total + grad * unit
                grad = grad * gains_ref[kind]
                along = jnp.mean(grad * unit, axis=0, keepdims=True)
                outs[kind].append(scales[kind][head] * (grad - unit * along))
            gain_grad_ref[kind] += total
        grads = jnp.concatenate(outs[0] + outs[1] + outs[2], axis=0).astype(bf16)
        out_ref[group, :, tokens] = grads
        return carry

    lax.fori_loop(0, own, heads_of, 0, unroll=True)

    @pl.when(group == pl.num_programs(0) - 1)
    def _():
        def leave(image, carry):
            tokens = place(image)
            mods = mods_ref[image]
            grad = 0.0
            for other in range(out_ref.shape[0]):
                grad = grad + dot_00(out_ref[other, :, tokens], w_ref[other, : 3 * rows_all])
            unit, scale = rms(chunk_rows(latent_ref, image).astype(f32))
            sums = {SHIFT_ONE: row_sum(grad), SCALE_ONE: row_sum(grad * unit)}
            put_rows(sums_ref, image, sums)
            grad = grad_ref[tokens, :] + rms_back(grad, unit, scale, row_of(mods, SCALE_ONE))
            put_chunks(chunks_ref, image, grad.astype(bf16))
            return carry

        lax.fori_loop(0, own, leave, 0)


def whole_spec(shape):
    return pl.BlockSpec(shape, lambda g: (0,) * len(shape), pipeline_mode=pl.Buffered(1))


def attend(latent, mods, weights, gains, tables):
    groups, rows, width = weights.shape[0], weights.shape[1] // 4, weights.shape[2]
    own = mods.shape[0]
    length, head_dim = tables[0].shape[1], gains.shape[1]
    tokens = own * length
    total, turned = (tokens, width), (width, tokens)
    const = lambda shape: pl.BlockSpec(shape, lambda g: (0,) * len(shape))
    return pl.pallas_call(
        attend_kernel,
        grid=(groups,),
        in_specs=[
            whole_spec(latent.shape),
            whole_spec(mods.shape),
            pl.BlockSpec((1, 4 * rows, width), lambda g: (g, 0, 0)),
            pl.BlockSpec((groups, rows, width), lambda g: (0, 3, 0), pipeline_mode=pl.Buffered(1)),
            whole_spec(gains.shape),
            whole_spec(tables[0].shape),
            whole_spec(tables[0].shape),
        ],
        out_specs=[
            pl.BlockSpec((1, 3 * rows, tokens), lambda g: (g, 0, 0)),
            const((groups, rows, tokens)),
            const(total),
            const(turned),
            const(total),
            const(total),
            const(turned),
        ],
        out_shape=[
            jax.ShapeDtypeStruct((groups, 3 * rows, tokens), f32),
            jax.ShapeDtypeStruct((groups, rows, tokens), bf16),
            jax.ShapeDtypeStruct(total, bf16),
            jax.ShapeDtypeStruct(turned, bf16),
            jax.ShapeDtypeStruct(total, f32),
            jax.ShapeDtypeStruct(total, bf16),
            jax.ShapeDtypeStruct(turned, bf16),
        ],
        scratch_shapes=[pltpu.VMEM(total, bf16)],
        compiler_params=pltpu.CompilerParams(vmem_limit_bytes=62 << 20),
        cost_estimate=lasting(160),
        name="attend",
    )(latent, mods, weights, weights, gains, *tables)


def attend_back(latent, proj, low, weights, gains, tables, grad, mods):
    groups, rows, width = weights.shape[0], weights.shape[1] // 4, weights.shape[2]
    own = mods.shape[0]
    tokens = low.shape[0]
    length, head_dim = tokens // own, gains.shape[1]
    const = lambda shape: pl.BlockSpec(shape, lambda g: (0,) * len(shape))
    gain_shape = (2, head_dim, length)
    return pl.pallas_call(
        attend_back_kernel,
        grid=(groups,),
        in_specs=[
            whole_spec(latent.shape),
            pl.BlockSpec((1, 3 * rows, tokens), lambda g: (g, 0, 0)),
            whole_spec(low.shape),
            whole_spec(weights.shape),
            whole_spec(gains.shape),
            whole_spec(tables[0].shape),
            whole_spec(tables[0].shape),
            whole_spec(grad.shape),
            whole_spec(mods.shape),
        ],
        out_specs=[const(proj.shape), const(gain_shape), const(mods.shape), const(latent.shape)],
        out_shape=[
            jax.ShapeDtypeStruct(proj.shape, bf16),
            jax.ShapeDtypeStruct(gain_shape, f32),
            jax.ShapeDtypeStruct(mods.shape, f32),
            jax.ShapeDtypeStruct(latent.shape, bf16),
        ],
        scratch_shapes=[pltpu.VMEM((rows, tokens), f32)],
        compiler_params=pltpu.CompilerParams(vmem_limit_bytes=62 << 20),
        cost_estimate=lasting(1),
        name="attend_back",
    )(latent, proj, low, weights, gains, *tables, grad, mods)


def finish_kernel(
    branch_ref, middle_ref, cot_ref, mods_ref, low_ref, lowt_ref, chunks_ref, sums_ref
):
    branch, mods = branch_ref[...], mods_ref[0]
    gate = row_of(mods, GATE_TWO)
    result = (middle_ref[...] + gate * branch).astype(bf16)
    put_chunks(chunks_ref, 0, result)
    cot = chunk_rows(cot_ref, 0).astype(f32) * row_of(mods, WEIGHT)
    low = (gate * cot).astype(bf16)
    low_ref[...] = low
    lowt_ref[...] = low.T
    put_rows(sums_ref, 0, {GATE_TWO: row_sum(cot * branch)})


def middle_kernel(
    one_ref, other_ref, middle_ref, branch_ref, cot_ref, mods_ref,
    grad_ref, low_ref, lowt_ref, sums_ref,
):
    mods = mods_ref[0]
    grad = one_ref[...] + other_ref[...]
    unit, scale = rms(middle_ref[...])
    sums = {SHIFT_TWO: row_sum(grad), SCALE_TWO: row_sum(grad * unit)}
    cot = chunk_rows(cot_ref, 0).astype(f32) * row_of(mods, WEIGHT)
    grad = cot + rms_back(grad, unit, scale, row_of(mods, SCALE_TWO))
    grad_ref[...] = grad
    low = (row_of(mods, GATE_ONE) * grad).astype(bf16)
    low_ref[...] = low
    lowt_ref[...] = low.T
    sums[GATE_ONE] = row_sum(grad * branch_ref[...].astype(f32))
    put_rows(sums_ref, 0, sums)


def by_image(kernel, name, microseconds, rows, chunks, mods, outs):
    own, sums, width = mods.shape
    tokens = rows[0].shape[0]
    length = tokens // own
    block = pl.BlockSpec((length, width), lambda i: (i, 0))
    turned = pl.BlockSpec((width, length), lambda i: (0, i))
    chunk = pl.BlockSpec((chunks.shape[0], 1) + chunks.shape[2:], lambda i: (0, i, 0, 0))
    whole = pl.BlockSpec((1, sums, width), lambda i: (i, 0, 0))
    specs, shapes = [], []
    for out in outs:
        if out is True:
            specs.append(turned)
            shapes.append(jax.ShapeDtypeStruct((width, tokens), bf16))
        elif out is False:
            specs.append(chunk)
            shapes.append(jax.ShapeDtypeStruct(chunks.shape, bf16))
        else:
            specs.append(block)
            shapes.append(jax.ShapeDtypeStruct((tokens, width), out))
    return pl.pallas_call(
        kernel,
        grid=(own,),
        in_specs=[block] * len(rows) + [chunk, whole],
        out_specs=specs + [whole],
        out_shape=shapes + [jax.ShapeDtypeStruct(mods.shape, f32)],
        compiler_params=pltpu.CompilerParams(vmem_limit_bytes=60 << 20),
        cost_estimate=lasting(microseconds),
        name=name,
    )(*rows, chunks, mods)


def modulate_kernel(silu_ref, ada_ref, out_ref):
    out_ref[0] = dot_10(silu_ref[...], ada_ref[0])


def modulate(silu, ada):
    kinds, width = ada.shape[:2]
    return pl.pallas_call(
        modulate_kernel,
        grid=(kinds,),
        in_specs=[
            pl.BlockSpec(silu.shape, lambda k: (0, 0)),
            pl.BlockSpec((1, width, width), lambda k: (k, 0, 0)),
        ],
        out_specs=pl.BlockSpec((1,) + silu.shape, lambda k: (k, 0, 0)),
        out_shape=jax.ShapeDtypeStruct((kinds,) + silu.shape, f32),
        compiler_params=pltpu.CompilerParams(vmem_limit_bytes=60 << 20),
        cost_estimate=lasting(0),
        name="modulate",
    )(silu, ada)


def add_rows(out_ref, part, first, index, length):
    rows = pl.ds(pl.multiple_of(index * length, length), length)

    @pl.when(first)
    def _():
        out_ref[rows, :] = part

    @pl.when(jnp.logical_not(first))
    def _():
        out_ref[rows, :] += part


def sigmoid(values):
    return 1.0 / (1.0 + jnp.exp(-values))


def mlp_kernel(count, e_ref, x_ref, *refs):
    first = pl.program_id(0) == 0
    save_ref, out_ref, w_ref = refs[count:]
    unit = min(ref.shape[2] for ref in refs[:count])
    for index, ref in enumerate(refs[:count]):
        rows = pl.ds(pl.multiple_of(e_ref[index] * unit, unit), ref.shape[2])
        for kind in range(3):
            w_ref[0, kind, rows, :] = ref[0, kind]
    x = x_ref[...]
    gate = dot_11(x, w_ref[0, 0])
    up = dot_11(x, w_ref[0, 1])
    save_ref[0, 0] = gate.astype(bf16)
    save_ref[0, 1] = up.astype(bf16)
    hidden = (gate * sigmoid(gate) * up).astype(bf16)
    part = dot_10(hidden, w_ref[0, 2])
    add_rows(out_ref, part, first, 0, x.shape[0])


def mlp(x, order, pieces):
    groups, _, _, width = pieces[0].shape
    units, tokens = sum(piece.shape[2] for piece in pieces), x.shape[0]
    return pl.pallas_call(
        functools.partial(mlp_kernel, len(pieces)),
        grid_spec=pltpu.PrefetchScalarGridSpec(
            num_scalar_prefetch=1,
            grid=(groups,),
            in_specs=[pl.BlockSpec((tokens, width), lambda g, e: (0, 0), pipeline_mode=pl.Buffered(1))]
            + [pl.BlockSpec((1,) + piece.shape[1:], lambda g, e: (g, 0, 0, 0)) for piece in pieces],
            out_specs=[
                pl.BlockSpec((1, 2, tokens, units), lambda g, e: (g, 0, 0, 0)),
                pl.BlockSpec((tokens, width), lambda g, e: (0, 0)),
                pl.BlockSpec((1, 3, units, width), lambda g, e: (g, 0, 0, 0)),
            ],
        ),
        out_shape=[
            jax.ShapeDtypeStruct((groups, 2, tokens, units), bf16),
            jax.ShapeDtypeStruct((tokens, width), f32),
            jax.ShapeDtypeStruct((groups, 3, units, width), bf16),
        ],
        compiler_params=pltpu.CompilerParams(vmem_limit_bytes=62 << 20),
        cost_estimate=lasting(1),
        name="mlp",
    )(order, x, *pieces)


def fill_rows(order_ref, source_ref, target_ref, base=0):
    blocks, rows = source_ref.shape[0], source_ref.shape[1]
    for place in range(blocks):
        target_ref[place * rows : (place + 1) * rows, :] = source_ref[order_ref[base + place]]


def mlp_back_kernel(
    e_ref, xt_ref, lowt_ref, low_ref, save_ref, w_ref,
    keep_ref, send_ref, two_ref, xs, lows, parts,
):
    first = pl.program_id(0) == 0
    tokens, width = low_ref.shape
    step = math.gcd(tokens, 512)

    @pl.when(first)
    def _():
        fill_rows(e_ref, xt_ref, xs)
        fill_rows(e_ref, lowt_ref, lows)

    for index in range(tokens // step):
        rows = pl.ds(index * step, step)
        hidden_grad = dot_11(low_ref[rows, :], w_ref[0, 2])
        gate = save_ref[0, 0, rows, :].astype(f32)
        up = save_ref[0, 1, rows, :].astype(f32)
        sig = sigmoid(gate)
        swish = gate * sig
        gate_low = (hidden_grad * up * (sig + swish * (1.0 - sig))).astype(bf16)
        up_low = (hidden_grad * swish).astype(bf16)
        parts[0, rows, :] = gate_low
        parts[1, rows, :] = up_low
        parts[2, rows, :] = (swish * up).astype(bf16)
        part = dot_10(gate_low, w_ref[0, 0]) + dot_10(up_low, w_ref[0, 1])
        add_rows(two_ref, part, first, index, step)

    half = width // 2
    for out_ref, rows in ((keep_ref, slice(0, half)), (send_ref, slice(half, width))):
        x_rows = xs[rows, :]
        for kind in range(2):
            out_ref[0, kind] = dot_10(x_rows, parts[kind]).astype(bf16)
        out_ref[0, 2] = dot_10(lows[rows, :], parts[2]).astype(bf16)


def mlp_back(which, e_order, xt, lowt, low, save, weights):
    groups, _, units, width = weights.shape
    tokens = low.shape[0]
    blocks = groups // 2
    base = which * blocks
    once = pl.Buffered(1)
    whole = lambda p, e: (0, 0)
    whole3 = lambda p, e: (0, 0, 0)
    half = jax.ShapeDtypeStruct((blocks, 3, width // 2, units), bf16)
    half_spec = pl.BlockSpec((1, 3, width // 2, units), lambda p, e: (p, 0, 0, 0))
    return pl.pallas_call(
        mlp_back_kernel,
        grid_spec=pltpu.PrefetchScalarGridSpec(
            num_scalar_prefetch=1,
            grid=(blocks,),
            in_specs=[
                pl.BlockSpec(xt.shape, whole3, pipeline_mode=once),
                pl.BlockSpec(lowt.shape, whole3, pipeline_mode=once),
                pl.BlockSpec((tokens, width), whole, pipeline_mode=once),
                pl.BlockSpec((1, 2, tokens, units), lambda p, e: (base + p, 0, 0, 0)),
                pl.BlockSpec((1, 3, units, width), lambda p, e: (base + p, 0, 0, 0)),
            ],
            out_specs=[half_spec, half_spec, pl.BlockSpec((tokens, width), whole)],
            scratch_shapes=[
                pltpu.VMEM((width, tokens), bf16),
                pltpu.VMEM((width, tokens), bf16),
                pltpu.VMEM((3, tokens, units), bf16),
            ],
        ),
        out_shape=[half, half, jax.ShapeDtypeStruct((tokens, width), f32)],
        compiler_params=pltpu.CompilerParams(vmem_limit_bytes=62 << 20),
        cost_estimate=lasting(150),
        name="mlp_back",
    )(e_order, xt, lowt, low, save, weights)


def attend_grads_kernel(
    m_ref, e_ref, xt_ref, lowt_ref, proj_ref, att_ref, keep_ref, send_ref, xs, lows
):
    first = pl.num_programs(0) // 2 == pl.program_id(0)
    base = jnp.where(first, xt_ref.shape[0], 0)

    @pl.when(first | (pl.program_id(0) == 0))
    def _():
        fill_rows(e_ref, xt_ref, xs, base)
        fill_rows(e_ref, lowt_ref, lows, base)

    width = xs.shape[0]
    half = width // 2
    columns = proj_ref.shape[1]

    for out_ref, rows in ((keep_ref, slice(0, half)), (send_ref, slice(half, width))):
        out_ref[0, :, :columns] = dot_11(xs[rows, :], proj_ref[0]).astype(bf16)
        out_ref[0, :, columns:] = dot_11(lows[rows, :], att_ref[0]).astype(bf16)


def attend_grads(m_order, e_orders, xt, lowt, proj, att):
    rows, tokens = att.shape[1:]
    width = xt.shape[0] * xt.shape[1]
    blocks = m_order.shape[0]
    whole3 = lambda p, m, e: (0, 0, 0)
    half = jax.ShapeDtypeStruct((blocks, width // 2, 4 * rows), bf16)
    half_spec = pl.BlockSpec((1, width // 2, 4 * rows), lambda p, m, e: (p, 0, 0))
    return pl.pallas_call(
        attend_grads_kernel,
        grid_spec=pltpu.PrefetchScalarGridSpec(
            num_scalar_prefetch=2,
            grid=(blocks,),
            in_specs=[
                pl.BlockSpec(xt.shape, whole3, pipeline_mode=pl.Buffered(1)),
                pl.BlockSpec(lowt.shape, whole3, pipeline_mode=pl.Buffered(1)),
                pl.BlockSpec((1, 3 * rows, tokens), lambda p, m, e: (m[p], 0, 0)),
                pl.BlockSpec((1, rows, tokens), lambda p, m, e: (m[p], 0, 0)),
            ],
            out_specs=[half_spec, half_spec],
            scratch_shapes=[
                pltpu.VMEM((width, tokens), bf16),
                pltpu.VMEM((width, tokens), bf16),
            ],
        ),
        out_shape=[half, half],
        compiler_params=pltpu.CompilerParams(vmem_limit_bytes=56 << 20),
        cost_estimate=lasting(0),
        name="attend_grads",
    )(m_order, e_orders, xt, lowt, proj, att)


def dot(a, b):
    return jnp.dot(a, b, preferred_element_type=f32)


def ein(spec, a, b):
    return jnp.einsum(spec, a, b, preferred_element_type=f32)


def gather_pieces(piece, mp_size):
    whole = lax.all_gather(piece, ("mp", "dp"), axis=0, tiled=False)
    return whole.reshape((mp_size, -1) + piece.shape)


def pick_rows(values, index):
    return values.at[index].get(mode="promise_in_bounds")


def take_rows_kernel(index_ref, *refs):
    out_ref = refs[-1]
    count = len(refs) - 1
    base = pl.program_id(0) * count
    for place, ref in enumerate(refs[:-1]):
        live = index_ref[base + place] >= 0

        @pl.when(live)
        def _():
            out_ref[place] = ref[0]

        @pl.when(jnp.logical_not(live))
        def _():
            out_ref[place] = jnp.zeros_like(ref[0])


def take_rows(values, index, microseconds=0):
    number = index.shape[0]
    count = math.gcd(number, 4)
    block = values.shape[1:]
    specs = [
        pl.BlockSpec(
            (1,) + block,
            functools.partial(
                lambda place, i, index: (jnp.maximum(index[i * count + place], 0), 0, 0), place
            ),
        )
        for place in range(count)
    ]
    return pl.pallas_call(
        take_rows_kernel,
        grid_spec=pltpu.PrefetchScalarGridSpec(
            num_scalar_prefetch=1,
            grid=(number // count,),
            in_specs=specs,
            out_specs=pl.BlockSpec((count,) + block, lambda i, index: (i, 0, 0)),
        ),
        out_shape=jax.ShapeDtypeStruct((number,) + block, values.dtype),
        compiler_params=pltpu.CompilerParams(vmem_limit_bytes=60 << 20),
        cost_estimate=lasting(microseconds),
        name="take_rows",
    )(index.astype(jnp.int32), *([values] * count))


def sum_quarters_kernel(kept_ref, got_ref, *out_refs):
    total = (kept_ref[0].astype(f32) + got_ref[0].astype(f32)).astype(bf16)
    half = total.shape[0] // 2
    later = pl.program_id(0) >= pl.num_programs(0) // 2

    @pl.when(jnp.logical_not(later))
    def _():
        out_refs[0][0] = total[:half]
        out_refs[1][0] = total[half:]

    @pl.when(later)
    def _():
        out_refs[2][0] = total[:half]
        out_refs[3][0] = total[half:]


def sum_quarters(kept, got):
    groups, rows, columns = kept.shape
    if rows % 32:
        halves = split(add_low(kept, got), 0)
        return split(halves[0], 1) + split(halves[1], 1)
    part = groups // 2
    whole = pl.BlockSpec((1, rows, columns), lambda i: (i, 0, 0))
    block = (1, rows // 2, columns)
    early = pl.BlockSpec(block, lambda i: (jnp.minimum(i, part - 1), 0, 0))
    late = pl.BlockSpec(block, lambda i: (jnp.maximum(i - part, 0), 0, 0))
    return pl.pallas_call(
        sum_quarters_kernel,
        grid=(groups,),
        in_specs=[whole, whole],
        out_specs=[early, early, late, late],
        out_shape=[jax.ShapeDtypeStruct((part, rows // 2, columns), bf16)] * 4,
        compiler_params=pltpu.CompilerParams(vmem_limit_bytes=60 << 20),
        cost_estimate=lasting(0),
        name="sum_quarters",
    )(kept, got)


def whole_arrays(kernel, name, microseconds, shape, *arrays):
    specs = [pl.BlockSpec(array.shape, functools.partial(lambda n: (0,) * n, array.ndim)) for array in arrays]
    return pl.pallas_call(
        kernel,
        in_specs=specs,
        out_specs=pl.BlockSpec(shape, lambda: (0,) * len(shape)),
        out_shape=jax.ShapeDtypeStruct(shape, arrays[0].dtype),
        compiler_params=pltpu.CompilerParams(vmem_limit_bytes=60 << 20),
        cost_estimate=lasting(microseconds),
        name=name,
    )(*arrays)


def copy_kernel(value_ref, out_ref):
    out_ref[...] = value_ref[...]


def append_kernel(one_ref, other_ref, out_ref):
    count = one_ref.shape[0]
    out_ref[:count] = one_ref[...]
    out_ref[count:] = other_ref[...]


def append(one, other, microseconds):
    shape = (2 * one.shape[0],) + one.shape[1:]
    return whole_arrays(append_kernel, "append", microseconds, shape, one, other)


def bits_of(size):
    return [1 << i for i in range(size.bit_length() - 1)]


def swap(values, axis, bit):
    size = lax.axis_size(axis)
    return lax.ppermute(values, axis, [(i, i ^ bit) for i in range(size)])


def halving_order(bits):
    order = [0]
    for bit in reversed(bits):
        order = order + [place ^ bit for place in order]
    return order


def add_low(kept, received):
    return (kept.astype(f32) + received.astype(f32)).astype(bf16)


def sum_halves_kernel(kept_ref, got_ref, first_ref, second_ref):
    total = (kept_ref[0].astype(f32) + got_ref[0].astype(f32)).astype(bf16)
    half = first_ref.shape[1]
    first_ref[0] = total[:half]
    second_ref[0] = total[half:]


def sum_halves(kept, got, microseconds=0):
    rows, columns = kept.shape[-2:]
    if rows % 32:
        return split(add_low(kept, got), kept.ndim - 2)
    shape = kept.shape[:-2] + (rows // 2, columns)
    kept, got = kept.reshape(-1, rows, columns), got.reshape(-1, rows, columns)
    whole = pl.BlockSpec((1, rows, columns), lambda i: (i, 0, 0))
    half = pl.BlockSpec((1, rows // 2, columns), lambda i: (i, 0, 0))
    halves = pl.pallas_call(
        sum_halves_kernel,
        grid=(kept.shape[0],),
        in_specs=[whole, whole],
        out_specs=[half, half],
        out_shape=[jax.ShapeDtypeStruct((kept.shape[0], rows // 2, columns), bf16)] * 2,
        compiler_params=pltpu.CompilerParams(vmem_limit_bytes=60 << 20),
        cost_estimate=lasting(microseconds),
        name="sum_halves",
    )(kept, got)
    return halves[0].reshape(shape), halves[1].reshape(shape)


def tie(*values):
    return lax.optimization_barrier(values)


def split(values, dim):
    size = values.shape[dim] // 2
    return [
        lax.slice_in_dim(values, 0, size, axis=dim),
        lax.slice_in_dim(values, size, 2 * size, axis=dim),
    ]


def halve(values, axis, bits, dim):
    for bit in bits:
        kept, sent = split(values, dim)
        values = add_low(kept, swap(sent, axis, bit))
    return values


def shards(
    patches,
    cotangent,
    time_bins,
    labels,
    image_counts,
    dest_perm,
    time_table,
    class_table,
    ada_weight,
    qkv_weight,
    norm_gains,
    out_weight,
    expand_weight,
    down_weight,
):
    dp_size = lax.axis_size("dp")
    mp_size = lax.axis_size("mp")
    capacity = patches.shape[0]
    slot_count = capacity // dp_size
    images = cotangent.shape[0]
    local_len = patches.shape[1]
    model_width = patches.shape[2]
    length = local_len * mp_size
    head_dim = norm_gains.shape[1]
    local_dim = out_weight.shape[0]
    unit_count = down_weight.shape[0]
    own = images // mp_size
    total_images = images * dp_size
    order = np.array(feature_order(head_dim)[0])
    columns = np.arange(4 * local_dim)
    places = columns // head_dim * head_dim + order[columns % head_dim]
    places = np.where(columns < 2 * local_dim, places, columns).astype(np.int32)
    gains_f = norm_gains.astype(f32)[:, order]
    gains_f = (gains_f * jnp.array([[head_dim ** (-0.5)], [1.0]], f32))[:, :, None]
    dp_index = lax.axis_index("dp")
    mp_index = lax.axis_index("mp")
    dp_bits = bits_of(dp_size)
    dp_bits = (dp_bits, dp_bits[:1] + dp_bits[1:][::-1])
    mp_bits = bits_of(mp_size)

    tables = rope_tables(jnp.arange(length), head_dim)

    def turn(chunks):
        return lax.all_to_all(chunks, "mp", split_axis=0, concat_axis=0, tiled=True)

    starts = jnp.cumsum(image_counts) - image_counts
    finish = starts + image_counts
    my_start = starts[dp_index]
    my_count = image_counts[dp_index]
    device_ids = jnp.arange(dp_size)
    matches = (dest_perm[:, None] == device_ids[None, :]).astype(jnp.int32)
    inverse = jnp.sum(device_ids[:, None] * matches, axis=0)
    my_place = inverse[dp_index]
    pair_ids = jnp.arange(dp_size * slot_count)
    pair_peer = pair_ids // slot_count
    pair_slot = pair_ids % slot_count
    send_index = pair_slot * dp_size + jnp.mod(inverse[pair_peer] - my_start, dp_size)
    send_index = jnp.minimum(send_index, capacity - 1)
    send_patches = pick_rows(patches, send_index)
    qkv_weight, out_weight, expand_weight, down_weight, send_patches = tie(
        qkv_weight, out_weight, expand_weight, down_weight, send_patches
    )
    recv_patches = lax.all_to_all(send_patches, "dp", split_axis=0, concat_axis=0, tiled=True)
    info = jnp.stack([time_bins, labels])[None]
    got_info = swap(info, "dp", dp_bits[0][0])

    share = 4 * local_dim // dp_size
    spots = lax.dynamic_slice_in_dim(jnp.array(places), dp_index * share, share, 0)
    take_qkv = (spots[:, None] == jnp.arange(3 * local_dim)[None, :]).astype(bf16)
    take_out = (spots[:, None] - 3 * local_dim == jnp.arange(local_dim)[None, :]).astype(bf16)
    attend_piece = dot(take_qkv, qkv_weight.transpose(1, 2, 0).reshape(-1, model_width))
    attend_piece = (attend_piece + dot(take_out, out_weight)).astype(bf16)
    share = unit_count // dp_size
    spots = dp_index * share + jnp.arange(share)
    take_units = (spots[:, None] == jnp.arange(unit_count)[None, :]).astype(bf16)
    expand_kinds = tie(expand_weight.swapaxes(0, 1))[0]
    mlp_piece = jnp.stack(
        [
            dot_11(take_units, expand_kinds[0]).astype(bf16),
            dot_11(take_units, expand_kinds[1]).astype(bf16),
            lax.dynamic_slice_in_dim(down_weight, dp_index * share, share, 0),
        ]
    )
    attend_full = gather_pieces(attend_piece, mp_size).reshape(mp_size, 4 * local_dim, -1)
    by_permutes = share % 32 == 0 and dp_size == 8 and mp_size == 4
    if by_permutes:
        mlp_near = mlp_piece[None]
        far_near = swap(mlp_near, "mp", 2)
    else:
        mlp_full = gather_pieces(mlp_piece, mp_size)
        mlp_full = mlp_full.swapaxes(1, 2).reshape(mp_size, 3, unit_count, model_width)
        mlp_pieces = [mlp_full[mp_index ^ jnp.array(halving_order(mp_bits))]]
        mlp_order = jnp.zeros((1,), jnp.int32)

    rank_ids = jnp.arange(images) * dp_size + my_place
    source = jnp.sum((finish[None, :] <= rank_ids[:, None]).astype(jnp.int32), axis=1)
    within = rank_ids - starts[source]
    recv_index = source * slot_count + within // dp_size

    info_places = [0]
    for step, bit in enumerate(dp_bits[0]):
        info = append(info, got_info, 200 if step < 2 else 0)
        info_places = info_places + [place ^ bit for place in info_places]
        if by_permutes and step == 0:
            mlp_near = jnp.concatenate([mlp_near, far_near], axis=0)
            far_near = swap(mlp_near, "mp", 1)
            info, mlp_near = tie(info, mlp_near)
        if by_permutes and step == 1:
            latent = pick_rows(recv_patches, recv_index)
            far_near, info, _ = tie(far_near, info, latent)
            mlp_near = append(mlp_near, far_near, 200)
            halves = split(mlp_near, 2)
        if step + 1 < len(dp_bits[0]):
            got_info = swap(info, "dp", dp_bits[0][step + 1])
    if not by_permutes:
        latent = pick_rows(recv_patches, recv_index)
    latent = turn(latent.reshape(mp_size, own, local_len, model_width))

    info = info.swapaxes(0, 1).reshape(2, -1)
    info_owner = jnp.repeat(dp_index ^ jnp.array(info_places), capacity)
    info_slot = jnp.tile(jnp.arange(capacity), dp_size)
    info_count = jnp.sum(
        jnp.where(info_owner[:, None] == device_ids[None, :], image_counts[None, :], 0), axis=1
    )
    live_all = info_slot < info_count
    bin_totals = jnp.sum(
        ((info[0][:, None] == jnp.arange(NBINS)[None, :]) & live_all[:, None]).astype(f32), axis=0
    )
    gather_bits = [("mp", bit) for bit in mp_bits[::-1]]
    gather_bits = gather_bits + [("dp", bit) for bit in dp_bits[0][1:] + dp_bits[0][:1]]
    spread = {"dp": [0], "mp": [0]}
    for axis, bit in gather_bits:
        spread = {
            name: spread[name] + [place ^ (bit if name == axis else 0) for place in spread[name]]
            for name in spread
        }
    owner_all = jnp.repeat(dp_index ^ jnp.array(spread["dp"]), own)
    group_all = jnp.repeat(mp_index ^ jnp.array(spread["mp"]), own)
    row_all = group_all * own + jnp.tile(jnp.arange(own), dp_size * mp_size)
    place_all = jnp.sum(
        jnp.where(owner_all[:, None] == device_ids[None, :], inverse[None, :], 0), axis=1
    )
    rank_all = row_all * dp_size + place_all
    source_all = jnp.sum((finish[None, :] <= rank_all[:, None]).astype(jnp.int32), axis=1)
    start_all = jnp.sum(
        jnp.where(source_all[:, None] == device_ids[None, :], starts[None, :], 0), axis=1
    )
    slots_all = source_all * capacity + rank_all - start_all
    slot_hit = slots_all[:, None] == (info_owner * capacity + info_slot)[None, :]
    bins_all = jnp.sum(jnp.where(slot_hit, info[0][None, :], 0), axis=1)
    labels_all = jnp.sum(jnp.where(slot_hit, info[1][None, :], 0), axis=1)
    bin_hot = (bins_all[:, None] == jnp.arange(NBINS)[None, :])
    label_hot = (labels_all[:, None] == jnp.arange(NCLS)[None, :])
    weights_all = total_images / (NBINS * jnp.sum(bin_hot.astype(f32) * bin_totals[None, :], axis=1))
    bin_hot = bin_hot.astype(bf16)
    label_hot = label_hot.astype(bf16)
    cond_all = (dot(bin_hot, time_table) + dot(label_hot, class_table)).astype(bf16).astype(f32)
    silu_all = jax.nn.silu(cond_all).astype(bf16)
    silu_cond = silu_all[:own]
    weights = weights_all[:own]

    ada_kinds = ada_weight.swapaxes(0, 1)
    modulation = modulate(jnp.pad(silu_cond, ((0, -own % 16), (0, 0))), ada_kinds)[:, :own]
    mods = jnp.concatenate(
        [
            modulation.swapaxes(0, 1),
            jnp.broadcast_to(weights[:, None, None], (own, 1, model_width)),
            jnp.zeros((own, 1, model_width), f32),
        ],
        axis=1,
    )
    mods, starts, image_counts, dest_perm, my_place = tie(mods, starts, image_counts, dest_perm, my_place)
    back_within = pair_slot * dp_size + jnp.mod(my_place - starts[pair_peer], dp_size)
    back_valid = back_within < image_counts[pair_peer]
    back_slot = jnp.clip((starts[pair_peer] + back_within - my_place) // dp_size, 0, images - 1)
    back_slot = jnp.where(back_valid, back_slot, -1)
    slot_ids = jnp.arange(capacity)
    home_peer = dest_perm[jnp.mod(my_start + slot_ids, dp_size)]
    home_index = home_peer * slot_count + jnp.minimum(slot_ids // dp_size, slot_count - 1)
    mods, back_slot, home_index = tie(mods, back_slot, home_index)

    if by_permutes:
        orders = ((2, 4), (4, 2))
        parts = [{bit: swap(halves[half], "dp", bit) for bit in orders[half]} for half in range(2)]
        cored = swap(mlp_near, "dp", 1)
        latent, parts[0][2], parts[1][4], cored = tie(latent, parts[0][2], parts[1][4], cored)
        got = [swap(parts[half][orders[half][0]], "dp", orders[half][1]) for half in range(2)]

    cotangent, latent = tie(cotangent, latent)
    proj, attended, branch_one, normed_t, middle, two, two_t = attend(
        latent, mods, attend_full, gains_f, tables
    )
    cot = turn(cotangent.reshape(mp_size, own, local_len, model_width))
    if by_permutes:
        got[0], got[1], attended = tie(got[0], got[1], attended)
        mlp_pieces, mlp_order = [mlp_near, cored], [dp_index * 2, (dp_index ^ 1) * 2]
        for half in range(2):
            parts[half][6] = got[half]
            for near, part in parts[half].items():
                mlp_pieces += [part, swap(part, "dp", 1)]
                mlp_order += [(dp_index ^ near) * 2 + half, (dp_index ^ near ^ 1) * 2 + half]
        mlp_order = jnp.stack(mlp_order).astype(jnp.int32)
    save, branch_two, mlp_full = mlp(two, mlp_order, mlp_pieces)
    branch_two, cot = tie(branch_two, cot)
    down_low, down_t, result, sums_finish = by_image(
        finish_kernel, "finish", 1, (branch_two, middle), cot, mods, (bf16, True, False)
    )
    result = turn(result)

    e_orders = [(dp_index ^ jnp.array(halving_order(bits))).astype(jnp.int32) for bits in dp_bits]
    m_order = (mp_index ^ jnp.array(halving_order(mp_bits))).astype(jnp.int32)

    def by_owner(values):
        return values.reshape(dp_size, model_width // dp_size, -1)

    two_t, down_t = by_owner(two_t), by_owner(down_t)
    kept_one, sent_one, two_one = mlp_back(
        1, e_orders[1], two_t, down_t, down_low, save, mlp_full
    )
    got_one = swap(sent_one, "dp", dp_bits[1][0])
    kept_zero, sent_zero, two_zero = mlp_back(
        0, e_orders[0], two_t, down_t, down_low, save, mlp_full
    )
    got_zero = swap(sent_zero, "dp", dp_bits[0][0])
    kept_one, sent_one = sum_halves(kept_one, got_one)
    kept_zero, sent_zero = sum_halves(kept_zero, got_zero)
    two_zero, kept_one, kept_zero = tie(two_zero, kept_one, kept_zero)
    got_one = swap(sent_one, "dp", dp_bits[1][1])
    got_zero = swap(sent_zero, "dp", dp_bits[0][1])
    middle_grad, branch_low, branch_t, sums_middle = by_image(
        middle_kernel,
        "middle",
        100,
        (two_zero, two_one, middle, branch_one),
        cot,
        mods,
        (f32, bf16, True),
    )
    projected_low, gains_grad, sums_entry, latent_back = attend_back(
        latent, proj, branch_low, attend_full, gains_f, tables, middle_grad, mods
    )
    gains_grad = jnp.sum(gains_grad, axis=2) * jnp.array([[head_dim ** (-0.5)], [1.0]], f32)
    projected_low, got_one, got_zero = tie(projected_low, got_one, got_zero)
    packed = sums_finish + sums_middle + sums_entry
    gains_row = jnp.pad(gains_grad.reshape(1, 1, -1), ((0, own - 1), (7, 0), (0, model_width - 2 * head_dim)))
    packed = jnp.where(jnp.arange(8)[:, None] == 7, gains_row, packed).astype(bf16)
    packed = packed[None]
    stage, got_packed = 0, swap(packed, *gather_bits[0])

    def more(after, microseconds=0):
        nonlocal packed, got_packed, stage
        after, got_packed = tie(after, got_packed)
        packed = append(packed, got_packed, microseconds)
        stage += 1
        if stage < len(gather_bits):
            got_packed = swap(packed, *gather_bits[stage])
        return after

    kept_one, sent_one = sum_halves(kept_one, got_one, 200)
    kept_one = more(kept_one)
    kept_one, kept_zero = tie(kept_one, kept_zero)
    kept_zero, sent_zero = sum_halves(kept_zero, got_zero)
    normed_t, kept_one, kept_zero, result = tie(normed_t, kept_one, kept_zero, result)
    got_one = swap(sent_one, "dp", dp_bits[1][2])
    got_zero = swap(sent_zero, "dp", dp_bits[0][2])
    latent_back = turn(latent_back)

    normed_t, branch_t = by_owner(normed_t), by_owner(branch_t)

    attend_kept, attend_sent = attend_grads(
        m_order, jnp.concatenate(e_orders), normed_t, branch_t, projected_low, attended
    )
    attend_got = swap(attend_sent, "dp", dp_bits[0][0])

    attend_kept, got_one, got_zero, latent_back, got_packed = tie(
        attend_kept, got_one, got_zero, latent_back, got_packed
    )
    attend_kept = more(attend_kept, 200)
    attend_got, packed = tie(attend_got, packed)
    attend_zero, sent_zero, attend_one, sent_one = sum_quarters(attend_kept, attend_got)
    mlp_one = halve(add_low(kept_one, got_one), "dp", dp_bits[1][3:], 2)
    mlp_zero = halve(add_low(kept_zero, got_zero), "dp", dp_bits[0][3:], 2)
    mlp_got = swap(mlp_one, "mp", mp_bits[0])

    latent_back, attend_zero, attend_one = tie(latent_back, attend_zero, attend_one)
    latent_back = latent_back.reshape(images, local_len, model_width)
    back_patches = take_rows(latent_back, back_slot, 200)
    attend_got_one = swap(sent_one, "dp", dp_bits[1][1])
    attend_got_zero = swap(sent_zero, "dp", dp_bits[0][1])
    back_patches, attend_zero, attend_one, result = tie(
        back_patches, attend_zero, attend_one, result
    )
    result = whole_arrays(copy_kernel, "copy_result", 0, result.shape, result)
    attend_zero, attend_one, result = tie(attend_zero, attend_one, result)
    attend_zero = more(attend_zero)
    attend_one, sent_one = sum_halves(attend_one, attend_got_one)
    attend_zero, sent_zero = sum_halves(attend_zero, attend_got_zero)
    back_patches, sent_one, sent_zero, mlp_zero = tie(back_patches, sent_one, sent_zero, mlp_zero)
    got_patches = lax.all_to_all(back_patches, "dp", split_axis=0, concat_axis=0, tiled=True)
    patch_grad = pick_rows(got_patches, home_index)
    attend_got_one = swap(sent_one, "dp", dp_bits[1][2])
    attend_got_zero = swap(sent_zero, "dp", dp_bits[0][2])
    while stage < len(gather_bits):
        mlp_zero = more(mlp_zero)
    packed = packed.reshape(total_images, 8, model_width)
    mod_all = packed[:, :6]
    gains_total = packed.reshape(-1, own, 8, model_width)[:, 0, 7, : 2 * head_dim]
    gains_total = jnp.sum(gains_total.astype(f32), axis=0).reshape(2, head_dim)
    gains_total = jnp.sum(
        jnp.where(order[:, None] == jnp.arange(head_dim)[None, :], gains_total[:, :, None], 0.0), axis=1
    )
    width_dp = model_width // dp_size
    width_mp = model_width // mp_size
    row0 = dp_index * width_dp
    silu_rows = lax.dynamic_slice_in_dim(silu_all, row0, width_dp, 1)
    mod_cols = lax.dynamic_slice_in_dim(mod_all, mp_index * width_mp, width_mp, 2)
    ada_grad = ein("id,ikc->dkc", silu_rows, mod_cols)
    ada_rows = lax.dynamic_slice_in_dim(ada_kinds, row0, width_dp, 1)
    silu_grad = ein("ikc,kdc->id", mod_all, ada_rows)
    cond_rows = lax.dynamic_slice_in_dim(cond_all, row0, width_dp, 1)
    silu_val, silu_pull = jax.vjp(jax.nn.silu, cond_rows)
    condition_low = silu_pull(silu_grad)[0].astype(bf16)
    time_grad = ein("in,id->nd", bin_hot, condition_low)
    class_grad = ein("in,id->nd", label_hot, condition_low)

    attend_one = halve(add_low(attend_one, attend_got_one), "dp", dp_bits[1][3:], 1)
    attend_zero = halve(add_low(attend_zero, attend_got_zero), "dp", dp_bits[0][3:], 1)
    mlp_grad = halve(add_low(mlp_zero, mlp_got), "mp", mp_bits[1:], 0)[0].astype(f32)
    attend_grad = add_low(attend_zero, swap(attend_one, "mp", mp_bits[0]))
    attend_grad = halve(attend_grad, "mp", mp_bits[1:], 0)[0].astype(f32)

    expand_grad = mlp_grad[:2].swapaxes(0, 1)
    down_grad = mlp_grad[2].T
    out_grad = attend_grad[:, 3 * local_dim :].T
    qkv_grad = lax.dot_general(
        attend_grad[:, : 3 * local_dim],
        jnp.array(places[: 3 * local_dim, None] == columns[: 3 * local_dim], f32),
        (((1,), (0,)), ((), ())),
        precision=lax.Precision.HIGHEST,
        preferred_element_type=f32,
    )
    qkv_grad = qkv_grad.reshape(-1, 3, local_dim)
    return (
        result.reshape(images, local_len, model_width),
        patch_grad,
        time_grad,
        class_grad,
        ada_grad,
        qkv_grad,
        gains_total,
        out_grad,
        expand_grad,
        down_grad,
    )


def solution(mesh):
    in_specs = (
        P("dp", "mp", None),
        P("dp", "mp", None),
        P("dp"),
        P("dp"),
        P(),
        P(),
        P(),
        P(),
        P(),
        P(None, None, "mp"),
        P(),
        P("mp", None),
        P(None, None, "mp"),
        P("mp", None),
    )
    out_specs = (
        P("dp", "mp", None),
        P("dp", "mp", None),
        P(None, "dp"),
        P(None, "dp"),
        P("dp", None, "mp"),
        P("dp", None, "mp"),
        P(),
        P("mp", "dp"),
        P("dp", None, "mp"),
        P("mp", "dp"),
    )
    return jax.shard_map(shards, mesh=mesh, in_specs=in_specs, out_specs=out_specs, check_vma=False)
```

```python
import functools
import math

import jax
import jax.numpy as jnp
import numpy as np
from jax import lax
from jax.experimental import pallas as pl
from jax.experimental.pallas import tpu as pltpu
from jax.sharding import PartitionSpec as P

GRID = 16
NCLS = 1000
NBINS = 16

epsilon = 1e-06
rope_base = 10000.0
f32 = jnp.float32
bf16 = jnp.bfloat16


def feature_order(head_dim):
    quarter = head_dim // 4
    firsts = list(range(quarter)) + list(range(2 * quarter, 3 * quarter))
    cut = len(firsts) // 8 * 8
    seconds = [i + quarter for i in firsts]
    return firsts[:cut] + seconds[:cut] + firsts[cut:] + seconds[cut:], cut


def rope_tables(position, head_dim):
    quarter = head_dim // 4
    order, cut = feature_order(head_dim)
    places = jnp.stack([position // GRID, position % GRID]).astype(f32)
    frequency = rope_base ** (-jnp.arange(quarter).astype(f32) / quarter)
    angle = (frequency[None, :, None] * places[:, None, :]).reshape(2 * quarter, -1)
    cosine, sine = jnp.cos(angle), jnp.sin(angle)
    cos_tab = jnp.concatenate([cosine[:cut], cosine[:cut], cosine[cut:], cosine[cut:]])
    sin_tab = jnp.concatenate([-sine[:cut], sine[:cut], -sine[cut:], sine[cut:]])
    return cos_tab, sin_tab


def partner(values, cut):
    rest = values[2 * cut :]
    half = rest.shape[0] // 2
    return jnp.concatenate(
        [values[cut : 2 * cut], values[:cut], pltpu.roll(rest, half, 0)], axis=0
    )


def head_scale(values):
    return lax.rsqrt(jnp.mean(values * values, axis=0, keepdims=True) + epsilon)


def dot_00(a, b):
    return lax.dot_general(a, b, (((0,), (0,)), ((), ())), preferred_element_type=f32)


def dot_11(a, b):
    return lax.dot_general(a, b, (((1,), (1,)), ((), ())), preferred_element_type=f32)


def dot_10(a, b):
    return lax.dot_general(a, b, (((1,), (0,)), ((), ())), preferred_element_type=f32)


def softmax_first(scores):
    shifted = jnp.exp(scores - jnp.max(scores, axis=0, keepdims=True))
    return shifted * (1.0 / jnp.sum(shifted, axis=0, keepdims=True))


def lasting(microseconds):
    return pl.CostEstimate(
        flops=int(microseconds * 1.1e9), bytes_accessed=1 << 10, transcendentals=0
    )


SHIFT_ONE, SCALE_ONE, GATE_ONE, SHIFT_TWO, SCALE_TWO, GATE_TWO, WEIGHT = range(7)


def row_of(mods, which):
    return mods[which : which + 1, :]


def rms(values):
    scale = lax.rsqrt(jnp.mean(values * values, -1, keepdims=True) + epsilon)
    return values * scale, scale


def rms_back(grad, unit, scale, scaling):
    grad = grad * (1.0 + scaling)
    return scale * (grad - unit * jnp.mean(grad * unit, -1, keepdims=True))


def row_sum(values):
    return jnp.sum(values, axis=0, keepdims=True)


def put_rows(sums_ref, image, rows):
    for which in range(sums_ref.shape[1]):
        value = rows.get(which, jnp.zeros((1, sums_ref.shape[2]), f32))
        sums_ref[image, which : which + 1, :] = value


def chunk_rows(ref, image):
    return jnp.concatenate([ref[chunk, image] for chunk in range(ref.shape[0])], axis=0)


def put_chunks(ref, image, values):
    size = ref.shape[2]
    for chunk in range(ref.shape[0]):
        ref[chunk, image] = values[chunk * size : (chunk + 1) * size]


def attend_kernel(
    latent_ref, mods_ref, w_ref, wo_ref, gains_ref, cos_ref, sin_ref,
    proj_ref, att_ref, branch_ref, xt_ref, middle_ref, two_ref, twot_ref, x_ref,
):
    own = mods_ref.shape[0]
    head_dim = gains_ref.shape[1]
    rows_all = att_ref.shape[1]
    length = xt_ref.shape[1] // own
    heads = range(rows_all // head_dim)
    cut = feature_order(head_dim)[1]
    group = pl.program_id(0)

    def place(image):
        return pl.ds(pl.multiple_of(image * length, length), length)

    @pl.when(group == 0)
    def _():
        def entry(image, carry):
            mods = mods_ref[image]
            unit = rms(chunk_rows(latent_ref, image).astype(f32))[0]
            x = (unit * (1.0 + row_of(mods, SCALE_ONE)) + row_of(mods, SHIFT_ONE)).astype(bf16)
            x_ref[place(image), :] = x
            xt_ref[:, place(image)] = x.T
            return carry

        lax.fori_loop(0, own, entry, 0)

    proj_ref[0] = dot_11(w_ref[0, : 3 * rows_all], x_ref[...])

    def heads_of(image, carry):
        tokens = place(image)
        cos_tab, sin_tab = cos_ref[...], sin_ref[...]
        lows = [[], [], []]
        for kind in range(2):
            for head in heads:
                start = kind * rows_all + head * head_dim
                raw = proj_ref[0, start : start + head_dim, tokens]
                scaled = raw * head_scale(raw) * gains_ref[kind]
                turned = scaled * cos_tab + partner(scaled, cut) * sin_tab
                lows[kind].append(turned.astype(bf16))
        for head in heads:
            start = 2 * rows_all + head * head_dim
            lows[2].append(proj_ref[0, start : start + head_dim, tokens].astype(bf16))
        scores = [dot_00(lows[1][head], lows[0][head]) for head in heads]
        probs = [softmax_first(score).astype(bf16) for score in scores]
        outs = [dot_10(lows[2][head], probs[head]) for head in heads]
        att_ref[group, :, tokens] = jnp.concatenate(outs, axis=0).astype(bf16)
        return carry

    lax.fori_loop(0, own, heads_of, 0, unroll=True)

    @pl.when(group == pl.num_programs(0) - 1)
    def _():
        groups = att_ref.shape[0]

        def leave(image, carry):
            tokens = place(image)
            mods = mods_ref[image]
            att = att_ref[:, :, tokens].reshape(groups * rows_all, length)
            branch = dot_00(att, wo_ref[...].reshape(groups * rows_all, -1))
            branch_ref[tokens, :] = branch.astype(bf16)
            latent = chunk_rows(latent_ref, image).astype(f32)
            middle = latent + row_of(mods, GATE_ONE) * branch
            middle_ref[tokens, :] = middle
            two = rms(middle)[0] * (1.0 + row_of(mods, SCALE_TWO)) + row_of(mods, SHIFT_TWO)
            two = two.astype(bf16)
            two_ref[tokens, :] = two
            twot_ref[:, tokens] = two.T
            return carry

        lax.fori_loop(0, own, leave, 0)


def attend_back_kernel(
    latent_ref, proj_ref, low_ref, w_ref, gains_ref, cos_ref, sin_ref, grad_ref, mods_ref,
    out_ref, gain_grad_ref, sums_ref, chunks_ref, cot_ref,
):
    own = mods_ref.shape[0]
    head_dim = gains_ref.shape[1]
    rows_all, tokens_all = proj_ref.shape[1] // 3, proj_ref.shape[2]
    length = tokens_all // own
    heads = range(rows_all // head_dim)
    cut = feature_order(head_dim)[1]
    group = pl.program_id(0)

    def place(image):
        return pl.ds(pl.multiple_of(image * length, length), length)

    @pl.when(group == 0)
    def _():
        gain_grad_ref[...] = jnp.zeros_like(gain_grad_ref)

    cot_ref[...] = dot_11(w_ref[group, 3 * rows_all :], low_ref[...])

    def heads_of(image, carry):
        tokens = place(image)
        cos_tab, sin_tab = cos_ref[...], sin_ref[...]
        lows, units, scales = [[], [], []], [[], []], [[], []]
        for kind in range(2):
            for head in heads:
                start = kind * rows_all + head * head_dim
                raw = proj_ref[0, start : start + head_dim, tokens]
                scale = head_scale(raw)
                unit = raw * scale
                scaled = unit * gains_ref[kind]
                turned = scaled * cos_tab + partner(scaled, cut) * sin_tab
                lows[kind].append(turned.astype(bf16))
                units[kind].append(unit)
                scales[kind].append(scale)
        cots = []
        for head in heads:
            start = 2 * rows_all + head * head_dim
            lows[2].append(proj_ref[0, start : start + head_dim, tokens].astype(bf16))
            cots.append(cot_ref[head * head_dim : (head + 1) * head_dim, tokens].astype(bf16))
        scores = [dot_00(lows[1][head], lows[0][head]) for head in heads]
        prob_grads = [dot_00(lows[2][head], cots[head]) for head in heads]
        probs = [softmax_first(score) for score in scores]
        outs = [[], [], []]
        outs[2] = [dot_11(cots[head], probs[head].astype(bf16)) for head in heads]
        score_lows = []
        for head in heads:
            mean = jnp.sum(probs[head] * prob_grads[head], axis=0, keepdims=True)
            score_lows.append((probs[head] * (prob_grads[head] - mean)).astype(bf16))
        turned_grads = [
            [dot_10(lows[1][head], score_lows[head]) for head in heads],
            [dot_11(lows[0][head], score_lows[head]) for head in heads],
        ]
        for kind in range(2):
            total = 0.0
            for head in heads:
                grad, unit = turned_grads[kind][head], units[kind][head]
                grad = grad * cos_tab + partner(grad * sin_tab, cut)
                total = total + grad * unit
                grad = grad * gains_ref[kind]
                along = jnp.mean(grad * unit, axis=0, keepdims=True)
                outs[kind].append(scales[kind][head] * (grad - unit * along))
            gain_grad_ref[kind] += total
        grads = jnp.concatenate(outs[0] + outs[1] + outs[2], axis=0).astype(bf16)
        out_ref[group, :, tokens] = grads
        return carry

    lax.fori_loop(0, own, heads_of, 0, unroll=True)

    @pl.when(group == pl.num_programs(0) - 1)
    def _():
        def leave(image, carry):
            tokens = place(image)
            mods = mods_ref[image]
            grad = 0.0
            for other in range(out_ref.shape[0]):
                grad = grad + dot_00(out_ref[other, :, tokens], w_ref[other, : 3 * rows_all])
            unit, scale = rms(chunk_rows(latent_ref, image).astype(f32))
            sums = {SHIFT_ONE: row_sum(grad), SCALE_ONE: row_sum(grad * unit)}
            put_rows(sums_ref, image, sums)
            grad = grad_ref[tokens, :] + rms_back(grad, unit, scale, row_of(mods, SCALE_ONE))
            put_chunks(chunks_ref, image, grad.astype(bf16))
            return carry

        lax.fori_loop(0, own, leave, 0)


def whole_spec(shape):
    return pl.BlockSpec(shape, lambda g: (0,) * len(shape), pipeline_mode=pl.Buffered(1))


def attend(latent, mods, weights, gains, tables):
    groups, rows, width = weights.shape[0], weights.shape[1] // 4, weights.shape[2]
    own = mods.shape[0]
    length, head_dim = tables[0].shape[1], gains.shape[1]
    tokens = own * length
    total, turned = (tokens, width), (width, tokens)
    const = lambda shape: pl.BlockSpec(shape, lambda g: (0,) * len(shape))
    return pl.pallas_call(
        attend_kernel,
        grid=(groups,),
        in_specs=[
            whole_spec(latent.shape),
            whole_spec(mods.shape),
            pl.BlockSpec((1, 4 * rows, width), lambda g: (g, 0, 0)),
            pl.BlockSpec((groups, rows, width), lambda g: (0, 3, 0), pipeline_mode=pl.Buffered(1)),
            whole_spec(gains.shape),
            whole_spec(tables[0].shape),
            whole_spec(tables[0].shape),
        ],
        out_specs=[
            pl.BlockSpec((1, 3 * rows, tokens), lambda g: (g, 0, 0)),
            const((groups, rows, tokens)),
            const(total),
            const(turned),
            const(total),
            const(total),
            const(turned),
        ],
        out_shape=[
            jax.ShapeDtypeStruct((groups, 3 * rows, tokens), f32),
            jax.ShapeDtypeStruct((groups, rows, tokens), bf16),
            jax.ShapeDtypeStruct(total, bf16),
            jax.ShapeDtypeStruct(turned, bf16),
            jax.ShapeDtypeStruct(total, f32),
            jax.ShapeDtypeStruct(total, bf16),
            jax.ShapeDtypeStruct(turned, bf16),
        ],
        scratch_shapes=[pltpu.VMEM(total, bf16)],
        compiler_params=pltpu.CompilerParams(vmem_limit_bytes=62 << 20),
        cost_estimate=lasting(160),
        name="attend",
    )(latent, mods, weights, weights, gains, *tables)


def attend_back(latent, proj, low, weights, gains, tables, grad, mods):
    groups, rows, width = weights.shape[0], weights.shape[1] // 4, weights.shape[2]
    own = mods.shape[0]
    tokens = low.shape[0]
    length, head_dim = tokens // own, gains.shape[1]
    const = lambda shape: pl.BlockSpec(shape, lambda g: (0,) * len(shape))
    gain_shape = (2, head_dim, length)
    return pl.pallas_call(
        attend_back_kernel,
        grid=(groups,),
        in_specs=[
            whole_spec(latent.shape),
            pl.BlockSpec((1, 3 * rows, tokens), lambda g: (g, 0, 0)),
            whole_spec(low.shape),
            whole_spec(weights.shape),
            whole_spec(gains.shape),
            whole_spec(tables[0].shape),
            whole_spec(tables[0].shape),
            whole_spec(grad.shape),
            whole_spec(mods.shape),
        ],
        out_specs=[const(proj.shape), const(gain_shape), const(mods.shape), const(latent.shape)],
        out_shape=[
            jax.ShapeDtypeStruct(proj.shape, bf16),
            jax.ShapeDtypeStruct(gain_shape, f32),
            jax.ShapeDtypeStruct(mods.shape, f32),
            jax.ShapeDtypeStruct(latent.shape, bf16),
        ],
        scratch_shapes=[pltpu.VMEM((rows, tokens), f32)],
        compiler_params=pltpu.CompilerParams(vmem_limit_bytes=62 << 20),
        cost_estimate=lasting(1),
        name="attend_back",
    )(latent, proj, low, weights, gains, *tables, grad, mods)


def finish_kernel(
    branch_ref, middle_ref, cot_ref, mods_ref, low_ref, lowt_ref, chunks_ref, sums_ref
):
    branch, mods = branch_ref[...], mods_ref[0]
    gate = row_of(mods, GATE_TWO)
    result = (middle_ref[...] + gate * branch).astype(bf16)
    put_chunks(chunks_ref, 0, result)
    cot = chunk_rows(cot_ref, 0).astype(f32) * row_of(mods, WEIGHT)
    low = (gate * cot).astype(bf16)
    low_ref[...] = low
    lowt_ref[...] = low.T
    put_rows(sums_ref, 0, {GATE_TWO: row_sum(cot * branch)})


def middle_kernel(
    one_ref, other_ref, middle_ref, branch_ref, cot_ref, mods_ref,
    grad_ref, low_ref, lowt_ref, sums_ref,
):
    mods = mods_ref[0]
    grad = one_ref[...] + other_ref[...]
    unit, scale = rms(middle_ref[...])
    sums = {SHIFT_TWO: row_sum(grad), SCALE_TWO: row_sum(grad * unit)}
    cot = chunk_rows(cot_ref, 0).astype(f32) * row_of(mods, WEIGHT)
    grad = cot + rms_back(grad, unit, scale, row_of(mods, SCALE_TWO))
    grad_ref[...] = grad
    low = (row_of(mods, GATE_ONE) * grad).astype(bf16)
    low_ref[...] = low
    lowt_ref[...] = low.T
    sums[GATE_ONE] = row_sum(grad * branch_ref[...].astype(f32))
    put_rows(sums_ref, 0, sums)


def by_image(kernel, name, microseconds, rows, chunks, mods, outs):
    own, sums, width = mods.shape
    tokens = rows[0].shape[0]
    length = tokens // own
    block = pl.BlockSpec((length, width), lambda i: (i, 0))
    turned = pl.BlockSpec((width, length), lambda i: (0, i))
    chunk = pl.BlockSpec((chunks.shape[0], 1) + chunks.shape[2:], lambda i: (0, i, 0, 0))
    whole = pl.BlockSpec((1, sums, width), lambda i: (i, 0, 0))
    specs, shapes = [], []
    for out in outs:
        if out is True:
            specs.append(turned)
            shapes.append(jax.ShapeDtypeStruct((width, tokens), bf16))
        elif out is False:
            specs.append(chunk)
            shapes.append(jax.ShapeDtypeStruct(chunks.shape, bf16))
        else:
            specs.append(block)
            shapes.append(jax.ShapeDtypeStruct((tokens, width), out))
    return pl.pallas_call(
        kernel,
        grid=(own,),
        in_specs=[block] * len(rows) + [chunk, whole],
        out_specs=specs + [whole],
        out_shape=shapes + [jax.ShapeDtypeStruct(mods.shape, f32)],
        compiler_params=pltpu.CompilerParams(vmem_limit_bytes=60 << 20),
        cost_estimate=lasting(microseconds),
        name=name,
    )(*rows, chunks, mods)


def modulate_kernel(silu_ref, ada_ref, out_ref):
    out_ref[0] = dot_10(silu_ref[...], ada_ref[0])


def modulate(silu, ada):
    kinds, width = ada.shape[:2]
    return pl.pallas_call(
        modulate_kernel,
        grid=(kinds,),
        in_specs=[
            pl.BlockSpec(silu.shape, lambda k: (0, 0)),
            pl.BlockSpec((1, width, width), lambda k: (k, 0, 0)),
        ],
        out_specs=pl.BlockSpec((1,) + silu.shape, lambda k: (k, 0, 0)),
        out_shape=jax.ShapeDtypeStruct((kinds,) + silu.shape, f32),
        compiler_params=pltpu.CompilerParams(vmem_limit_bytes=60 << 20),
        cost_estimate=lasting(0),
        name="modulate",
    )(silu, ada)


def add_rows(out_ref, part, first, index, length):
    rows = pl.ds(pl.multiple_of(index * length, length), length)

    @pl.when(first)
    def _():
        out_ref[rows, :] = part

    @pl.when(jnp.logical_not(first))
    def _():
        out_ref[rows, :] += part


def sigmoid(values):
    return 1.0 / (1.0 + jnp.exp(-values))


def mlp_kernel(count, e_ref, x_ref, *refs):
    first = pl.program_id(0) == 0
    save_ref, out_ref, w_ref = refs[count:]
    unit = min(ref.shape[2] for ref in refs[:count])
    for index, ref in enumerate(refs[:count]):
        rows = pl.ds(pl.multiple_of(e_ref[index] * unit, unit), ref.shape[2])
        for kind in range(3):
            w_ref[0, kind, rows, :] = ref[0, kind]
    x = x_ref[...]
    gate = dot_11(x, w_ref[0, 0])
    up = dot_11(x, w_ref[0, 1])
    save_ref[0, 0] = gate.astype(bf16)
    save_ref[0, 1] = up.astype(bf16)
    hidden = (gate * sigmoid(gate) * up).astype(bf16)
    part = dot_10(hidden, w_ref[0, 2])
    add_rows(out_ref, part, first, 0, x.shape[0])


def mlp(x, order, pieces):
    groups, _, _, width = pieces[0].shape
    units, tokens = sum(piece.shape[2] for piece in pieces), x.shape[0]
    return pl.pallas_call(
        functools.partial(mlp_kernel, len(pieces)),
        grid_spec=pltpu.PrefetchScalarGridSpec(
            num_scalar_prefetch=1,
            grid=(groups,),
            in_specs=[pl.BlockSpec((tokens, width), lambda g, e: (0, 0), pipeline_mode=pl.Buffered(1))]
            + [pl.BlockSpec((1,) + piece.shape[1:], lambda g, e: (g, 0, 0, 0)) for piece in pieces],
            out_specs=[
                pl.BlockSpec((1, 2, tokens, units), lambda g, e: (g, 0, 0, 0)),
                pl.BlockSpec((tokens, width), lambda g, e: (0, 0)),
                pl.BlockSpec((1, 3, units, width), lambda g, e: (g, 0, 0, 0)),
            ],
        ),
        out_shape=[
            jax.ShapeDtypeStruct((groups, 2, tokens, units), bf16),
            jax.ShapeDtypeStruct((tokens, width), f32),
            jax.ShapeDtypeStruct((groups, 3, units, width), bf16),
        ],
        compiler_params=pltpu.CompilerParams(vmem_limit_bytes=62 << 20),
        cost_estimate=lasting(1),
        name="mlp",
    )(order, x, *pieces)


def fill_rows(order_ref, source_ref, target_ref, base=0):
    blocks, rows = source_ref.shape[0], source_ref.shape[1]
    for place in range(blocks):
        target_ref[place * rows : (place + 1) * rows, :] = source_ref[order_ref[base + place]]


def mlp_back_kernel(
    e_ref, xt_ref, lowt_ref, low_ref, save_ref, w_ref,
    keep_ref, send_ref, two_ref, xs, lows, parts,
):
    first = pl.program_id(0) == 0
    tokens, width = low_ref.shape
    step = math.gcd(tokens, 512)

    @pl.when(first)
    def _():
        fill_rows(e_ref, xt_ref, xs)
        fill_rows(e_ref, lowt_ref, lows)

    for index in range(tokens // step):
        rows = pl.ds(index * step, step)
        hidden_grad = dot_11(low_ref[rows, :], w_ref[0, 2])
        gate = save_ref[0, 0, rows, :].astype(f32)
        up = save_ref[0, 1, rows, :].astype(f32)
        sig = sigmoid(gate)
        swish = gate * sig
        gate_low = (hidden_grad * up * (sig + swish * (1.0 - sig))).astype(bf16)
        up_low = (hidden_grad * swish).astype(bf16)
        parts[0, rows, :] = gate_low
        parts[1, rows, :] = up_low
        parts[2, rows, :] = (swish * up).astype(bf16)
        part = dot_10(gate_low, w_ref[0, 0]) + dot_10(up_low, w_ref[0, 1])
        add_rows(two_ref, part, first, index, step)

    half = width // 2
    for out_ref, rows in ((keep_ref, slice(0, half)), (send_ref, slice(half, width))):
        x_rows = xs[rows, :]
        for kind in range(2):
            out_ref[0, kind] = dot_10(x_rows, parts[kind]).astype(bf16)
        out_ref[0, 2] = dot_10(lows[rows, :], parts[2]).astype(bf16)


def mlp_back(which, e_order, xt, lowt, low, save, weights):
    groups, _, units, width = weights.shape
    tokens = low.shape[0]
    blocks = groups // 2
    base = which * blocks
    once = pl.Buffered(1)
    whole = lambda p, e: (0, 0)
    whole3 = lambda p, e: (0, 0, 0)
    half = jax.ShapeDtypeStruct((blocks, 3, width // 2, units), bf16)
    half_spec = pl.BlockSpec((1, 3, width // 2, units), lambda p, e: (p, 0, 0, 0))
    return pl.pallas_call(
        mlp_back_kernel,
        grid_spec=pltpu.PrefetchScalarGridSpec(
            num_scalar_prefetch=1,
            grid=(blocks,),
            in_specs=[
                pl.BlockSpec(xt.shape, whole3, pipeline_mode=once),
                pl.BlockSpec(lowt.shape, whole3, pipeline_mode=once),
                pl.BlockSpec((tokens, width), whole, pipeline_mode=once),
                pl.BlockSpec((1, 2, tokens, units), lambda p, e: (base + p, 0, 0, 0)),
                pl.BlockSpec((1, 3, units, width), lambda p, e: (base + p, 0, 0, 0)),
            ],
            out_specs=[half_spec, half_spec, pl.BlockSpec((tokens, width), whole)],
            scratch_shapes=[
                pltpu.VMEM((width, tokens), bf16),
                pltpu.VMEM((width, tokens), bf16),
                pltpu.VMEM((3, tokens, units), bf16),
            ],
        ),
        out_shape=[half, half, jax.ShapeDtypeStruct((tokens, width), f32)],
        compiler_params=pltpu.CompilerParams(vmem_limit_bytes=62 << 20),
        cost_estimate=lasting(150),
        name="mlp_back",
    )(e_order, xt, lowt, low, save, weights)


def attend_grads_kernel(
    m_ref, e_ref, xt_ref, lowt_ref, proj_ref, att_ref, keep_ref, send_ref, xs, lows
):
    first = pl.num_programs(0) // 2 == pl.program_id(0)
    base = jnp.where(first, xt_ref.shape[0], 0)

    @pl.when(first | (pl.program_id(0) == 0))
    def _():
        fill_rows(e_ref, xt_ref, xs, base)
        fill_rows(e_ref, lowt_ref, lows, base)

    width = xs.shape[0]
    half = width // 2
    columns = proj_ref.shape[1]

    for out_ref, rows in ((keep_ref, slice(0, half)), (send_ref, slice(half, width))):
        out_ref[0, :, :columns] = dot_11(xs[rows, :], proj_ref[0]).astype(bf16)
        out_ref[0, :, columns:] = dot_11(lows[rows, :], att_ref[0]).astype(bf16)


def attend_grads(m_order, e_orders, xt, lowt, proj, att):
    rows, tokens = att.shape[1:]
    width = xt.shape[0] * xt.shape[1]
    blocks = m_order.shape[0]
    whole3 = lambda p, m, e: (0, 0, 0)
    half = jax.ShapeDtypeStruct((blocks, width // 2, 4 * rows), bf16)
    half_spec = pl.BlockSpec((1, width // 2, 4 * rows), lambda p, m, e: (p, 0, 0))
    return pl.pallas_call(
        attend_grads_kernel,
        grid_spec=pltpu.PrefetchScalarGridSpec(
            num_scalar_prefetch=2,
            grid=(blocks,),
            in_specs=[
                pl.BlockSpec(xt.shape, whole3, pipeline_mode=pl.Buffered(1)),
                pl.BlockSpec(lowt.shape, whole3, pipeline_mode=pl.Buffered(1)),
                pl.BlockSpec((1, 3 * rows, tokens), lambda p, m, e: (m[p], 0, 0)),
                pl.BlockSpec((1, rows, tokens), lambda p, m, e: (m[p], 0, 0)),
            ],
            out_specs=[half_spec, half_spec],
            scratch_shapes=[
                pltpu.VMEM((width, tokens), bf16),
                pltpu.VMEM((width, tokens), bf16),
            ],
        ),
        out_shape=[half, half],
        compiler_params=pltpu.CompilerParams(vmem_limit_bytes=56 << 20),
        cost_estimate=lasting(0),
        name="attend_grads",
    )(m_order, e_orders, xt, lowt, proj, att)


def dot(a, b):
    return jnp.dot(a, b, preferred_element_type=f32)


def ein(spec, a, b):
    return jnp.einsum(spec, a, b, preferred_element_type=f32)


def gather_pieces(piece, mp_size):
    whole = lax.all_gather(piece, ("mp", "dp"), axis=0, tiled=False)
    return whole.reshape((mp_size, -1) + piece.shape)


def pick_rows(values, index):
    return values.at[index].get(mode="promise_in_bounds")


def take_rows_kernel(index_ref, *refs):
    out_ref = refs[-1]
    count = len(refs) - 1
    base = pl.program_id(0) * count
    for place, ref in enumerate(refs[:-1]):
        live = index_ref[base + place] >= 0

        @pl.when(live)
        def _():
            out_ref[place] = ref[0]

        @pl.when(jnp.logical_not(live))
        def _():
            out_ref[place] = jnp.zeros_like(ref[0])


def take_rows(values, index, microseconds=0):
    number = index.shape[0]
    count = math.gcd(number, 4)
    block = values.shape[1:]
    specs = [
        pl.BlockSpec(
            (1,) + block,
            functools.partial(
                lambda place, i, index: (jnp.maximum(index[i * count + place], 0), 0, 0), place
            ),
        )
        for place in range(count)
    ]
    return pl.pallas_call(
        take_rows_kernel,
        grid_spec=pltpu.PrefetchScalarGridSpec(
            num_scalar_prefetch=1,
            grid=(number // count,),
            in_specs=specs,
            out_specs=pl.BlockSpec((count,) + block, lambda i, index: (i, 0, 0)),
        ),
        out_shape=jax.ShapeDtypeStruct((number,) + block, values.dtype),
        compiler_params=pltpu.CompilerParams(vmem_limit_bytes=60 << 20),
        cost_estimate=lasting(microseconds),
        name="take_rows",
    )(index.astype(jnp.int32), *([values] * count))


def sum_quarters_kernel(kept_ref, got_ref, *out_refs):
    total = (kept_ref[0].astype(f32) + got_ref[0].astype(f32)).astype(bf16)
    half = total.shape[0] // 2
    later = pl.program_id(0) >= pl.num_programs(0) // 2

    @pl.when(jnp.logical_not(later))
    def _():
        out_refs[0][0] = total[:half]
        out_refs[1][0] = total[half:]

    @pl.when(later)
    def _():
        out_refs[2][0] = total[:half]
        out_refs[3][0] = total[half:]


def sum_quarters(kept, got):
    groups, rows, columns = kept.shape
    if rows % 32:
        halves = split(add_low(kept, got), 0)
        return split(halves[0], 1) + split(halves[1], 1)
    part = groups // 2
    whole = pl.BlockSpec((1, rows, columns), lambda i: (i, 0, 0))
    block = (1, rows // 2, columns)
    early = pl.BlockSpec(block, lambda i: (jnp.minimum(i, part - 1), 0, 0))
    late = pl.BlockSpec(block, lambda i: (jnp.maximum(i - part, 0), 0, 0))
    return pl.pallas_call(
        sum_quarters_kernel,
        grid=(groups,),
        in_specs=[whole, whole],
        out_specs=[early, early, late, late],
        out_shape=[jax.ShapeDtypeStruct((part, rows // 2, columns), bf16)] * 4,
        compiler_params=pltpu.CompilerParams(vmem_limit_bytes=60 << 20),
        cost_estimate=lasting(0),
        name="sum_quarters",
    )(kept, got)


def whole_arrays(kernel, name, microseconds, shape, *arrays):
    specs = [pl.BlockSpec(array.shape, functools.partial(lambda n: (0,) * n, array.ndim)) for array in arrays]
    return pl.pallas_call(
        kernel,
        in_specs=specs,
        out_specs=pl.BlockSpec(shape, lambda: (0,) * len(shape)),
        out_shape=jax.ShapeDtypeStruct(shape, arrays[0].dtype),
        compiler_params=pltpu.CompilerParams(vmem_limit_bytes=60 << 20),
        cost_estimate=lasting(microseconds),
        name=name,
    )(*arrays)


def copy_kernel(value_ref, out_ref):
    out_ref[...] = value_ref[...]


def append_kernel(one_ref, other_ref, out_ref):
    count = one_ref.shape[0]
    out_ref[:count] = one_ref[...]
    out_ref[count:] = other_ref[...]


def append(one, other, microseconds):
    shape = (2 * one.shape[0],) + one.shape[1:]
    return whole_arrays(append_kernel, "append", microseconds, shape, one, other)


def bits_of(size):
    return [1 << i for i in range(size.bit_length() - 1)]


def swap(values, axis, bit):
    size = lax.axis_size(axis)
    return lax.ppermute(values, axis, [(i, i ^ bit) for i in range(size)])


def halving_order(bits):
    order = [0]
    for bit in reversed(bits):
        order = order + [place ^ bit for place in order]
    return order


def add_low(kept, received):
    return (kept.astype(f32) + received.astype(f32)).astype(bf16)


def sum_halves_kernel(kept_ref, got_ref, first_ref, second_ref):
    total = (kept_ref[0].astype(f32) + got_ref[0].astype(f32)).astype(bf16)
    half = first_ref.shape[1]
    first_ref[0] = total[:half]
    second_ref[0] = total[half:]


def sum_halves(kept, got, microseconds=0):
    rows, columns = kept.shape[-2:]
    if rows % 32:
        return split(add_low(kept, got), kept.ndim - 2)
    shape = kept.shape[:-2] + (rows // 2, columns)
    kept, got = kept.reshape(-1, rows, columns), got.reshape(-1, rows, columns)
    whole = pl.BlockSpec((1, rows, columns), lambda i: (i, 0, 0))
    half = pl.BlockSpec((1, rows // 2, columns), lambda i: (i, 0, 0))
    halves = pl.pallas_call(
        sum_halves_kernel,
        grid=(kept.shape[0],),
        in_specs=[whole, whole],
        out_specs=[half, half],
        out_shape=[jax.ShapeDtypeStruct((kept.shape[0], rows // 2, columns), bf16)] * 2,
        compiler_params=pltpu.CompilerParams(vmem_limit_bytes=60 << 20),
        cost_estimate=lasting(microseconds),
        name="sum_halves",
    )(kept, got)
    return halves[0].reshape(shape), halves[1].reshape(shape)


def tie(*values):
    return lax.optimization_barrier(values)


def split(values, dim):
    size = values.shape[dim] // 2
    return [
        lax.slice_in_dim(values, 0, size, axis=dim),
        lax.slice_in_dim(values, size, 2 * size, axis=dim),
    ]


def halve(values, axis, bits, dim):
    for bit in bits:
        kept, sent = split(values, dim)
        values = add_low(kept, swap(sent, axis, bit))
    return values


def shards(
    patches,
    cotangent,
    time_bins,
    labels,
    image_counts,
    dest_perm,
    time_table,
    class_table,
    ada_weight,
    qkv_weight,
    norm_gains,
    out_weight,
    expand_weight,
    down_weight,
):
    dp_size = lax.axis_size("dp")
    mp_size = lax.axis_size("mp")
    capacity = patches.shape[0]
    slot_count = capacity // dp_size
    images = cotangent.shape[0]
    local_len = patches.shape[1]
    model_width = patches.shape[2]
    length = local_len * mp_size
    head_dim = norm_gains.shape[1]
    local_dim = out_weight.shape[0]
    unit_count = down_weight.shape[0]
    own = images // mp_size
    total_images = images * dp_size
    order = np.array(feature_order(head_dim)[0])
    columns = np.arange(4 * local_dim)
    places = columns // head_dim * head_dim + order[columns % head_dim]
    places = np.where(columns < 2 * local_dim, places, columns).astype(np.int32)
    gains_f = norm_gains.astype(f32)[:, order]
    gains_f = (gains_f * jnp.array([[head_dim ** (-0.5)], [1.0]], f32))[:, :, None]
    dp_index = lax.axis_index("dp")
    mp_index = lax.axis_index("mp")
    dp_bits = bits_of(dp_size)
    dp_bits = (dp_bits, dp_bits[:1] + dp_bits[1:][::-1])
    mp_bits = bits_of(mp_size)

    tables = rope_tables(jnp.arange(length), head_dim)

    def turn(chunks):
        return lax.all_to_all(chunks, "mp", split_axis=0, concat_axis=0, tiled=True)

    starts = jnp.cumsum(image_counts) - image_counts
    finish = starts + image_counts
    my_start = starts[dp_index]
    my_count = image_counts[dp_index]
    device_ids = jnp.arange(dp_size)
    matches = (dest_perm[:, None] == device_ids[None, :]).astype(jnp.int32)
    inverse = jnp.sum(device_ids[:, None] * matches, axis=0)
    my_place = inverse[dp_index]
    pair_ids = jnp.arange(dp_size * slot_count)
    pair_peer = pair_ids // slot_count
    pair_slot = pair_ids % slot_count
    send_index = pair_slot * dp_size + jnp.mod(inverse[pair_peer] - my_start, dp_size)
    send_index = jnp.minimum(send_index, capacity - 1)
    send_patches = pick_rows(patches, send_index)
    time_bins, labels, send_patches = tie(time_bins, labels, send_patches)
    recv_patches = lax.all_to_all(send_patches, "dp", split_axis=0, concat_axis=0, tiled=True)
    info = append(time_bins[None], labels[None], 200)[None]
    qkv_weight, out_weight, expand_weight, down_weight, info = tie(
        qkv_weight, out_weight, expand_weight, down_weight, info
    )
    got_info = swap(info, "dp", dp_bits[0][0])

    share = 4 * local_dim // dp_size
    spots = lax.dynamic_slice_in_dim(jnp.array(places), dp_index * share, share, 0)
    take_qkv = (spots[:, None] == jnp.arange(3 * local_dim)[None, :]).astype(bf16)
    take_out = (spots[:, None] - 3 * local_dim == jnp.arange(local_dim)[None, :]).astype(bf16)
    attend_piece = dot(take_qkv, qkv_weight.transpose(1, 2, 0).reshape(-1, model_width))
    attend_piece = (attend_piece + dot(take_out, out_weight)).astype(bf16)
    share = unit_count // dp_size
    spots = dp_index * share + jnp.arange(share)
    take_units = (spots[:, None] == jnp.arange(unit_count)[None, :]).astype(bf16)
    expand_kinds = tie(expand_weight.swapaxes(0, 1))[0]
    mlp_piece = jnp.stack(
        [
            dot_11(take_units, expand_kinds[0]).astype(bf16),
            dot_11(take_units, expand_kinds[1]).astype(bf16),
            lax.dynamic_slice_in_dim(down_weight, dp_index * share, share, 0),
        ]
    )
    attend_full = gather_pieces(attend_piece, mp_size).reshape(mp_size, 4 * local_dim, -1)
    by_permutes = share % 32 == 0 and dp_size == 8 and mp_size == 4
    if by_permutes:
        mlp_near = mlp_piece[None]
        far_near = swap(mlp_near, "mp", 2)
    else:
        mlp_full = gather_pieces(mlp_piece, mp_size)
        mlp_full = mlp_full.swapaxes(1, 2).reshape(mp_size, 3, unit_count, model_width)
        mlp_pieces = [mlp_full[mp_index ^ jnp.array(halving_order(mp_bits))]]
        mlp_order = jnp.zeros((1,), jnp.int32)

    rank_ids = jnp.arange(images) * dp_size + my_place
    source = jnp.sum((finish[None, :] <= rank_ids[:, None]).astype(jnp.int32), axis=1)
    within = rank_ids - starts[source]
    recv_index = source * slot_count + within // dp_size

    info_places = [0]
    for step, bit in enumerate(dp_bits[0]):
        info = append(info, got_info, 200 if step == 1 else 0)
        info_places = info_places + [place ^ bit for place in info_places]
        if by_permutes and step == 0:
            mlp_near = jnp.concatenate([mlp_near, far_near], axis=0)
            far_near = swap(mlp_near, "mp", 1)
            info, mlp_near = tie(info, mlp_near)
        if by_permutes and step == 1:
            latent = pick_rows(recv_patches, recv_index)
            far_near, info, _ = tie(far_near, info, latent)
            mlp_near = append(mlp_near, far_near, 200)
            halves = split(mlp_near, 2)
        if step + 1 < len(dp_bits[0]):
            got_info = swap(info, "dp", dp_bits[0][step + 1])
    if not by_permutes:
        latent = pick_rows(recv_patches, recv_index)
    latent = turn(latent.reshape(mp_size, own, local_len, model_width))

    info = info.swapaxes(0, 1).reshape(2, -1)
    info_owner = jnp.repeat(dp_index ^ jnp.array(info_places), capacity)
    info_slot = jnp.tile(jnp.arange(capacity), dp_size)
    info_count = jnp.sum(
        jnp.where(info_owner[:, None] == device_ids[None, :], image_counts[None, :], 0), axis=1
    )
    live_all = info_slot < info_count
    bin_totals = jnp.sum(
        ((info[0][:, None] == jnp.arange(NBINS)[None, :]) & live_all[:, None]).astype(f32), axis=0
    )
    gather_bits = [("mp", bit) for bit in mp_bits[::-1]]
    gather_bits = gather_bits + [("dp", bit) for bit in dp_bits[0][1:] + dp_bits[0][:1]]
    spread = {"dp": [0], "mp": [0]}
    for axis, bit in gather_bits:
        spread = {
            name: spread[name] + [place ^ (bit if name == axis else 0) for place in spread[name]]
            for name in spread
        }
    owner_all = jnp.repeat(dp_index ^ jnp.array(spread["dp"]), own)
    group_all = jnp.repeat(mp_index ^ jnp.array(spread["mp"]), own)
    row_all = group_all * own + jnp.tile(jnp.arange(own), dp_size * mp_size)
    place_all = jnp.sum(
        jnp.where(owner_all[:, None] == device_ids[None, :], inverse[None, :], 0), axis=1
    )
    rank_all = row_all * dp_size + place_all
    source_all = jnp.sum((finish[None, :] <= rank_all[:, None]).astype(jnp.int32), axis=1)
    start_all = jnp.sum(
        jnp.where(source_all[:, None] == device_ids[None, :], starts[None, :], 0), axis=1
    )
    slots_all = source_all * capacity + rank_all - start_all
    slot_hit = slots_all[:, None] == (info_owner * capacity + info_slot)[None, :]
    bins_all = jnp.sum(jnp.where(slot_hit, info[0][None, :], 0), axis=1)
    labels_all = jnp.sum(jnp.where(slot_hit, info[1][None, :], 0), axis=1)
    bin_hot = (bins_all[:, None] == jnp.arange(NBINS)[None, :])
    label_hot = (labels_all[:, None] == jnp.arange(NCLS)[None, :])
    weights_all = total_images / (NBINS * jnp.sum(bin_hot.astype(f32) * bin_totals[None, :], axis=1))
    bin_hot = bin_hot.astype(bf16)
    label_hot = label_hot.astype(bf16)
    cond_all = (dot(bin_hot, time_table) + dot(label_hot, class_table)).astype(bf16).astype(f32)
    silu_all = jax.nn.silu(cond_all).astype(bf16)
    silu_cond = silu_all[:own]
    weights = weights_all[:own]

    ada_kinds = ada_weight.swapaxes(0, 1)
    modulation = modulate(jnp.pad(silu_cond, ((0, -own % 16), (0, 0))), ada_kinds)[:, :own]
    mods = jnp.concatenate(
        [
            modulation.swapaxes(0, 1),
            jnp.broadcast_to(weights[:, None, None], (own, 1, model_width)),
            jnp.zeros((own, 1, model_width), f32),
        ],
        axis=1,
    )
    mods, starts, image_counts, dest_perm, my_place = tie(mods, starts, image_counts, dest_perm, my_place)
    back_within = pair_slot * dp_size + jnp.mod(my_place - starts[pair_peer], dp_size)
    back_valid = back_within < image_counts[pair_peer]
    back_slot = jnp.clip((starts[pair_peer] + back_within - my_place) // dp_size, 0, images - 1)
    back_slot = jnp.where(back_valid, back_slot, -1)
    slot_ids = jnp.arange(capacity)
    home_peer = dest_perm[jnp.mod(my_start + slot_ids, dp_size)]
    home_index = home_peer * slot_count + jnp.minimum(slot_ids // dp_size, slot_count - 1)
    mods, back_slot, home_index = tie(mods, back_slot, home_index)

    if by_permutes:
        orders = ((2, 4), (4, 2))
        parts = [{bit: swap(halves[half], "dp", bit) for bit in orders[half]} for half in range(2)]
        cored = swap(mlp_near, "dp", 1)
        latent, parts[0][2], parts[1][4], cored = tie(latent, parts[0][2], parts[1][4], cored)
        got = [swap(parts[half][orders[half][0]], "dp", orders[half][1]) for half in range(2)]

    cotangent, latent = tie(cotangent, latent)
    proj, attended, branch_one, normed_t, middle, two, two_t = attend(
        latent, mods, attend_full, gains_f, tables
    )
    cot = turn(cotangent.reshape(mp_size, own, local_len, model_width))
    if by_permutes:
        got[0], got[1], attended = tie(got[0], got[1], attended)
        mlp_pieces, mlp_order = [mlp_near, cored], [dp_index * 2, (dp_index ^ 1) * 2]
        for half in range(2):
            parts[half][6] = got[half]
            for near, part in parts[half].items():
                mlp_pieces += [part, swap(part, "dp", 1)]
                mlp_order += [(dp_index ^ near) * 2 + half, (dp_index ^ near ^ 1) * 2 + half]
        mlp_order = jnp.stack(mlp_order).astype(jnp.int32)
    save, branch_two, mlp_full = mlp(two, mlp_order, mlp_pieces)
    branch_two, cot = tie(branch_two, cot)
    down_low, down_t, result, sums_finish = by_image(
        finish_kernel, "finish", 1, (branch_two, middle), cot, mods, (bf16, True, False)
    )
    result = turn(result)

    e_orders = [(dp_index ^ jnp.array(halving_order(bits))).astype(jnp.int32) for bits in dp_bits]
    m_order = (mp_index ^ jnp.array(halving_order(mp_bits))).astype(jnp.int32)

    def by_owner(values):
        return values.reshape(dp_size, model_width // dp_size, -1)

    two_t, down_t = by_owner(two_t), by_owner(down_t)
    kept_one, sent_one, two_one = mlp_back(
        1, e_orders[1], two_t, down_t, down_low, save, mlp_full
    )
    got_one = swap(sent_one, "dp", dp_bits[1][0])
    kept_zero, sent_zero, two_zero = mlp_back(
        0, e_orders[0], two_t, down_t, down_low, save, mlp_full
    )
    got_zero = swap(sent_zero, "dp", dp_bits[0][0])
    kept_one, sent_one = sum_halves(kept_one, got_one)
    kept_zero, sent_zero = sum_halves(kept_zero, got_zero)
    two_zero, kept_one, kept_zero = tie(two_zero, kept_one, kept_zero)
    got_one = swap(sent_one, "dp", dp_bits[1][1])
    got_zero = swap(sent_zero, "dp", dp_bits[0][1])
    middle_grad, branch_low, branch_t, sums_middle = by_image(
        middle_kernel,
        "middle",
        100,
        (two_zero, two_one, middle, branch_one),
        cot,
        mods,
        (f32, bf16, True),
    )
    projected_low, gains_grad, sums_entry, latent_back = attend_back(
        latent, proj, branch_low, attend_full, gains_f, tables, middle_grad, mods
    )
    gains_grad = jnp.sum(gains_grad, axis=2) * jnp.array([[head_dim ** (-0.5)], [1.0]], f32)
    projected_low, got_one, got_zero = tie(projected_low, got_one, got_zero)
    packed = sums_finish + sums_middle + sums_entry
    gains_row = jnp.pad(gains_grad.reshape(1, 1, -1), ((0, own - 1), (7, 0), (0, model_width - 2 * head_dim)))
    packed = jnp.where(jnp.arange(8)[:, None] == 7, gains_row, packed).astype(bf16)
    packed = packed[None]
    stage, got_packed = 0, swap(packed, *gather_bits[0])

    def more(after, microseconds=0):
        nonlocal packed, got_packed, stage
        after, got_packed = tie(after, got_packed)
        packed = append(packed, got_packed, microseconds)
        stage += 1
        if stage < len(gather_bits):
            got_packed = swap(packed, *gather_bits[stage])
        return after

    kept_one, sent_one = sum_halves(kept_one, got_one, 200)
    kept_one = more(kept_one)
    kept_one, kept_zero = tie(kept_one, kept_zero)
    kept_zero, sent_zero = sum_halves(kept_zero, got_zero)
    normed_t, kept_one, kept_zero, result = tie(normed_t, kept_one, kept_zero, result)
    got_one = swap(sent_one, "dp", dp_bits[1][2])
    got_zero = swap(sent_zero, "dp", dp_bits[0][2])
    latent_back = turn(latent_back)

    normed_t, branch_t = by_owner(normed_t), by_owner(branch_t)

    attend_kept, attend_sent = attend_grads(
        m_order, jnp.concatenate(e_orders), normed_t, branch_t, projected_low, attended
    )
    attend_got = swap(attend_sent, "dp", dp_bits[0][0])

    attend_kept, got_one, got_zero, latent_back, got_packed = tie(
        attend_kept, got_one, got_zero, latent_back, got_packed
    )
    attend_kept = more(attend_kept, 200)
    attend_got, packed = tie(attend_got, packed)
    attend_zero, sent_zero, attend_one, sent_one = sum_quarters(attend_kept, attend_got)
    mlp_one = halve(add_low(kept_one, got_one), "dp", dp_bits[1][3:], 2)
    mlp_zero = halve(add_low(kept_zero, got_zero), "dp", dp_bits[0][3:], 2)
    mlp_got = swap(mlp_one, "mp", mp_bits[0])

    latent_back, attend_zero, attend_one = tie(latent_back, attend_zero, attend_one)
    latent_back = latent_back.reshape(images, local_len, model_width)
    back_patches = take_rows(latent_back, back_slot, 200)
    attend_got_one = swap(sent_one, "dp", dp_bits[1][1])
    attend_got_zero = swap(sent_zero, "dp", dp_bits[0][1])
    back_patches, attend_zero, attend_one, result = tie(
        back_patches, attend_zero, attend_one, result
    )
    result = whole_arrays(copy_kernel, "copy_result", 0, result.shape, result)
    attend_zero, attend_one, result = tie(attend_zero, attend_one, result)
    attend_zero = more(attend_zero)
    attend_one, sent_one = sum_halves(attend_one, attend_got_one)
    attend_zero, sent_zero = sum_halves(attend_zero, attend_got_zero)
    back_patches, sent_one, sent_zero, mlp_zero = tie(back_patches, sent_one, sent_zero, mlp_zero)
    got_patches = lax.all_to_all(back_patches, "dp", split_axis=0, concat_axis=0, tiled=True)
    patch_grad = pick_rows(got_patches, home_index)
    attend_got_one = swap(sent_one, "dp", dp_bits[1][2])
    attend_got_zero = swap(sent_zero, "dp", dp_bits[0][2])
    while stage < len(gather_bits):
        mlp_zero = more(mlp_zero)
    packed = packed.reshape(total_images, 8, model_width)
    mod_all = packed[:, :6]
    gains_total = packed.reshape(-1, own, 8, model_width)[:, 0, 7, : 2 * head_dim]
    gains_total = jnp.sum(gains_total.astype(f32), axis=0).reshape(2, head_dim)
    gains_total = jnp.sum(
        jnp.where(order[:, None] == jnp.arange(head_dim)[None, :], gains_total[:, :, None], 0.0), axis=1
    )
    width_dp = model_width // dp_size
    width_mp = model_width // mp_size
    row0 = dp_index * width_dp
    silu_rows = lax.dynamic_slice_in_dim(silu_all, row0, width_dp, 1)
    mod_cols = lax.dynamic_slice_in_dim(mod_all, mp_index * width_mp, width_mp, 2)
    ada_grad = ein("id,ikc->dkc", silu_rows, mod_cols)
    ada_rows = lax.dynamic_slice_in_dim(ada_kinds, row0, width_dp, 1)
    silu_grad = ein("ikc,kdc->id", mod_all, ada_rows)
    cond_rows = lax.dynamic_slice_in_dim(cond_all, row0, width_dp, 1)
    silu_val, silu_pull = jax.vjp(jax.nn.silu, cond_rows)
    condition_low = silu_pull(silu_grad)[0].astype(bf16)
    time_grad = ein("in,id->nd", bin_hot, condition_low)
    class_grad = ein("in,id->nd", label_hot, condition_low)

    attend_one = halve(add_low(attend_one, attend_got_one), "dp", dp_bits[1][3:], 1)
    attend_zero = halve(add_low(attend_zero, attend_got_zero), "dp", dp_bits[0][3:], 1)
    mlp_grad = halve(add_low(mlp_zero, mlp_got), "mp", mp_bits[1:], 0)[0].astype(f32)
    attend_grad = add_low(attend_zero, swap(attend_one, "mp", mp_bits[0]))
    attend_grad = halve(attend_grad, "mp", mp_bits[1:], 0)[0].astype(f32)

    expand_grad = mlp_grad[:2].swapaxes(0, 1)
    down_grad = mlp_grad[2].T
    out_grad = attend_grad[:, 3 * local_dim :].T
    qkv_grad = lax.dot_general(
        attend_grad[:, : 3 * local_dim],
        jnp.array(places[: 3 * local_dim, None] == columns[: 3 * local_dim], f32),
        (((1,), (0,)), ((), ())),
        precision=lax.Precision.HIGHEST,
        preferred_element_type=f32,
    )
    qkv_grad = qkv_grad.reshape(-1, 3, local_dim)
    return (
        result.reshape(images, local_len, model_width),
        patch_grad,
        time_grad,
        class_grad,
        ada_grad,
        qkv_grad,
        gains_total,
        out_grad,
        expand_grad,
        down_grad,
    )


def solution(mesh):
    in_specs = (
        P("dp", "mp", None),
        P("dp", "mp", None),
        P("dp"),
        P("dp"),
        P(),
        P(),
        P(),
        P(),
        P(),
        P(None, None, "mp"),
        P(),
        P("mp", None),
        P(None, None, "mp"),
        P("mp", None),
    )
    out_specs = (
        P("dp", "mp", None),
        P("dp", "mp", None),
        P(None, "dp"),
        P(None, "dp"),
        P("dp", None, "mp"),
        P("dp", None, "mp"),
        P(),
        P("mp", "dp"),
        P("dp", None, "mp"),
        P("mp", "dp"),
    )
    return jax.shard_map(shards, mesh=mesh, in_specs=in_specs, out_specs=out_specs, check_vma=False)
```
